32 devices in a mesh: seq: 16 (over z, x, core), heads: 2 (over y).
Axes of the slice: x: 2, y: 2, z: 4, core: 2. Of those that a mesh axis runs over, the one named last changes fastest.
Arguments:
- tokens: bfloat16 [16384, 768], P('seq'), may hold values from -6 to 6
- cotangent: float32 [16384, 768], P('seq'), may hold values from -6 to 6
- valid_tiles: int32 [16384], P('seq'), may hold values from 0 to 1, as said below
- gain_first: float32 [768], replicated, may hold values from 0.25 to 1.75
- shift_first: float32 [768], replicated, may hold values from -4 to 4
- w_project: bfloat16 [768, 3, 768], P(None, None, 'heads'), may hold values from -0.21875 to 0.21875
- bias_project: float32 [2, 768], P(None, 'heads'), may hold values from -0.3125 to 0.3125
- w_output: bfloat16 [768, 768], P('heads'), may hold values from -4 to 4
- bias_output: float32 [768], replicated, may hold values from -4 to 4
- gain_second: float32 [768], replicated, may hold values from 0.25 to 1.75
- shift_second: float32 [768], replicated, may hold values from -4 to 4
- w_expand: bfloat16 [768, 3072], P(None, 'heads'), may hold values from -0.21875 to 0.21875
- bias_expand: float32 [3072], P('heads'), may hold values from -4 to 4
- w_reduce: bfloat16 [3072, 768], P('heads'), may hold values from -0.109375 to 0.109375
- bias_reduce: float32 [768], replicated, may hold values from -4 to 4
Outputs:
- layer_out: float32 [16384, 768], P('seq')
- grad_tokens: float32 [16384, 768], P('seq')
- grad_gain_first: float32 [768], replicated
- grad_shift_first: float32 [768], replicated
- grad_w_project: float32 [768, 3, 768], P(None, None, 'heads')
- grad_bias_project: float32 [2, 768], P(None, 'heads')
- grad_w_output: float32 [768, 768], P('heads')
- grad_bias_output: float32 [768], replicated
- grad_gain_second: float32 [768], replicated
- grad_shift_second: float32 [768], replicated
- grad_w_expand: float32 [768, 3072], P(None, 'heads')
- grad_bias_expand: float32 [3072], P('heads')
- grad_w_reduce: float32 [3072, 768], P('heads')
- grad_bias_reduce: float32 [768], replicated
The draws below stay inside these ranges and needn't reach their ends.
Inputs may be any that keep to these rules, and one draw needn't show every extreme that they name: `valid_tiles`: in each aligned run of 16384 tiles the valid ones come first and at least one is valid; in some run more than 15360 are valid and at least one is padding.
All inputs are finite; a program needn't handle non-finite values.
Results may differ from the reference program's by a relative error of at most 0.02.
Values may be sent and summed in bfloat16 or wider, within the bound.
A program may use at most 256 MiB of HBM per device.

```python
import jax
import jax.numpy as jnp
from jax import lax

D = 768
HEADS = 16
HEAD_DIM = 48
FF = 3072
SEGMENT = 1024
BRANCHES = 5
SPAN = 16384
TOK_DEV = 1024
TOKENS = 16384
N_HEADS = 2


def draw_valid_tiles(key, part):
    key = jax.random.fold_in(key, 11)
    level_key, jitter_key, reach_key, short_key = jax.random.split(key, 4)
    run_count = TOKENS // SPAN
    level = jax.random.randint(level_key, (run_count,), 0, 5)
    base = jnp.where(level < 2, SPAN, jnp.right_shift(jnp.int32(SPAN), jnp.maximum(level - 1, 0)))
    jitter = jax.random.randint(jitter_key, (run_count,), 0, 1 << 30) % (base // 16 + 1)
    jitter = jnp.where(level < 2, 0, jitter)
    counts = base - jitter
    reach_run = jax.random.randint(reach_key, (), 0, run_count)
    reach_count = SPAN - 1 - jax.random.randint(short_key, (), 0, TOK_DEV - 1)
    counts = jnp.where(jnp.arange(run_count, dtype=jnp.int32) == reach_run, reach_count, counts)
    places = jnp.arange(TOKENS, dtype=jnp.int32)
    return (places % SPAN < counts[places // SPAN]).astype(jnp.int32)


def shard_levels(stream_key, shape, shards, smallest, top_value):
    level = 1.0
    for dim, shards_of in shards:
        steps = jax.random.uniform(jax.random.fold_in(jax.random.fold_in(stream_key, 6), dim), (shards_of,), jnp.float32, smallest / len(shards), top_value / len(shards))
        level = level * jnp.repeat(jnp.exp(steps), shape[dim] // shards_of).reshape((-1,) + (1,) * (len(shape) - 1 - dim))
    return level


def gaussian(rng, dims, scale, most, shards=(), held_as=jnp.bfloat16):
    loudness = shard_levels(rng, dims, shards, -0.22, 0.18) if shards else 1.0
    entries = jax.random.normal(rng, dims, jnp.float32) * scale * loudness
    return jnp.minimum(jnp.maximum(entries, -most), most).astype(held_as)


def setup_inputs(seed: int = 0) -> dict:
    splits = jax.random.split(jax.random.key(seed), 16)
    return {
        "tokens": gaussian(splits[0], (TOKENS, D), 1.0, 6.0, ((0, 16),)),
        "cotangent": gaussian(splits[1], (TOKENS, D), 1.0, 6.0, ((0, 16),), jnp.float32),
        "valid_tiles": draw_valid_tiles(jax.random.fold_in(splits[15], 71), 0),
        "gain_first": jnp.clip(1.0 + 0.15 * jax.random.normal(splits[3], (D,), jnp.float32), 0.25, 1.75),
        "shift_first": gaussian(splits[4], (D,), 0.3, 4.0, (), jnp.float32),
        "w_project": gaussian(splits[5], (D, 3, D), D ** -0.5, 0.21875, ((2, 2),)),
        "bias_project": gaussian(splits[6], (2, D), 0.02, 0.3125, ((1, 2),), jnp.float32),
        "w_output": gaussian(splits[7], (D, D), 1.0, 4.0, ((0, 2),)),
        "bias_output": gaussian(splits[8], (D,), 0.3, 4.0, (), jnp.float32),
        "gain_second": jnp.clip(1.0 + 0.15 * jax.random.normal(splits[9], (D,), jnp.float32), 0.25, 1.75),
        "shift_second": gaussian(splits[10], (D,), 0.3, 4.0, (), jnp.float32),
        "w_expand": gaussian(splits[11], (D, FF), D ** -0.5, 0.21875, ((1, 2),)),
        "bias_expand": gaussian(splits[12], (FF,), 0.3, 4.0, ((0, 2),), jnp.float32),
        "w_reduce": gaussian(splits[13], (FF, D), FF ** -0.5, 0.109375, ((0, 2),)),
        "bias_reduce": gaussian(splits[14], (D,), 0.3, 4.0, (), jnp.float32),
    }


@jax.custom_vjp
def low(v):
    return lax.optimization_barrier(v.astype(jnp.bfloat16)).astype(jnp.float32)

@jax.custom_vjp
def low_back(v):
    return v

def low_keep(v):
    return (low(v), None)

def low_pass(kept, grad):
    return (grad,)

def back_keep(v):
    return (v, None)

def back_low(kept, grad):
    return (low(grad),)
low.defvjp(low_keep, low_pass)
low_back.defvjp(back_keep, back_low)
highest = lax.Precision.HIGHEST
masked_score = -1000000000.0
absent_top = -1e+30

def norm_rows(values, gain, shift):
    mean_row = lax.optimization_barrier(jnp.mean(values, axis=-1, keepdims=True))
    centered = values - mean_row
    variance = lax.optimization_barrier(jnp.mean(centered * centered, axis=-1, keepdims=True))
    return centered * lax.rsqrt(variance + 1e-05) * gain + shift

def pick_rows(rows, stride, offset):
    seg_width = SEGMENT * stride
    shaped = rows.reshape((rows.shape[0] // seg_width, SEGMENT, stride) + rows.shape[1:])
    return lax.dynamic_index_in_dim(shaped, offset, axis=2, keepdims=False)

def spread_rows(part, stride, offset, filler):
    chosen = (jnp.arange(stride, dtype=jnp.int32) == offset).reshape((1, 1, stride) + (1,) * (part.ndim - 2))
    expanded = jnp.where(chosen, jnp.expand_dims(part, 2), filler)
    return expanded.reshape((part.shape[0] * part.shape[1] * stride,) + part.shape[2:])

def head_attention(queries, key_rows, value_rows, key_valid, head_number):
    score_scale = HEAD_DIM ** (-0.5)
    branch_list = []
    best = jnp.full((SPAN,), absent_top, jnp.float32)
    for branch in range(BRANCHES):
        stride = 2 ** branch
        offset = head_number % stride
        scores = jnp.einsum('sqd,skd->sqk', pick_rows(queries, stride, offset), pick_rows(key_rows, stride, offset), precision=highest)
        scores = low_back(scores * score_scale)
        live = pick_rows(key_valid, stride, offset)
        scores = jnp.where(live[:, None, :] > 0, scores, masked_score)
        best = jnp.maximum(best, spread_rows(lax.optimization_barrier(jnp.max(scores, axis=-1)), stride, offset, absent_top))
        branch_list.append((scores, stride, offset))
    row_total = jnp.zeros((SPAN,), jnp.float32)
    raised_list = []
    for scores, stride, offset in branch_list:
        raised = jnp.exp(scores - pick_rows(best, stride, offset)[:, :, None])
        row_total = row_total + spread_rows(lax.optimization_barrier(jnp.sum(raised, axis=-1)), stride, offset, 0.0)
        raised_list.append(raised)
    result = jnp.zeros((SPAN, HEAD_DIM), jnp.float32)
    for (scores, stride, offset), raised in zip(branch_list, raised_list):
        probs = low(raised / pick_rows(row_total, stride, offset)[:, :, None])
        mixed = jnp.einsum('sqk,skd->sqd', probs, pick_rows(value_rows, stride, offset), precision=highest)
        result = result + spread_rows(mixed, stride, offset, 0.0)
    return result

def block_attention(queries, key_rows, value_rows, key_valid):

    def by_heads(array):
        return array.reshape(SPAN, HEADS, HEAD_DIM).transpose(1, 0, 2)

    def one_head(pieces):
        return head_attention(pieces[0], pieces[1], pieces[2], key_valid, pieces[3])
    heads_out = lax.map(jax.checkpoint(one_head), (by_heads(queries), by_heads(key_rows), by_heads(value_rows), jnp.arange(HEADS, dtype=jnp.int32)))
    return heads_out.transpose(1, 0, 2).reshape(SPAN, D)

def block_layer(params, inputs, key_valid):
    gain_first, shift_first, w_project, bias_project, w_output, bias_output, gain_second, shift_second, w_expand, bias_expand, w_reduce, bias_reduce = params
    group_width = D // N_HEADS
    group_hidden = FF // N_HEADS
    normed = low(norm_rows(inputs, gain_first, shift_first))
    query_parts, key_parts, value_parts = ([], [], [])
    for group in range(N_HEADS):
        columns = slice(group * group_width, (group + 1) * group_width)
        entry = low_back(normed)
        project = jnp.einsum('td,dce->tce', entry, w_project[:, :, columns], precision=highest)
        query_parts.append(low(low_back(project[:, 0]) + bias_project[0, columns]))
        key_parts.append(low(low_back(project[:, 1])))
        value_parts.append(low(low_back(project[:, 2]) + bias_project[1, columns]))
    queries = jnp.concatenate(query_parts, axis=1)
    key_rows = jnp.concatenate(key_parts, axis=1)
    value_rows = jnp.concatenate(value_parts, axis=1)
    attended = low_back(low(block_attention(queries, key_rows, value_rows, key_valid)))
    branch_out = bias_output
    for group in range(N_HEADS):
        columns = slice(group * group_width, (group + 1) * group_width)
        branch_out = branch_out + low_back(low(jnp.dot(attended[:, columns], w_output[columns], precision=highest)))
    middle = inputs + branch_out
    normed_two = low(norm_rows(middle, gain_second, shift_second))
    reduced = bias_reduce
    for group in range(N_HEADS):
        columns = slice(group * group_hidden, (group + 1) * group_hidden)
        entry = low_back(normed_two)
        expand = low_back(jnp.dot(entry, w_expand[:, columns], precision=highest)) + bias_expand[columns]
        active = low(jax.nn.gelu(expand, approximate=True))
        reduced = reduced + low_back(low(jnp.dot(active, w_reduce[columns], precision=highest)))
    return middle + reduced

def reference(tokens, cotangent, valid_tiles, gain_first, shift_first, w_project, bias_project, w_output, bias_output, gain_second, shift_second, w_expand, bias_expand, w_reduce, bias_reduce):
    params = tuple((entry.astype(jnp.float32) for entry in (gain_first, shift_first, w_project, bias_project, w_output, bias_output, gain_second, shift_second, w_expand, bias_expand, w_reduce, bias_reduce)))
    inputs = tokens.astype(jnp.float32)

    def forward(rows_in, weights):
        blocks_in = rows_in.reshape(TOKENS // SPAN, SPAN, D)
        blocks_valid = valid_tiles.reshape(TOKENS // SPAN, SPAN)

        def one_block(pair):
            return block_layer(weights, pair[0], pair[1])
        outputs = lax.map(jax.checkpoint(one_block), (blocks_in, blocks_valid))
        return outputs.reshape(TOKENS, D)
    layer_out, pullback = jax.vjp(forward, inputs, params)
    grad_tokens, grads = pullback(cotangent.astype(jnp.float32))
    return (layer_out, grad_tokens, grads[0], grads[1], grads[2], grads[3], grads[4], grads[5], grads[6], grads[7], grads[8], grads[9], grads[10], grads[11])
```

```python
import functools
import math

import jax
import jax.numpy as jnp
from jax import lax
from jax.experimental import pallas as pl
from jax.experimental.pallas import tpu as pltpu
from jax.sharding import PartitionSpec as P

HEADS = 16
HEAD_DIM = 48
SEGMENT = 1024
BRANCHES = 5
LOCAL = 8

MESH = pl.DeviceIdType.MESH
BF = jnp.bfloat16
F32 = jnp.float32
NT = (((1,), (1,)), ((), ()))
TN = (((0,), (0,)), ((), ()))
NN = (((1,), (0,)), ((), ()))

masked_score = -1000000000.0
layer_eps = 1e-05
SCALE = HEAD_DIM ** (-0.5)
LOG2E = math.log2(math.e)


def dot(a, b, dims):
    return lax.dot_general(a, b, dims, preferred_element_type=F32)


def lanes(shape):
    return lax.broadcasted_iota(jnp.int32, shape, len(shape) - 1)


def reversed_bits(value, bits):
    out = value * 0
    for k in range(bits):
        out = out * 2 + (value // 2**k) % 2
    return out


def split3(value):
    high = value.astype(BF).astype(F32)
    rest = value - high
    middle = rest.astype(BF).astype(F32)
    return high, middle, rest - middle


class Place:
    def __init__(self):
        self.me = lax.axis_index("seq")
        self.y = lax.axis_index("heads")

    def member(self, b):
        return self.me % 2**b

    def device(self, b, j):
        return (self.me // 2**b * 2**b + j, self.y)

    def start(self, b, head):
        stride = 2**b
        place = (self.y * LOCAL + head) % stride
        return pl.multiple_of(reversed_bits(place, b) * (SEGMENT // stride), SEGMENT // stride)

    def greet(self):
        barrier = pltpu.get_barrier_semaphore()
        i = self.member(4)

        def signal(d, _):
            pl.semaphore_signal(barrier, inc=1, device_id=self.device(4, (i + d) % 16), device_id_type=MESH)
            return 0

        lax.fori_loop(1, 16, signal, 0)
        pl.semaphore_wait(barrier, 15)


def remote(src, dst, send, recv, device):
    return pltpu.make_async_remote_copy(
        src_ref=src, dst_ref=dst, send_sem=send, recv_sem=recv, device_id=device, device_id_type=MESH
    )


def over_peers(b, body):
    tiles = max(LOCAL // 2**b, 1)

    def step(d, _):
        for t in range(tiles):
            body(d, t)
        return 0

    lax.fori_loop(1, 2**b, step, 0)


def ds(start, size):
    return pl.ds(pl.multiple_of(start, size), size)


def attend(q, kv):
    scores = dot(q, kv, NT)
    top = jnp.max(scores, axis=1, keepdims=True)
    raised = jnp.exp2(scores - top).astype(BF)
    return dot(raised, kv, NN), top


def packed(out, top):
    lane = lanes(out.shape)
    total = out[:, 112:113]
    tile = jnp.where(lane == 112, 1.0, out * (1.0 / total))
    for k, piece in enumerate(split3(top) + split3(total)):
        tile = jnp.where(lane == 114 + k, piece, tile)
    return tile.astype(BF)


def forward_kernel(
    x_ref, fin_ref, att_ref, x1, x2, x3, q4, kv4, acc, tops, o1, o2, o3, o4, r1, r2, r3, r4, *sems
):
    place = Place()
    me = place.me
    xs, os, rs = (None, x1, x2, x3), (None, o1, o2, o3, o4), (None, r1, r2, r3, r4)
    go_send, go_recv, back_send, back_recv = sems[0:4], sems[4:8], sems[8:12], sems[12:16]

    def go(b, d, t):
        n, tiles = SEGMENT // 2**b, max(LOCAL // 2**b, 1)
        i = place.member(b)
        j = (i + d) % 2**b
        if b < 4:
            head = j * tiles + t
            k = (d - 1) * tiles + t
            return [
                remote(
                    x_ref.at[head, pl.ds(place.start(b, head), n), :],
                    xs[b].at[t, ds(i * n, n), :],
                    go_send[b - 1].at[k],
                    go_recv[b - 1].at[k],
                    place.device(b, j),
                )
            ]
        head, half = j // 2, j % 2
        start = place.start(4, head)
        k = (d - 1) * 2
        return [
            remote(
                x_ref.at[head, ds(start + half * 32, 32), 0:128],
                q4.at[ds(i * 32, 32), :],
                go_send[3].at[k],
                go_recv[3].at[k],
                place.device(4, j),
            ),
            remote(
                x_ref.at[head, pl.ds(start, 64), 128:256],
                kv4.at[ds(i * 64, 64), :],
                go_send[3].at[k + 1],
                go_recv[3].at[k + 1],
                place.device(4, j),
            ),
        ]

    def back(b, d, t):
        n, tiles = SEGMENT // 2**b, max(LOCAL // 2**b, 1)
        i = place.member(b)
        j = (i + d) % 2**b
        k = (d - 1) * tiles + t
        if b < 4:
            src, dst = o_at(b, t, j), rs[b].at[i * tiles + t]
        else:
            src, dst = o4.at[ds(j * 32, 32), :], r4.at[i // 2, ds(i % 2 * 32, 32), :]
        return remote(src, dst, back_send[b - 1].at[k], back_recv[b - 1].at[k], place.device(b, j))

    def o_at(b, t, j):
        n = SEGMENT // 2**b
        return os[b].at[t, ds(j * n, n), :]

    place.greet()
    for b in (4, 3, 2, 1):
        over_peers(b, lambda d, t: [c.start() for c in go(b, d, t)])

    for b in (1, 2, 3):
        n, tiles = SEGMENT // 2**b, LOCAL // 2**b
        i = place.member(b)
        for t in range(tiles):
            head = i * tiles + t
            xs[b][t, ds(i * n, n), :] = x_ref[head, pl.ds(place.start(b, head), n), :]
    i = place.member(4)
    start = place.start(4, i // 2)
    q4[ds(i * 32, 32), :] = x_ref[i // 2, ds(start + i % 2 * 32, 32), 0:128]
    kv4[ds(i * 64, 64), :] = x_ref[i // 2, pl.ds(start, 64), 128:256]

    def local_head(h, _):
        for half in range(2):
            rows = pl.ds(half * 512, 512)
            out, top = attend(x_ref[h, rows, 0:128], x_ref[h, :, 128:256])
            acc[h, rows, :] = out
            tops[h, rows, :] = jnp.broadcast_to(top, out.shape)
        return 0

    lax.fori_loop(0, 4, local_head, 0)

    over_peers(4, lambda d, t: [c.wait_recv() for c in go(4, d, t)])
    o4[...] = packed(*attend(q4[...], kv4[...]))
    over_peers(4, lambda d, t: back(4, d, t).start())
    r4[i // 2, ds(i % 2 * 32, 32), :] = o4[ds(i * 32, 32), :]
    for b in (3, 2, 1):
        n, tiles = SEGMENT // 2**b, LOCAL // 2**b
        over_peers(b, lambda d, t: [c.wait_recv() for c in go(b, d, t)])

        def tile(t, _):
            for half in range(2):
                rows = pl.ds(half * 512, 512)
                os[b][t, rows, :] = packed(*attend(xs[b][t, rows, 0:128], xs[b][t, :, 128:256]))
            return 0

        lax.fori_loop(0, tiles, tile, 0)
        over_peers(b, lambda d, t: back(b, d, t).start())
        j = place.member(b)
        for t in range(tiles):
            rs[b][j * tiles + t] = os[b][t, ds(j * n, n), :]

    lax.fori_loop(4, 8, local_head, 0)

    for b in (4, 3, 2, 1):
        over_peers(b, lambda d, t: back(b, d, t).wait_recv())

    row = lax.broadcasted_iota(jnp.int32, (128, 256), 0)
    column = lax.broadcasted_iota(jnp.int32, (128, 256), 1)
    first = jnp.where(column < 128, 114, 117)
    picks = jnp.where((row >= first) & (row < first + 3), 1.0, 0.0).astype(BF)

    def merge_head(h):
        for b in (1, 2, 3, 4):
            n = SEGMENT // 2**b
            rows = pl.ds(place.start(b, h), n)
            part = rs[b][h]
            stats = dot(part, picks, NN)
            top = jnp.maximum(tops[h, rows, :], stats[:, 0:128])
            keep = jnp.exp2(tops[h, rows, :] - top)
            gain = jnp.exp2(stats[:, 0:128] - top) * stats[:, 128:256]
            acc[h, rows, :] = acc[h, rows, :] * keep + part.astype(F32) * gain
            tops[h, rows, :] = top
        out = acc[h]
        lane = lanes(out.shape)
        inverse = 1.0 / out[:, 112:113]
        out = jnp.where((lane >= 64) & (lane < 112), out * inverse, 0.0)
        fin_ref[h] = jnp.where(lane == 112, inverse, jnp.where(lane == 113, tops[h], out))
        return out

    def pair(k, _):
        even, odd = merge_head(k * 2), merge_head(k * 2 + 1)
        att_ref[:, ds(k * 128, 128)] = (pltpu.roll(even, 64, 1) + odd).astype(BF)
        return 0

    lax.fori_loop(0, LOCAL // 2, pair, 0)

    for b in (4, 3, 2, 1):
        over_peers(b, lambda d, t: [c.wait_send() for c in go(b, d, t)])
        over_peers(b, lambda d, t: back(b, d, t).wait_send())


def sem_shapes(per_copy):
    counts = [4, 6, 7, 15 * per_copy]
    return [pltpu.SemaphoreType.DMA((c,)) for c in counts]


VMEM = pl.BlockSpec(memory_space=pltpu.VMEM)


def attention_forward(x):
    shapes = [
        ((LOCAL, SEGMENT, 128), F32),
        ((SEGMENT, LOCAL * 64), BF),
        ((4, SEGMENT, 256), BF),
        ((2, SEGMENT, 256), BF),
        ((1, SEGMENT, 256), BF),
        ((512, 128), BF),
        ((SEGMENT, 128), BF),
    ]
    scratch = [
        ((LOCAL, SEGMENT, 128), F32),
        ((LOCAL, SEGMENT, 128), F32),
        ((4, SEGMENT, 128), BF),
        ((2, SEGMENT, 128), BF),
        ((1, SEGMENT, 128), BF),
        ((512, 128), BF),
        ((LOCAL, 512, 128), BF),
        ((LOCAL, 256, 128), BF),
        ((LOCAL, 128, 128), BF),
        ((LOCAL, 64, 128), BF),
    ]
    return pl.pallas_call(
        forward_kernel,
        out_shape=[jax.ShapeDtypeStruct(*s) for s in shapes],
        in_specs=[VMEM],
        out_specs=[VMEM] * len(shapes),
        scratch_shapes=[pltpu.VMEM(*s) for s in scratch]
        + sem_shapes(2) + sem_shapes(2) + sem_shapes(1) + sem_shapes(1),
        compiler_params=pltpu.CompilerParams(
            collective_id=0, has_side_effects=True, vmem_limit_bytes=56 * 2**20
        ),
        name="attention_forward",
    )(x)


def pair_grads(q, d, kv_at, put):
    lane = lanes(q.shape)
    zero = jnp.zeros_like(d)
    queries = q + jnp.where(lane < 64, d, zero)
    grads = jnp.where(lane < 64, zero, d)
    total = None
    for half in range(2):
        kv = kv_at(half)
        probs = jnp.exp2(dot(kv, queries, NT))
        grad_scores = (probs * dot(kv, grads, NT)).astype(BF)
        put(half, dot(grad_scores, queries, NN) + dot(probs.astype(BF), grads, NN))
        part = dot(kv, grad_scores, TN)
        total = part if total is None else total + part
    return total.T


def backward_kernel(
    x_ref, x1, x2, x3, q4, kv4, fin_ref, do_ref, g_ref, sum_ref,
    d0, d1, d2, d3, d4, total, g1, g2, g3, gq4, gkv4, r1, r2, r3, rq4, rkv4, *sems
):
    place = Place()
    me = place.me
    xs, dd, gs, rs = (None, x1, x2, x3), (None, d1, d2, d3), (None, g1, g2, g3), (None, r1, r2, r3)
    go_send, go_recv, back_send, back_recv = sems[0:4], sems[4:8], sems[8:12], sems[12:16]

    def go(b, d, t):
        n, tiles = SEGMENT // 2**b, max(LOCAL // 2**b, 1)
        i = place.member(b)
        j = (i + d) % 2**b
        k = (d - 1) * tiles + t
        if b < 4:
            head = j * tiles + t
            src, dst = d0.at[head, pl.ds(place.start(b, head), n), :], dd[b].at[t, ds(i * n, n), :]
        else:
            start = place.start(4, j // 2)
            src, dst = d0.at[j // 2, ds(start + j % 2 * 32, 32), :], d4.at[ds(i * 32, 32), :]
        return remote(src, dst, go_send[b - 1].at[k], go_recv[b - 1].at[k], place.device(b, j))

    def back(b, d, t):
        n, tiles = SEGMENT // 2**b, max(LOCAL // 2**b, 1)
        i = place.member(b)
        j = (i + d) % 2**b
        device = place.device(b, j)
        if b < 4:
            k = (d - 1) * tiles + t
            return [
                remote(
                    gs[b].at[t, ds(j * n, n), :],
                    rs[b].at[i * tiles + t],
                    back_send[b - 1].at[k],
                    back_recv[b - 1].at[k],
                    device,
                )
            ]
        k = (d - 1) * 2
        return [
            remote(
                gq4.at[ds(j * 32, 32), :],
                rq4.at[i // 2, ds(i % 2 * 32, 32), :],
                back_send[3].at[k],
                back_recv[3].at[k],
                device,
            ),
            remote(
                gkv4.at[ds(j * 64, 64), :],
                rkv4.at[i % 2, i // 2],
                back_send[3].at[k + 1],
                back_recv[3].at[k + 1],
                device,
            ),
        ]

    def prepare(h, _):
        fin = fin_ref[h]
        lane = lanes(fin.shape)
        value_lane = (lane >= 64) & (lane < 112)
        grad = (do_ref[:, ds(h * 128, 128)].astype(F32) * fin[:, 112:113]).astype(BF).astype(F32)
        delta = jnp.sum(jnp.where(value_lane, grad * fin, 0.0), axis=1, keepdims=True)
        tile = jnp.where(value_lane, grad, 0.0)
        high, middle, low = split3(-delta)
        tile = jnp.where(lane == 112, high, jnp.where(lane == 113, middle, tile))
        for k, piece in enumerate(split3(-fin[:, 113:114])):
            tile = jnp.where(lane == 52 + k, piece, tile)
        d0[h] = tile.astype(BF)
        return 0

    lax.fori_loop(0, LOCAL, prepare, 0)
    place.greet()
    for b in (4, 3, 2, 1):
        over_peers(b, lambda d, t: go(b, d, t).start())
    for b in (1, 2, 3):
        n, tiles = SEGMENT // 2**b, LOCAL // 2**b
        i = place.member(b)
        for t in range(tiles):
            head = i * tiles + t
            dd[b][t, ds(i * n, n), :] = d0[head, pl.ds(place.start(b, head), n), :]
    i = place.member(4)
    d4[ds(i * 32, 32), :] = d0[i // 2, ds(place.start(4, i // 2) + i % 2 * 32, 32), :]

    def local_head(h, _):
        def put(half, grad):
            total[h, pl.ds(half * 512, 512), 128:256] = grad

        total[h, :, 0:128] = pair_grads(
            x_ref[h, :, 0:128], d0[h], lambda half: x_ref[h, pl.ds(half * 512, 512), 128:256], put
        )
        return 0

    lax.fori_loop(0, 4, local_head, 0)

    over_peers(4, lambda d, t: go(4, d, t).wait_recv())

    def put4(half, grad):
        gkv4[pl.ds(half * 512, 512), :] = grad.astype(BF)

    gq4[...] = pair_grads(q4[...], d4[...], lambda half: kv4[pl.ds(half * 512, 512), :], put4).astype(BF)
    over_peers(4, lambda d, t: [c.start() for c in back(4, d, t)])
    rq4[i // 2, ds(i % 2 * 32, 32), :] = gq4[ds(i * 32, 32), :]
    rkv4[i % 2, i // 2] = gkv4[ds(i * 64, 64), :]
    for b in (3, 2, 1):
        n, tiles = SEGMENT // 2**b, LOCAL // 2**b
        over_peers(b, lambda d, t: go(b, d, t).wait_recv())

        def tile(t, _):
            def put(half, grad):
                gs[b][t, pl.ds(half * 512, 512), 128:256] = grad.astype(BF)

            gs[b][t, :, 0:128] = pair_grads(
                xs[b][t, :, 0:128], dd[b][t], lambda half: xs[b][t, pl.ds(half * 512, 512), 128:256], put
            ).astype(BF)
            return 0

        lax.fori_loop(0, tiles, tile, 0)
        over_peers(b, lambda d, t: [c.start() for c in back(b, d, t)])
        j = place.member(b)
        for t in range(tiles):
            rs[b][j * tiles + t] = gs[b][t, ds(j * n, n), :]

    lax.fori_loop(4, 8, local_head, 0)

    for b in (4, 3, 2, 1):
        over_peers(b, lambda d, t: [c.wait_recv() for c in back(b, d, t)])

    def finish(h, _):
        for b in (1, 2, 3):
            n = SEGMENT // 2**b
            rows = pl.ds(place.start(b, h), n)
            total[h, rows, :] += rs[b][h].astype(F32)
        rows = pl.ds(place.start(4, h), 64)
        total[h, rows, 0:128] += rq4[h].astype(F32)
        total[h, rows, 128:256] += rkv4[0, h].astype(F32) + rkv4[1, h].astype(F32)
        grad = total[h]
        lane = lanes(grad.shape)
        live = (x_ref[h, :, 176:177].astype(F32) >= 0.0).astype(F32)
        key_factor = live * (1.0 / LOG2E)
        grad = jnp.where(
            lane < 48,
            grad * SCALE,
            jnp.where(
                (lane >= 128) & (lane < 176),
                grad * key_factor,
                jnp.where((lane >= 192) & (lane < 240), grad, 0.0),
            ),
        )
        g_ref[h] = grad.astype(BF)
        sum_ref[h] = jnp.broadcast_to(jnp.sum(grad, axis=0, keepdims=True), (8, 256))
        return 0

    lax.fori_loop(0, LOCAL, finish, 0)

    for b in (4, 3, 2, 1):
        over_peers(b, lambda d, t: go(b, d, t).wait_send())
        over_peers(b, lambda d, t: [c.wait_send() for c in back(b, d, t)])


def attention_backward(x, saved, fin, grad_out):
    shapes = [((LOCAL, SEGMENT, 256), BF), ((LOCAL, 8, 256), F32)]
    scratch = [
        ((LOCAL, SEGMENT, 128), BF),
        ((4, SEGMENT, 128), BF),
        ((2, SEGMENT, 128), BF),
        ((1, SEGMENT, 128), BF),
        ((512, 128), BF),
        ((LOCAL, SEGMENT, 256), F32),
        ((4, SEGMENT, 256), BF),
        ((2, SEGMENT, 256), BF),
        ((1, SEGMENT, 256), BF),
        ((512, 128), BF),
        ((SEGMENT, 128), BF),
        ((LOCAL, 512, 256), BF),
        ((LOCAL, 256, 256), BF),
        ((LOCAL, 128, 256), BF),
        ((LOCAL, 64, 128), BF),
        ((2, LOCAL, 64, 128), BF),
    ]
    return pl.pallas_call(
        backward_kernel,
        out_shape=[jax.ShapeDtypeStruct(*s) for s in shapes],
        in_specs=[VMEM] * 8,
        out_specs=[VMEM] * len(shapes),
        scratch_shapes=[pltpu.VMEM(*s) for s in scratch]
        + sem_shapes(1) + sem_shapes(1) + sem_shapes(2) + sem_shapes(2),
        compiler_params=pltpu.CompilerParams(
            collective_id=1, has_side_effects=True, vmem_limit_bytes=60 * 2**20
        ),
        name="attention_backward",
    )(x, *saved, fin, grad_out)


def norm_rows(values, gain, shift):
    mean_row = jnp.mean(values, axis=-1, keepdims=True)
    centered = values - mean_row
    variance = jnp.mean(centered * centered, axis=-1, keepdims=True)
    return centered * lax.rsqrt(variance + layer_eps) * gain + shift


def gelu_tanh(values):
    return jax.nn.gelu(values, approximate=True)


ORDER = tuple(int(f"{c:04b}"[::-1], 2) for c in range(16))


def by_residue(rows):
    shaped = rows.reshape((rows.shape[0] // 16, 2, 2, 2, 2) + rows.shape[1:])
    rest = tuple(range(5, shaped.ndim))
    return shaped.transpose((4, 3, 2, 1, 0) + rest).reshape(rows.shape)


def from_residue(rows):
    shaped = rows.reshape((2, 2, 2, 2, rows.shape[0] // 16) + rows.shape[1:])
    rest = tuple(range(5, shaped.ndim))
    return shaped.transpose((4, 3, 2, 1, 0) + rest).reshape(rows.shape)


def wide(q, k, v):
    pad = lambda a, n: jnp.pad(a, [(0, 0)] * (a.ndim - 1) + [(0, n)])
    return jnp.concatenate([pad(q, 80), pad(k, 16), pad(v, 16)], axis=-1)


def body(
    tokens,
    cotangent,
    valid_tiles,
    gain_first,
    shift_first,
    w_project,
    bias_project,
    w_output,
    bias_output,
    gain_second,
    shift_second,
    w_expand,
    bias_expand,
    w_reduce,
    bias_reduce,
):
    rows = tokens.shape[0]
    width = tokens.shape[1]
    tokens = by_residue(tokens)
    cotangent = by_residue(cotangent)
    valid = by_residue(valid_tiles).astype(F32)
    inputs = tokens.astype(F32)
    normed, undo_first = jax.vjp(norm_rows, inputs, gain_first, shift_first)
    normed_low = normed.astype(BF)

    w_heads = w_project.reshape(width, 3, LOCAL, HEAD_DIM)
    w_wide = wide(w_heads[:, 0], w_heads[:, 1], w_heads[:, 2])
    b_heads = bias_project.reshape(2, LOCAL, HEAD_DIM)
    b_wide = wide(b_heads[0], jnp.zeros_like(b_heads[0]), b_heads[1])
    lane = jnp.arange(256)
    ones = (lane == 48) | ((lane >= 180) & (lane < 183)) | (lane == 240) | (lane == 241)
    x = jnp.einsum("td,dhe->hte", normed_low, w_wide, preferred_element_type=F32) + b_wide[:, None]
    x = jnp.where(lane < 48, x * (SCALE * LOG2E), x)
    x = jnp.where((lane >= 128) & (lane < 176), x * valid[:, None], x)
    x = jnp.where(ones, 1.0, jnp.where(lane == 176, ((1.0 - valid) * masked_score)[:, None], x)).astype(BF)

    fin, attended, *saved = attention_forward(x)

    w_out_rows = jnp.pad(w_output.reshape(LOCAL, HEAD_DIM, width), ((0, 0), (0, 16), (0, 0))).reshape(-1, width)
    w_out_wide = jnp.pad(w_output.reshape(LOCAL, HEAD_DIM, width), ((0, 0), (64, 16), (0, 0))).reshape(-1, width)
    branch_out = (
        lax.psum(jnp.dot(attended, w_out_rows, preferred_element_type=F32).astype(BF), "heads").astype(F32)
        + bias_output
    )
    middle = inputs + branch_out
    normed_two, undo_second = jax.vjp(norm_rows, middle, gain_second, shift_second)
    normed_two_low = normed_two.astype(BF)
    expand = jnp.dot(normed_two_low, w_expand, preferred_element_type=F32) + bias_expand
    active, undo_gelu = jax.vjp(gelu_tanh, expand)
    active_low = active.astype(BF)
    reduced = (
        lax.psum(jnp.dot(active_low, w_reduce, preferred_element_type=F32).astype(BF), "heads").astype(F32)
        + bias_reduce
    )
    layer_out = middle + reduced
    grad_bias_reduce = jnp.sum(cotangent, axis=0)
    cotangent_low = cotangent.astype(BF)
    grad_w_reduce = jnp.einsum("tf,td->fd", active_low, cotangent_low, preferred_element_type=F32)
    grad_active = jnp.einsum("td,fd->tf", cotangent_low, w_reduce, preferred_element_type=F32)
    (grad_expand,) = undo_gelu(grad_active)
    grad_bias_expand = jnp.sum(grad_expand, axis=0)
    grad_expand_low = grad_expand.astype(BF)
    grad_w_expand = jnp.einsum("td,tf->df", normed_two_low, grad_expand_low, preferred_element_type=F32)
    grad_normed_two = lax.psum(
        jnp.einsum("tf,df->td", grad_expand_low, w_expand, preferred_element_type=F32).astype(BF), "heads"
    ).astype(F32)
    grad_middle_part, grad_gain_second, grad_shift_second = undo_second(grad_normed_two)
    grad_middle = cotangent + grad_middle_part
    grad_bias_output = jnp.sum(grad_middle, axis=0)
    grad_middle_low = grad_middle.astype(BF)
    grad_w_output = (
        jnp.einsum("te,td->ed", attended, grad_middle_low, preferred_element_type=F32)
        .reshape(LOCAL, 64, width)[:, :HEAD_DIM]
        .reshape(-1, width)
    )
    grad_attended = jnp.einsum("td,ed->te", grad_middle_low, w_out_wide, preferred_element_type=F32).astype(BF)
    early = lax.psum(
        (grad_w_output.astype(BF), grad_w_expand.astype(BF), grad_w_reduce.astype(BF)), "seq"
    )

    g, g_sums = attention_backward(x, saved, fin, grad_attended)
    g_sums = g_sums[:, 0]
    grad_bias_project = jnp.stack([g_sums[:, 0:48].reshape(-1), g_sums[:, 192:240].reshape(-1)])
    grad_w_wide = jnp.einsum("td,hte->dhe", normed_low, g, preferred_element_type=F32)
    grad_w_project = jnp.stack(
        [grad_w_wide[:, :, k : k + 48].reshape(width, -1) for k in (0, 128, 192)], axis=1
    )
    grad_normed = lax.psum(
        jnp.einsum("hte,dhe->td", g, w_wide, preferred_element_type=F32).astype(BF), "heads"
    ).astype(F32)
    grad_inputs_part, grad_gain_first, grad_shift_first = undo_first(grad_normed)
    grad_tokens = grad_middle + grad_inputs_part
    grad_w_project = lax.psum(grad_w_project.astype(BF), "seq")
    summed = lax.psum(
        (
            grad_gain_first,
            grad_shift_first,
            grad_bias_project,
            grad_bias_output,
            grad_gain_second,
            grad_shift_second,
            grad_bias_expand,
            grad_bias_reduce,
        ),
        "seq",
    )
    return (
        from_residue(layer_out),
        from_residue(grad_tokens),
        summed[0],
        summed[1],
        grad_w_project.astype(F32),
        summed[2],
        early[0].astype(F32),
        summed[3],
        summed[4],
        summed[5],
        early[1].astype(F32),
        summed[6],
        early[2].astype(F32),
        summed[7],
    )


def solution(mesh):
    in_specs = (
        P("seq", None),
        P("seq", None),
        P("seq"),
        P(),
        P(),
        P(None, None, "heads"),
        P(None, "heads"),
        P("heads", None),
        P(),
        P(),
        P(),
        P(None, "heads"),
        P("heads"),
        P("heads", None),
        P(),
    )
    out_specs = (
        P("seq", None),
        P("seq", None),
        P(),
        P(),
        P(None, None, "heads"),
        P(None, "heads"),
        P("heads", None),
        P(),
        P(),
        P(),
        P(None, "heads"),
        P("heads"),
        P("heads", None),
        P(),
    )
    return jax.shard_map(body, mesh=mesh, in_specs=in_specs, out_specs=out_specs, check_vma=False)
```

```python
import functools
import math

import jax
import jax.numpy as jnp
from jax import lax
from jax.experimental import pallas as pl
from jax.experimental.pallas import tpu as pltpu
from jax.sharding import PartitionSpec as P

HEADS = 16
HEAD_DIM = 48
SEGMENT = 1024
BRANCHES = 5
LOCAL = 8

MESH = pl.DeviceIdType.MESH
BF = jnp.bfloat16
F32 = jnp.float32
NT = (((1,), (1,)), ((), ()))
TN = (((0,), (0,)), ((), ()))
NN = (((1,), (0,)), ((), ()))

masked_score = -1000000000.0
layer_eps = 1e-05
SCALE = HEAD_DIM ** (-0.5)
LOG2E = math.log2(math.e)


def dot(a, b, dims):
    return lax.dot_general(a, b, dims, preferred_element_type=F32)


def lanes(shape):
    return lax.broadcasted_iota(jnp.int32, shape, len(shape) - 1)


def reversed_bits(value, bits):
    out = value * 0
    for k in range(bits):
        out = out * 2 + (value // 2**k) % 2
    return out


def split3(value):
    high = value.astype(BF).astype(F32)
    rest = value - high
    middle = rest.astype(BF).astype(F32)
    return high, middle, rest - middle


class Place:
    def __init__(self):
        self.me = lax.axis_index("seq")
        self.y = lax.axis_index("heads")

    def member(self, b):
        return self.me % 2**b

    def device(self, b, j):
        return (self.me // 2**b * 2**b + j, self.y)

    def start(self, b, head):
        stride = 2**b
        place = (self.y * LOCAL + head) % stride
        return pl.multiple_of(reversed_bits(place, b) * (SEGMENT // stride), SEGMENT // stride)

    def bit(self, k):
        return self.me // 2**k % 2

    def partner(self, k):
        return (self.me + 2**k * (1 - 2 * self.bit(k)), self.y)

    def low(self, k):
        return sum((self.bit(i) * HALVES[i] for i in range(k)), self.me * 0)

    def greet(self, seq=16, other=False):
        barrier = pltpu.get_barrier_semaphore()
        i = self.member(4)
        count = 15
        if other:
            pl.semaphore_signal(barrier, inc=1, device_id=(self.me, 1 - self.y), device_id_type=MESH)
            count += 1
        for k in far_bits(seq):
            pl.semaphore_signal(barrier, inc=1, device_id=self.partner(k), device_id_type=MESH)
            count += 1

        def signal(d, _):
            pl.semaphore_signal(barrier, inc=1, device_id=self.device(4, (i + d) % 16), device_id_type=MESH)
            return 0

        lax.fori_loop(1, 16, signal, 0)
        pl.semaphore_wait(barrier, count)


def remote(src, dst, send, recv, device):
    return pltpu.make_async_remote_copy(
        src_ref=src, dst_ref=dst, send_sem=send, recv_sem=recv, device_id=device, device_id_type=MESH
    )


def over_peers(b, body):
    tiles = max(LOCAL // 2**b, 1)

    def step(d, _):
        for t in range(tiles):
            body(d, t)
        return 0

    lax.fori_loop(1, 2**b, step, 0)


def ds(start, size):
    return pl.ds(pl.multiple_of(start, size), size)


def attend(q, kv):
    scores = dot(q, kv, NT)
    top = jnp.max(scores, axis=1, keepdims=True)
    raised = jnp.exp2(scores - top).astype(BF)
    return dot(raised, kv, NN), top


def packed(out, top):
    lane = lanes(out.shape)
    total = out[:, 112:113]
    tile = jnp.where(lane == 112, 1.0, out * (1.0 / total))
    for k, piece in enumerate(split3(top) + split3(total)):
        tile = jnp.where(lane == 114 + k, piece, tile)
    return tile.astype(BF)


def forward_kernel(
    x_ref, fin_ref, att_ref, x1, x2, x3, q4, kv4, acc, tops, o1, o2, o3, o4, r1, r2, r3, r4, *sems
):
    place = Place()
    me = place.me
    xs, os, rs = (None, x1, x2, x3), (None, o1, o2, o3, o4), (None, r1, r2, r3, r4)
    go_send, go_recv, back_send, back_recv = sems[0:4], sems[4:8], sems[8:12], sems[12:16]

    def go(b, d, t):
        n, tiles = SEGMENT // 2**b, max(LOCAL // 2**b, 1)
        i = place.member(b)
        j = (i + d) % 2**b
        if b < 4:
            head = j * tiles + t
            k = (d - 1) * tiles + t
            return [
                remote(
                    x_ref.at[head, pl.ds(place.start(b, head), n), :],
                    xs[b].at[t, ds(i * n, n), :],
                    go_send[b - 1].at[k],
                    go_recv[b - 1].at[k],
                    place.device(b, j),
                )
            ]
        head, half = j // 2, j % 2
        start = place.start(4, head)
        k = (d - 1) * 2
        return [
            remote(
                x_ref.at[head, ds(start + half * 32, 32), 0:128],
                q4.at[ds(i * 32, 32), :],
                go_send[3].at[k],
                go_recv[3].at[k],
                place.device(4, j),
            ),
            remote(
                x_ref.at[head, pl.ds(start, 64), 128:256],
                kv4.at[ds(i * 64, 64), :],
                go_send[3].at[k + 1],
                go_recv[3].at[k + 1],
                place.device(4, j),
            ),
        ]

    def back(b, d, t):
        n, tiles = SEGMENT // 2**b, max(LOCAL // 2**b, 1)
        i = place.member(b)
        j = (i + d) % 2**b
        k = (d - 1) * tiles + t
        if b < 4:
            src, dst = o_at(b, t, j), rs[b].at[i * tiles + t]
        else:
            src, dst = o4.at[ds(j * 32, 32), :], r4.at[i // 2, ds(i % 2 * 32, 32), :]
        return remote(src, dst, back_send[b - 1].at[k], back_recv[b - 1].at[k], place.device(b, j))

    def o_at(b, t, j):
        n = SEGMENT // 2**b
        return os[b].at[t, ds(j * n, n), :]

    place.greet()
    for b in (4, 3, 2, 1):
        over_peers(b, lambda d, t: [c.start() for c in go(b, d, t)])

    for b in (1, 2, 3):
        n, tiles = SEGMENT // 2**b, LOCAL // 2**b
        i = place.member(b)
        for t in range(tiles):
            head = i * tiles + t
            xs[b][t, ds(i * n, n), :] = x_ref[head, pl.ds(place.start(b, head), n), :]
    i = place.member(4)
    start = place.start(4, i // 2)
    q4[ds(i * 32, 32), :] = x_ref[i // 2, ds(start + i % 2 * 32, 32), 0:128]
    kv4[ds(i * 64, 64), :] = x_ref[i // 2, pl.ds(start, 64), 128:256]

    def local_head(h, _):
        for half in range(2):
            rows = pl.ds(half * 512, 512)
            out, top = attend(x_ref[h, rows, 0:128], x_ref[h, :, 128:256])
            acc[h, rows, :] = out
            tops[h, rows, :] = jnp.broadcast_to(top, out.shape)
        return 0

    lax.fori_loop(0, 4, local_head, 0)

    over_peers(4, lambda d, t: [c.wait_recv() for c in go(4, d, t)])
    o4[...] = packed(*attend(q4[...], kv4[...]))
    over_peers(4, lambda d, t: back(4, d, t).start())
    r4[i // 2, ds(i % 2 * 32, 32), :] = o4[ds(i * 32, 32), :]
    for b in (3, 2, 1):
        n, tiles = SEGMENT // 2**b, LOCAL // 2**b
        over_peers(b, lambda d, t: [c.wait_recv() for c in go(b, d, t)])

        def tile(t, _):
            for half in range(2):
                rows = pl.ds(half * 512, 512)
                os[b][t, rows, :] = packed(*attend(xs[b][t, rows, 0:128], xs[b][t, :, 128:256]))
            return 0

        lax.fori_loop(0, tiles, tile, 0)
        over_peers(b, lambda d, t: back(b, d, t).start())
        j = place.member(b)
        for t in range(tiles):
            rs[b][j * tiles + t] = os[b][t, ds(j * n, n), :]

    lax.fori_loop(4, 8, local_head, 0)

    for b in (4, 3, 2, 1):
        over_peers(b, lambda d, t: back(b, d, t).wait_recv())

    row = lax.broadcasted_iota(jnp.int32, (128, 256), 0)
    column = lax.broadcasted_iota(jnp.int32, (128, 256), 1)
    first = jnp.where(column < 128, 114, 117)
    picks = jnp.where((row >= first) & (row < first + 3), 1.0, 0.0).astype(BF)

    def merge_head(h):
        for b in (1, 2, 3, 4):
            n = SEGMENT // 2**b
            rows = pl.ds(place.start(b, h), n)
            part = rs[b][h]
            stats = dot(part, picks, NN)
            top = jnp.maximum(tops[h, rows, :], stats[:, 0:128])
            keep = jnp.exp2(tops[h, rows, :] - top)
            gain = jnp.exp2(stats[:, 0:128] - top) * stats[:, 128:256]
            acc[h, rows, :] = acc[h, rows, :] * keep + part.astype(F32) * gain
            tops[h, rows, :] = top
        out = acc[h]
        lane = lanes(out.shape)
        inverse = 1.0 / out[:, 112:113]
        out = jnp.where((lane >= 64) & (lane < 112), out * inverse, 0.0)
        fin_ref[h] = jnp.where(lane == 112, inverse, jnp.where(lane == 113, tops[h], out))
        return out

    def pair(k, _):
        even, odd = merge_head(k * 2), merge_head(k * 2 + 1)
        att_ref[:, ds(k * 128, 128)] = (pltpu.roll(even, 64, 1) + odd).astype(BF)
        return 0

    lax.fori_loop(0, LOCAL // 2, pair, 0)

    for b in (4, 3, 2, 1):
        over_peers(b, lambda d, t: [c.wait_send() for c in go(b, d, t)])
        over_peers(b, lambda d, t: back(b, d, t).wait_send())


ROWS = 768
HALVES = (384, 192, 96, 48)
LANDING = (0, 384, 576, 672, 720)


def far_bits(seq):
    return list(range(4, seq.bit_length() - 1))


class Halving:
    def __init__(self, place, seq, pieces, grads, shares, scratch):
        self.place, self.seq, self.pieces, self.grads, self.shares = place, seq, pieces, grads, shares
        self.landing, self.send, self.recv, self.far_send, self.far_recv = scratch

    @staticmethod
    def scratch(seq, pieces):
        far = len(far_bits(seq))
        return (
            [pltpu.VMEM((pieces, 720 + 48 * far, ROWS), BF)]
            + [pltpu.SemaphoreType.DMA((pieces * 4,)) for _ in range(2)]
            + [pltpu.SemaphoreType.DMA((pieces * max(far, 1),)) for _ in range(2)]
        )

    def copy(self, c, k):
        size = HALVES[k]
        start = self.place.low(k) + (1 - self.place.bit(k)) * size
        return remote(
            self.grads.at[c, pl.ds(pl.multiple_of(start, 48), size), :],
            self.landing.at[c, pl.ds(LANDING[k], size), :],
            self.send.at[c * 4 + k],
            self.recv.at[c * 4 + k],
            self.place.partner(k),
        )

    def add(self, c, k):
        start = self.place.low(k + 1)

        def step(i, _):
            rows = pl.ds(pl.multiple_of(start + i * 48, 48), 48)
            arrived = self.landing[c, pl.ds(pl.multiple_of(LANDING[k] + i * 48, 48), 48), :]
            value = (self.grads[c, rows, :].astype(F32) + arrived.astype(F32)).astype(BF)
            if k < 3:
                self.grads[c, rows, :] = value
            else:
                self.shares[c] = value
            return 0

        lax.fori_loop(0, HALVES[k] // 48, step, 0)

    def step(self, c, k):
        if k > 0:
            self.copy(c, k - 1).wait_recv()
            self.add(c, k - 1)
        if k < 4:
            self.copy(c, k).start()
            return
        bits = far_bits(self.seq)
        for n, bit in enumerate(bits):
            at = pl.ds(720 + 48 * n, 48)
            copy = remote(
                self.shares.at[c],
                self.landing.at[c, at, :],
                self.far_send.at[c * len(bits) + n],
                self.far_recv.at[c * len(bits) + n],
                self.place.partner(bit),
            )
            copy.start()
            copy.wait()
            self.shares[c] = (self.shares[c].astype(F32) + self.landing[c, at, :].astype(F32)).astype(BF)

    def finish(self):
        def piece(c, _):
            for k in range(4):
                self.copy(c, k).wait_send()
            return 0

        lax.fori_loop(0, self.pieces, piece, 0)


class Doubling:
    def __init__(self, place, pieces, shares, result, sems, first=0):
        self.place, self.pieces, self.shares, self.result, self.first = place, pieces, shares, result, first
        self.send, self.recv = sems

    @staticmethod
    def scratch(pieces):
        return [pltpu.SemaphoreType.DMA((pieces * 4,)) for _ in range(2)]

    def copy(self, c, k):
        rows = pl.ds(pl.multiple_of(self.place.low(k + 1), 48), HALVES[k])
        view = self.result.at[self.first + c, rows, :]
        return remote(view, view, self.send.at[c * 4 + k], self.recv.at[c * 4 + k], self.place.partner(k))

    def step(self, c, k):
        if k == 0:
            rows = pl.ds(pl.multiple_of(self.place.low(4), 48), 48)
            self.result[self.first + c, rows, :] = self.shares[c]
        else:
            self.copy(c, 4 - k).wait_recv()
        if k < 4:
            self.copy(c, 3 - k).start()

    def finish(self):
        def piece(c, _):
            for k in range(4):
                self.copy(c, k).wait_send()
            return 0

        lax.fori_loop(0, self.pieces, piece, 0)


def run_at(slot, work, table):
    for k in range(len(table[0])):
        c = sum((jnp.where(slot == times[k], n + 1, 0) for n, times in enumerate(table)), slot * 0)

        @pl.when(c > 0)
        def _():
            work.step(c - 1, k)


def sem_shapes(per_copy):
    counts = [4, 6, 7, 15 * per_copy]
    return [pltpu.SemaphoreType.DMA((c,)) for c in counts]


VMEM = pl.BlockSpec(memory_space=pltpu.VMEM)
ANY = pl.BlockSpec(memory_space=pl.ANY)
ORDER = tuple(int(f"{c:04b}"[::-1], 2) for c in range(16))


def attention_forward(x):
    shapes = [
        ((LOCAL, SEGMENT, 128), F32),
        ((SEGMENT, LOCAL * 64), BF),
        ((4, SEGMENT, 256), BF),
        ((2, SEGMENT, 256), BF),
        ((1, SEGMENT, 256), BF),
        ((512, 128), BF),
        ((SEGMENT, 128), BF),
    ]
    scratch = [
        ((LOCAL, SEGMENT, 128), F32),
        ((LOCAL, SEGMENT, 128), F32),
        ((4, SEGMENT, 128), BF),
        ((2, SEGMENT, 128), BF),
        ((1, SEGMENT, 128), BF),
        ((512, 128), BF),
        ((LOCAL, 512, 128), BF),
        ((LOCAL, 256, 128), BF),
        ((LOCAL, 128, 128), BF),
        ((LOCAL, 64, 128), BF),
    ]
    return pl.pallas_call(
        forward_kernel,
        out_shape=[jax.ShapeDtypeStruct(*s) for s in shapes],
        in_specs=[VMEM],
        out_specs=[VMEM] * len(shapes),
        scratch_shapes=[pltpu.VMEM(*s) for s in scratch]
        + sem_shapes(2) + sem_shapes(2) + sem_shapes(1) + sem_shapes(1),
        compiler_params=pltpu.CompilerParams(
            collective_id=0, has_side_effects=True, vmem_limit_bytes=56 * 2**20
        ),
        name="attention_forward",
    )(x)


def pair_grads(q, d, kv_at, put):
    lane = lanes(q.shape)
    zero = jnp.zeros_like(d)
    queries = q + jnp.where(lane < 64, d, zero)
    grads = jnp.where(lane < 64, zero, d)
    total = None
    for half in range(2):
        kv = kv_at(half)
        probs = jnp.exp2(dot(kv, queries, NT))
        grad_scores = (probs * dot(kv, grads, NT)).astype(BF)
        put(half, dot(grad_scores, queries, NN) + dot(probs.astype(BF), grads, NN))
        part = dot(kv, grad_scores, TN)
        total = part if total is None else total + part
    return total.T


def put_48(pieces, head, value):
    lane = lanes(value.shape)
    at = head * 48
    tile, off = at // 128, at % 128
    value = jnp.where(lane < 48, value, 0.0)
    if off:
        value = pltpu.roll(value, off, 1)
    if off + 48 > 128:
        parts = [(tile, jnp.where(lane >= off, value, 0.0)), (tile + 1, jnp.where(lane < off - 80, value, 0.0))]
    else:
        parts = [(tile, value)]
    for k, part in parts:
        pieces[k] = part if pieces[k] is None else pieces[k] + part


def backward_kernel(
    seq, x_ref, x1, x2, x3, q4, kv4, fin_ref, do_ref, ffn_ref, grads_in, g_ref, sum_ref, ffn_other, shares_ref,
    grads, d0, d1, d2, d3, d4, total, g1, g2, g3, gq4, gkv4, r1, r2, r3, rq4, rkv4, *sems
):
    place = Place()
    *sems, fill_sem, ffn_send, ffn_recv = sems
    halving = Halving(place, seq, 4, grads, shares_ref, sems[16:])

    def reduce_at(slot):
        run_at(slot, halving, ((0, 1, 4, 5, 6), (2, 3, 6, 7, 8), (8, 9, 12, 13, 14), (10, 11, 14, 15, 16)))

    for c in range(4):
        pltpu.make_async_copy(grads_in.at[c], grads.at[c], fill_sem.at[c]).start()
    ffn_copy = remote(ffn_ref, ffn_other, ffn_send, ffn_recv, (place.me, 1 - place.y))
    me = place.me
    xs, dd, gs, rs = (None, x1, x2, x3), (None, d1, d2, d3), (None, g1, g2, g3), (None, r1, r2, r3)
    go_send, go_recv, back_send, back_recv = sems[0:4], sems[4:8], sems[8:12], sems[12:16]

    def go(b, d, t):
        n, tiles = SEGMENT // 2**b, max(LOCAL // 2**b, 1)
        i = place.member(b)
        j = (i + d) % 2**b
        k = (d - 1) * tiles + t
        if b < 4:
            head = j * tiles + t
            src, dst = d0.at[head, pl.ds(place.start(b, head), n), :], dd[b].at[t, ds(i * n, n), :]
        else:
            start = place.start(4, j // 2)
            src, dst = d0.at[j // 2, ds(start + j % 2 * 32, 32), :], d4.at[ds(i * 32, 32), :]
        return remote(src, dst, go_send[b - 1].at[k], go_recv[b - 1].at[k], place.device(b, j))

    def back(b, d, t):
        n, tiles = SEGMENT // 2**b, max(LOCAL // 2**b, 1)
        i = place.member(b)
        j = (i + d) % 2**b
        device = place.device(b, j)
        if b < 4:
            k = (d - 1) * tiles + t
            return [
                remote(
                    gs[b].at[t, ds(j * n, n), :],
                    rs[b].at[i * tiles + t],
                    back_send[b - 1].at[k],
                    back_recv[b - 1].at[k],
                    device,
                )
            ]
        k = (d - 1) * 2
        return [
            remote(
                gq4.at[ds(j * 32, 32), :],
                rq4.at[i // 2, ds(i % 2 * 32, 32), :],
                back_send[3].at[k],
                back_recv[3].at[k],
                device,
            ),
            remote(
                gkv4.at[ds(j * 64, 64), :],
                rkv4.at[i % 2, i // 2],
                back_send[3].at[k + 1],
                back_recv[3].at[k + 1],
                device,
            ),
        ]

    def prepare(h, _):
        fin = fin_ref[h]
        lane = lanes(fin.shape)
        value_lane = (lane >= 64) & (lane < 112)
        grad = (do_ref[:, ds(h * 128, 128)].astype(F32) * fin[:, 112:113]).astype(BF).astype(F32)
        delta = jnp.sum(jnp.where(value_lane, grad * fin, 0.0), axis=1, keepdims=True)
        tile = jnp.where(value_lane, grad, 0.0)
        high, middle, low = split3(-delta)
        tile = jnp.where(lane == 112, high, jnp.where(lane == 113, middle, tile))
        for k, piece in enumerate(split3(-fin[:, 113:114])):
            tile = jnp.where(lane == 52 + k, piece, tile)
        d0[h] = tile.astype(BF)
        return 0

    lax.fori_loop(0, LOCAL, prepare, 0)
    place.greet(seq, True)
    for b in (4, 3, 2, 1):
        over_peers(b, lambda d, t: go(b, d, t).start())
    ffn_copy.start()
    for c in range(4):
        pltpu.make_async_copy(grads_in.at[c], grads.at[c], fill_sem.at[c]).wait()
    for b in (1, 2, 3):
        n, tiles = SEGMENT // 2**b, LOCAL // 2**b
        i = place.member(b)
        for t in range(tiles):
            head = i * tiles + t
            dd[b][t, ds(i * n, n), :] = d0[head, pl.ds(place.start(b, head), n), :]
    i = place.member(4)
    d4[ds(i * 32, 32), :] = d0[i // 2, ds(place.start(4, i // 2) + i % 2 * 32, 32), :]

    def local_head(h, _):
        def put(half, grad):
            total[h, pl.ds(half * 512, 512), 128:256] = grad

        total[h, :, 0:128] = pair_grads(
            x_ref[h, :, 0:128], d0[h], lambda half: x_ref[h, pl.ds(half * 512, 512), 128:256], put
        )
        reduce_at(jnp.where(h < 4, h, h + 8))
        return 0

    lax.fori_loop(0, 4, local_head, 0)

    over_peers(4, lambda d, t: go(4, d, t).wait_recv())

    def put4(half, grad):
        gkv4[pl.ds(half * 512, 512), :] = grad.astype(BF)

    gq4[...] = pair_grads(q4[...], d4[...], lambda half: kv4[pl.ds(half * 512, 512), :], put4).astype(BF)
    over_peers(4, lambda d, t: [c.start() for c in back(4, d, t)])
    rq4[i // 2, ds(i % 2 * 32, 32), :] = gq4[ds(i * 32, 32), :]
    rkv4[i % 2, i // 2] = gkv4[ds(i * 64, 64), :]
    reduce_at(jnp.int32(4))
    slot = 5
    for b in (3, 2, 1):
        n, tiles = SEGMENT // 2**b, LOCAL // 2**b
        over_peers(b, lambda d, t: go(b, d, t).wait_recv())

        def tile(t, _):
            def put(half, grad):
                gs[b][t, pl.ds(half * 512, 512), 128:256] = grad.astype(BF)

            gs[b][t, :, 0:128] = pair_grads(
                xs[b][t, :, 0:128], dd[b][t], lambda half: xs[b][t, pl.ds(half * 512, 512), 128:256], put
            ).astype(BF)
            reduce_at(slot + t)
            return 0

        lax.fori_loop(0, tiles, tile, 0)
        slot += tiles
        over_peers(b, lambda d, t: [c.start() for c in back(b, d, t)])
        j = place.member(b)
        for t in range(tiles):
            rs[b][j * tiles + t] = gs[b][t, ds(j * n, n), :]

    lax.fori_loop(4, 8, local_head, 0)

    for b in (4, 3, 2, 1):
        over_peers(b, lambda d, t: [c.wait_recv() for c in back(b, d, t)])

    def finish(h, _):
        for b in (1, 2, 3):
            n = SEGMENT // 2**b
            rows = pl.ds(place.start(b, h), n)
            total[h, rows, :] += rs[b][h].astype(F32)
        rows = pl.ds(place.start(4, h), 64)
        total[h, rows, 0:128] += rq4[h].astype(F32)
        total[h, rows, 128:256] += rkv4[0, h].astype(F32) + rkv4[1, h].astype(F32)
        return 0

    lax.fori_loop(0, LOCAL, finish, 0)
    reduce_at(jnp.int32(16))
    sum_ref[...] = jnp.zeros_like(sum_ref)

    def compact(i, _):
        rows = ds(i * 256, 256)
        pieces = [[None] * 3 for _ in range(3)]
        for h in range(LOCAL):
            live = (x_ref[h, rows, 176:177].astype(F32) >= 0.0).astype(F32)
            grad_kv = total[h, rows, 128:256]
            put_48(pieces[0], h, total[h, rows, 0:128] * SCALE)
            put_48(pieces[1], h, grad_kv * (live * (1.0 / LOG2E)))
            put_48(pieces[2], h, pltpu.roll(grad_kv, 64, 1))
        for k in range(3):
            for n in range(3):
                at = pl.ds(n * 128, 128)
                g_ref[k, rows, at] = pieces[k][n].astype(BF)
                sum_ref[k, :, at] += jnp.broadcast_to(jnp.sum(pieces[k][n], axis=0, keepdims=True), (8, 128))
        return 0

    lax.fori_loop(0, 4, compact, 0)

    for b in (4, 3, 2, 1):
        over_peers(b, lambda d, t: go(b, d, t).wait_send())
        over_peers(b, lambda d, t: [c.wait_send() for c in back(b, d, t)])
    halving.finish()
    ffn_copy.wait()


def attention_backward(x, saved, fin, grad_out, ffn_part, grads):
    seq = lax.axis_size("seq")
    shapes = [
        ((3, SEGMENT, LOCAL * HEAD_DIM), BF),
        ((3, 8, LOCAL * HEAD_DIM), F32),
        (ffn_part.shape, BF),
        ((4, 48, ROWS), BF),
    ]
    scratch = [
        (grads.shape, BF),
        ((LOCAL, SEGMENT, 128), BF),
        ((4, SEGMENT, 128), BF),
        ((2, SEGMENT, 128), BF),
        ((1, SEGMENT, 128), BF),
        ((512, 128), BF),
        ((LOCAL, SEGMENT, 256), F32),
        ((4, SEGMENT, 256), BF),
        ((2, SEGMENT, 256), BF),
        ((1, SEGMENT, 256), BF),
        ((512, 128), BF),
        ((SEGMENT, 128), BF),
        ((LOCAL, 512, 256), BF),
        ((LOCAL, 256, 256), BF),
        ((LOCAL, 128, 256), BF),
        ((LOCAL, 64, 128), BF),
        ((2, LOCAL, 64, 128), BF),
    ]
    return pl.pallas_call(
        functools.partial(backward_kernel, seq),
        out_shape=[jax.ShapeDtypeStruct(*s) for s in shapes],
        in_specs=[VMEM] * 8 + [ANY] * 2,
        out_specs=[VMEM, VMEM, ANY, VMEM],
        scratch_shapes=[pltpu.VMEM(*s) for s in scratch]
        + sem_shapes(1) + sem_shapes(1) + sem_shapes(2) + sem_shapes(2)
        + Halving.scratch(seq, 4)
        + [pltpu.SemaphoreType.DMA((4,)), pltpu.SemaphoreType.DMA, pltpu.SemaphoreType.DMA],
        compiler_params=pltpu.CompilerParams(
            collective_id=1, has_side_effects=True, vmem_limit_bytes=60 * 2**20
        ),
        name="attention_backward",
    )(x, *saved, fin, grad_out, ffn_part, grads)


CHUNK = 128


def put_spread(planes, block, value):
    for t in range(value.shape[1] // 128):
        planes[t, pl.ds(ORDER[block], 64, stride=16), :] = value[:, t * 128 : (t + 1) * 128]


def from_planes(planes, out):
    def step(i, _):
        rows = ds(i * 128, 128)
        for t in range(planes.shape[0]):
            out[rows, pl.ds(t * 128, 128)] = planes[t, rows, :]
        return 0

    lax.fori_loop(0, SEGMENT // 128, step, 0)


def last_kernel(
    seq, g_ref, w_ref, normed_ref, tokens_ref, middle_ref, gain_ref, w_out_ref, small_ref, shares_in,
    out_ref, grads_ref, early_ref, late_ref,
    grads, shares, part, other, early_in, late, late_in, sums, planes, part_send, part_recv, early_send, early_recv, late_send, late_recv,
    *sems
):
    place = Place()
    halving = Halving(place, seq, 2, grads, shares, sems[0:5])
    gathers = Doubling(place, 4, shares_in, grads_ref, sems[5:7])
    last_gathers = Doubling(place, 2, shares, grads_ref, sems[7:9], 4)
    far_send, far_recv = sems[9:]
    i = place.member(4)
    chunks = SEGMENT // CHUNK

    def to_all(src, landing, send, recv):
        def each(action):
            def step(d, _):
                action(remote(src, landing.at[i], send.at[d - 1], recv.at[d - 1], place.device(4, (i + d) % 16)))
                return 0

            lax.fori_loop(1, 16, step, 0)

        return each

    def total_of(src, landing):
        def step(j, value):
            return value + landing[j]

        landing[i] = src[...]
        return lax.fori_loop(1, 16, step, landing[0])

    def far_total(result, n):
        for k, bit in enumerate(far_bits(seq)):
            landing = (early_in, late_in)[n].at[16 + k]
            copy = remote(result, landing, far_send.at[n * 8 + k], far_recv.at[n * 8 + k], place.partner(bit))
            copy.start()
            copy.wait()
            result[...] = result[...] + landing[...]

    def exchange(n):
        rows = ds(n * CHUNK, CHUNK)
        return remote(
            part.at[rows, :], other.at[rows, :], part_send.at[n], part_recv.at[n], (place.me, 1 - place.y)
        )

    def partial(n, _):
        rows = ds(n * CHUNK, CHUNK)
        value = dot(g_ref[0, rows, :], w_ref[0], NT)
        value += dot(g_ref[1, rows, :], w_ref[1], NT)
        value += dot(g_ref[2, rows, :], w_ref[2], NT)
        part[rows, :] = value.astype(BF)
        exchange(n).start()
        return 0

    place.greet(seq, True)
    lax.fori_loop(0, 2, partial, 0)
    early_all = to_all(small_ref, early_in, early_send, early_recv)
    early_all(lambda copy: copy.start())
    for k in range(3):
        at = pl.ds(k % 2 * 384, 384)
        grads[k // 2, :, at] = dot(normed_ref[...], g_ref[k], TN).astype(BF)
        if k == 1:
            halving.step(0, 0)
    grads[1, :, pl.ds(384, 384)] = w_out_ref[...]
    halving.step(1, 0)
    lax.fori_loop(2, chunks, partial, 0)
    sums[...] = jnp.zeros_like(sums)

    for n in range(chunks):
        exchange(n).wait_recv()
        for block in range(CHUNK // 64):
            b = n * (CHUNK // 64) + block
            rows = pl.ds(b * 64, 64)
            x = tokens_ref[rows, :].astype(F32)
            centered = x - jnp.mean(x, axis=1, keepdims=True)
            rs = lax.rsqrt(jnp.mean(centered * centered, axis=1, keepdims=True) + layer_eps)
            xhat = centered * rs
            grad = part[rows, :].astype(F32) + other[rows, :].astype(F32)
            sums[0:8] += jnp.sum((grad * xhat).reshape(8, 8, -1), axis=0)
            sums[8:16] += jnp.sum(grad.reshape(8, 8, -1), axis=0)
            grad = grad * gain_ref[...]
            grad = grad - jnp.mean(grad, axis=1, keepdims=True) - xhat * jnp.mean(grad * xhat, axis=1, keepdims=True)
            put_spread(planes, b, middle_ref[rows, :] + rs * grad)
        for c in range(2):
            if 1 <= n + 1 - c <= 4:
                halving.step(c, n + 1 - c)
            if 0 <= n - 3 - c <= 4:
                last_gathers.step(c, n - 3 - c)
        for c in range(4):
            if 0 <= n - c <= 4:
                gathers.step(c, n - c)
    for k in range(2):
        value = jnp.sum(sums[k * 8 : k * 8 + 8], axis=0, keepdims=True)
        for t in range(6):
            late[pl.ds(k * 8 + t, 1), :] = value[:, t * 128 : (t + 1) * 128]
        late[pl.ds(k * 8 + 6, 2), :] = jnp.zeros((2, 128), F32)
    late_all = to_all(late, late_in, late_send, late_recv)
    late_all(lambda copy: copy.start())
    last_gathers.step(1, 4)
    from_planes(planes, out_ref)
    early_all(lambda copy: copy.wait_recv())
    early_ref[...] = total_of(small_ref, early_in)
    far_total(early_ref, 0)
    late_all(lambda copy: copy.wait_recv())
    late_ref[...] = total_of(late, late_in)
    far_total(late_ref, 1)

    def sent(n, _):
        exchange(n).wait_send()
        return 0

    lax.fori_loop(0, chunks, sent, 0)
    early_all(lambda copy: copy.wait_send())
    late_all(lambda copy: copy.wait_send())
    halving.finish()
    gathers.finish()
    last_gathers.finish()


def last_part(g, w_project, normed, tokens, grad_middle, gain, grad_w_out, small, shares):
    seq = lax.axis_size("seq")
    far = len(far_bits(seq))
    width = normed.shape[1]
    shapes = [
        (normed.shape, F32),
        ((6, ROWS, ROWS), BF),
        (small.shape, F32),
        ((16, 128), F32),
    ]
    scratch = [
        ((2, ROWS, ROWS), BF),
        ((2, 48, ROWS), BF),
        (normed.shape, BF),
        (normed.shape, BF),
        ((16 + far,) + small.shape, F32),
        ((16, 128), F32),
        ((16 + far, 16, 128), F32),
        ((16, width), F32),
        ((width // 128, SEGMENT, 128), F32),
    ]
    chunks = SEGMENT // CHUNK
    counts = (chunks, chunks, 15, 15, 15, 15)
    return pl.pallas_call(
        functools.partial(last_kernel, seq),
        out_shape=[jax.ShapeDtypeStruct(*s) for s in shapes],
        in_specs=[VMEM] * 9,
        out_specs=[VMEM] * len(shapes),
        scratch_shapes=[pltpu.VMEM(*s) for s in scratch]
        + [pltpu.SemaphoreType.DMA((c,)) for c in counts]
        + Halving.scratch(seq, 2) + Doubling.scratch(4) + Doubling.scratch(2)
        + [pltpu.SemaphoreType.DMA((16,)) for _ in range(2)],
        compiler_params=pltpu.CompilerParams(
            collective_id=2, has_side_effects=True, vmem_limit_bytes=56 * 2**20
        ),
        name="last_part",
    )(g, w_project, normed, tokens, grad_middle, gain, grad_w_out, small, shares)


def norm_rows(values, gain, shift):
    mean_row = jnp.mean(values, axis=-1, keepdims=True)
    centered = values - mean_row
    variance = jnp.mean(centered * centered, axis=-1, keepdims=True)
    return centered * lax.rsqrt(variance + layer_eps) * gain + shift


def gelu_tanh(values):
    return jax.nn.gelu(values, approximate=True)


def by_residue(rows):
    shaped = rows.reshape((rows.shape[0] // 16, 2, 2, 2, 2) + rows.shape[1:])
    rest = tuple(range(5, shaped.ndim))
    return shaped.transpose((4, 3, 2, 1, 0) + rest).reshape(rows.shape)


def from_residue(rows):
    shaped = rows.reshape((2, 2, 2, 2, rows.shape[0] // 16) + rows.shape[1:])
    rest = tuple(range(5, shaped.ndim))
    return shaped.transpose((4, 3, 2, 1, 0) + rest).reshape(rows.shape)


def wide(q, k, v):
    pad = lambda a, n: jnp.pad(a, [(0, 0)] * (a.ndim - 1) + [(0, n)])
    return jnp.concatenate([pad(q, 80), pad(k, 16), pad(v, 16)], axis=-1)


def body(
    tokens,
    cotangent,
    valid_tiles,
    gain_first,
    shift_first,
    w_project,
    bias_project,
    w_output,
    bias_output,
    gain_second,
    shift_second,
    w_expand,
    bias_expand,
    w_reduce,
    bias_reduce,
):
    rows = tokens.shape[0]
    width = tokens.shape[1]
    tokens = by_residue(tokens)
    cotangent = by_residue(cotangent)
    valid = by_residue(valid_tiles).astype(F32)
    inputs = tokens.astype(F32)
    normed, undo_first = jax.vjp(norm_rows, inputs, gain_first, shift_first)
    normed_low = normed.astype(BF)

    w_heads = w_project.reshape(width, 3, LOCAL, HEAD_DIM)
    w_wide = wide(w_heads[:, 0], w_heads[:, 1], w_heads[:, 2])
    b_heads = bias_project.reshape(2, LOCAL, HEAD_DIM)
    b_wide = wide(b_heads[0], jnp.zeros_like(b_heads[0]), b_heads[1])
    lane = jnp.arange(256)
    ones = (lane == 48) | ((lane >= 180) & (lane < 183)) | (lane == 240) | (lane == 241)
    x = jnp.einsum("td,dhe->hte", normed_low, w_wide, preferred_element_type=F32) + b_wide[:, None]
    x = jnp.where(lane < 48, x * (SCALE * LOG2E), x)
    x = jnp.where((lane >= 128) & (lane < 176), x * valid[:, None], x)
    x = jnp.where(ones, 1.0, jnp.where(lane == 176, ((1.0 - valid) * masked_score)[:, None], x)).astype(BF)

    fin, attended, *saved = attention_forward(x)

    w_out_rows = jnp.pad(w_output.reshape(LOCAL, HEAD_DIM, width), ((0, 0), (0, 16), (0, 0))).reshape(-1, width)
    w_out_wide = jnp.pad(w_output.reshape(LOCAL, HEAD_DIM, width), ((0, 0), (64, 16), (0, 0))).reshape(-1, width)
    branch_out = (
        lax.psum(jnp.dot(attended, w_out_rows, preferred_element_type=F32).astype(BF), "heads").astype(F32)
        + bias_output
    )
    middle = inputs + branch_out
    normed_two, undo_second = jax.vjp(norm_rows, middle, gain_second, shift_second)
    normed_two_low = normed_two.astype(BF)
    expand = jnp.dot(normed_two_low, w_expand, preferred_element_type=F32) + bias_expand
    active, undo_gelu = jax.vjp(gelu_tanh, expand)
    active_low = active.astype(BF)
    ffn_part = jnp.dot(active_low, w_reduce, preferred_element_type=F32).astype(BF)
    grad_bias_reduce = jnp.sum(cotangent, axis=0)
    cotangent_low = cotangent.astype(BF)
    grad_w_reduce = jnp.einsum("tf,td->fd", active_low, cotangent_low, preferred_element_type=F32)
    grad_active = jnp.einsum("td,fd->tf", cotangent_low, w_reduce, preferred_element_type=F32)
    (grad_expand,) = undo_gelu(grad_active)
    grad_bias_expand = jnp.sum(grad_expand, axis=0)
    grad_expand_low = grad_expand.astype(BF)
    grad_w_expand = jnp.einsum("td,tf->df", normed_two_low, grad_expand_low, preferred_element_type=F32)
    grad_normed_two = lax.psum(
        jnp.einsum("tf,df->td", grad_expand_low, w_expand, preferred_element_type=F32).astype(BF), "heads"
    ).astype(F32)
    grad_middle_part, grad_gain_second, grad_shift_second = undo_second(grad_normed_two)
    grad_middle = cotangent + grad_middle_part
    grad_bias_output = jnp.sum(grad_middle, axis=0)
    grad_middle_low = grad_middle.astype(BF)
    grad_w_output = (
        jnp.einsum("te,td->ed", attended, grad_middle_low, preferred_element_type=F32)
        .reshape(LOCAL, 64, width)[:, :HEAD_DIM]
        .reshape(-1, width)
        .astype(BF)
    )
    half = width // 2
    grad_w_output = jnp.concatenate([grad_w_output[:, :half], grad_w_output[:, half:]], axis=0)
    grad_attended = jnp.einsum("td,ed->te", grad_middle_low, w_out_wide, preferred_element_type=F32).astype(BF)
    grad_w_reduce, grad_w_expand = grad_w_reduce.astype(BF), grad_w_expand.astype(BF)
    grads = jnp.stack(
        [grad_w_reduce[:width], grad_w_reduce[width:], grad_w_expand[:, :width], grad_w_expand[:, width:]]
    )

    g, g_sums, ffn_other, shares = attention_backward(x, saved, fin, grad_attended, ffn_part, grads)
    layer_out = middle + (ffn_part.astype(F32) + ffn_other.astype(F32)) + bias_reduce
    small = jnp.concatenate(
        [
            g_sums[0, 0],
            g_sums[2, 0],
            grad_bias_output,
            grad_gain_second,
            grad_shift_second,
            grad_bias_expand,
            grad_bias_reduce,
            jnp.zeros((6 * 128,), F32),
        ]
    ).reshape(48, 128)
    grad_tokens, grads, small, late = last_part(
        g, w_project.transpose(1, 0, 2), normed_low, tokens, grad_middle, gain_first[None], grad_w_output, small, shares
    )
    small = small.reshape(-1)
    grads = grads.astype(F32)
    last_grads = grads[4:]
    grad_w_project = jnp.stack(
        [last_grads[0, :, :half], last_grads[0, :, half:], last_grads[1, :, :half]], axis=1
    )
    grad_w_output = jnp.concatenate([last_grads[1, :half, half:], last_grads[1, half:, half:]], axis=1)
    late = late.reshape(2, 8 * 128)[:, :width]
    parts = [small[k * width : (k + 1) * width] for k in range(7)]
    return (
        from_residue(layer_out),
        grad_tokens,
        late[0],
        late[1],
        grad_w_project,
        parts[0].reshape(2, half),
        grad_w_output,
        parts[1],
        parts[2],
        parts[3],
        jnp.concatenate([grads[2], grads[3]], axis=1),
        small[4 * width : 6 * width],
        jnp.concatenate([grads[0], grads[1]], axis=0),
        parts[6],
    )


def solution(mesh):
    in_specs = (
        P("seq", None),
        P("seq", None),
        P("seq"),
        P(),
        P(),
        P(None, None, "heads"),
        P(None, "heads"),
        P("heads", None),
        P(),
        P(),
        P(),
        P(None, "heads"),
        P("heads"),
        P("heads", None),
        P(),
    )
    out_specs = (
        P("seq", None),
        P("seq", None),
        P(),
        P(),
        P(None, None, "heads"),
        P(None, "heads"),
        P("heads", None),
        P(),
        P(),
        P(),
        P(None, "heads"),
        P("heads"),
        P("heads", None),
        P(),
    )
    return jax.shard_map(body, mesh=mesh, in_specs=in_specs, out_specs=out_specs, check_vma=False)
```

```python
import functools
import math

import jax
import jax.numpy as jnp
from jax import lax
from jax.experimental import pallas as pl
from jax.experimental.pallas import tpu as pltpu
from jax.sharding import PartitionSpec as P

HEADS = 16
HEAD_DIM = 48
SEGMENT = 1024
BRANCHES = 5
LOCAL = 8

MESH = pl.DeviceIdType.MESH
BF = jnp.bfloat16
F32 = jnp.float32
NT = (((1,), (1,)), ((), ()))
TN = (((0,), (0,)), ((), ()))
NN = (((1,), (0,)), ((), ()))

masked_score = -1000000000.0
layer_eps = 1e-05
SCALE = HEAD_DIM ** (-0.5)
LOG2E = math.log2(math.e)


def dot(a, b, dims):
    return lax.dot_general(a, b, dims, preferred_element_type=F32)


def lanes(shape):
    return lax.broadcasted_iota(jnp.int32, shape, len(shape) - 1)


def reversed_bits(value, bits):
    out = value * 0
    for k in range(bits):
        out = out * 2 + (value // 2**k) % 2
    return out


def split3(value):
    high = value.astype(BF).astype(F32)
    rest = value - high
    middle = rest.astype(BF).astype(F32)
    return high, middle, rest - middle


def put_48(pieces, head, value, source=0):
    lane = lanes(value.shape)
    tile, off = head * 48 // 128, head * 48 % 128
    value = jnp.where((lane >= source) & (lane < source + 48), value, 0.0)
    if off != source:
        value = pltpu.roll(value, (off - source) % 128, 1)
    if off + 48 > 128:
        parts = [(tile, jnp.where(lane >= off, value, 0.0)), (tile + 1, jnp.where(lane < off - 80, value, 0.0))]
    else:
        parts = [(tile, value)]
    for k, part in parts:
        pieces[k] = part if pieces[k] is None else pieces[k] + part


def take_48(value, head, at):
    tile, off = head * 48 // 128, head * 48 % 128
    shift = (at - off) % 128
    turn = lambda k: pltpu.roll(value[:, k * 128 : (k + 1) * 128], shift, 1) if shift else value[:, k * 128 : (k + 1) * 128]
    out = turn(tile)
    lane = lanes(out.shape)
    if off + 48 > 128:
        out = jnp.where(lane < at + 128 - off, out, turn(tile + 1))
    return jnp.where((lane >= at) & (lane < at + 48), out, 0.0)


def row_mean(value):
    ones = jnp.ones((value.shape[1], 128), BF)
    high = value.astype(BF)
    low = (value - high.astype(F32)).astype(BF)
    return (dot(high, ones, NN) + dot(low, ones, NN)) * (1.0 / value.shape[1])


def widen(tile, like):
    return jnp.concatenate([tile] * (like.shape[1] // 128), axis=1)


def row_sums(value):
    return jnp.sum(value.reshape(value.shape[0] // 8, 8, value.shape[1]), axis=0)


def put_vector(rows, first, partial):
    value = jnp.sum(partial, axis=0, keepdims=True)
    for t in range(value.shape[1] // 128):
        rows[pl.ds(first + t, 1), :] = value[:, t * 128 : (t + 1) * 128]


def norm_stats(value):
    mean = row_mean(value)
    centered = value - widen(mean, value)
    rs = lax.rsqrt(row_mean(centered * centered) + layer_eps)
    return mean, rs


def norm_back(grad, xhat, rs, gain):
    grad = grad * gain
    return rs * (grad - widen(row_mean(grad), grad) - xhat * widen(row_mean(grad * xhat), grad))


class Place:
    def __init__(self):
        self.me = lax.axis_index("seq")
        self.y = lax.axis_index("heads")

    def member(self, b):
        return self.me % 2**b

    def device(self, b, j):
        return (self.me // 2**b * 2**b + j, self.y)

    def start(self, b, head):
        stride = 2**b
        place = (self.y * LOCAL + head) % stride
        return pl.multiple_of(reversed_bits(place, b) * (SEGMENT // stride), SEGMENT // stride)

    def bit(self, k):
        return self.me // 2**k % 2

    def partner(self, k):
        return (self.me + 2**k * (1 - 2 * self.bit(k)), self.y)

    def low(self, k):
        return sum((self.bit(i) * HALVES[i] for i in range(k)), self.me * 0)

    def greet(self, seq=16, other=False):
        barrier = pltpu.get_barrier_semaphore()
        i = self.member(4)
        count = 15
        if other:
            pl.semaphore_signal(barrier, inc=1, device_id=(self.me, 1 - self.y), device_id_type=MESH)
            count += 1
        for k in far_bits(seq):
            pl.semaphore_signal(barrier, inc=1, device_id=self.partner(k), device_id_type=MESH)
            count += 1

        def signal(d, _):
            pl.semaphore_signal(barrier, inc=1, device_id=self.device(4, (i + d) % 16), device_id_type=MESH)
            return 0

        lax.fori_loop(1, 16, signal, 0)
        pl.semaphore_wait(barrier, count)


def remote(src, dst, send, recv, device):
    return pltpu.make_async_remote_copy(
        src_ref=src, dst_ref=dst, send_sem=send, recv_sem=recv, device_id=device, device_id_type=MESH
    )


def over_peers(b, body):
    tiles = max(LOCAL // 2**b, 1)

    def step(d, _):
        for t in range(tiles):
            body(d, t)
        return 0

    lax.fori_loop(1, 2**b, step, 0)


def ds(start, size):
    return pl.ds(pl.multiple_of(start, size), size)


def attend(q, kv):
    scores = dot(q, kv, NT)
    top = jnp.max(scores, axis=1, keepdims=True)
    raised = jnp.exp2(scores - top).astype(BF)
    return dot(raised, kv, NN), top


def packed(out, top):
    lane = lanes(out.shape)
    total = out[:, 112:113]
    tile = jnp.where(lane == 112, 1.0, out * (1.0 / total))
    for k, piece in enumerate(split3(top) + split3(total)):
        tile = jnp.where(lane == 114 + k, piece, tile)
    return tile.astype(BF)


def forward_kernel(
    x_ref, w_out_ref, fin_ref, att_ref, w_out_other, x1, x2, x3, q4, kv4, acc, tops, o1, o2, o3, o4, r1, r2, r3, r4, *sems
):
    place = Place()
    me = place.me
    xs, os, rs = (None, x1, x2, x3), (None, o1, o2, o3, o4), (None, r1, r2, r3, r4)
    go_send, go_recv, back_send, back_recv = sems[0:4], sems[4:8], sems[8:12], sems[12:16]

    def go(b, d, t):
        n, tiles = SEGMENT // 2**b, max(LOCAL // 2**b, 1)
        i = place.member(b)
        j = (i + d) % 2**b
        if b < 4:
            head = j * tiles + t
            k = (d - 1) * tiles + t
            return [
                remote(
                    x_ref.at[head, pl.ds(place.start(b, head), n), :],
                    xs[b].at[t, ds(i * n, n), :],
                    go_send[b - 1].at[k],
                    go_recv[b - 1].at[k],
                    place.device(b, j),
                )
            ]
        head, half = j // 2, j % 2
        start = place.start(4, head)
        k = (d - 1) * 2
        return [
            remote(
                x_ref.at[head, ds(start + half * 32, 32), 0:128],
                q4.at[ds(i * 32, 32), :],
                go_send[3].at[k],
                go_recv[3].at[k],
                place.device(4, j),
            ),
            remote(
                x_ref.at[head, pl.ds(start, 64), 128:256],
                kv4.at[ds(i * 64, 64), :],
                go_send[3].at[k + 1],
                go_recv[3].at[k + 1],
                place.device(4, j),
            ),
        ]

    def back(b, d, t):
        n, tiles = SEGMENT // 2**b, max(LOCAL // 2**b, 1)
        i = place.member(b)
        j = (i + d) % 2**b
        k = (d - 1) * tiles + t
        if b < 4:
            src, dst = o_at(b, t, j), rs[b].at[i * tiles + t]
        else:
            src, dst = o4.at[ds(j * 32, 32), :], r4.at[i // 2, ds(i % 2 * 32, 32), :]
        return remote(src, dst, back_send[b - 1].at[k], back_recv[b - 1].at[k], place.device(b, j))

    def o_at(b, t, j):
        n = SEGMENT // 2**b
        return os[b].at[t, ds(j * n, n), :]

    *sems, w_send, w_recv = sems
    place.greet(16, True)
    for b in (4, 3, 2, 1):
        over_peers(b, lambda d, t: [c.start() for c in go(b, d, t)])
    w_copy = remote(w_out_ref, w_out_other, w_send, w_recv, (me, 1 - place.y))
    w_copy.start()

    for b in (1, 2, 3):
        n, tiles = SEGMENT // 2**b, LOCAL // 2**b
        i = place.member(b)
        for t in range(tiles):
            head = i * tiles + t
            xs[b][t, ds(i * n, n), :] = x_ref[head, pl.ds(place.start(b, head), n), :]
    i = place.member(4)
    start = place.start(4, i // 2)
    q4[ds(i * 32, 32), :] = x_ref[i // 2, ds(start + i % 2 * 32, 32), 0:128]
    kv4[ds(i * 64, 64), :] = x_ref[i // 2, pl.ds(start, 64), 128:256]

    def local_head(h, _):
        for half in range(2):
            rows = pl.ds(half * 512, 512)
            out, top = attend(x_ref[h, rows, 0:128], x_ref[h, :, 128:256])
            acc[h, rows, :] = out
            tops[h, rows, :] = jnp.broadcast_to(top, out.shape)
        return 0

    lax.fori_loop(0, 4, local_head, 0)

    over_peers(4, lambda d, t: [c.wait_recv() for c in go(4, d, t)])
    o4[...] = packed(*attend(q4[...], kv4[...]))
    over_peers(4, lambda d, t: back(4, d, t).start())
    r4[i // 2, ds(i % 2 * 32, 32), :] = o4[ds(i * 32, 32), :]
    for b in (3, 2, 1):
        n, tiles = SEGMENT // 2**b, LOCAL // 2**b
        over_peers(b, lambda d, t: [c.wait_recv() for c in go(b, d, t)])

        def tile(t, _):
            for half in range(2):
                rows = pl.ds(half * 512, 512)
                os[b][t, rows, :] = packed(*attend(xs[b][t, rows, 0:128], xs[b][t, :, 128:256]))
            return 0

        lax.fori_loop(0, tiles, tile, 0)
        over_peers(b, lambda d, t: back(b, d, t).start())
        j = place.member(b)
        for t in range(tiles):
            rs[b][j * tiles + t] = os[b][t, ds(j * n, n), :]

    lax.fori_loop(4, 8, local_head, 0)

    for b in (4, 3, 2, 1):
        over_peers(b, lambda d, t: back(b, d, t).wait_recv())

    row = lax.broadcasted_iota(jnp.int32, (128, 256), 0)
    column = lax.broadcasted_iota(jnp.int32, (128, 256), 1)
    first = jnp.where(column < 128, 114, 117)
    picks = jnp.where((row >= first) & (row < first + 3), 1.0, 0.0).astype(BF)

    def merge_head(h, _):
        for b in (1, 2, 3, 4):
            n = SEGMENT // 2**b
            rows = pl.ds(place.start(b, h), n)
            part = rs[b][h]
            stats = dot(part, picks, NN)
            top = jnp.maximum(tops[h, rows, :], stats[:, 0:128])
            keep = jnp.exp2(tops[h, rows, :] - top)
            gain = jnp.exp2(stats[:, 0:128] - top) * stats[:, 128:256]
            acc[h, rows, :] = acc[h, rows, :] * keep + part.astype(F32) * gain
            tops[h, rows, :] = top
        out = acc[h]
        lane = lanes(out.shape)
        inverse = 1.0 / out[:, 112:113]
        out = jnp.where((lane >= 64) & (lane < 112), out * inverse, 0.0)
        fin_ref[h] = jnp.where(lane == 112, inverse, jnp.where(lane == 113, tops[h], out))
        return 0

    lax.fori_loop(0, LOCAL, merge_head, 0)

    def compact(n, _):
        rows = ds(n * 256, 256)
        pieces = [None] * 3
        for h in range(LOCAL):
            put_48(pieces, h, fin_ref[h, rows, :], 64)
        for k in range(3):
            att_ref[rows, pl.ds(k * 128, 128)] = pieces[k].astype(BF)
        return 0

    lax.fori_loop(0, 4, compact, 0)

    for b in (4, 3, 2, 1):
        over_peers(b, lambda d, t: [c.wait_send() for c in go(b, d, t)])
        over_peers(b, lambda d, t: back(b, d, t).wait_send())
    w_copy.wait()


ROWS = 768
HALVES = (384, 192, 96, 48)
LANDING = (0, 384, 576, 672, 720)


def far_bits(seq):
    return list(range(4, seq.bit_length() - 1))


class Halving:
    def __init__(self, place, seq, pieces, grads, shares, scratch):
        self.place, self.seq, self.pieces, self.grads, self.shares = place, seq, pieces, grads, shares
        self.landing, self.send, self.recv, self.far_send, self.far_recv = scratch

    @staticmethod
    def scratch(seq, pieces):
        far = len(far_bits(seq))
        return (
            [pltpu.VMEM((pieces, 720 + 48 * far, ROWS), BF)]
            + [pltpu.SemaphoreType.DMA((pieces * 4,)) for _ in range(2)]
            + [pltpu.SemaphoreType.DMA((pieces * max(far, 1),)) for _ in range(2)]
        )

    def copy(self, c, k):
        size = HALVES[k]
        start = self.place.low(k) + (1 - self.place.bit(k)) * size
        return remote(
            self.grads.at[c, pl.ds(pl.multiple_of(start, 48), size), :],
            self.landing.at[c, pl.ds(LANDING[k], size), :],
            self.send.at[c * 4 + k],
            self.recv.at[c * 4 + k],
            self.place.partner(k),
        )

    def add(self, c, k):
        start = self.place.low(k + 1)

        def step(i, _):
            rows = pl.ds(pl.multiple_of(start + i * 48, 48), 48)
            arrived = self.landing[c, pl.ds(pl.multiple_of(LANDING[k] + i * 48, 48), 48), :]
            value = (self.grads[c, rows, :].astype(F32) + arrived.astype(F32)).astype(BF)
            if k < 3:
                self.grads[c, rows, :] = value
            else:
                self.shares[c] = value
            return 0

        lax.fori_loop(0, HALVES[k] // 48, step, 0)

    def step(self, c, k):
        if k > 0:
            self.copy(c, k - 1).wait_recv()
            self.add(c, k - 1)
        if k < 4:
            self.copy(c, k).start()
            return
        bits = far_bits(self.seq)
        for n, bit in enumerate(bits):
            at = pl.ds(720 + 48 * n, 48)
            copy = remote(
                self.shares.at[c],
                self.landing.at[c, at, :],
                self.far_send.at[c * len(bits) + n],
                self.far_recv.at[c * len(bits) + n],
                self.place.partner(bit),
            )
            copy.start()
            copy.wait()
            self.shares[c] = (self.shares[c].astype(F32) + self.landing[c, at, :].astype(F32)).astype(BF)

    def finish(self):
        def piece(c, _):
            for k in range(4):
                self.copy(c, k).wait_send()
            return 0

        lax.fori_loop(0, self.pieces, piece, 0)


class Doubling:
    def __init__(self, place, pieces, shares, result, sems, first=0):
        self.place, self.pieces, self.shares, self.result, self.first = place, pieces, shares, result, first
        self.send, self.recv = sems

    @staticmethod
    def scratch(pieces):
        return [pltpu.SemaphoreType.DMA((pieces * 4,)) for _ in range(2)]

    def copy(self, c, k):
        rows = pl.ds(pl.multiple_of(self.place.low(k + 1), 48), HALVES[k])
        view = self.result.at[self.first + c, rows, :]
        return remote(view, view, self.send.at[c * 4 + k], self.recv.at[c * 4 + k], self.place.partner(k))

    def step(self, c, k):
        if k == 0:
            rows = pl.ds(pl.multiple_of(self.place.low(4), 48), 48)
            self.result[self.first + c, rows, :] = self.shares[c]
        else:
            self.copy(c, 4 - k).wait_recv()
        if k < 4:
            self.copy(c, 3 - k).start()

    def finish(self):
        def piece(c, _):
            for k in range(4):
                self.copy(c, k).wait_send()
            return 0

        lax.fori_loop(0, self.pieces, piece, 0)


def run_at(slot, work, table):
    for k in range(len(table[0])):
        c = sum((jnp.where(slot == times[k], n + 1, 0) for n, times in enumerate(table)), slot * 0)

        @pl.when(c > 0)
        def _():
            work.step(c - 1, k)


def sem_shapes(per_copy):
    counts = [4, 6, 7, 15 * per_copy]
    return [pltpu.SemaphoreType.DMA((c,)) for c in counts]


VMEM = pl.BlockSpec(memory_space=pltpu.VMEM)
ANY = pl.BlockSpec(memory_space=pl.ANY)
ORDER = tuple(int(f"{c:04b}"[::-1], 2) for c in range(16))


def attention_forward(x, w_output):
    shapes = [
        ((LOCAL, SEGMENT, 128), F32),
        ((SEGMENT, LOCAL * HEAD_DIM), BF),
        (w_output.shape, BF),
        ((4, SEGMENT, 256), BF),
        ((2, SEGMENT, 256), BF),
        ((1, SEGMENT, 256), BF),
        ((512, 128), BF),
        ((SEGMENT, 128), BF),
    ]
    scratch = [
        ((LOCAL, SEGMENT, 128), F32),
        ((LOCAL, SEGMENT, 128), F32),
        ((4, SEGMENT, 128), BF),
        ((2, SEGMENT, 128), BF),
        ((1, SEGMENT, 128), BF),
        ((512, 128), BF),
        ((LOCAL, 512, 128), BF),
        ((LOCAL, 256, 128), BF),
        ((LOCAL, 128, 128), BF),
        ((LOCAL, 64, 128), BF),
    ]
    return pl.pallas_call(
        forward_kernel,
        out_shape=[jax.ShapeDtypeStruct(*s) for s in shapes],
        in_specs=[VMEM, ANY],
        out_specs=[VMEM, VMEM, ANY] + [VMEM] * 5,
        scratch_shapes=[pltpu.VMEM(*s) for s in scratch]
        + sem_shapes(2) + sem_shapes(2) + sem_shapes(1) + sem_shapes(1) + [pltpu.SemaphoreType.DMA] * 2,
        compiler_params=pltpu.CompilerParams(
            collective_id=0, has_side_effects=True, vmem_limit_bytes=56 * 2**20
        ),
        name="attention_forward",
    )(x, w_output)


def pair_grads(q, d, kv_at, put):
    lane = lanes(q.shape)
    zero = jnp.zeros_like(d)
    queries = q + jnp.where(lane < 64, d, zero)
    grads = jnp.where(lane < 64, zero, d)
    total = None
    for half in range(2):
        kv = kv_at(half)
        probs = jnp.exp2(dot(kv, queries, NT))
        grad_scores = (probs * dot(kv, grads, NT)).astype(BF)
        put(half, dot(grad_scores, queries, NN) + dot(probs.astype(BF), grads, NN))
        part = dot(kv, grad_scores, TN)
        total = part if total is None else total + part
    return total.T


def backward_kernel(
    seq, x_ref, x1, x2, x3, q4, kv4, fin_ref, do_ref, ffn_ref, grads_in, shares_in, g_ref, sum_ref, ffn_other, shares_ref, grads_r,
    grads, d0, d1, d2, d3, d4, total, g1, g2, g3, gq4, gkv4, r1, r2, r3, rq4, rkv4, *sems
):
    place = Place()
    *sems, fill_sem, ffn_send, ffn_recv = sems
    halving = Halving(place, seq, 2, grads, shares_ref, sems[16:21])
    doubling = Doubling(place, 2, shares_in, grads_r, sems[21:])

    def reduce_at(slot):
        run_at(slot, doubling, ((0, 1, 3, 5, 6), (4, 5, 7, 9, 10)))
        run_at(slot, halving, ((8, 9, 12, 13, 14), (10, 11, 14, 15, 16)))

    for c in range(2):
        pltpu.make_async_copy(grads_in.at[c], grads.at[c], fill_sem.at[c]).start()
    ffn_copy = remote(ffn_ref, ffn_other, ffn_send, ffn_recv, (place.me, 1 - place.y))
    me = place.me
    xs, dd, gs, rs = (None, x1, x2, x3), (None, d1, d2, d3), (None, g1, g2, g3), (None, r1, r2, r3)
    go_send, go_recv, back_send, back_recv = sems[0:4], sems[4:8], sems[8:12], sems[12:16]

    def go(b, d, t):
        n, tiles = SEGMENT // 2**b, max(LOCAL // 2**b, 1)
        i = place.member(b)
        j = (i + d) % 2**b
        k = (d - 1) * tiles + t
        if b < 4:
            head = j * tiles + t
            src, dst = d0.at[head, pl.ds(place.start(b, head), n), :], dd[b].at[t, ds(i * n, n), :]
        else:
            start = place.start(4, j // 2)
            src, dst = d0.at[j // 2, ds(start + j % 2 * 32, 32), :], d4.at[ds(i * 32, 32), :]
        return remote(src, dst, go_send[b - 1].at[k], go_recv[b - 1].at[k], place.device(b, j))

    def back(b, d, t):
        n, tiles = SEGMENT // 2**b, max(LOCAL // 2**b, 1)
        i = place.member(b)
        j = (i + d) % 2**b
        device = place.device(b, j)
        if b < 4:
            k = (d - 1) * tiles + t
            return [
                remote(
                    gs[b].at[t, ds(j * n, n), :],
                    rs[b].at[i * tiles + t],
                    back_send[b - 1].at[k],
                    back_recv[b - 1].at[k],
                    device,
                )
            ]
        k = (d - 1) * 2
        return [
            remote(
                gq4.at[ds(j * 32, 32), :],
                rq4.at[i // 2, ds(i % 2 * 32, 32), :],
                back_send[3].at[k],
                back_recv[3].at[k],
                device,
            ),
            remote(
                gkv4.at[ds(j * 64, 64), :],
                rkv4.at[i % 2, i // 2],
                back_send[3].at[k + 1],
                back_recv[3].at[k + 1],
                device,
            ),
        ]

    def prepare(h, _):
        fin = fin_ref[h]
        lane = lanes(fin.shape)
        value_lane = (lane >= 64) & (lane < 112)
        grad = (do_ref[:, ds(h * 128, 128)].astype(F32) * fin[:, 112:113]).astype(BF).astype(F32)
        delta = jnp.sum(jnp.where(value_lane, grad * fin, 0.0), axis=1, keepdims=True)
        tile = jnp.where(value_lane, grad, 0.0)
        high, middle, low = split3(-delta)
        tile = jnp.where(lane == 112, high, jnp.where(lane == 113, middle, tile))
        for k, piece in enumerate(split3(-fin[:, 113:114])):
            tile = jnp.where(lane == 52 + k, piece, tile)
        d0[h] = tile.astype(BF)
        return 0

    lax.fori_loop(0, LOCAL, prepare, 0)
    place.greet(seq, True)
    for b in (4, 3, 2, 1):
        over_peers(b, lambda d, t: go(b, d, t).start())
    ffn_copy.start()
    for c in range(2):
        pltpu.make_async_copy(grads_in.at[c], grads.at[c], fill_sem.at[c]).wait()
    for b in (1, 2, 3):
        n, tiles = SEGMENT // 2**b, LOCAL // 2**b
        i = place.member(b)
        for t in range(tiles):
            head = i * tiles + t
            dd[b][t, ds(i * n, n), :] = d0[head, pl.ds(place.start(b, head), n), :]
    i = place.member(4)
    d4[ds(i * 32, 32), :] = d0[i // 2, ds(place.start(4, i // 2) + i % 2 * 32, 32), :]

    def local_head(h, _):
        def put(half, grad):
            total[h, pl.ds(half * 512, 512), 128:256] = grad

        total[h, :, 0:128] = pair_grads(
            x_ref[h, :, 0:128], d0[h], lambda half: x_ref[h, pl.ds(half * 512, 512), 128:256], put
        )
        reduce_at(jnp.where(h < 4, h, h + 8))
        return 0

    lax.fori_loop(0, 4, local_head, 0)

    over_peers(4, lambda d, t: go(4, d, t).wait_recv())

    def put4(half, grad):
        gkv4[pl.ds(half * 512, 512), :] = grad.astype(BF)

    gq4[...] = pair_grads(q4[...], d4[...], lambda half: kv4[pl.ds(half * 512, 512), :], put4).astype(BF)
    over_peers(4, lambda d, t: [c.start() for c in back(4, d, t)])
    rq4[i // 2, ds(i % 2 * 32, 32), :] = gq4[ds(i * 32, 32), :]
    rkv4[i % 2, i // 2] = gkv4[ds(i * 64, 64), :]
    reduce_at(jnp.int32(4))
    slot = 5
    for b in (3, 2, 1):
        n, tiles = SEGMENT // 2**b, LOCAL // 2**b
        over_peers(b, lambda d, t: go(b, d, t).wait_recv())

        def tile(t, _):
            def put(half, grad):
                gs[b][t, pl.ds(half * 512, 512), 128:256] = grad.astype(BF)

            gs[b][t, :, 0:128] = pair_grads(
                xs[b][t, :, 0:128], dd[b][t], lambda half: xs[b][t, pl.ds(half * 512, 512), 128:256], put
            ).astype(BF)
            reduce_at(slot + t)
            return 0

        lax.fori_loop(0, tiles, tile, 0)
        slot += tiles
        over_peers(b, lambda d, t: [c.start() for c in back(b, d, t)])
        j = place.member(b)
        for t in range(tiles):
            rs[b][j * tiles + t] = gs[b][t, ds(j * n, n), :]

    lax.fori_loop(4, 8, local_head, 0)

    for b in (4, 3, 2, 1):
        over_peers(b, lambda d, t: [c.wait_recv() for c in back(b, d, t)])

    def finish(h, _):
        for b in (1, 2, 3):
            n = SEGMENT // 2**b
            rows = pl.ds(place.start(b, h), n)
            total[h, rows, :] += rs[b][h].astype(F32)
        rows = pl.ds(place.start(4, h), 64)
        total[h, rows, 0:128] += rq4[h].astype(F32)
        total[h, rows, 128:256] += rkv4[0, h].astype(F32) + rkv4[1, h].astype(F32)
        return 0

    lax.fori_loop(0, LOCAL, finish, 0)
    reduce_at(jnp.int32(16))
    sum_ref[...] = jnp.zeros_like(sum_ref)

    def compact(i, _):
        rows = ds(i * 256, 256)
        pieces = [[None] * 3 for _ in range(3)]
        for h in range(LOCAL):
            live = (x_ref[h, rows, 176:177].astype(F32) >= 0.0).astype(F32)
            grad_kv = total[h, rows, 128:256]
            put_48(pieces[0], h, total[h, rows, 0:128] * SCALE)
            put_48(pieces[1], h, grad_kv * (live * (1.0 / LOG2E)))
            put_48(pieces[2], h, pltpu.roll(grad_kv, 64, 1))
        for k in range(3):
            for n in range(3):
                at = pl.ds(n * 128, 128)
                g_ref[k, rows, at] = pieces[k][n].astype(BF)
                sum_ref[k, :, at] += jnp.broadcast_to(jnp.sum(pieces[k][n], axis=0, keepdims=True), (8, 128))
        return 0

    lax.fori_loop(0, 4, compact, 0)

    for b in (4, 3, 2, 1):
        over_peers(b, lambda d, t: go(b, d, t).wait_send())
        over_peers(b, lambda d, t: [c.wait_send() for c in back(b, d, t)])
    halving.finish()
    doubling.finish()
    ffn_copy.wait()


def attention_backward(x, saved, fin, grad_out, ffn_part, grads, shares):
    seq = lax.axis_size("seq")
    shapes = [
        ((3, SEGMENT, LOCAL * HEAD_DIM), BF),
        ((3, 8, LOCAL * HEAD_DIM), F32),
        (ffn_part.shape, BF),
        ((2, 48, ROWS), BF),
        ((2, ROWS, ROWS), BF),
    ]
    scratch = [
        (grads.shape, BF),
        ((LOCAL, SEGMENT, 128), BF),
        ((4, SEGMENT, 128), BF),
        ((2, SEGMENT, 128), BF),
        ((1, SEGMENT, 128), BF),
        ((512, 128), BF),
        ((LOCAL, SEGMENT, 256), F32),
        ((4, SEGMENT, 256), BF),
        ((2, SEGMENT, 256), BF),
        ((1, SEGMENT, 256), BF),
        ((512, 128), BF),
        ((SEGMENT, 128), BF),
        ((LOCAL, 512, 256), BF),
        ((LOCAL, 256, 256), BF),
        ((LOCAL, 128, 256), BF),
        ((LOCAL, 64, 128), BF),
        ((2, LOCAL, 64, 128), BF),
    ]
    return pl.pallas_call(
        functools.partial(backward_kernel, seq),
        out_shape=[jax.ShapeDtypeStruct(*s) for s in shapes],
        in_specs=[VMEM] * 8 + [ANY, ANY, VMEM],
        out_specs=[VMEM, VMEM, ANY, VMEM, VMEM],
        scratch_shapes=[pltpu.VMEM(*s) for s in scratch]
        + sem_shapes(1) + sem_shapes(1) + sem_shapes(2) + sem_shapes(2)
        + Halving.scratch(seq, 2)
        + Doubling.scratch(2)
        + [pltpu.SemaphoreType.DMA((2,)), pltpu.SemaphoreType.DMA, pltpu.SemaphoreType.DMA],
        compiler_params=pltpu.CompilerParams(
            collective_id=1, has_side_effects=True, vmem_limit_bytes=60 * 2**20
        ),
        name="attention_backward",
    )(x, *saved, fin, grad_out, ffn_part, grads, shares)


CHUNK = 128


def put_spread(planes, block, value):
    for t in range(value.shape[1] // 128):
        planes[t, pl.ds(ORDER[block], 64, stride=16), :] = value[:, t * 128 : (t + 1) * 128]


def from_planes(planes, out):
    def step(i, _):
        rows = ds(i * 128, 128)
        for t in range(planes.shape[0]):
            out[rows, pl.ds(t * 128, 128)] = planes[t, rows, :]
        return 0

    lax.fori_loop(0, SEGMENT // 128, step, 0)


def to_planes(value_ref, planes):
    def step(i, _):
        rows = ds(i * 128, 128)
        for t in range(planes.shape[0]):
            planes[t, rows, :] = value_ref[rows, pl.ds(t * 128, 128)].astype(F32)
        return 0

    lax.fori_loop(0, SEGMENT // 128, step, 0)


def take_spread(planes, block):
    return jnp.concatenate(
        [planes[t, pl.ds(ORDER[block], 64, stride=16), :] for t in range(planes.shape[0])], axis=1
    )


def first_kernel(
    tokens_ref, cot_ref, valid_ref, gain_ref, shift_ref, w_ref, bias_ref,
    x_ref, normed_ref, tokens_out, cot_out, stats_ref, planes
):
    to_planes(tokens_ref, planes)
    for b in range(16):
        tokens_out[pl.ds(b * 64, 64), :] = take_spread(planes, b).astype(BF)
    to_planes(cot_ref, planes)
    for b in range(16):
        cot_out[pl.ds(b * 64, 64), :] = take_spread(planes, b)
    count = jnp.sum(valid_ref[...])

    def chunk(n, _):
        rows = ds(n * 256, 256)
        x = tokens_out[rows, :].astype(F32)
        mean, rs = norm_stats(x)
        stats_ref[0, rows, :], stats_ref[1, rows, :] = mean, rs
        normed = ((x - widen(mean, x)) * widen(rs, x) * gain_ref[...] + shift_ref[...]).astype(BF)
        normed_ref[rows, :] = normed
        queries = (dot(normed, w_ref[0], NN) + bias_ref[0:1, :]) * (SCALE * LOG2E)
        keys = dot(normed, w_ref[1], NN)
        values = dot(normed, w_ref[2], NN) + bias_ref[1:2, :]
        at = n * 256 + lax.broadcasted_iota(jnp.int32, (256, 128), 0)
        live = (at % 64 * 16 + reversed_bits(at // 64, 4)) < count
        lane = lanes((256, 128))
        padding = jnp.where(live, 0.0, masked_score)
        ones = ((lane >= 52) & (lane < 55)) | (lane == 112) | (lane == 113)
        for h in range(LOCAL):
            x_ref[h, rows, 0:128] = jnp.where(lane == 48, 1.0, take_48(queries, h, 0)).astype(BF)
            key = jnp.where(live, take_48(keys, h, 0), 0.0) + take_48(values, h, 64)
            x_ref[h, rows, 128:256] = jnp.where(ones, 1.0, jnp.where(lane == 48, padding, key)).astype(BF)
        return 0

    lax.fori_loop(0, 4, chunk, 0)


def first_part(tokens, cotangent, valid, gain, shift, w_project, bias):
    width = tokens.shape[1]
    shapes = [
        ((LOCAL, SEGMENT, 256), BF),
        (tokens.shape, BF),
        (tokens.shape, BF),
        (tokens.shape, F32),
        ((2, SEGMENT, 128), F32),
    ]
    return pl.pallas_call(
        first_kernel,
        out_shape=[jax.ShapeDtypeStruct(*s) for s in shapes],
        in_specs=[VMEM] * 7,
        out_specs=[VMEM] * len(shapes),
        scratch_shapes=[pltpu.VMEM((width // 128, SEGMENT, 128), F32)],
        compiler_params=pltpu.CompilerParams(vmem_limit_bytes=56 * 2**20),
        name="first_part",
    )(tokens, cotangent, valid, gain, shift, w_project, bias)


GELU_C = math.sqrt(2 / math.pi)


def middle_kernel(
    seq, att_ref, w_out_ref, w_out_other, tokens_ref, cot_ref, w_expand, b_expand, w_reduce, b_output, gain_ref, shift_ref,
    middle_ref, gm_ref, do_ref, ffn_ref, grads_e, shares_ref, grads_o, small_ref,
    att, w_out, stats, normed, active, grad_expand, cot_low, part, other, gm_low, grads_r, sums, sums_e,
    att_send, att_recv, part_send, part_recv, *sems
):
    place = Place()
    y = place.y
    peer = (place.me, 1 - y)
    halving = Halving(place, seq, 2, grads_r, shares_ref, sems)
    chunk, chunks, width = 256, SEGMENT // 256, tokens_ref.shape[1]

    def att_copy(n):
        rows = ds(n * chunk, chunk)
        return remote(att_ref.at[rows, :], att.at[y, rows, :], att_send.at[n], att_recv.at[n], peer)

    def part_copy(n):
        rows = ds(n * chunk, chunk)
        return remote(part.at[rows, :], other.at[rows, :], part_send.at[n], part_recv.at[n], peer)

    place.greet(seq, True)
    for n in range(chunks):
        att_copy(n).start()
    att[y] = att_ref[...]
    w_out[y] = w_out_ref[...]
    w_out[1 - y] = w_out_other[...]
    sums[...] = jnp.zeros_like(sums)
    sums_e[...] = jnp.zeros_like(sums_e)

    def ahead(n, _):
        rows = ds(n * chunk, chunk)
        cot = cot_ref[rows, :]
        sums[0:8] += row_sums(cot)
        low = cot.astype(BF)
        cot_low[rows, :] = low
        att_copy(n).wait_recv()
        branch = dot(att[0, rows, :], w_out[0], NN) + dot(att[1, rows, :], w_out[1], NN)
        middle = tokens_ref[rows, :].astype(F32) + (branch + b_output[...])
        middle_ref[rows, :] = middle
        mean, rs = norm_stats(middle)
        stats[0, rows, :], stats[1, rows, :] = mean, rs
        norm = ((middle - widen(mean, middle)) * widen(rs, middle) * gain_ref[...] + shift_ref[...]).astype(BF)
        normed[rows, :] = norm
        value = None
        for k in range(w_expand.shape[1] // width):
            at = pl.ds(k * width, width)
            expand = dot(norm, w_expand[:, at], NN) + b_expand[:, at]
            square = expand * expand
            bent = jnp.tanh(GELU_C * expand * (1.0 + 0.044715 * square))
            gate = 0.5 * (1.0 + bent)
            active[rows, at] = (expand * gate).astype(BF)
            slope = gate + (0.5 * GELU_C) * expand * (1.0 - bent * bent) * (1.0 + (3 * 0.044715) * square)
            grad = dot(low, w_reduce[at, :], NT) * slope
            sums_e[:, at] += row_sums(grad)
            grad = grad.astype(BF)
            grad_expand[rows, at] = grad
            piece = dot(grad, w_expand[:, at], NT)
            value = piece if value is None else value + piece
        part[rows, :] = value.astype(BF)
        part_copy(n).start()
        return 0

    lax.fori_loop(0, chunks, ahead, 0)

    def behind(n, _):
        rows = ds(n * chunk, chunk)
        part_copy(n).wait_recv()
        grad = part[rows, :].astype(F32) + other[rows, :].astype(F32)
        rs = widen(stats[1, rows, :], grad)
        xhat = (middle_ref[rows, :] - widen(stats[0, rows, :], grad)) * rs
        sums[8:16] += row_sums(grad * xhat)
        sums[16:24] += row_sums(grad)
        gm = cot_ref[rows, :] + norm_back(grad, xhat, rs, gain_ref[...])
        gm_ref[rows, :] = gm
        sums[24:32] += row_sums(gm)
        low = gm.astype(BF)
        gm_low[rows, :] = low
        grad_att = dot(low, w_out_ref[...], NT)
        for h in range(LOCAL):
            do_ref[rows, pl.ds(h * 128, 128)] = take_48(grad_att, h, 64).astype(BF)
        return 0

    for k in range(2):
        grads_r[k] = dot(active[:, pl.ds(k * width, width)], cot_low[...], TN).astype(BF)
        halving.step(k, 0)
    behind(0, 0)
    halving.step(0, 1)
    halving.step(1, 1)
    grads_e[0] = dot(normed[...], grad_expand[:, pl.ds(0, width)], TN).astype(BF)
    halving.step(0, 2)
    behind(1, 0)
    halving.step(1, 2)
    halving.step(0, 3)
    grads_e[1] = dot(normed[...], grad_expand[:, pl.ds(width, width)], TN).astype(BF)
    halving.step(1, 3)
    ffn_ref[...] = dot(active[...], w_reduce[...], NN).astype(BF)
    behind(2, 0)
    halving.step(0, 4)
    halving.step(1, 4)
    behind(3, 0)
    for k in range(2):
        at = pl.ds(k * (width // 2), width // 2)
        grads_o[pl.ds(k * 384, 384), :] = dot(att_ref[...], gm_low[:, at], TN).astype(BF)
    put_vector(small_ref, 0, sums[24:32])
    put_vector(small_ref, 6, sums[8:16])
    put_vector(small_ref, 12, sums[16:24])
    put_vector(small_ref, 18, sums_e[...])
    put_vector(small_ref, 30, sums[0:8])
    small_ref[36:48, :] = jnp.zeros((12, 128), F32)
    for n in range(chunks):
        att_copy(n).wait_send()
        part_copy(n).wait_send()
    halving.finish()


def middle_part(attended, w_output, w_out_other, tokens, cot, w_expand, b_expand, w_reduce, b_output, gain, shift):
    seq = lax.axis_size("seq")
    rows, width = tokens.shape
    hidden = w_expand.shape[1]
    shapes = [
        ((rows, width), F32),
        ((rows, width), F32),
        ((rows, LOCAL * 128), BF),
        ((rows, width), BF),
        ((2, ROWS, ROWS), BF),
        ((2, 48, ROWS), BF),
        ((ROWS, ROWS // 2), BF),
        ((48, 128), F32),
    ]
    scratch = [
        ((2,) + attended.shape, BF),
        ((2,) + w_output.shape, BF),
        ((2, rows, 128), F32),
        ((rows, width), BF),
        ((rows, hidden), BF),
        ((rows, hidden), BF),
        ((rows, width), BF),
        ((rows, width), BF),
        ((rows, width), BF),
        ((rows, width), BF),
        ((2, ROWS, ROWS), BF),
        ((32, width), F32),
        ((8, hidden), F32),
    ]
    return pl.pallas_call(
        functools.partial(middle_kernel, seq),
        out_shape=[jax.ShapeDtypeStruct(*s) for s in shapes],
        in_specs=[VMEM] * 11,
        out_specs=[VMEM] * len(shapes),
        scratch_shapes=[pltpu.VMEM(*s) for s in scratch]
        + [pltpu.SemaphoreType.DMA((4,)) for _ in range(4)]
        + Halving.scratch(seq, 2),
        compiler_params=pltpu.CompilerParams(
            collective_id=3, has_side_effects=True, vmem_limit_bytes=60 * 2**20
        ),
        name="middle_part",
    )(attended, w_output, w_out_other, tokens, cot, w_expand, b_expand, w_reduce, b_output, gain, shift)


def last_kernel(
    seq, g_ref, w_ref, normed_ref, tokens_ref, middle_ref, gain_ref, w_out_ref, small_in, sum_ref, shares_in, stats,
    out_ref, grads_ref, early_ref, late_ref,
    grads, shares, part, other, small_ref, early_in, late, late_in, sums, planes, part_send, part_recv, early_send, early_recv, late_send, late_recv,
    *sems
):
    place = Place()
    halving = Halving(place, seq, 2, grads, shares, sems[0:5])
    gathers = Doubling(place, 2, shares_in, grads_ref, sems[5:7])
    last_gathers = Doubling(place, 2, shares, grads_ref, sems[7:9], 2)
    far_send, far_recv = sems[9:]
    i = place.member(4)
    chunks = SEGMENT // CHUNK
    put_vector(small_ref, 0, sum_ref[0] * 0.125)
    put_vector(small_ref, 3, sum_ref[2] * 0.125)
    small_ref[6:48, :] = small_in[0:42, :]

    def to_all(src, landing, send, recv):
        def each(action):
            def step(d, _):
                action(remote(src, landing.at[i], send.at[d - 1], recv.at[d - 1], place.device(4, (i + d) % 16)))
                return 0

            lax.fori_loop(1, 16, step, 0)

        return each

    def total_of(src, landing):
        def step(j, value):
            return value + landing[j]

        landing[i] = src[...]
        return lax.fori_loop(1, 16, step, landing[0])

    def far_total(result, n):
        for k, bit in enumerate(far_bits(seq)):
            landing = (early_in, late_in)[n].at[16 + k]
            copy = remote(result, landing, far_send.at[n * 8 + k], far_recv.at[n * 8 + k], place.partner(bit))
            copy.start()
            copy.wait()
            result[...] = result[...] + landing[...]

    def exchange(n):
        rows = ds(n * CHUNK, CHUNK)
        return remote(
            part.at[rows, :], other.at[rows, :], part_send.at[n], part_recv.at[n], (place.me, 1 - place.y)
        )

    def partial(n, _):
        rows = ds(n * CHUNK, CHUNK)
        value = dot(g_ref[0, rows, :], w_ref[0], NT)
        value += dot(g_ref[1, rows, :], w_ref[1], NT)
        value += dot(g_ref[2, rows, :], w_ref[2], NT)
        part[rows, :] = value.astype(BF)
        exchange(n).start()
        return 0

    place.greet(seq, True)
    lax.fori_loop(0, 2, partial, 0)
    early_all = to_all(small_ref, early_in, early_send, early_recv)
    early_all(lambda copy: copy.start())
    for k in range(3):
        at = pl.ds(k % 2 * 384, 384)
        grads[k // 2, :, at] = dot(normed_ref[...], g_ref[k], TN).astype(BF)
        if k == 1:
            halving.step(0, 0)
    grads[1, :, pl.ds(384, 384)] = w_out_ref[...]
    halving.step(1, 0)
    lax.fori_loop(2, chunks, partial, 0)
    sums[...] = jnp.zeros_like(sums)

    for n in range(chunks):
        exchange(n).wait_recv()
        rows = pl.ds(n * CHUNK, CHUNK)
        grad = part[rows, :].astype(F32) + other[rows, :].astype(F32)
        rs = widen(stats[1, rows, :], grad)
        xhat = (tokens_ref[rows, :].astype(F32) - widen(stats[0, rows, :], grad)) * rs
        sums[0:8] += row_sums(grad * xhat)
        sums[8:16] += row_sums(grad)
        grad = middle_ref[rows, :] + norm_back(grad, xhat, rs, gain_ref[...])
        for k in range(CHUNK // 64):
            put_spread(planes, n * (CHUNK // 64) + k, grad[k * 64 : (k + 1) * 64])
        for c in range(2):
            if 1 <= n + 1 - c <= 4:
                halving.step(c, n + 1 - c)
            if 0 <= n - 3 - c <= 4:
                last_gathers.step(c, n - 3 - c)
        for c in range(2):
            if 0 <= n - c <= 4:
                gathers.step(c, n - c)
    for k in range(2):
        put_vector(late, k * 8, sums[k * 8 : k * 8 + 8])
        late[pl.ds(k * 8 + 6, 2), :] = jnp.zeros((2, 128), F32)
    late_all = to_all(late, late_in, late_send, late_recv)
    late_all(lambda copy: copy.start())
    last_gathers.step(1, 4)
    from_planes(planes, out_ref)
    early_all(lambda copy: copy.wait_recv())
    early_ref[...] = total_of(small_ref, early_in)
    far_total(early_ref, 0)
    late_all(lambda copy: copy.wait_recv())
    late_ref[...] = total_of(late, late_in)
    far_total(late_ref, 1)

    def sent(n, _):
        exchange(n).wait_send()
        return 0

    lax.fori_loop(0, chunks, sent, 0)
    early_all(lambda copy: copy.wait_send())
    late_all(lambda copy: copy.wait_send())
    halving.finish()
    gathers.finish()
    last_gathers.finish()


def last_part(g, w_project, normed, tokens, grad_middle, gain, grad_w_out, small, g_sums, shares, stats):
    seq = lax.axis_size("seq")
    far = len(far_bits(seq))
    width = normed.shape[1]
    shapes = [
        (normed.shape, F32),
        ((4, ROWS, ROWS), BF),
        (small.shape, F32),
        ((16, 128), F32),
    ]
    scratch = [
        ((2, ROWS, ROWS), BF),
        ((2, 48, ROWS), BF),
        (normed.shape, BF),
        (normed.shape, BF),
        (small.shape, F32),
        ((16 + far,) + small.shape, F32),
        ((16, 128), F32),
        ((16 + far, 16, 128), F32),
        ((16, width), F32),
        ((width // 128, SEGMENT, 128), F32),
    ]
    chunks = SEGMENT // CHUNK
    counts = (chunks, chunks, 15, 15, 15, 15)
    return pl.pallas_call(
        functools.partial(last_kernel, seq),
        out_shape=[jax.ShapeDtypeStruct(*s) for s in shapes],
        in_specs=[VMEM] * 11,
        out_specs=[VMEM] * len(shapes),
        scratch_shapes=[pltpu.VMEM(*s) for s in scratch]
        + [pltpu.SemaphoreType.DMA((c,)) for c in counts]
        + Halving.scratch(seq, 2) + Doubling.scratch(2) + Doubling.scratch(2)
        + [pltpu.SemaphoreType.DMA((16,)) for _ in range(2)],
        compiler_params=pltpu.CompilerParams(
            collective_id=2, has_side_effects=True, vmem_limit_bytes=56 * 2**20
        ),
        name="last_part",
    )(g, w_project, normed, tokens, grad_middle, gain, grad_w_out, small, g_sums, shares, stats)


def from_residue(rows):
    shaped = rows.reshape((2, 2, 2, 2, rows.shape[0] // 16) + rows.shape[1:])
    rest = tuple(range(5, shaped.ndim))
    return shaped.transpose((4, 3, 2, 1, 0) + rest).reshape(rows.shape)


def body(
    tokens,
    cotangent,
    valid_tiles,
    gain_first,
    shift_first,
    w_project,
    bias_project,
    w_output,
    bias_output,
    gain_second,
    shift_second,
    w_expand,
    bias_expand,
    w_reduce,
    bias_reduce,
):
    width = tokens.shape[1]
    half = width // 2
    w_project = w_project.transpose(1, 0, 2)
    x, normed, tokens, cot, stats = first_part(
        tokens, cotangent, valid_tiles.reshape(8, -1), gain_first[None], shift_first[None], w_project, bias_project
    )
    fin, attended, w_out_other, *saved = attention_forward(x, w_output)
    middle, grad_middle, grad_attended, ffn_part, grads_e, shares_r, grads_o, small = middle_part(
        attended, w_output, w_out_other, tokens, cot, w_expand, bias_expand[None], w_reduce,
        bias_output[None], gain_second[None], shift_second[None],
    )
    g, g_sums, ffn_other, shares_e, grads_r = attention_backward(
        x, saved, fin, grad_attended, ffn_part, grads_e, shares_r
    )
    layer_out = middle + (ffn_part.astype(F32) + ffn_other.astype(F32)) + bias_reduce
    grad_tokens, grads, small, late = last_part(
        g, w_project, normed, tokens, grad_middle, gain_first[None], grads_o, small, g_sums, shares_e, stats
    )
    small = small.reshape(-1)
    late = late.reshape(2, 8 * 128)[:, :width]
    parts = [small[k * width : (k + 1) * width] for k in range(7)]
    grads_r, grads = grads_r.astype(F32), grads.astype(F32)
    grad_w_project = jnp.stack([grads[2, :, :half], grads[2, :, half:], grads[3, :, :half]], axis=1)
    grad_w_output = jnp.concatenate([grads[3, :half, half:], grads[3, half:, half:]], axis=1)
    return (
        from_residue(layer_out),
        grad_tokens,
        late[0],
        late[1],
        grad_w_project,
        parts[0].reshape(2, half),
        grad_w_output,
        parts[1],
        parts[2],
        parts[3],
        jnp.concatenate([grads[0], grads[1]], axis=1),
        small[4 * width : 6 * width],
        grads_r.reshape(-1, width),
        parts[6],
    )


def solution(mesh):
    in_specs = (
        P("seq", None),
        P("seq", None),
        P("seq"),
        P(),
        P(),
        P(None, None, "heads"),
        P(None, "heads"),
        P("heads", None),
        P(),
        P(),
        P(),
        P(None, "heads"),
        P("heads"),
        P("heads", None),
        P(),
    )
    out_specs = (
        P("seq", None),
        P("seq", None),
        P(),
        P(),
        P(None, None, "heads"),
        P(None, "heads"),
        P("heads", None),
        P(),
        P(),
        P(),
        P(None, "heads"),
        P("heads"),
        P("heads", None),
        P(),
    )
    return jax.shard_map(body, mesh=mesh, in_specs=in_specs, out_specs=out_specs, check_vma=False)
```

```python
import functools
import math

import jax
import jax.numpy as jnp
from jax import lax
from jax.experimental import pallas as pl
from jax.experimental.pallas import tpu as pltpu
from jax.sharding import PartitionSpec as P

HEADS = 16
HEAD_DIM = 48
SEGMENT = 1024
BRANCHES = 5
LOCAL = 8

MESH = pl.DeviceIdType.MESH
BF = jnp.bfloat16
F32 = jnp.float32
NT = (((1,), (1,)), ((), ()))
TN = (((0,), (0,)), ((), ()))
NN = (((1,), (0,)), ((), ()))

masked_score = -1000000000.0
layer_eps = 1e-05
SCALE = HEAD_DIM ** (-0.5)
LOG2E = math.log2(math.e)


def dot(a, b, dims):
    return lax.dot_general(a, b, dims, preferred_element_type=F32)


def lanes(shape):
    return lax.broadcasted_iota(jnp.int32, shape, len(shape) - 1)


def reversed_bits(value, bits):
    out = value * 0
    for k in range(bits):
        out = out * 2 + (value // 2**k) % 2
    return out


def split3(value):
    high = value.astype(BF).astype(F32)
    rest = value - high
    middle = rest.astype(BF).astype(F32)
    return high, middle, rest - middle


def put_48(pieces, head, value, source=0):
    lane = lanes(value.shape)
    tile, off = head * 48 // 128, head * 48 % 128
    value = jnp.where((lane >= source) & (lane < source + 48), value, 0.0)
    if off != source:
        value = pltpu.roll(value, (off - source) % 128, 1)
    if off + 48 > 128:
        parts = [(tile, jnp.where(lane >= off, value, 0.0)), (tile + 1, jnp.where(lane < off - 80, value, 0.0))]
    else:
        parts = [(tile, value)]
    for k, part in parts:
        pieces[k] = part if pieces[k] is None else pieces[k] + part


def take_48(value, head, at):
    tile, off = head * 48 // 128, head * 48 % 128
    shift = (at - off) % 128
    turn = lambda k: pltpu.roll(value[:, k * 128 : (k + 1) * 128], shift, 1) if shift else value[:, k * 128 : (k + 1) * 128]
    out = turn(tile)
    lane = lanes(out.shape)
    if off + 48 > 128:
        out = jnp.where(lane < at + 128 - off, out, turn(tile + 1))
    return jnp.where((lane >= at) & (lane < at + 48), out, 0.0)


def row_mean(value):
    ones = jnp.ones((value.shape[1], 128), BF)
    high = value.astype(BF)
    low = (value - high.astype(F32)).astype(BF)
    return (dot(high, ones, NN) + dot(low, ones, NN)) * (1.0 / value.shape[1])


def widen(tile, like):
    return jnp.concatenate([tile] * (like.shape[1] // 128), axis=1)


def row_sums(value):
    return jnp.sum(value.reshape(value.shape[0] // 8, 8, value.shape[1]), axis=0)


def put_vector(rows, first, partial):
    value = jnp.sum(partial, axis=0, keepdims=True)
    for t in range(value.shape[1] // 128):
        rows[pl.ds(first + t, 1), :] = value[:, t * 128 : (t + 1) * 128]


def norm_stats(value):
    mean = row_mean(value)
    centered = value - widen(mean, value)
    rs = lax.rsqrt(row_mean(centered * centered) + layer_eps)
    return mean, rs


def norm_back(grad, xhat, rs, gain):
    grad = grad * gain
    return rs * (grad - widen(row_mean(grad), grad) - xhat * widen(row_mean(grad * xhat), grad))


class Place:
    def __init__(self):
        self.me = lax.axis_index("seq")
        self.y = lax.axis_index("heads")

    def member(self, b):
        return self.me % 2**b

    def device(self, b, j):
        return (self.me // 2**b * 2**b + j, self.y)

    def start(self, b, head):
        stride = 2**b
        place = (self.y * LOCAL + head) % stride
        return pl.multiple_of(reversed_bits(place, b) * (SEGMENT // stride), SEGMENT // stride)

    def bit(self, k):
        return self.me // 2**k % 2

    def partner(self, k):
        return (self.me + 2**k * (1 - 2 * self.bit(k)), self.y)

    def low(self, order, k):
        return sum((self.bit(order[i]) * HALVES[i] for i in range(k)), self.me * 0)

    def greet(self, seq=16, other=False):
        barrier = pltpu.get_barrier_semaphore()
        i = self.member(4)
        count = 15
        if other:
            pl.semaphore_signal(barrier, inc=1, device_id=(self.me, 1 - self.y), device_id_type=MESH)
            count += 1
        for k in far_bits(seq):
            pl.semaphore_signal(barrier, inc=1, device_id=self.partner(k), device_id_type=MESH)
            count += 1

        def signal(d, _):
            pl.semaphore_signal(barrier, inc=1, device_id=self.device(4, (i + d) % 16), device_id_type=MESH)
            return 0

        lax.fori_loop(1, 16, signal, 0)
        pl.semaphore_wait(barrier, count)


def remote(src, dst, send, recv, device):
    return pltpu.make_async_remote_copy(
        src_ref=src, dst_ref=dst, send_sem=send, recv_sem=recv, device_id=device, device_id_type=MESH
    )


def over_peers(b, body):
    tiles = max(LOCAL // 2**b, 1)

    def step(d, _):
        for t in range(tiles):
            body(d, t)
        return 0

    lax.fori_loop(1, 2**b, step, 0)


def ds(start, size):
    return pl.ds(pl.multiple_of(start, size), size)


def attend(q, kv):
    scores = dot(q, kv, NT)
    top = jnp.max(scores, axis=1, keepdims=True)
    raised = jnp.exp2(scores - top).astype(BF)
    return dot(raised, kv, NN), top


def packed(out, top):
    lane = lanes(out.shape)
    total = out[:, 112:113]
    tile = jnp.where(lane == 112, 1.0, out * (1.0 / total))
    for k, piece in enumerate(split3(top) + split3(total)):
        tile = jnp.where(lane == 114 + k, piece, tile)
    return tile.astype(BF)


def forward_kernel(
    x_ref, w_out_ref, fin_ref, att_ref, w_out_other, x1, x2, x3, q4, kv4, acc, tops, o1, o2, o3, o4, r1, r2, r3, r4, *sems
):
    place = Place()
    me = place.me
    xs, os, rs = (None, x1, x2, x3), (None, o1, o2, o3, o4), (None, r1, r2, r3, r4)
    go_send, go_recv, back_send, back_recv = sems[0:4], sems[4:8], sems[8:12], sems[12:16]

    def go(b, d, t):
        n, tiles = SEGMENT // 2**b, max(LOCAL // 2**b, 1)
        i = place.member(b)
        j = (i + d) % 2**b
        if b < 4:
            head = j * tiles + t
            k = (d - 1) * tiles + t
            return [
                remote(
                    x_ref.at[head, pl.ds(place.start(b, head), n), :],
                    xs[b].at[t, ds(i * n, n), :],
                    go_send[b - 1].at[k],
                    go_recv[b - 1].at[k],
                    place.device(b, j),
                )
            ]
        head, half = j // 2, j % 2
        start = place.start(4, head)
        k = (d - 1) * 2
        return [
            remote(
                x_ref.at[head, ds(start + half * 32, 32), 0:128],
                q4.at[ds(i * 32, 32), :],
                go_send[3].at[k],
                go_recv[3].at[k],
                place.device(4, j),
            ),
            remote(
                x_ref.at[head, pl.ds(start, 64), 128:256],
                kv4.at[ds(i * 64, 64), :],
                go_send[3].at[k + 1],
                go_recv[3].at[k + 1],
                place.device(4, j),
            ),
        ]

    def back(b, d, t):
        n, tiles = SEGMENT // 2**b, max(LOCAL // 2**b, 1)
        i = place.member(b)
        j = (i + d) % 2**b
        k = (d - 1) * tiles + t
        if b < 4:
            src, dst = o_at(b, t, j), rs[b].at[i * tiles + t]
        else:
            src, dst = o4.at[ds(j * 32, 32), :], r4.at[i // 2, ds(i % 2 * 32, 32), :]
        return remote(src, dst, back_send[b - 1].at[k], back_recv[b - 1].at[k], place.device(b, j))

    def o_at(b, t, j):
        n = SEGMENT // 2**b
        return os[b].at[t, ds(j * n, n), :]

    *sems, w_send, w_recv = sems
    place.greet(16, True)
    for b in (1, 4, 3, 2):
        over_peers(b, lambda d, t: [c.start() for c in go(b, d, t)])
    w_copy = remote(w_out_ref, w_out_other, w_send, w_recv, (me, 1 - place.y))
    w_copy.start()

    for b in (1, 2, 3):
        n, tiles = SEGMENT // 2**b, LOCAL // 2**b
        i = place.member(b)
        for t in range(tiles):
            head = i * tiles + t
            xs[b][t, ds(i * n, n), :] = x_ref[head, pl.ds(place.start(b, head), n), :]
    i = place.member(4)
    start = place.start(4, i // 2)
    q4[ds(i * 32, 32), :] = x_ref[i // 2, ds(start + i % 2 * 32, 32), 0:128]
    kv4[ds(i * 64, 64), :] = x_ref[i // 2, pl.ds(start, 64), 128:256]

    def local_head(h, _):
        for half in range(2):
            rows = pl.ds(half * 512, 512)
            out, top = attend(x_ref[h, rows, 0:128], x_ref[h, :, 128:256])
            acc[h, rows, :] = out
            tops[h, rows, :] = jnp.broadcast_to(top, out.shape)
        return 0

    def branch(b):
        n, tiles = SEGMENT // 2**b, LOCAL // 2**b
        over_peers(b, lambda d, t: [c.wait_recv() for c in go(b, d, t)])

        def tile(t, _):
            for half in range(2):
                rows = pl.ds(half * 512, 512)
                os[b][t, rows, :] = packed(*attend(xs[b][t, rows, 0:128], xs[b][t, :, 128:256]))
            return 0

        lax.fori_loop(0, tiles, tile, 0)
        over_peers(b, lambda d, t: back(b, d, t).start())
        j = place.member(b)
        for t in range(tiles):
            rs[b][j * tiles + t] = os[b][t, ds(j * n, n), :]

    lax.fori_loop(0, 5, local_head, 0)
    branch(1)
    over_peers(4, lambda d, t: [c.wait_recv() for c in go(4, d, t)])
    o4[...] = packed(*attend(q4[...], kv4[...]))
    over_peers(4, lambda d, t: back(4, d, t).start())
    r4[i // 2, ds(i % 2 * 32, 32), :] = o4[ds(i * 32, 32), :]
    branch(3)
    branch(2)
    lax.fori_loop(5, 8, local_head, 0)

    for b in (4, 3, 2, 1):
        over_peers(b, lambda d, t: back(b, d, t).wait_recv())

    row = lax.broadcasted_iota(jnp.int32, (128, 256), 0)
    column = lax.broadcasted_iota(jnp.int32, (128, 256), 1)
    first = jnp.where(column < 128, 114, 117)
    picks = jnp.where((row >= first) & (row < first + 3), 1.0, 0.0).astype(BF)

    def merge_head(h, _):
        for b in (1, 2, 3, 4):
            n = SEGMENT // 2**b
            rows = pl.ds(place.start(b, h), n)
            part = rs[b][h]
            stats = dot(part, picks, NN)
            top = jnp.maximum(tops[h, rows, :], stats[:, 0:128])
            keep = jnp.exp2(tops[h, rows, :] - top)
            gain = jnp.exp2(stats[:, 0:128] - top) * stats[:, 128:256]
            acc[h, rows, :] = acc[h, rows, :] * keep + part.astype(F32) * gain
            tops[h, rows, :] = top
        out = acc[h]
        lane = lanes(out.shape)
        inverse = 1.0 / out[:, 112:113]
        out = jnp.where((lane >= 64) & (lane < 112), out * inverse, 0.0)
        fin_ref[h] = jnp.where(lane == 112, inverse, jnp.where(lane == 113, tops[h], out))
        return 0

    lax.fori_loop(0, LOCAL, merge_head, 0)

    def compact(n, _):
        rows = ds(n * 256, 256)
        pieces = [None] * 3
        for h in range(LOCAL):
            put_48(pieces, h, fin_ref[h, rows, :], 64)
        for k in range(3):
            att_ref[rows, pl.ds(k * 128, 128)] = pieces[k].astype(BF)
        return 0

    lax.fori_loop(0, 4, compact, 0)

    for b in (4, 3, 2, 1):
        over_peers(b, lambda d, t: [c.wait_send() for c in go(b, d, t)])
        over_peers(b, lambda d, t: back(b, d, t).wait_send())
    w_copy.wait()


ROWS = 768
HALVES = (384, 192, 96, 48)
LANDING = (0, 384, 576, 672, 720)


def far_bits(seq):
    return list(range(4, seq.bit_length() - 1))


X_FIRST = (0, 1, 2, 3)
Z_FIRST = (0, 2, 3, 1)


class Halving:
    def __init__(self, place, seq, order, grads, share, scratch):
        self.place, self.seq, self.order, self.grads, self.share = place, seq, order, grads, share
        self.landing, self.send, self.recv, self.far_send, self.far_recv = scratch

    @staticmethod
    def scratch(seq):
        far = len(far_bits(seq))
        return [pltpu.VMEM((720 + 48 * far, ROWS), BF)] + [pltpu.SemaphoreType.DMA((max(4, far),)) for _ in range(4)]

    def copy(self, k):
        size = HALVES[k]
        bit = self.order[k]
        start = self.place.low(self.order, k) + (1 - self.place.bit(bit)) * size
        return remote(
            self.grads.at[pl.ds(pl.multiple_of(start, 48), size), :],
            self.landing.at[pl.ds(LANDING[k], size), :],
            self.send.at[k],
            self.recv.at[k],
            self.place.partner(bit),
        )

    def add(self, k):
        start = self.place.low(self.order, k + 1)

        def step(i, _):
            rows = pl.ds(pl.multiple_of(start + i * 48, 48), 48)
            arrived = self.landing[pl.ds(pl.multiple_of(LANDING[k] + i * 48, 48), 48), :]
            value = (self.grads[rows, :].astype(F32) + arrived.astype(F32)).astype(BF)
            if k < 3:
                self.grads[rows, :] = value
            else:
                self.share[...] = value
            return 0

        lax.fori_loop(0, HALVES[k] // 48, step, 0)

    def step(self, k):
        if k > 0:
            self.copy(k - 1).wait_recv()
            self.add(k - 1)
        if k < 4:
            self.copy(k).start()
            return
        for n, bit in enumerate(far_bits(self.seq)):
            landing = self.landing.at[pl.ds(720 + 48 * n, 48), :]
            copy = remote(self.share, landing, self.far_send.at[n], self.far_recv.at[n], self.place.partner(bit))
            copy.start()
            copy.wait()
            self.share[...] = (self.share[...].astype(F32) + landing[...].astype(F32)).astype(BF)

    def finish(self):
        for k in range(4):
            self.copy(k).wait_send()


class Doubling:
    def __init__(self, place, order, share, result, sems):
        self.place, self.order, self.share, self.result = place, order, share, result
        self.send, self.recv = sems

    @staticmethod
    def scratch():
        return [pltpu.SemaphoreType.DMA((4,)) for _ in range(2)]

    def copy(self, k):
        rows = pl.ds(pl.multiple_of(self.place.low(self.order, k + 1), 48), HALVES[k])
        view = self.result.at[rows, :]
        return remote(view, view, self.send.at[k], self.recv.at[k], self.place.partner(self.order[k]))

    def step(self, k):
        if k == 0:
            self.result[pl.ds(pl.multiple_of(self.place.low(self.order, 4), 48), 48), :] = self.share[...]
        else:
            self.copy(4 - k).wait_recv()
        if k < 4:
            self.copy(3 - k).start()

    def finish(self):
        for k in range(4):
            self.copy(k).wait_send()


def run_at(slot, work, times):
    for k, time in enumerate(times):

        @pl.when(slot == time)
        def _():
            work.step(k)


def sem_shapes(per_copy):
    counts = [4, 6, 7, 15 * per_copy]
    return [pltpu.SemaphoreType.DMA((c,)) for c in counts]


VMEM = pl.BlockSpec(memory_space=pltpu.VMEM)
ANY = pl.BlockSpec(memory_space=pl.ANY)
ORDER = tuple(int(f"{c:04b}"[::-1], 2) for c in range(16))


def attention_forward(x, w_output):
    shapes = [
        ((LOCAL, SEGMENT, 128), F32),
        ((SEGMENT, LOCAL * HEAD_DIM), BF),
        (w_output.shape, BF),
        ((4, SEGMENT, 256), BF),
        ((2, SEGMENT, 256), BF),
        ((1, SEGMENT, 256), BF),
        ((512, 128), BF),
        ((SEGMENT, 128), BF),
    ]
    scratch = [
        ((LOCAL, SEGMENT, 128), F32),
        ((LOCAL, SEGMENT, 128), F32),
        ((4, SEGMENT, 128), BF),
        ((2, SEGMENT, 128), BF),
        ((1, SEGMENT, 128), BF),
        ((512, 128), BF),
        ((LOCAL, 512, 128), BF),
        ((LOCAL, 256, 128), BF),
        ((LOCAL, 128, 128), BF),
        ((LOCAL, 64, 128), BF),
    ]
    return pl.pallas_call(
        forward_kernel,
        out_shape=[jax.ShapeDtypeStruct(*s) for s in shapes],
        in_specs=[VMEM, ANY],
        out_specs=[VMEM, VMEM, ANY] + [VMEM] * 5,
        scratch_shapes=[pltpu.VMEM(*s) for s in scratch]
        + sem_shapes(2) + sem_shapes(2) + sem_shapes(1) + sem_shapes(1) + [pltpu.SemaphoreType.DMA] * 2,
        compiler_params=pltpu.CompilerParams(
            collective_id=0, has_side_effects=True, vmem_limit_bytes=56 * 2**20
        ),
        name="attention_forward",
    )(x, w_output)


def pair_grads(q, d, kv_at, put):
    lane = lanes(q.shape)
    zero = jnp.zeros_like(d)
    queries = q + jnp.where(lane < 64, d, zero)
    grads = jnp.where(lane < 64, zero, d)
    total = None
    for half in range(2):
        kv = kv_at(half)
        probs = jnp.exp2(dot(kv, queries, NT))
        grad_scores = (probs * dot(kv, grads, NT)).astype(BF)
        put(half, dot(grad_scores, queries, NN) + dot(probs.astype(BF), grads, NN))
        part = dot(kv, grad_scores, TN)
        total = part if total is None else total + part
    return total.T


def backward_kernel(
    seq, x_ref, x1, x2, x3, q4, kv4, fin_ref, do_ref, ffn_ref, grads_in, shares_in, g_ref, sum_ref, ffn_other, shares_ref, grads_r,
    grads, d0, d1, d2, d3, d4, total, g1, g2, g3, gq4, gkv4, r1, r2, r3, rq4, rkv4, *sems
):
    place = Place()
    *sems, fill_sem, ffn_send, ffn_recv = sems
    orders = (X_FIRST, Z_FIRST)
    halving = [
        Halving(place, seq, orders[c], grads.at[c], shares_ref.at[c], sems[16 + 5 * c : 21 + 5 * c]) for c in range(2)
    ]
    doubling = [
        Doubling(place, orders[c], shares_in.at[c], grads_r.at[c], sems[26 + 2 * c : 28 + 2 * c]) for c in range(2)
    ]

    def reduce_at(slot):
        run_at(slot, halving[0], (0, 1, 4, 6, 7))
        run_at(slot, halving[1], (1, 2, 5, 8, 9))
        run_at(slot, doubling[0], (2, 4, 6, 9, 10))
        run_at(slot, doubling[1], (3, 4, 7, 10, 11))

    for c in range(2):
        pltpu.make_async_copy(grads_in.at[c], grads.at[c], fill_sem.at[c]).start()
    ffn_copy = remote(ffn_ref, ffn_other, ffn_send, ffn_recv, (place.me, 1 - place.y))
    me = place.me
    xs, dd, gs, rs = (None, x1, x2, x3), (None, d1, d2, d3), (None, g1, g2, g3), (None, r1, r2, r3)
    go_send, go_recv, back_send, back_recv = sems[0:4], sems[4:8], sems[8:12], sems[12:16]

    def go(b, d, t):
        n, tiles = SEGMENT // 2**b, max(LOCAL // 2**b, 1)
        i = place.member(b)
        j = (i + d) % 2**b
        k = (d - 1) * tiles + t
        if b < 4:
            head = j * tiles + t
            src, dst = d0.at[head, pl.ds(place.start(b, head), n), :], dd[b].at[t, ds(i * n, n), :]
        else:
            start = place.start(4, j // 2)
            src, dst = d0.at[j // 2, ds(start + j % 2 * 32, 32), :], d4.at[ds(i * 32, 32), :]
        return remote(src, dst, go_send[b - 1].at[k], go_recv[b - 1].at[k], place.device(b, j))

    def back(b, d, t):
        n, tiles = SEGMENT // 2**b, max(LOCAL // 2**b, 1)
        i = place.member(b)
        j = (i + d) % 2**b
        device = place.device(b, j)
        if b < 4:
            k = (d - 1) * tiles + t
            return [
                remote(
                    gs[b].at[t, ds(j * n, n), :],
                    rs[b].at[i * tiles + t],
                    back_send[b - 1].at[k],
                    back_recv[b - 1].at[k],
                    device,
                )
            ]
        k = (d - 1) * 2
        return [
            remote(
                gq4.at[ds(j * 32, 32), :],
                rq4.at[i // 2, ds(i % 2 * 32, 32), :],
                back_send[3].at[k],
                back_recv[3].at[k],
                device,
            ),
            remote(
                gkv4.at[ds(j * 64, 64), :],
                rkv4.at[i % 2, i // 2],
                back_send[3].at[k + 1],
                back_recv[3].at[k + 1],
                device,
            ),
        ]

    def prepare(h, _):
        fin = fin_ref[h]
        lane = lanes(fin.shape)
        value_lane = (lane >= 64) & (lane < 112)
        grad = (do_ref[:, ds(h * 128, 128)].astype(F32) * fin[:, 112:113]).astype(BF).astype(F32)
        delta = jnp.sum(jnp.where(value_lane, grad * fin, 0.0), axis=1, keepdims=True)
        tile = jnp.where(value_lane, grad, 0.0)
        high, middle, low = split3(-delta)
        tile = jnp.where(lane == 112, high, jnp.where(lane == 113, middle, tile))
        for k, piece in enumerate(split3(-fin[:, 113:114])):
            tile = jnp.where(lane == 52 + k, piece, tile)
        d0[h] = tile.astype(BF)
        return 0

    lax.fori_loop(0, LOCAL, prepare, 0)
    place.greet(seq, True)
    for b in (4, 3, 2, 1):
        over_peers(b, lambda d, t: go(b, d, t).start())
    ffn_copy.start()
    for c in range(2):
        pltpu.make_async_copy(grads_in.at[c], grads.at[c], fill_sem.at[c]).wait()
    for b in (1, 2, 3):
        n, tiles = SEGMENT // 2**b, LOCAL // 2**b
        i = place.member(b)
        for t in range(tiles):
            head = i * tiles + t
            dd[b][t, ds(i * n, n), :] = d0[head, pl.ds(place.start(b, head), n), :]
    i = place.member(4)
    d4[ds(i * 32, 32), :] = d0[i // 2, ds(place.start(4, i // 2) + i % 2 * 32, 32), :]

    def local_head(h, _):
        def put(half, grad):
            total[h, pl.ds(half * 512, 512), 128:256] = grad

        total[h, :, 0:128] = pair_grads(
            x_ref[h, :, 0:128], d0[h], lambda half: x_ref[h, pl.ds(half * 512, 512), 128:256], put
        )
        reduce_at(jnp.where(h < 4, h, h + 8))
        return 0

    lax.fori_loop(0, 4, local_head, 0)

    def put4(half, grad):
        gkv4[pl.ds(half * 512, 512), :] = grad.astype(BF)

    def branch(b, slot):
        n, tiles = SEGMENT // 2**b, LOCAL // 2**b
        over_peers(b, lambda d, t: go(b, d, t).wait_recv())

        def tile(t, _):
            def put(half, grad):
                gs[b][t, pl.ds(half * 512, 512), 128:256] = grad.astype(BF)

            gs[b][t, :, 0:128] = pair_grads(
                xs[b][t, :, 0:128], dd[b][t], lambda half: xs[b][t, pl.ds(half * 512, 512), 128:256], put
            ).astype(BF)
            reduce_at(slot + t)
            return 0

        lax.fori_loop(0, tiles, tile, 0)
        over_peers(b, lambda d, t: [c.start() for c in back(b, d, t)])
        j = place.member(b)
        for t in range(tiles):
            rs[b][j * tiles + t] = gs[b][t, ds(j * n, n), :]

    branch(1, 4)
    over_peers(4, lambda d, t: go(4, d, t).wait_recv())
    gq4[...] = pair_grads(q4[...], d4[...], lambda half: kv4[pl.ds(half * 512, 512), :], put4).astype(BF)
    over_peers(4, lambda d, t: [c.start() for c in back(4, d, t)])
    rq4[i // 2, ds(i % 2 * 32, 32), :] = gq4[ds(i * 32, 32), :]
    rkv4[i % 2, i // 2] = gkv4[ds(i * 64, 64), :]
    reduce_at(jnp.int32(8))
    branch(3, 9)
    branch(2, 10)
    lax.fori_loop(4, 8, local_head, 0)

    for b in (4, 3, 2, 1):
        over_peers(b, lambda d, t: [c.wait_recv() for c in back(b, d, t)])

    def finish(h, _):
        for b in (1, 2, 3):
            n = SEGMENT // 2**b
            rows = pl.ds(place.start(b, h), n)
            total[h, rows, :] += rs[b][h].astype(F32)
        rows = pl.ds(place.start(4, h), 64)
        total[h, rows, 0:128] += rq4[h].astype(F32)
        total[h, rows, 128:256] += rkv4[0, h].astype(F32) + rkv4[1, h].astype(F32)
        return 0

    lax.fori_loop(0, LOCAL, finish, 0)
    sum_ref[...] = jnp.zeros_like(sum_ref)

    def compact(i, _):
        rows = ds(i * 256, 256)
        pieces = [[None] * 3 for _ in range(3)]
        for h in range(LOCAL):
            live = (x_ref[h, rows, 176:177].astype(F32) >= 0.0).astype(F32)
            grad_kv = total[h, rows, 128:256]
            put_48(pieces[0], h, total[h, rows, 0:128] * SCALE)
            put_48(pieces[1], h, grad_kv * (live * (1.0 / LOG2E)))
            put_48(pieces[2], h, pltpu.roll(grad_kv, 64, 1))
        for k in range(3):
            for n in range(3):
                at = pl.ds(n * 128, 128)
                g_ref[k, rows, at] = pieces[k][n].astype(BF)
                sum_ref[k, :, at] += jnp.broadcast_to(jnp.sum(pieces[k][n], axis=0, keepdims=True), (8, 128))
        return 0

    lax.fori_loop(0, 4, compact, 0)

    for b in (4, 3, 2, 1):
        over_peers(b, lambda d, t: go(b, d, t).wait_send())
        over_peers(b, lambda d, t: [c.wait_send() for c in back(b, d, t)])
    for c in range(2):
        halving[c].finish()
        doubling[c].finish()
    ffn_copy.wait()


def attention_backward(x, saved, fin, grad_out, ffn_part, grads, shares):
    seq = lax.axis_size("seq")
    shapes = [
        ((3, SEGMENT, LOCAL * HEAD_DIM), BF),
        ((3, 8, LOCAL * HEAD_DIM), F32),
        (ffn_part.shape, BF),
        ((2, 48, ROWS), BF),
        ((2, ROWS, ROWS), BF),
    ]
    scratch = [
        (grads.shape, BF),
        ((LOCAL, SEGMENT, 128), BF),
        ((4, SEGMENT, 128), BF),
        ((2, SEGMENT, 128), BF),
        ((1, SEGMENT, 128), BF),
        ((512, 128), BF),
        ((LOCAL, SEGMENT, 256), F32),
        ((4, SEGMENT, 256), BF),
        ((2, SEGMENT, 256), BF),
        ((1, SEGMENT, 256), BF),
        ((512, 128), BF),
        ((SEGMENT, 128), BF),
        ((LOCAL, 512, 256), BF),
        ((LOCAL, 256, 256), BF),
        ((LOCAL, 128, 256), BF),
        ((LOCAL, 64, 128), BF),
        ((2, LOCAL, 64, 128), BF),
    ]
    return pl.pallas_call(
        functools.partial(backward_kernel, seq),
        out_shape=[jax.ShapeDtypeStruct(*s) for s in shapes],
        in_specs=[VMEM] * 8 + [ANY, ANY, VMEM],
        out_specs=[VMEM, VMEM, ANY, VMEM, VMEM],
        scratch_shapes=[pltpu.VMEM(*s) for s in scratch]
        + sem_shapes(1) + sem_shapes(1) + sem_shapes(2) + sem_shapes(2)
        + Halving.scratch(seq) + Halving.scratch(seq)
        + Doubling.scratch() + Doubling.scratch()
        + [pltpu.SemaphoreType.DMA((2,)), pltpu.SemaphoreType.DMA, pltpu.SemaphoreType.DMA],
        compiler_params=pltpu.CompilerParams(
            collective_id=1, has_side_effects=True, vmem_limit_bytes=60 * 2**20
        ),
        name="attention_backward",
    )(x, *saved, fin, grad_out, ffn_part, grads, shares)


CHUNK = 128


def put_spread(planes, block, value):
    for t in range(value.shape[1] // 128):
        planes[t, pl.ds(ORDER[block], 64, stride=16), :] = value[:, t * 128 : (t + 1) * 128]


def from_planes(planes, out):
    def step(i, _):
        rows = ds(i * 128, 128)
        for t in range(planes.shape[0]):
            out[rows, pl.ds(t * 128, 128)] = planes[t, rows, :]
        return 0

    lax.fori_loop(0, SEGMENT // 128, step, 0)


def to_planes(value_ref, planes):
    def step(i, _):
        rows = ds(i * 128, 128)
        for t in range(planes.shape[0]):
            planes[t, rows, :] = value_ref[rows, pl.ds(t * 128, 128)].astype(F32)
        return 0

    lax.fori_loop(0, SEGMENT // 128, step, 0)


def take_spread(planes, block):
    return jnp.concatenate(
        [planes[t, pl.ds(ORDER[block], 64, stride=16), :] for t in range(planes.shape[0])], axis=1
    )


def first_kernel(
    tokens_ref, cot_ref, valid_ref, vec_ref, w_ref, bias_ref,
    x_ref, normed_ref, tokens_out, cot_out, stats_ref, planes
):
    to_planes(tokens_ref, planes)
    for b in range(16):
        tokens_out[pl.ds(b * 64, 64), :] = take_spread(planes, b).astype(BF)
    to_planes(cot_ref, planes)
    for b in range(16):
        cot_out[pl.ds(b * 64, 64), :] = take_spread(planes, b)
    count = jnp.sum(valid_ref[...])

    def chunk(n, _):
        rows = ds(n * 256, 256)
        x = tokens_out[rows, :].astype(F32)
        mean, rs = norm_stats(x)
        stats_ref[0, rows, :], stats_ref[1, rows, :] = mean, rs
        normed = ((x - widen(mean, x)) * widen(rs, x) * vec_ref[0:1, :] + vec_ref[1:2, :]).astype(BF)
        normed_ref[rows, :] = normed
        queries = (dot(normed, w_ref[0], NN) + bias_ref[0:1, :]) * (SCALE * LOG2E)
        keys = dot(normed, w_ref[1], NN)
        values = dot(normed, w_ref[2], NN) + bias_ref[1:2, :]
        at = n * 256 + lax.broadcasted_iota(jnp.int32, (256, 128), 0)
        live = (at % 64 * 16 + reversed_bits(at // 64, 4)) < count
        lane = lanes((256, 128))
        padding = jnp.where(live, 0.0, masked_score)
        ones = ((lane >= 52) & (lane < 55)) | (lane == 112) | (lane == 113)
        for h in range(LOCAL):
            x_ref[h, rows, 0:128] = jnp.where(lane == 48, 1.0, take_48(queries, h, 0)).astype(BF)
            key = jnp.where(live, take_48(keys, h, 0), 0.0) + take_48(values, h, 64)
            x_ref[h, rows, 128:256] = jnp.where(ones, 1.0, jnp.where(lane == 48, padding, key)).astype(BF)
        return 0

    lax.fori_loop(0, 4, chunk, 0)


def first_part(tokens, cotangent, valid, vectors, w_project, bias):
    width = tokens.shape[1]
    shapes = [
        ((LOCAL, SEGMENT, 256), BF),
        (tokens.shape, BF),
        (tokens.shape, BF),
        (tokens.shape, F32),
        ((2, SEGMENT, 128), F32),
    ]
    return pl.pallas_call(
        first_kernel,
        out_shape=[jax.ShapeDtypeStruct(*s) for s in shapes],
        in_specs=[VMEM] * 6,
        out_specs=[VMEM] * len(shapes),
        scratch_shapes=[pltpu.VMEM((width // 128, SEGMENT, 128), F32)],
        compiler_params=pltpu.CompilerParams(vmem_limit_bytes=56 * 2**20),
        name="first_part",
    )(tokens, cotangent, valid, vectors, w_project, bias)


GELU_C = math.sqrt(2 / math.pi)


def middle_kernel(
    seq, att_ref, w_out_ref, w_out_other, tokens_ref, cot_ref, w_expand, w_reduce, vec_ref,
    middle_ref, gm_ref, do_ref, ffn_ref, grads_e, shares_ref, grads_o, small_ref,
    att, w_out, stats, normed, active, grad_expand, cot_low, part, other, gm_low, grads_r, sums, sums_e,
    att_send, att_recv, part_send, part_recv, *sems
):
    place = Place()
    y = place.y
    peer = (place.me, 1 - y)
    b_output, gain, shift = (vec_ref[k : k + 1, :] for k in (2, 3, 4))
    n = len(sems) // 2
    halving = [
        Halving(place, seq, order, grads_r.at[c], shares_ref.at[c], sems[c * n : c * n + n])
        for c, order in enumerate((X_FIRST, Z_FIRST))
    ]
    chunk, chunks, width = 256, SEGMENT // 256, tokens_ref.shape[1]

    def att_copy(n):
        rows = ds(n * chunk, chunk)
        return remote(att_ref.at[rows, :], att.at[y, rows, :], att_send.at[n], att_recv.at[n], peer)

    def part_copy(n):
        rows = ds(n * chunk, chunk)
        return remote(part.at[rows, :], other.at[rows, :], part_send.at[n], part_recv.at[n], peer)

    place.greet(seq, True)
    for n in range(chunks):
        att_copy(n).start()
    att[y] = att_ref[...]
    w_out[y] = w_out_ref[...]
    w_out[1 - y] = w_out_other[...]
    sums[...] = jnp.zeros_like(sums)
    sums_e[...] = jnp.zeros_like(sums_e)

    def ahead(n, _):
        rows = ds(n * chunk, chunk)
        cot = cot_ref[rows, :]
        sums[0:8] += row_sums(cot)
        low = cot.astype(BF)
        cot_low[rows, :] = low
        att_copy(n).wait_recv()
        branch = dot(att[0, rows, :], w_out[0], NN) + dot(att[1, rows, :], w_out[1], NN)
        middle = tokens_ref[rows, :].astype(F32) + (branch + b_output)
        middle_ref[rows, :] = middle
        mean, rs = norm_stats(middle)
        stats[0, rows, :], stats[1, rows, :] = mean, rs
        norm = ((middle - widen(mean, middle)) * widen(rs, middle) * gain + shift).astype(BF)
        normed[rows, :] = norm
        value = None
        for k in range(w_expand.shape[1] // width):
            at = pl.ds(k * width, width)
            expand = dot(norm, w_expand[:, at], NN) + vec_ref[5 + k : 6 + k, :]
            square = expand * expand
            bent = jnp.tanh(GELU_C * expand * (1.0 + 0.044715 * square))
            gate = 0.5 * (1.0 + bent)
            active[rows, at] = (expand * gate).astype(BF)
            slope = gate + (0.5 * GELU_C) * expand * (1.0 - bent * bent) * (1.0 + (3 * 0.044715) * square)
            grad = dot(low, w_reduce[at, :], NT) * slope
            sums_e[:, at] += row_sums(grad)
            grad = grad.astype(BF)
            grad_expand[rows, at] = grad
            piece = dot(grad, w_expand[:, at], NT)
            value = piece if value is None else value + piece
        part[rows, :] = value.astype(BF)
        part_copy(n).start()
        return 0

    lax.fori_loop(0, chunks, ahead, 0)

    def behind(n, _):
        rows = ds(n * chunk, chunk)
        part_copy(n).wait_recv()
        grad = part[rows, :].astype(F32) + other[rows, :].astype(F32)
        rs = widen(stats[1, rows, :], grad)
        xhat = (middle_ref[rows, :] - widen(stats[0, rows, :], grad)) * rs
        sums[8:16] += row_sums(grad * xhat)
        sums[16:24] += row_sums(grad)
        gm = cot_ref[rows, :] + norm_back(grad, xhat, rs, gain)
        gm_ref[rows, :] = gm
        sums[24:32] += row_sums(gm)
        low = gm.astype(BF)
        gm_low[rows, :] = low
        grad_att = dot(low, w_out_ref[...], NT)
        for h in range(LOCAL):
            do_ref[rows, pl.ds(h * 128, 128)] = take_48(grad_att, h, 64).astype(BF)
        return 0

    for k in range(2):
        grads_r[k] = dot(active[:, pl.ds(k * width, width)], cot_low[...], TN).astype(BF)
        halving[k].step(0)
    behind(0, 0)
    halving[0].step(1)
    halving[1].step(1)
    grads_e[0] = dot(normed[...], grad_expand[:, pl.ds(0, width)], TN).astype(BF)
    behind(1, 0)
    halving[0].step(2)
    halving[1].step(2)
    grads_e[1] = dot(normed[...], grad_expand[:, pl.ds(width, width)], TN).astype(BF)
    ffn_ref[...] = dot(active[...], w_reduce[...], NN).astype(BF)
    halving[0].step(3)
    behind(2, 0)
    halving[1].step(3)
    halving[0].step(4)
    behind(3, 0)
    halving[1].step(4)
    for k in range(2):
        at = pl.ds(k * (width // 2), width // 2)
        grads_o[pl.ds(k * 384, 384), :] = dot(att_ref[...], gm_low[:, at], TN).astype(BF)
    put_vector(small_ref, 0, sums[24:32])
    put_vector(small_ref, 6, sums[8:16])
    put_vector(small_ref, 12, sums[16:24])
    put_vector(small_ref, 18, sums_e[...])
    put_vector(small_ref, 30, sums[0:8])
    small_ref[36:48, :] = jnp.zeros((12, 128), F32)
    for n in range(chunks):
        att_copy(n).wait_send()
        part_copy(n).wait_send()
    halving[0].finish()
    halving[1].finish()


def middle_part(attended, w_output, w_out_other, tokens, cot, w_expand, w_reduce, vectors):
    seq = lax.axis_size("seq")
    rows, width = tokens.shape
    hidden = w_expand.shape[1]
    shapes = [
        ((rows, width), F32),
        ((rows, width), F32),
        ((rows, LOCAL * 128), BF),
        ((rows, width), BF),
        ((2, ROWS, ROWS), BF),
        ((2, 48, ROWS), BF),
        ((ROWS, ROWS // 2), BF),
        ((48, 128), F32),
    ]
    scratch = [
        ((2,) + attended.shape, BF),
        ((2,) + w_output.shape, BF),
        ((2, rows, 128), F32),
        ((rows, width), BF),
        ((rows, hidden), BF),
        ((rows, hidden), BF),
        ((rows, width), BF),
        ((rows, width), BF),
        ((rows, width), BF),
        ((rows, width), BF),
        ((2, ROWS, ROWS), BF),
        ((32, width), F32),
        ((8, hidden), F32),
    ]
    return pl.pallas_call(
        functools.partial(middle_kernel, seq),
        out_shape=[jax.ShapeDtypeStruct(*s) for s in shapes],
        in_specs=[VMEM] * 8,
        out_specs=[VMEM] * len(shapes),
        scratch_shapes=[pltpu.VMEM(*s) for s in scratch]
        + [pltpu.SemaphoreType.DMA((4,)) for _ in range(4)]
        + Halving.scratch(seq) + Halving.scratch(seq),
        compiler_params=pltpu.CompilerParams(
            collective_id=3, has_side_effects=True, vmem_limit_bytes=60 * 2**20
        ),
        name="middle_part",
    )(attended, w_output, w_out_other, tokens, cot, w_expand, w_reduce, vectors)


def last_kernel(
    seq, g_ref, w_ref, normed_ref, w_out_ref, small_in, sum_ref, shares_in, vec_ref,
    tokens_in, gm_in, stats_in, middle_in, ffn_in, ffn_other_in,
    out_ref, layer_ref, grads_ref, early_ref, late_ref,
    tokens_ref, gm_ref, stats, middle_ref, ffn_ref, ffn_other,
    grads, shares, part, other, small_ref, early_in, late, late_in, sums, planes, fill_sem,
    part_send, part_recv, early_send, early_recv, late_send, late_recv, far_send, far_recv, *sems
):
    place = Place()
    orders = (X_FIRST, Z_FIRST)
    halving = [Halving(place, seq, orders[c], grads.at[c], shares.at[c], sems[5 * c : 5 * c + 5]) for c in range(2)]
    gathers = [
        Doubling(place, orders[c], shares_in.at[c], grads_ref.at[c], sems[10 + 2 * c : 12 + 2 * c]) for c in range(2)
    ]
    last_gathers = [
        Doubling(place, orders[c], shares.at[c], grads_ref.at[2 + c], sems[14 + 2 * c : 16 + 2 * c]) for c in range(2)
    ]
    i = place.member(4)
    chunks = SEGMENT // CHUNK
    fills = [
        pltpu.make_async_copy(src, dst, fill_sem.at[k])
        for k, (src, dst) in enumerate(
            zip(
                (tokens_in, gm_in, stats_in, middle_in, ffn_in, ffn_other_in),
                (tokens_ref, gm_ref, stats, middle_ref, ffn_ref, ffn_other),
            )
        )
    ]
    for fill in fills:
        fill.start()
    put_vector(small_ref, 0, sum_ref[0] * 0.125)
    put_vector(small_ref, 3, sum_ref[2] * 0.125)
    small_ref[6:48, :] = small_in[0:42, :]

    def to_all(src, landing, send, recv):
        def each(action):
            def step(d, _):
                action(remote(src, landing.at[i], send.at[d - 1], recv.at[d - 1], place.device(4, (i + d) % 16)))
                return 0

            lax.fori_loop(1, 16, step, 0)

        return each

    def total_of(src, landing):
        def step(j, value):
            return value + landing[j]

        landing[i] = src[...]
        return lax.fori_loop(1, 16, step, landing[0])

    def far_total(result, n):
        for k, bit in enumerate(far_bits(seq)):
            landing = (early_in, late_in)[n].at[16 + k]
            copy = remote(result, landing, far_send.at[n * 8 + k], far_recv.at[n * 8 + k], place.partner(bit))
            copy.start()
            copy.wait()
            result[...] = result[...] + landing[...]

    def exchange(n):
        rows = ds(n * CHUNK, CHUNK)
        return remote(
            part.at[rows, :], other.at[rows, :], part_send.at[n], part_recv.at[n], (place.me, 1 - place.y)
        )

    def partial(n, _):
        rows = ds(n * CHUNK, CHUNK)
        value = dot(g_ref[0, rows, :], w_ref[0], NT)
        value += dot(g_ref[1, rows, :], w_ref[1], NT)
        value += dot(g_ref[2, rows, :], w_ref[2], NT)
        part[rows, :] = value.astype(BF)
        exchange(n).start()
        return 0

    def grad_w(k):
        at = pl.ds(k % 2 * 384, 384)
        grads[k // 2, :, at] = dot(normed_ref[...], g_ref[k], TN).astype(BF)

    place.greet(seq, True)
    gathers[0].step(0)
    gathers[1].step(0)
    lax.fori_loop(0, 2, partial, 0)
    early_all = to_all(small_ref, early_in, early_send, early_recv)
    grad_w(0)
    grad_w(1)
    halving[0].step(0)
    gathers[0].step(1)
    gathers[1].step(1)
    grads[1, :, pl.ds(384, 384)] = w_out_ref[...]
    grad_w(2)
    halving[1].step(0)
    gathers[0].step(2)
    lax.fori_loop(2, chunks, partial, 0)
    early_all(lambda copy: copy.start())
    sums[...] = jnp.zeros_like(sums)
    halving[0].step(1)
    halving[1].step(1)
    after = (
        (),
        ((gathers[1], 2),),
        ((gathers[0], 3), (halving[0], 2)),
        ((gathers[0], 4), (halving[1], 2)),
        ((halving[0], 3), (gathers[1], 3)),
        ((halving[0], 4), (halving[1], 3), (last_gathers[0], 0), (gathers[1], 4)),
        ((halving[1], 4), (last_gathers[0], 1), (last_gathers[1], 0)),
        ((last_gathers[0], 2), (last_gathers[1], 1)),
    )
    for fill in fills[:3]:
        fill.wait()
    for n in range(chunks):
        exchange(n).wait_recv()
        rows = pl.ds(n * CHUNK, CHUNK)
        grad = part[rows, :].astype(F32) + other[rows, :].astype(F32)
        rs = widen(stats[1, rows, :], grad)
        xhat = (tokens_ref[rows, :].astype(F32) - widen(stats[0, rows, :], grad)) * rs
        sums[0:8] += row_sums(grad * xhat)
        sums[8:16] += row_sums(grad)
        grad = gm_ref[rows, :] + norm_back(grad, xhat, rs, vec_ref[0:1, :])
        for k in range(CHUNK // 64):
            put_spread(planes, n * (CHUNK // 64) + k, grad[k * 64 : (k + 1) * 64])
        for work, k in after[n]:
            work.step(k)
    for k in range(2):
        put_vector(late, k * 8, sums[k * 8 : k * 8 + 8])
        late[pl.ds(k * 8 + 6, 2), :] = jnp.zeros((2, 128), F32)
    late_all = to_all(late, late_in, late_send, late_recv)
    late_all(lambda copy: copy.start())
    from_planes(planes, out_ref)
    for fill in fills[3:]:
        fill.wait()

    def layer(b):
        rows = pl.ds(b * 64, 64)
        total = ffn_ref[rows, :].astype(F32) + ffn_other[rows, :].astype(F32)
        put_spread(planes, b, middle_ref[rows, :] + total + vec_ref[7:8, :])

    for b in range(8):
        layer(b)
    last_gathers[1].step(2)
    last_gathers[0].step(3)
    for b in range(8, 16):
        layer(b)
    last_gathers[1].step(3)
    from_planes(planes, layer_ref)
    early_all(lambda copy: copy.wait_recv())
    early_ref[...] = total_of(small_ref, early_in)
    far_total(early_ref, 0)
    late_all(lambda copy: copy.wait_recv())
    late_ref[...] = total_of(late, late_in)
    far_total(late_ref, 1)
    last_gathers[0].step(4)
    last_gathers[1].step(4)

    def sent(n, _):
        exchange(n).wait_send()
        return 0

    lax.fori_loop(0, chunks, sent, 0)
    early_all(lambda copy: copy.wait_send())
    late_all(lambda copy: copy.wait_send())
    for work in halving + gathers + last_gathers:
        work.finish()


def last_part(g, w_project, normed, grad_w_out, small, g_sums, shares, vectors, *late_inputs):
    seq = lax.axis_size("seq")
    far = len(far_bits(seq))
    width = normed.shape[1]
    shapes = [
        (normed.shape, F32),
        (normed.shape, F32),
        ((4, ROWS, ROWS), BF),
        (small.shape, F32),
        ((16, 128), F32),
    ]
    scratch = [(a.shape, a.dtype) for a in late_inputs] + [
        ((2, ROWS, ROWS), BF),
        ((2, 48, ROWS), BF),
        (normed.shape, BF),
        (normed.shape, BF),
        (small.shape, F32),
        ((16 + far,) + small.shape, F32),
        ((16, 128), F32),
        ((16 + far, 16, 128), F32),
        ((16, width), F32),
        ((width // 128, SEGMENT, 128), F32),
    ]
    chunks = SEGMENT // CHUNK
    counts = (len(late_inputs), chunks, chunks, 15, 15, 15, 15, 16, 16)
    return pl.pallas_call(
        functools.partial(last_kernel, seq),
        out_shape=[jax.ShapeDtypeStruct(*s) for s in shapes],
        in_specs=[VMEM] * 8 + [ANY] * len(late_inputs),
        out_specs=[VMEM] * len(shapes),
        scratch_shapes=[pltpu.VMEM(*s) for s in scratch]
        + [pltpu.SemaphoreType.DMA((c,)) for c in counts]
        + Halving.scratch(seq) + Halving.scratch(seq)
        + Doubling.scratch() + Doubling.scratch() + Doubling.scratch() + Doubling.scratch(),
        compiler_params=pltpu.CompilerParams(
            collective_id=2, has_side_effects=True, vmem_limit_bytes=58 * 2**20
        ),
        name="last_part",
    )(g, w_project, normed, grad_w_out, small, g_sums, shares, vectors, *late_inputs)


def out_kernel(r_ref, e_ref, p_ref, o_ref, o2_ref, r_out, e_out, p_out, o_out):
    half = ROWS // 2
    r_out[...] = r_ref[...].astype(F32)
    for k in range(2):
        e_out[:, k * ROWS : (k + 1) * ROWS] = e_ref[k].astype(F32)
    p_out[0] = p_ref[0, :, :half].astype(F32)
    p_out[1] = p_ref[0, :, half:].astype(F32)
    p_out[2] = p_ref[1, :, :half].astype(F32)
    o_out[:, :half] = o_ref[0].astype(F32)
    o_out[:, half:] = o2_ref[0].astype(F32)


def widen_out(grads_r, grads):
    half = ROWS // 2
    n = 8
    return pl.pallas_call(
        out_kernel,
        grid=(n,),
        out_shape=[
            jax.ShapeDtypeStruct((2 * ROWS, ROWS), F32),
            jax.ShapeDtypeStruct((ROWS, 2 * ROWS), F32),
            jax.ShapeDtypeStruct((3, ROWS, half), F32),
            jax.ShapeDtypeStruct((half, ROWS), F32),
        ],
        in_specs=[
            pl.BlockSpec((2 * ROWS // n, ROWS), lambda i: (i, 0)),
            pl.BlockSpec((2, ROWS // n, ROWS), lambda i: (0, i, 0)),
            pl.BlockSpec((2, ROWS // n, ROWS), lambda i: (1, i, 0)),
            pl.BlockSpec((1, half // n, half), lambda i: (3, i, 1)),
            pl.BlockSpec((1, half // n, half), lambda i: (3, n + i, 1)),
        ],
        out_specs=[
            pl.BlockSpec((2 * ROWS // n, ROWS), lambda i: (i, 0)),
            pl.BlockSpec((ROWS // n, 2 * ROWS), lambda i: (i, 0)),
            pl.BlockSpec((3, ROWS // n, half), lambda i: (0, i, 0)),
            pl.BlockSpec((half // n, ROWS), lambda i: (i, 0)),
        ],
        name="widen_out",
    )(grads_r.reshape(-1, ROWS), grads, grads, grads, grads)


def body(
    tokens,
    cotangent,
    valid_tiles,
    gain_first,
    shift_first,
    w_project,
    bias_project,
    w_output,
    bias_output,
    gain_second,
    shift_second,
    w_expand,
    bias_expand,
    w_reduce,
    bias_reduce,
):
    width = tokens.shape[1]
    half = width // 2
    w_project = w_project.transpose(1, 0, 2)
    vectors = jnp.stack(
        [gain_first, shift_first, bias_output, gain_second, shift_second, bias_expand[:width], bias_expand[width:], bias_reduce]
    )
    x, normed, tokens, cot, stats = first_part(
        tokens, cotangent, valid_tiles.reshape(8, -1), vectors, w_project, bias_project
    )
    fin, attended, w_out_other, *saved = attention_forward(x, w_output)
    middle, grad_middle, grad_attended, ffn_part, grads_e, shares_r, grads_o, small = middle_part(
        attended, w_output, w_out_other, tokens, cot, w_expand, w_reduce, vectors
    )
    g, g_sums, ffn_other, shares_e, grads_r = attention_backward(
        x, saved, fin, grad_attended, ffn_part, grads_e, shares_r
    )
    grad_tokens, layer_out, grads, small, late = last_part(
        g, w_project, normed, grads_o, small, g_sums, shares_e, vectors,
        tokens, grad_middle, stats, middle, ffn_part, ffn_other,
    )
    small = small.reshape(-1)
    late = late.reshape(2, 8 * 128)[:, :width]
    parts = [small[k * width : (k + 1) * width] for k in range(7)]
    grad_w_reduce, grad_w_expand, grad_w_project, grad_w_output = widen_out(grads_r, grads)
    return (
        layer_out,
        grad_tokens,
        late[0],
        late[1],
        grad_w_project.transpose(1, 0, 2),
        parts[0].reshape(2, half),
        grad_w_output,
        parts[1],
        parts[2],
        parts[3],
        grad_w_expand,
        small[4 * width : 6 * width],
        grad_w_reduce,
        parts[6],
    )


def solution(mesh):
    in_specs = (
        P("seq", None),
        P("seq", None),
        P("seq"),
        P(),
        P(),
        P(None, None, "heads"),
        P(None, "heads"),
        P("heads", None),
        P(),
        P(),
        P(),
        P(None, "heads"),
        P("heads"),
        P("heads", None),
        P(),
    )
    out_specs = (
        P("seq", None),
        P("seq", None),
        P(),
        P(),
        P(None, None, "heads"),
        P(None, "heads"),
        P("heads", None),
        P(),
        P(),
        P(),
        P(None, "heads"),
        P("heads"),
        P("heads", None),
        P(),
    )
    return jax.shard_map(body, mesh=mesh, in_specs=in_specs, out_specs=out_specs, check_vma=False)
```

```python
import functools
import math

import jax
import jax.numpy as jnp
from jax import lax
from jax.experimental import pallas as pl
from jax.experimental.pallas import tpu as pltpu
from jax.sharding import PartitionSpec as P

HEADS = 16
HEAD_DIM = 48
SEGMENT = 1024
BRANCHES = 5
LOCAL = 8

MESH = pl.DeviceIdType.MESH
BF = jnp.bfloat16
F32 = jnp.float32
NT = (((1,), (1,)), ((), ()))
TN = (((0,), (0,)), ((), ()))
NN = (((1,), (0,)), ((), ()))

masked_score = -1000000000.0
layer_eps = 1e-05
SCALE = HEAD_DIM ** (-0.5)
LOG2E = math.log2(math.e)


def dot(a, b, dims):
    return lax.dot_general(a, b, dims, preferred_element_type=F32)


def lanes(shape):
    return lax.broadcasted_iota(jnp.int32, shape, len(shape) - 1)


def reversed_bits(value, bits):
    out = value * 0
    for k in range(bits):
        out = out * 2 + (value // 2**k) % 2
    return out


def split3(value):
    high = value.astype(BF).astype(F32)
    rest = value - high
    middle = rest.astype(BF).astype(F32)
    return high, middle, rest - middle


def take_48(value, head, at):
    tile, off = head * 48 // 128, head * 48 % 128
    shift = (at - off) % 128
    turn = lambda k: pltpu.roll(value[:, k * 128 : (k + 1) * 128], shift, 1) if shift else value[:, k * 128 : (k + 1) * 128]
    out = turn(tile)
    lane = lanes(out.shape)
    if off + 48 > 128:
        out = jnp.where(lane < at + 128 - off, out, turn(tile + 1))
    return jnp.where((lane >= at) & (lane < at + 48), out, 0.0)


def fold(value, at):
    pairs = value.reshape(value.shape[0] // 32, 2, 16, 128)
    even, odd = pairs[:, 0].reshape(-1, 128), pairs[:, 1].reshape(-1, 128)
    return pltpu.roll(even, 64, 1) + odd if at else even + pltpu.roll(odd, 64, 1)


def unfold(value, at):
    value = value.astype(F32)
    keep = lanes(value.shape) >= 64 if at else lanes(value.shape) < 64
    turned = jnp.where(keep, pltpu.roll(value, 64, 1), 0.0)
    straight = jnp.where(keep, value, 0.0)
    even, odd = (turned, straight) if at else (straight, turned)
    pairs = [part.reshape(-1, 1, 16, 128) for part in (even, odd)]
    return jnp.concatenate(pairs, axis=1).reshape(-1, 128)


def placing(source, target, columns):
    row = lax.broadcasted_iota(jnp.int32, (LOCAL * 128, columns), 0)
    column = lax.broadcasted_iota(jnp.int32, (LOCAL * 128, columns), 1)
    lane = row % 128 - source
    hit = (lane >= 0) & (lane < HEAD_DIM) & (column == target + row // 128 * HEAD_DIM + lane)
    return jnp.where(hit, 1.0, 0.0)


def row_mean(value):
    ones = jnp.ones((value.shape[1], 128), BF)
    high = value.astype(BF)
    low = (value - high.astype(F32)).astype(BF)
    return (dot(high, ones, NN) + dot(low, ones, NN)) * (1.0 / value.shape[1])


def vector(ref, k, width=768):
    n = width // 128
    return jnp.concatenate([ref[k * n + t : k * n + t + 1, :] for t in range(n)], axis=1)


def widen(tile, like):
    return jnp.concatenate([tile] * (like.shape[1] // 128), axis=1)


def row_sums(value):
    return jnp.sum(value.reshape(value.shape[0] // 8, 8, value.shape[1]), axis=0)


def put_vector(rows, first, partial):
    value = jnp.sum(partial, axis=0, keepdims=True)
    for t in range(value.shape[1] // 128):
        rows[pl.ds(first + t, 1), :] = value[:, t * 128 : (t + 1) * 128]


def norm_stats(value):
    mean = row_mean(value)
    centered = value - widen(mean, value)
    rs = lax.rsqrt(row_mean(centered * centered) + layer_eps)
    return mean, rs


def norm_back(grad, xhat, rs, gain):
    grad = grad * gain
    return rs * (grad - widen(row_mean(grad), grad) - xhat * widen(row_mean(grad * xhat), grad))


class Place:
    def __init__(self):
        self.me = lax.axis_index("seq")
        self.y = lax.axis_index("heads")

    def member(self, b):
        return self.me % 2**b

    def device(self, b, j):
        return (self.me // 2**b * 2**b + j, self.y)

    def start(self, b, head):
        stride = 2**b
        place = (self.y * LOCAL + head) % stride
        return pl.multiple_of(reversed_bits(place, b) * (SEGMENT // stride), SEGMENT // stride)

    def bit(self, k):
        return self.me // 2**k % 2

    def partner(self, k):
        return (self.me + 2**k * (1 - 2 * self.bit(k)), self.y)

    def low(self, order, k):
        return sum((self.bit(order[i]) * HALVES[i] for i in range(k)), self.me * 0)

    def greet(self, seq=16, other=False):
        barrier = pltpu.get_barrier_semaphore()
        i = self.member(4)
        count = 15
        if other:
            pl.semaphore_signal(barrier, inc=1, device_id=(self.me, 1 - self.y), device_id_type=MESH)
            count += 1
        for k in far_bits(seq):
            pl.semaphore_signal(barrier, inc=1, device_id=self.partner(k), device_id_type=MESH)
            count += 1

        def signal(d, _):
            pl.semaphore_signal(barrier, inc=1, device_id=self.device(4, (i + d) % 16), device_id_type=MESH)
            return 0

        lax.fori_loop(1, 16, signal, 0)
        pl.semaphore_wait(barrier, count)


def remote(src, dst, send, recv, device):
    return pltpu.make_async_remote_copy(
        src_ref=src, dst_ref=dst, send_sem=send, recv_sem=recv, device_id=device, device_id_type=MESH
    )


def ds(start, size):
    return pl.ds(pl.multiple_of(start, size), size)


def attend(queries, kv):
    scores = dot(unfold(queries, 0).astype(BF), kv, NT)
    top = jnp.max(scores, axis=1, keepdims=True)
    raised = jnp.exp2(scores - top).astype(BF)
    return dot(raised, kv, NN), top


def packed(out, top):
    lane = lanes(out.shape)
    total = out[:, 112:113]
    tile = jnp.where(lane == 112, 1.0, jnp.where(lane >= 64, out * (1.0 / total), 0.0))
    for k, piece in enumerate(split3(top) + split3(total)):
        tile = jnp.where(lane == 114 + k, piece, tile)
    return fold(tile, 64).astype(BF)


class Trade:
    def __init__(self, place, b):
        self.place, self.b = place, b
        self.n = SEGMENT // 2**b
        self.tiles = max(LOCAL // 2**b, 1)
        self.folded = self.n // 2 if b < 4 else 16
        self.i = place.member(b)

    def head(self, j, t):
        return j * self.tiles + t if self.b < 4 else j // 2

    def rows(self, j, t):
        return pl.ds(self.place.start(self.b, self.head(j, t)), self.n)

    def folded_rows(self, j, t):
        start = self.place.start(self.b, self.head(j, t)) // 2
        if self.b == 4:
            start = start + j % 2 * 16
        return pl.ds(pl.multiple_of(start, 16), self.folded)

    def slot(self, j):
        return ds(j * self.n, self.n)

    def folded_slot(self, j):
        return ds(j * self.folded, self.folded)

    def home(self, ref, j, t):
        ref = ref.at[self.head(j, t)]
        return ref if self.b < 4 else ref.at[ds(j % 2 * 16, 16), :]

    def whole_home(self, ref, j, t):
        return ref.at[self.head(j, t)] if self.b < 4 else ref.at[j % 2, j // 2]

    def each(self, body):
        def step(d, _):
            j = (self.i + d) % 2**self.b
            for t in range(self.tiles):
                body(j, t, (d - 1) * self.tiles + t, self.place.device(self.b, j))
            return 0

        lax.fori_loop(1, 2**self.b, step, 0)


COPIES = (4, 6, 7, 15)


def forward_kernel(
    q_ref, kv_ref, w_out_ref, fin_ref, att_ref, w_out_other, q1, q2, q3, q4, kv1, kv2, kv3, kv4,
    acc, tops, o1, o2, o3, o4, r1, r2, r3, r4, places, *sems
):
    place = Place()
    trades = [None] + [Trade(place, b) for b in (1, 2, 3, 4)]
    qs, kvs = (None, q1, q2, q3, q4), (None, kv1, kv2, kv3, kv4)
    os, rs = (None, o1, o2, o3, o4), (None, r1, r2, r3, r4)
    *sems, w_send, w_recv = sems
    q_send, q_recv, kv_send, kv_recv, back_send, back_recv = (
        (None,) + tuple(sems[4 * k : 4 * k + 4]) for k in range(6)
    )

    def go(b, action):
        trade = trades[b]

        def body(j, t, k, device):
            for copy in (
                remote(
                    q_ref.at[trade.head(j, t), trade.folded_rows(j, t), :],
                    qs[b].at[t, trade.folded_slot(trade.i), :],
                    q_send[b].at[k],
                    q_recv[b].at[k],
                    device,
                ),
                remote(
                    kv_ref.at[trade.head(j, t), trade.rows(j, t), :],
                    kvs[b].at[t, trade.slot(trade.i), :],
                    kv_send[b].at[k],
                    kv_recv[b].at[k],
                    device,
                ),
            ):
                action(copy)

        trade.each(body)

    def back(b, action):
        trade = trades[b]

        def body(j, t, k, device):
            action(
                remote(
                    os[b].at[t, trade.folded_slot(j), :],
                    trade.home(rs[b], trade.i, t),
                    back_send[b].at[k],
                    back_recv[b].at[k],
                    device,
                )
            )

        trade.each(body)

    start, arrived, sent = (lambda c: c.start()), (lambda c: c.wait_recv()), (lambda c: c.wait_send())
    place.greet(16, True)
    for b in (1, 4, 3, 2):
        go(b, start)
    w_copy = remote(w_out_ref, w_out_other, w_send, w_recv, (place.me, 1 - place.y))
    w_copy.start()

    for b in (1, 2, 3, 4):
        trade = trades[b]
        for t in range(trade.tiles):
            head = trade.head(trade.i, t)
            qs[b][t, trade.folded_slot(trade.i), :] = q_ref[head, trade.folded_rows(trade.i, t), :]
            kvs[b][t, trade.slot(trade.i), :] = kv_ref[head, trade.rows(trade.i, t), :]
    places[...] = placing(64, 0, LOCAL * HEAD_DIM).astype(BF)

    def local_heads(k, _):
        for h in (k * 2, k * 2 + 1):
            for half in range(2):
                rows = pl.ds(half * 512, 512)
                out, top = attend(q_ref[h, pl.ds(half * 256, 256), :], kv_ref[h])
                acc[h, rows, :] = out
                tops[h, rows, :] = jnp.broadcast_to(top, out.shape)
        return 0

    def half_tile(b, t, half):
        rows = pl.ds(half * 256, 256)
        os[b][t, rows, :] = packed(*attend(qs[b][t, rows, :], kvs[b][t]))

    def send_back(b):
        trade = trades[b]
        back(b, start)
        for t in range(trade.tiles):
            trade.home(rs[b], trade.i, t)[...] = os[b][t, trade.folded_slot(trade.i), :]

    lax.fori_loop(0, 2, local_heads, 0)
    go(1, arrived)

    def tiles_1(k, _):
        for t in (k * 2, k * 2 + 1):
            for half in range(2):
                half_tile(1, t, half)
        return 0

    lax.fori_loop(0, 2, tiles_1, 0)
    send_back(1)
    go(4, arrived)
    go(3, arrived)
    half_tile(4, 0, 0)
    half_tile(3, 0, 0)
    half_tile(3, 0, 1)
    send_back(4)
    send_back(3)
    go(2, arrived)
    for t in range(2):
        for half in range(2):
            half_tile(2, t, half)
    send_back(2)
    lax.fori_loop(2, 4, local_heads, 0)

    for b in (1, 4, 3, 2):
        back(b, arrived)

    row = lax.broadcasted_iota(jnp.int32, (128, 256), 0)
    column = lax.broadcasted_iota(jnp.int32, (128, 256), 1)
    first = jnp.where(column < 128, 114, 117)
    picks = jnp.where((row >= first) & (row < first + 3), 1.0, 0.0).astype(BF)

    def merge_head(h, _):
        for b in (1, 2, 3, 4):
            n = SEGMENT // 2**b
            rows = pl.ds(place.start(b, h), n)
            part = unfold(rs[b][h], 64)
            stats = dot(part.astype(BF), picks, NN)
            top = jnp.maximum(tops[h, rows, :], stats[:, 0:128])
            keep = jnp.exp2(tops[h, rows, :] - top)
            gain = jnp.exp2(stats[:, 0:128] - top) * stats[:, 128:256]
            acc[h, rows, :] = acc[h, rows, :] * keep + part * gain
            tops[h, rows, :] = top
        out = acc[h]
        lane = lanes(out.shape)
        inverse = 1.0 / out[:, 112:113]
        out = jnp.where((lane >= 64) & (lane < 112), out * inverse, jnp.where(lane == 112, inverse, 0.0))
        for k, piece in enumerate(split3(-tops[h])):
            out = jnp.where(lane == 116 + k, piece, out)
        fin_ref[h] = out
        return 0

    lax.fori_loop(0, LOCAL, merge_head, 0)

    def compact(n, _):
        rows = ds(n * 256, 256)
        wide = jnp.concatenate([fin_ref[h, rows, :].astype(BF) for h in range(LOCAL)], axis=1)
        att_ref[rows, :] = dot(wide, places[...], NN).astype(BF)
        return 0

    lax.fori_loop(0, 4, compact, 0)

    for b in (4, 3, 2, 1):
        go(b, sent)
        back(b, sent)
    w_copy.wait()


ROWS = 768
HALVES = (384, 192, 96, 48)
LANDING = (0, 384, 576, 672, 720)


def far_bits(seq):
    return list(range(4, seq.bit_length() - 1))


X_FIRST = (0, 1, 2, 3)
Z_FIRST = (0, 2, 3, 1)
ORDERS = (X_FIRST, X_FIRST, X_FIRST, Z_FIRST)


class Halving:
    def __init__(self, place, seq, order, grads, share, scratch):
        self.place, self.seq, self.order, self.grads, self.share = place, seq, order, grads, share
        self.landing, self.send, self.recv, self.far_send, self.far_recv = scratch

    @staticmethod
    def scratch(seq, width=ROWS):
        far = len(far_bits(seq))
        return [pltpu.VMEM((720 + 48 * far, width), BF)] + [pltpu.SemaphoreType.DMA((max(4, far),)) for _ in range(4)]

    def copy(self, k):
        size = HALVES[k]
        bit = self.order[k]
        start = self.place.low(self.order, k) + (1 - self.place.bit(bit)) * size
        return remote(
            self.grads.at[pl.ds(pl.multiple_of(start, 48), size), :],
            self.landing.at[pl.ds(LANDING[k], size), :],
            self.send.at[k],
            self.recv.at[k],
            self.place.partner(bit),
        )

    def add(self, k):
        start = self.place.low(self.order, k + 1)

        def step(i, _):
            rows = pl.ds(pl.multiple_of(start + i * 48, 48), 48)
            arrived = self.landing[pl.ds(pl.multiple_of(LANDING[k] + i * 48, 48), 48), :]
            value = (self.grads[rows, :].astype(F32) + arrived.astype(F32)).astype(BF)
            if k < 3:
                self.grads[rows, :] = value
            else:
                self.share[...] = value
            return 0

        lax.fori_loop(0, HALVES[k] // 48, step, 0)

    def step(self, k):
        if k > 0:
            self.copy(k - 1).wait_recv()
            self.add(k - 1)
        if k < 4:
            self.copy(k).start()
            return
        for n, bit in enumerate(far_bits(self.seq)):
            landing = self.landing.at[pl.ds(720 + 48 * n, 48), :]
            copy = remote(self.share, landing, self.far_send.at[n], self.far_recv.at[n], self.place.partner(bit))
            copy.start()
            copy.wait()
            self.share[...] = (self.share[...].astype(F32) + landing[...].astype(F32)).astype(BF)

    def finish(self):
        for k in range(4):
            self.copy(k).wait_send()


class Doubling:
    def __init__(self, place, order, share, result, sems):
        self.place, self.order, self.share, self.result = place, order, share, result
        self.send, self.recv = sems

    @staticmethod
    def scratch():
        return [pltpu.SemaphoreType.DMA((4,)) for _ in range(2)]

    def copy(self, k):
        rows = pl.ds(pl.multiple_of(self.place.low(self.order, k + 1), 48), HALVES[k])
        view = self.result.at[rows, :]
        return remote(view, view, self.send.at[k], self.recv.at[k], self.place.partner(self.order[k]))

    def step(self, k):
        if k == 0:
            self.result[pl.ds(pl.multiple_of(self.place.low(self.order, 4), 48), 48), :] = self.share[...]
        else:
            self.copy(4 - k).wait_recv()
        if k < 4:
            self.copy(3 - k).start()

    def finish(self):
        for k in range(4):
            self.copy(k).wait_send()


def run_at(slot, work, times):
    for k, time in enumerate(times):

        @pl.when(slot == time)
        def _():
            work.step(k)


def sem_shapes(times):
    return [pltpu.SemaphoreType.DMA((c,)) for _ in range(times) for c in COPIES]


VMEM = pl.BlockSpec(memory_space=pltpu.VMEM)
ANY = pl.BlockSpec(memory_space=pl.ANY)
ORDER = tuple(int(f"{c:04b}"[::-1], 2) for c in range(16))


FOLDED = [((4, 512, 128), BF), ((2, 512, 128), BF), ((1, 512, 128), BF), ((1, 256, 128), BF)]
WHOLE = [((n, SEGMENT, 128), BF) for n in (4, 2, 1, 1)]
FOLDED_HOME = [((LOCAL, n, 128), BF) for n in (256, 128, 64, 32)]


def attention_forward(queries, key_values, w_output):
    shapes = [
        ((LOCAL, SEGMENT, 128), F32),
        ((SEGMENT, LOCAL * HEAD_DIM), BF),
        (w_output.shape, BF),
    ] + FOLDED + WHOLE
    scratch = (
        [((LOCAL, SEGMENT, 128), F32)] * 2 + FOLDED + FOLDED_HOME + [((LOCAL * 128, LOCAL * HEAD_DIM), BF)]
    )
    return pl.pallas_call(
        forward_kernel,
        out_shape=[jax.ShapeDtypeStruct(*s) for s in shapes],
        in_specs=[VMEM, VMEM, ANY],
        out_specs=[VMEM, VMEM, ANY] + [VMEM] * 8,
        scratch_shapes=[pltpu.VMEM(*s) for s in scratch] + sem_shapes(6) + [pltpu.SemaphoreType.DMA] * 2,
        compiler_params=pltpu.CompilerParams(
            collective_id=0, has_side_effects=True, vmem_limit_bytes=56 * 2**20
        ),
        name="attention_forward",
    )(queries, key_values, w_output)


def pair_grads(q, d, kv_at, put):
    d = unfold(d, 64)
    lane = lanes(d.shape)
    top = jnp.where((lane >= 52) & (lane < 55), pltpu.roll(d, 64, 1), 0.0)
    queries = (unfold(q, 0) + top).astype(BF)
    grads = d.astype(BF)
    total = None
    for half in range(2):
        kv = kv_at(half)
        probs = jnp.exp2(dot(kv, queries, NT))
        grad_scores = (probs * dot(kv, grads, NT)).astype(BF)
        put(half, dot(grad_scores, queries, NN) + dot(probs.astype(BF), grads, NN))
        part = dot(kv, grad_scores, TN)
        total = part if total is None else total + part
    return total.T


def backward_kernel(
    q_ref, kv_ref, q1, q2, q3, q4, kv1, kv2, kv3, kv4, fin_ref, do_ref, shares_in, ffn_ref,
    g_ref, sum_ref, grads, ffn_other,
    d0, d1, d2, d3, d4, total_q, total_kv, gq1, gq2, gq3, gq4, gkv1, gkv2, gkv3, gkv4,
    rq1, rq2, rq3, rq4, rkv1, rkv2, rkv3, rkv4, places_q, places_kv, *sems
):
    place = Place()
    trades = [None] + [Trade(place, b) for b in (1, 2, 3, 4)]
    qs, kvs, dd = (None, q1, q2, q3, q4), (None, kv1, kv2, kv3, kv4), (None, d1, d2, d3, d4)
    gqs, gkvs = (None, gq1, gq2, gq3, gq4), (None, gkv1, gkv2, gkv3, gkv4)
    rqs, rkvs = (None, rq1, rq2, rq3, rq4), (None, rkv1, rkv2, rkv3, rkv4)
    *sems, ffn_send, ffn_recv = sems
    go_send, go_recv, q_send, q_recv, kv_send, kv_recv = ((None,) + tuple(sems[4 * k : 4 * k + 4]) for k in range(6))
    doubling = [
        Doubling(place, ORDERS[c], shares_in.at[c], grads.at[c], sems[24 + 2 * c : 26 + 2 * c]) for c in range(4)
    ]

    def reduce_at(slot):
        run_at(slot, doubling[0], (0, 1, 2, 4, 5))
        run_at(slot, doubling[1], (2, 3, 5, 7, 8))
        run_at(slot, doubling[2], (5, 6, 8, 10, 11))
        run_at(slot, doubling[3], (0, 1, 4, 7, 8))

    ffn_copy = remote(ffn_ref, ffn_other, ffn_send, ffn_recv, (place.me, 1 - place.y))

    def go(b, action):
        trade = trades[b]

        def body(j, t, k, device):
            action(
                remote(
                    d0.at[trade.head(j, t), trade.folded_rows(j, t), :],
                    dd[b].at[t, trade.folded_slot(trade.i), :],
                    go_send[b].at[k],
                    go_recv[b].at[k],
                    device,
                )
            )

        trade.each(body)

    def back(b, action):
        trade = trades[b]

        def body(j, t, k, device):
            for copy in (
                remote(
                    gqs[b].at[t, trade.folded_slot(j), :],
                    trade.home(rqs[b], trade.i, t),
                    q_send[b].at[k],
                    q_recv[b].at[k],
                    device,
                ),
                remote(
                    gkvs[b].at[t, trade.slot(j), :],
                    trade.whole_home(rkvs[b], trade.i, t),
                    kv_send[b].at[k],
                    kv_recv[b].at[k],
                    device,
                ),
            ):
                action(copy)

        trade.each(body)

    start, arrived, sent = (lambda c: c.start()), (lambda c: c.wait_recv()), (lambda c: c.wait_send())

    def prepare(h, _):
        fin = fin_ref[h]
        lane = lanes(fin.shape)
        grad = (do_ref[:, ds(h * 128, 128)].astype(F32) * fin[:, 112:113]).astype(BF).astype(F32)
        delta = -jnp.sum(grad * fin, axis=1, keepdims=True)
        high = delta.astype(BF).astype(F32)
        tile = jnp.where(lane < 112, grad, jnp.where(lane < 116, 0.0, jnp.where(lane < 119, fin, 0.0)))
        tile = jnp.where(lane == 112, high, jnp.where(lane == 113, delta - high, tile))
        d0[h] = fold(tile, 64).astype(BF)
        return 0

    lax.fori_loop(0, LOCAL, prepare, 0)
    place.greet(16, True)
    for b in (1, 4, 3, 2):
        go(b, start)
    ffn_copy.start()
    for b in (1, 2, 3, 4):
        trade = trades[b]
        for t in range(trade.tiles):
            head = trade.head(trade.i, t)
            dd[b][t, trade.folded_slot(trade.i), :] = d0[head, trade.folded_rows(trade.i, t), :]
    places_q[...] = placing(0, 0, LOCAL * HEAD_DIM).astype(BF)
    places_kv[...] = (
        placing(0, 0, 2 * LOCAL * HEAD_DIM) + placing(64, LOCAL * HEAD_DIM, 2 * LOCAL * HEAD_DIM)
    ).astype(BF)

    def local_head(h, _):
        def put(half, grad):
            total_kv[h, pl.ds(half * 512, 512), :] = grad

        total_q[h] = pair_grads(q_ref[h], d0[h], lambda half: kv_ref[h, pl.ds(half * 512, 512), :], put)
        reduce_at(jnp.where(h < 4, h, h + 8))
        return 0

    def tile_grads(b, t):
        def put(half, grad):
            gkvs[b][t, pl.ds(half * 512, 512), :] = grad.astype(BF)

        grad = pair_grads(qs[b][t], dd[b][t], lambda half: kvs[b][t, pl.ds(half * 512, 512), :], put)
        gqs[b][t] = fold(jnp.where(lanes(grad.shape) < 64, grad, 0.0), 0).astype(BF)

    def branch(b, slot):
        trade = trades[b]
        go(b, arrived)

        def tile(t, _):
            tile_grads(b, t)
            reduce_at(slot + t)
            return 0

        lax.fori_loop(0, trade.tiles, tile, 0)
        back(b, start)
        for t in range(trade.tiles):
            trade.home(rqs[b], trade.i, t)[...] = gqs[b][t, trade.folded_slot(trade.i), :]
            trade.whole_home(rkvs[b], trade.i, t)[...] = gkvs[b][t, trade.slot(trade.i), :]

    lax.fori_loop(0, 4, local_head, 0)
    branch(1, 4)
    branch(4, 8)
    branch(3, 9)
    branch(2, 10)
    lax.fori_loop(4, 8, local_head, 0)

    for b in (1, 4, 3, 2):
        back(b, arrived)

    def finish(h, _):
        for b in (1, 2, 3, 4):
            rows = pl.ds(place.start(b, h), SEGMENT // 2**b)
            total_q[h, rows, :] += unfold(rqs[b][h], 0)
            if b < 4:
                total_kv[h, rows, :] += rkvs[b][h].astype(F32)
            else:
                total_kv[h, rows, :] += rkv4[0, h].astype(F32) + rkv4[1, h].astype(F32)
        return 0

    lax.fori_loop(0, LOCAL, finish, 0)
    sum_ref[...] = jnp.zeros_like(sum_ref)

    def compact(i, _):
        rows = ds(i * 256, 256)
        key_lane = lanes((256, 128)) < 64
        wide_q, wide_kv = [], []
        for h in range(LOCAL):
            factor = jnp.where(kv_ref[h, rows, 48:49].astype(F32) >= 0.0, 1.0 / LOG2E, 0.0)
            wide_q.append((total_q[h, rows, :] * SCALE).astype(BF))
            wide_kv.append((total_kv[h, rows, :] * jnp.where(key_lane, factor, 1.0)).astype(BF))
        grad_q = dot(jnp.concatenate(wide_q, axis=1), places_q[...], NN)
        grad_kv = dot(jnp.concatenate(wide_kv, axis=1), places_kv[...], NN)
        for k, grad in enumerate((grad_q, grad_kv[:, :384], grad_kv[:, 384:])):
            g_ref[k, rows, :] = grad.astype(BF)
            sum_ref[k] += row_sums(grad)
        return 0

    lax.fori_loop(0, 4, compact, 0)

    for b in (4, 3, 2, 1):
        go(b, sent)
        back(b, sent)
    for work in doubling:
        work.finish()
    ffn_copy.wait()


def attention_backward(queries, key_values, saved, fin, grad_out, shares, ffn_part):
    width = LOCAL * HEAD_DIM
    shapes = [
        ((3, SEGMENT, width), BF),
        ((3, 8, width), F32),
        ((4, ROWS, ROWS), BF),
        (ffn_part.shape, BF),
    ]
    scratch = (
        [((LOCAL, 512, 128), BF)]
        + FOLDED
        + [((LOCAL, SEGMENT, 128), F32)] * 2
        + FOLDED
        + WHOLE
        + FOLDED_HOME
        + [((LOCAL, n, 128), BF) for n in (512, 256, 128)]
        + [((2, LOCAL, 64, 128), BF), ((LOCAL * 128, width), BF), ((LOCAL * 128, 2 * width), BF)]
    )
    return pl.pallas_call(
        backward_kernel,
        out_shape=[jax.ShapeDtypeStruct(*s) for s in shapes],
        in_specs=[VMEM] * 13 + [ANY],
        out_specs=[VMEM, VMEM, VMEM, ANY],
        scratch_shapes=[pltpu.VMEM(*s) for s in scratch]
        + sem_shapes(6)
        + [shape for _ in range(4) for shape in Doubling.scratch()]
        + [pltpu.SemaphoreType.DMA] * 2,
        compiler_params=pltpu.CompilerParams(
            collective_id=1, has_side_effects=True, vmem_limit_bytes=60 * 2**20
        ),
        name="attention_backward",
    )(queries, key_values, *saved, fin, grad_out, shares, ffn_part)


CHUNK = 128


def put_spread(planes, block, value):
    for t in range(value.shape[1] // 128):
        planes[t, pl.ds(ORDER[block], 64, stride=16), :] = value[:, t * 128 : (t + 1) * 128]


def to_planes(value_ref, planes):
    def step(i, _):
        rows = ds(i * 128, 128)
        for t in range(planes.shape[0]):
            planes[t, rows, :] = value_ref[rows, pl.ds(t * 128, 128)].astype(F32)
        return 0

    lax.fori_loop(0, SEGMENT // 128, step, 0)


def take_spread(planes, block):
    return jnp.concatenate(
        [planes[t, pl.ds(ORDER[block], 64, stride=16), :] for t in range(planes.shape[0])], axis=1
    )


def first_kernel(
    tokens_ref, valid_ref, vec_ref, w_ref, bias_ref, q_ref, kv_ref, normed_ref, tokens_out, stats_ref, planes
):
    to_planes(tokens_ref, planes)
    for b in range(16):
        tokens_out[pl.ds(b * 64, 64), :] = take_spread(planes, b).astype(BF)
    count = jnp.sum(valid_ref[...])

    def chunk(n, _):
        rows = ds(n * 256, 256)
        x = tokens_out[rows, :].astype(F32)
        mean, rs = norm_stats(x)
        stats_ref[0, rows, :], stats_ref[1, rows, :] = mean, rs
        normed = ((x - widen(mean, x)) * widen(rs, x) * vector(vec_ref, 0) + vector(vec_ref, 1)).astype(BF)
        normed_ref[rows, :] = normed
        queries = (dot(normed, w_ref[0], NN) + bias_ref[0:1, :]) * (SCALE * LOG2E)
        keys = dot(normed, w_ref[1], NN)
        values = dot(normed, w_ref[2], NN) + bias_ref[1:2, :]
        at = n * 256 + lax.broadcasted_iota(jnp.int32, (256, 128), 0)
        live = (at % 64 * 16 + reversed_bits(at // 64, 4)) < count
        lane = lanes((256, 128))
        padding = jnp.where(live, 0.0, masked_score)
        ones = ((lane >= 52) & (lane < 55)) | (lane == 112) | (lane == 113)
        for h in range(LOCAL):
            query = jnp.where(lane == 48, 1.0, take_48(queries, h, 0))
            q_ref[h, ds(n * 128, 128), :] = fold(query, 0).astype(BF)
            key = jnp.where(live, take_48(keys, h, 0), 0.0) + take_48(values, h, 64)
            kv_ref[h, rows, :] = jnp.where(ones, 1.0, jnp.where(lane == 48, padding, key)).astype(BF)
        return 0

    lax.fori_loop(0, 4, chunk, 0)


def first_part(tokens, valid, vectors, w_project, bias):
    width = tokens.shape[1]
    shapes = [
        ((LOCAL, SEGMENT // 2, 128), BF),
        ((LOCAL, SEGMENT, 128), BF),
        (tokens.shape, BF),
        (tokens.shape, BF),
        ((2, SEGMENT, 128), F32),
    ]
    return pl.pallas_call(
        first_kernel,
        out_shape=[jax.ShapeDtypeStruct(*s) for s in shapes],
        in_specs=[VMEM] * 5,
        out_specs=[VMEM] * len(shapes),
        scratch_shapes=[pltpu.VMEM((width // 128, SEGMENT, 128), F32)],
        compiler_params=pltpu.CompilerParams(vmem_limit_bytes=56 * 2**20),
        name="first_part",
    )(tokens, valid, vectors, w_project, bias)


GELU_C = math.sqrt(2 / math.pi)


def middle_kernel(
    seq, att_ref, w_out_ref, w_out_other, tokens_ref, cot_ref, w_expand, w_reduce, vec_ref,
    middle_ref, gm_ref, do_ref, ffn_ref, shares_ref, grads_o, small_ref,
    att, w_out, stats, normed, active, grad_expand, cot_low, part, other, gm_low, grads, sums, sums_e, planes, cot,
    att_send, att_recv, part_send, part_recv, fill_sem, *sems
):
    place = Place()
    y = place.y
    peer = (place.me, 1 - y)
    b_output, gain, shift = (vector(vec_ref, k) for k in (2, 3, 4))
    n = len(sems) // 4
    halving = [
        Halving(place, seq, ORDERS[c], grads.at[c], shares_ref.at[c], sems[c * n : c * n + n]) for c in range(4)
    ]
    chunk, chunks, width = 256, SEGMENT // 256, tokens_ref.shape[1]

    def att_copy(n):
        rows = ds(n * chunk, chunk)
        return remote(att_ref.at[rows, :], att.at[y, rows, :], att_send.at[n], att_recv.at[n], peer)

    def part_copy(n):
        rows = ds(n * chunk, chunk)
        return remote(part.at[rows, :], other.at[rows, :], part_send.at[n], part_recv.at[n], peer)

    fills = [
        pltpu.make_async_copy(cot_ref.at[:, pl.ds(t * 128, 128)], planes.at[t], fill_sem.at[t])
        for t in range(width // 128)
    ]
    for fill in fills:
        fill.start()
    place.greet(seq, True)
    for n in range(chunks):
        att_copy(n).start()
    att[y] = att_ref[...]
    w_out[y] = w_out_ref[...]
    w_out[1 - y] = w_out_other[...]
    sums[...] = jnp.zeros_like(sums)
    sums_e[...] = jnp.zeros_like(sums_e)
    for fill in fills:
        fill.wait()
    for b in range(16):
        cot[pl.ds(b * 64, 64), :] = take_spread(planes, b)

    def ahead(n, _):
        rows = ds(n * chunk, chunk)
        grad_out = cot[rows, :]
        sums[0:8] += row_sums(grad_out)
        low = grad_out.astype(BF)
        cot_low[rows, :] = low
        att_copy(n).wait_recv()
        branch = dot(att[0, rows, :], w_out[0], NN) + dot(att[1, rows, :], w_out[1], NN)
        middle = tokens_ref[rows, :].astype(F32) + (branch + b_output)
        middle_ref[rows, :] = middle
        mean, rs = norm_stats(middle)
        stats[0, rows, :], stats[1, rows, :] = mean, rs
        norm = ((middle - widen(mean, middle)) * widen(rs, middle) * gain + shift).astype(BF)
        normed[rows, :] = norm
        value = None
        for k in range(w_expand.shape[1] // width):
            at = pl.ds(k * width, width)
            expand = dot(norm, w_expand[:, at], NN) + vector(vec_ref, 5 + k)
            square = expand * expand
            bent = jnp.tanh(GELU_C * expand * (1.0 + 0.044715 * square))
            gate = 0.5 * (1.0 + bent)
            active[rows, at] = (expand * gate).astype(BF)
            slope = gate + (0.5 * GELU_C) * expand * (1.0 - bent * bent) * (1.0 + (3 * 0.044715) * square)
            grad = dot(low, w_reduce[at, :], NT) * slope
            sums_e[:, at] += row_sums(grad)
            grad = grad.astype(BF)
            grad_expand[rows, at] = grad
            piece = dot(grad, w_expand[:, at], NT)
            value = piece if value is None else value + piece
        part[rows, :] = value.astype(BF)
        part_copy(n).start()
        return 0

    lax.fori_loop(0, chunks, ahead, 0)

    def behind(n, _):
        rows = ds(n * chunk, chunk)
        part_copy(n).wait_recv()
        grad = part[rows, :].astype(F32) + other[rows, :].astype(F32)
        rs = widen(stats[1, rows, :], grad)
        xhat = (middle_ref[rows, :] - widen(stats[0, rows, :], grad)) * rs
        sums[8:16] += row_sums(grad * xhat)
        sums[16:24] += row_sums(grad)
        gm = cot[rows, :] + norm_back(grad, xhat, rs, gain)
        gm_ref[rows, :] = gm
        sums[24:32] += row_sums(gm)
        low = gm.astype(BF)
        gm_low[rows, :] = low
        grad_att = dot(low, w_out_ref[...], NT)
        for h in range(LOCAL):
            do_ref[rows, pl.ds(h * 128, 128)] = take_48(grad_att, h, 64).astype(BF)
        return 0

    for k in range(2):
        grads[k] = dot(active[:, pl.ds(k * width, width)], cot_low[...], TN).astype(BF)
        halving[k].step(0)
    for k in range(2):
        grads[2 + k] = dot(normed[...], grad_expand[:, pl.ds(k * width, width)], TN).astype(BF)
        halving[2 + k].step(0)
        halving[k].step(1)
    halving[3].step(1)
    behind(0, 0)
    halving[0].step(2)
    halving[2].step(1)
    ffn_ref[...] = dot(active[...], w_reduce[...], NN).astype(BF)
    behind(1, 0)
    halving[1].step(2)
    halving[3].step(2)
    halving[0].step(3)
    behind(2, 0)
    halving[0].step(4)
    halving[1].step(3)
    halving[2].step(2)
    halving[3].step(3)
    behind(3, 0)
    halving[1].step(4)
    halving[2].step(3)
    halving[3].step(4)
    for k in range(2):
        at = pl.ds(k * (width // 2), width // 2)
        grads_o[pl.ds(k * 384, 384), :] = dot(att_ref[...], gm_low[:, at], TN).astype(BF)
    halving[2].step(4)
    put_vector(small_ref, 0, sums[24:32])
    put_vector(small_ref, 6, sums[8:16])
    put_vector(small_ref, 12, sums[16:24])
    put_vector(small_ref, 18, sums_e[...])
    put_vector(small_ref, 30, sums[0:8])
    small_ref[36:48, :] = jnp.zeros((12, 128), F32)
    for n in range(chunks):
        att_copy(n).wait_send()
        part_copy(n).wait_send()
    for work in halving:
        work.finish()


def middle_part(attended, w_output, w_out_other, tokens, cot, w_expand, w_reduce, vectors):
    seq = lax.axis_size("seq")
    rows, width = tokens.shape
    hidden = w_expand.shape[1]
    shapes = [
        ((rows, width), F32),
        ((rows, width), F32),
        ((rows, LOCAL * 128), BF),
        ((rows, width), BF),
        ((4, 48, ROWS), BF),
        ((ROWS, ROWS // 2), BF),
        ((48, 128), F32),
    ]
    scratch = [
        ((2,) + attended.shape, BF),
        ((2,) + w_output.shape, BF),
        ((2, rows, 128), F32),
        ((rows, width), BF),
        ((rows, hidden), BF),
        ((rows, hidden), BF),
        ((rows, width), BF),
        ((rows, width), BF),
        ((rows, width), BF),
        ((rows, width), BF),
        ((4, ROWS, ROWS), BF),
        ((32, width), F32),
        ((8, hidden), F32),
        ((width // 128, rows, 128), F32),
        ((rows, width), F32),
    ]
    return pl.pallas_call(
        functools.partial(middle_kernel, seq),
        out_shape=[jax.ShapeDtypeStruct(*s) for s in shapes],
        in_specs=[VMEM] * 4 + [ANY] + [VMEM] * 3,
        out_specs=[VMEM] * len(shapes),
        scratch_shapes=[pltpu.VMEM(*s) for s in scratch]
        + [pltpu.SemaphoreType.DMA((4,)) for _ in range(4)]
        + [pltpu.SemaphoreType.DMA((width // 128,))]
        + [shape for _ in range(4) for shape in Halving.scratch(seq)],
        compiler_params=pltpu.CompilerParams(
            collective_id=3, has_side_effects=True, vmem_limit_bytes=60 * 2**20
        ),
        name="middle_part",
    )(attended, w_output, w_out_other, tokens, cot, w_expand, w_reduce, vectors)


def last_kernel(
    seq, g_ref, w_ref, normed_ref, w_out_ref, small_in, sum_ref, vec_ref,
    tokens_in, gm_in, stats_in, middle_in, ffn_in, ffn_other_in,
    planes, layer_planes, grads_ref, early_ref, late_ref,
    tokens_ref, gm_ref, stats, middle_ref, ffn_ref, ffn_other,
    grads, shares, part, other, small_ref, early_in, late, late_in, sums, fill_sem,
    part_send, part_recv, early_send, early_recv, late_send, late_recv, far_send, far_recv, *sems
):
    place = Place()
    orders = (X_FIRST, X_FIRST, Z_FIRST, X_FIRST)
    halving = [Halving(place, seq, orders[c], grads.at[c], shares.at[c], sems[5 * c : 5 * c + 5]) for c in range(4)]
    gathers = [
        Doubling(place, orders[c], shares.at[c], grads_ref.at[c], sems[20 + 2 * c : 22 + 2 * c]) for c in range(4)
    ]
    i = place.member(4)
    chunks = SEGMENT // CHUNK
    fills = [
        pltpu.make_async_copy(src, dst, fill_sem.at[k])
        for k, (src, dst) in enumerate(
            zip(
                (tokens_in, gm_in, stats_in, middle_in, ffn_in, ffn_other_in),
                (tokens_ref, gm_ref, stats, middle_ref, ffn_ref, ffn_other),
            )
        )
    ]
    for fill in fills:
        fill.start()
    put_vector(small_ref, 0, sum_ref[0])
    put_vector(small_ref, 3, sum_ref[2])
    small_ref[6:48, :] = small_in[0:42, :]

    def to_all(src, landing, send, recv):
        def each(action):
            def step(d, _):
                action(remote(src, landing.at[i], send.at[d - 1], recv.at[d - 1], place.device(4, (i + d) % 16)))
                return 0

            lax.fori_loop(1, 16, step, 0)

        return each

    def total_of(src, landing):
        def step(j, value):
            return value + landing[j]

        landing[i] = src[...]
        return lax.fori_loop(1, 16, step, landing[0])

    def far_total(result, n):
        for k, bit in enumerate(far_bits(seq)):
            landing = (early_in, late_in)[n].at[16 + k]
            copy = remote(result, landing, far_send.at[n * 8 + k], far_recv.at[n * 8 + k], place.partner(bit))
            copy.start()
            copy.wait()
            result[...] = result[...] + landing[...]

    def exchange(n):
        rows = ds(n * CHUNK, CHUNK)
        return remote(
            part.at[rows, :], other.at[rows, :], part_send.at[n], part_recv.at[n], (place.me, 1 - place.y)
        )

    def partial(n, _):
        rows = ds(n * CHUNK, CHUNK)
        value = dot(g_ref[0, rows, :], w_ref[0], NT)
        value += dot(g_ref[1, rows, :], w_ref[1], NT)
        value += dot(g_ref[2, rows, :], w_ref[2], NT)
        part[rows, :] = value.astype(BF)
        exchange(n).start()
        return 0

    def grad_w(k):
        grads[k] = dot(normed_ref[...], g_ref[k], TN).astype(BF)

    def layer(b):
        rows = pl.ds(b * 64, 64)
        total = ffn_ref[rows, :].astype(F32) + ffn_other[rows, :].astype(F32)
        put_spread(layer_planes, b, middle_ref[rows, :] + total + vector(vec_ref, 7))

    place.greet(seq, True)
    grads[3] = w_out_ref[...]
    halving[3].step(0)
    lax.fori_loop(0, 2, partial, 0)
    halving[3].step(1)
    for k in range(3):
        grad_w(k)
        halving[k].step(0)
    halving[0].step(1)
    halving[2].step(1)
    lax.fori_loop(2, chunks, partial, 0)
    early_all = to_all(small_ref, early_in, early_send, early_recv)
    halving[3].step(2)
    halving[1].step(1)
    sums[...] = jnp.zeros_like(sums)
    early_all(lambda copy: copy.start())
    h0, h1, h2, h3, g0, g1, g2, g3 = halving + gathers
    after = (
        ((h0, 2), (h3, 3)),
        ((h1, 2), (h3, 4), (g3, 0), (h2, 2)),
        ((h0, 3), (g3, 1)),
        ((h0, 4), (g0, 0), (h1, 3), (g3, 2), (h2, 3)),
        ((h1, 4), (g1, 0), (h2, 4), (g2, 0), (g0, 1)),
        ((g3, 3), (g0, 2), (g1, 1), (g2, 1)),
        ((g3, 4), (g1, 2), (g2, 2)),
        ((g0, 3),),
    )
    for fill in fills:
        fill.wait()
    for n in range(chunks):
        for b in range(n * 2, n * 2 + 2):
            layer(b)
        exchange(n).wait_recv()
        rows = pl.ds(n * CHUNK, CHUNK)
        grad = part[rows, :].astype(F32) + other[rows, :].astype(F32)
        rs = widen(stats[1, rows, :], grad)
        xhat = (tokens_ref[rows, :].astype(F32) - widen(stats[0, rows, :], grad)) * rs
        sums[0:8] += row_sums(grad * xhat)
        sums[8:16] += row_sums(grad)
        grad = gm_ref[rows, :] + norm_back(grad, xhat, rs, vector(vec_ref, 0))
        for k in range(CHUNK // 64):
            put_spread(planes, n * (CHUNK // 64) + k, grad[k * 64 : (k + 1) * 64])
        for work, k in after[n]:
            work.step(k)
    for k in range(2):
        put_vector(late, k * 8, sums[k * 8 : k * 8 + 8])
        late[pl.ds(k * 8 + 6, 2), :] = jnp.zeros((2, 128), F32)
    late_all = to_all(late, late_in, late_send, late_recv)
    late_all(lambda copy: copy.start())
    g1.step(3)
    g2.step(3)
    early_all(lambda copy: copy.wait_recv())
    early_ref[...] = total_of(small_ref, early_in)
    far_total(early_ref, 0)
    late_all(lambda copy: copy.wait_recv())
    late_ref[...] = total_of(late, late_in)
    far_total(late_ref, 1)
    for work in (g0, g1, g2):
        work.step(4)

    def sent(n, _):
        exchange(n).wait_send()
        return 0

    lax.fori_loop(0, chunks, sent, 0)
    early_all(lambda copy: copy.wait_send())
    late_all(lambda copy: copy.wait_send())
    for work in halving + gathers:
        work.finish()


def last_part(g, w_project, normed, grad_w_out, small, g_sums, vectors, *late_inputs):
    seq = lax.axis_size("seq")
    far = len(far_bits(seq))
    width = normed.shape[1]
    shapes = [
        ((width // 128, SEGMENT, 128), F32),
        ((width // 128, SEGMENT, 128), F32),
        ((4, ROWS, ROWS // 2), BF),
        (small.shape, F32),
        ((16, 128), F32),
    ]
    scratch = [(a.shape, a.dtype) for a in late_inputs] + [
        ((4, ROWS, ROWS // 2), BF),
        ((4, 48, ROWS // 2), BF),
        (normed.shape, BF),
        (normed.shape, BF),
        (small.shape, F32),
        ((16 + far,) + small.shape, F32),
        ((16, 128), F32),
        ((16 + far, 16, 128), F32),
        ((16, width), F32),
    ]
    chunks = SEGMENT // CHUNK
    counts = (len(late_inputs), chunks, chunks, 15, 15, 15, 15, 16, 16)
    return pl.pallas_call(
        functools.partial(last_kernel, seq),
        out_shape=[jax.ShapeDtypeStruct(*s) for s in shapes],
        in_specs=[VMEM] * 7 + [ANY] * len(late_inputs),
        out_specs=[VMEM] * len(shapes),
        scratch_shapes=[pltpu.VMEM(*s) for s in scratch]
        + [pltpu.SemaphoreType.DMA((c,)) for c in counts]
        + [shape for _ in range(4) for shape in Halving.scratch(seq, ROWS // 2)]
        + [shape for _ in range(4) for shape in Doubling.scratch()],
        compiler_params=pltpu.CompilerParams(
            collective_id=2, has_side_effects=True, vmem_limit_bytes=58 * 2**20
        ),
        name="last_part",
    )(g, w_project, normed, grad_w_out, small, g_sums, vectors, *late_inputs)


def out_kernel(r_ref, e_ref, p_ref, o_ref, o2_ref, t_ref, l_ref, r_out, e_out, p_out, o_out, t_out, l_out):
    half = ROWS // 2
    r_out[...] = r_ref[...].astype(F32)
    for k in range(2):
        e_out[:, k * ROWS : (k + 1) * ROWS] = e_ref[k].astype(F32)
    p_out[...] = p_ref[...].astype(F32)
    o_out[:, :half] = o_ref[0].astype(F32)
    o_out[:, half:] = o2_ref[0].astype(F32)
    for k in range(t_ref.shape[0]):
        at = slice(k * 128, (k + 1) * 128)
        t_out[:, at] = t_ref[k]
        l_out[:, at] = l_ref[k]


def results(grads, grads_p, planes, layer_planes):
    half = ROWS // 2
    n = 8
    rows, width = planes.shape[1], planes.shape[0] * 128
    plane_spec = pl.BlockSpec((planes.shape[0], rows // n, 128), lambda i: (0, i, 0))
    row_spec = pl.BlockSpec((rows // n, width), lambda i: (i, 0))
    return pl.pallas_call(
        out_kernel,
        grid=(n,),
        out_shape=[
            jax.ShapeDtypeStruct((2 * ROWS, ROWS), F32),
            jax.ShapeDtypeStruct((ROWS, 2 * ROWS), F32),
            jax.ShapeDtypeStruct((3, ROWS, half), F32),
            jax.ShapeDtypeStruct((half, ROWS), F32),
            jax.ShapeDtypeStruct((rows, width), F32),
            jax.ShapeDtypeStruct((rows, width), F32),
        ],
        in_specs=[
            pl.BlockSpec((2 * ROWS // n, ROWS), lambda i: (i, 0)),
            pl.BlockSpec((2, ROWS // n, ROWS), lambda i: (1, i, 0)),
            pl.BlockSpec((3, ROWS // n, half), lambda i: (0, i, 0)),
            pl.BlockSpec((1, half // n, half), lambda i: (3, i, 0)),
            pl.BlockSpec((1, half // n, half), lambda i: (3, n + i, 0)),
            plane_spec,
            plane_spec,
        ],
        out_specs=[
            pl.BlockSpec((2 * ROWS // n, ROWS), lambda i: (i, 0)),
            pl.BlockSpec((ROWS // n, 2 * ROWS), lambda i: (i, 0)),
            pl.BlockSpec((3, ROWS // n, half), lambda i: (0, i, 0)),
            pl.BlockSpec((half // n, ROWS), lambda i: (i, 0)),
            row_spec,
            row_spec,
        ],
        name="results",
    )(grads.reshape(-1, ROWS), grads, grads_p, grads_p, grads_p, planes, layer_planes)


def body(
    tokens,
    cotangent,
    valid_tiles,
    gain_first,
    shift_first,
    w_project,
    bias_project,
    w_output,
    bias_output,
    gain_second,
    shift_second,
    w_expand,
    bias_expand,
    w_reduce,
    bias_reduce,
):
    width = tokens.shape[1]
    half = width // 2
    w_project = w_project.transpose(1, 0, 2)
    vectors = jnp.concatenate(
        [gain_first, shift_first, bias_output, gain_second, shift_second, bias_expand, bias_reduce]
    ).reshape(-1, 128)
    queries, key_values, normed, tokens, stats = first_part(
        tokens, valid_tiles.reshape(8, -1), vectors, w_project, bias_project
    )
    fin, attended, w_out_other, *saved = attention_forward(queries, key_values, w_output)
    middle, grad_middle, grad_attended, ffn_part, shares, grads_o, small = middle_part(
        attended, w_output, w_out_other, tokens, cotangent, w_expand, w_reduce, vectors
    )
    g, g_sums, grads, ffn_other = attention_backward(
        queries, key_values, saved, fin, grad_attended, shares, ffn_part
    )
    planes, layer_planes, grads_p, small, late = last_part(
        g, w_project, normed, grads_o, small, g_sums, vectors,
        tokens, grad_middle, stats, middle, ffn_part, ffn_other,
    )
    small = small.reshape(-1)
    late = late.reshape(2, 8 * 128)[:, :width]
    parts = [small[k * width : (k + 1) * width] for k in range(7)]
    grad_w_reduce, grad_w_expand, grad_w_project, grad_w_output, grad_tokens, layer_out = results(
        grads, grads_p, planes, layer_planes
    )
    return (
        layer_out,
        grad_tokens,
        late[0],
        late[1],
        grad_w_project.transpose(1, 0, 2),
        parts[0].reshape(2, half),
        grad_w_output,
        parts[1],
        parts[2],
        parts[3],
        grad_w_expand,
        small[4 * width : 6 * width],
        grad_w_reduce,
        parts[6],
    )


def solution(mesh):
    in_specs = (
        P("seq", None),
        P("seq", None),
        P("seq"),
        P(),
        P(),
        P(None, None, "heads"),
        P(None, "heads"),
        P("heads", None),
        P(),
        P(),
        P(),
        P(None, "heads"),
        P("heads"),
        P("heads", None),
        P(),
    )
    out_specs = (
        P("seq", None),
        P("seq", None),
        P(),
        P(),
        P(None, None, "heads"),
        P(None, "heads"),
        P("heads", None),
        P(),
        P(),
        P(),
        P(None, "heads"),
        P("heads"),
        P("heads", None),
        P(),
    )
    return jax.shard_map(body, mesh=mesh, in_specs=in_specs, out_specs=out_specs, check_vma=False)
```

```python
import functools
import math

import jax
import jax.numpy as jnp
from jax import lax
from jax.experimental import pallas as pl
from jax.experimental.pallas import tpu as pltpu
from jax.sharding import PartitionSpec as P

HEADS = 16
HEAD_DIM = 48
SEGMENT = 1024
BRANCHES = 5
LOCAL = 8

MESH = pl.DeviceIdType.MESH
BF = jnp.bfloat16
F32 = jnp.float32
NT = (((1,), (1,)), ((), ()))
TN = (((0,), (0,)), ((), ()))
NN = (((1,), (0,)), ((), ()))

masked_score = -1000000000.0
layer_eps = 1e-05
SCALE = HEAD_DIM ** (-0.5)
LOG2E = math.log2(math.e)


def dot(a, b, dims):
    return lax.dot_general(a, b, dims, preferred_element_type=F32)


def lanes(shape):
    return lax.broadcasted_iota(jnp.int32, shape, len(shape) - 1)


def reversed_bits(value, bits):
    out = value * 0
    for k in range(bits):
        out = out * 2 + (value // 2**k) % 2
    return out


def split3(value):
    high = value.astype(BF).astype(F32)
    rest = value - high
    middle = rest.astype(BF).astype(F32)
    return high, middle, rest - middle


def take_48(value, head, at):
    tile, off = head * 48 // 128, head * 48 % 128
    shift = (at - off) % 128
    turn = lambda k: pltpu.roll(value[:, k * 128 : (k + 1) * 128], shift, 1) if shift else value[:, k * 128 : (k + 1) * 128]
    out = turn(tile)
    lane = lanes(out.shape)
    if off + 48 > 128:
        out = jnp.where(lane < at + 128 - off, out, turn(tile + 1))
    return jnp.where((lane >= at) & (lane < at + 48), out, 0.0)


def fold(value, at):
    pairs = value.reshape(value.shape[0] // 32, 2, 16, 128)
    even, odd = pairs[:, 0].reshape(-1, 128), pairs[:, 1].reshape(-1, 128)
    return pltpu.roll(even, 64, 1) + odd if at else even + pltpu.roll(odd, 64, 1)


def unfold(value, at):
    value = value.astype(F32)
    keep = lanes(value.shape) >= 64 if at else lanes(value.shape) < 64
    turned = jnp.where(keep, pltpu.roll(value, 64, 1), 0.0)
    straight = jnp.where(keep, value, 0.0)
    even, odd = (turned, straight) if at else (straight, turned)
    pairs = [part.reshape(-1, 1, 16, 128) for part in (even, odd)]
    return jnp.concatenate(pairs, axis=1).reshape(-1, 128)


def placing(source, target, columns):
    row = lax.broadcasted_iota(jnp.int32, (LOCAL * 128, columns), 0)
    column = lax.broadcasted_iota(jnp.int32, (LOCAL * 128, columns), 1)
    lane = row % 128 - source
    hit = (lane >= 0) & (lane < HEAD_DIM) & (column == target + row // 128 * HEAD_DIM + lane)
    return jnp.where(hit, 1.0, 0.0)


def row_mean(value):
    ones = jnp.ones((value.shape[1], 128), BF)
    high = value.astype(BF)
    low = (value - high.astype(F32)).astype(BF)
    return (dot(high, ones, NN) + dot(low, ones, NN)) * (1.0 / value.shape[1])


def vector(ref, k, width=768):
    n = width // 128
    return jnp.concatenate([ref[k * n + t : k * n + t + 1, :] for t in range(n)], axis=1)


def widen(tile, like):
    return jnp.concatenate([tile] * (like.shape[1] // 128), axis=1)


def row_sums(value):
    return jnp.sum(value.reshape(value.shape[0] // 8, 8, value.shape[1]), axis=0)


def put_vector(rows, first, partial):
    value = jnp.sum(partial, axis=0, keepdims=True)
    for t in range(value.shape[1] // 128):
        rows[pl.ds(first + t, 1), :] = value[:, t * 128 : (t + 1) * 128]


def norm_stats(value):
    mean = row_mean(value)
    centered = value - widen(mean, value)
    rs = lax.rsqrt(row_mean(centered * centered) + layer_eps)
    return mean, rs


def norm_back(grad, xhat, rs, gain):
    grad = grad * gain
    return rs * (grad - widen(row_mean(grad), grad) - xhat * widen(row_mean(grad * xhat), grad))


class Place:
    def __init__(self):
        self.me = lax.axis_index("seq")
        self.y = lax.axis_index("heads")

    def member(self, b):
        return self.me % 2**b

    def device(self, b, j):
        return (self.me // 2**b * 2**b + j, self.y)

    def start(self, b, head):
        stride = 2**b
        place = (self.y * LOCAL + head) % stride
        return pl.multiple_of(reversed_bits(place, b) * (SEGMENT // stride), SEGMENT // stride)

    def bit(self, k):
        return self.me // 2**k % 2

    def partner(self, k):
        return (self.me + 2**k * (1 - 2 * self.bit(k)), self.y)

    def low(self, order, k):
        return sum((self.bit(order[i]) * HALVES[i] for i in range(k)), self.me * 0)

    def greet(self, seq=16, other=False):
        barrier = pltpu.get_barrier_semaphore()
        i = self.member(4)
        count = 15
        if other:
            pl.semaphore_signal(barrier, inc=1, device_id=(self.me, 1 - self.y), device_id_type=MESH)
            count += 1
        for k in far_bits(seq):
            pl.semaphore_signal(barrier, inc=1, device_id=self.partner(k), device_id_type=MESH)
            count += 1

        def signal(d, _):
            pl.semaphore_signal(barrier, inc=1, device_id=self.device(4, (i + d) % 16), device_id_type=MESH)
            return 0

        lax.fori_loop(1, 16, signal, 0)
        pl.semaphore_wait(barrier, count)


def remote(src, dst, send, recv, device):
    return pltpu.make_async_remote_copy(
        src_ref=src, dst_ref=dst, send_sem=send, recv_sem=recv, device_id=device, device_id_type=MESH
    )


def ds(start, size):
    return pl.ds(pl.multiple_of(start, size), size)


def attend(queries, kv):
    scores = dot(unfold(queries, 0).astype(BF), kv, NT)
    top = jnp.max(scores, axis=1, keepdims=True)
    raised = jnp.exp2(scores - top).astype(BF)
    return dot(raised, kv, NN), top


def packed(out, top):
    lane = lanes(out.shape)
    total = out[:, 112:113]
    tile = jnp.where(lane == 112, 1.0, jnp.where(lane >= 64, out * (1.0 / total), 0.0))
    for k, piece in enumerate(split3(top) + split3(total)):
        tile = jnp.where(lane == 114 + k, piece, tile)
    return fold(tile, 64).astype(BF)


class Trade:
    def __init__(self, place, b):
        self.place, self.b = place, b
        self.n = SEGMENT // 2**b
        self.tiles = max(LOCAL // 2**b, 1)
        self.folded = self.n // 2 if b < 4 else 16
        self.i = place.member(b)

    def head(self, j, t):
        return j * self.tiles + t if self.b < 4 else j // 2

    def rows(self, j, t):
        return pl.ds(self.place.start(self.b, self.head(j, t)), self.n)

    def folded_rows(self, j, t):
        start = self.place.start(self.b, self.head(j, t)) // 2
        if self.b == 4:
            start = start + j % 2 * 16
        return pl.ds(pl.multiple_of(start, 16), self.folded)

    def slot(self, j):
        return ds(j * self.n, self.n)

    def folded_slot(self, j):
        return ds(j * self.folded, self.folded)

    def home(self, ref, j, t):
        ref = ref.at[self.head(j, t)]
        return ref if self.b < 4 else ref.at[ds(j % 2 * 16, 16), :]

    def whole_home(self, ref, j, t):
        return ref.at[self.head(j, t)] if self.b < 4 else ref.at[j % 2, j // 2]

    def each(self, body):
        def step(d, _):
            j = (self.i + d) % 2**self.b
            for t in range(self.tiles):
                body(j, t, (d - 1) * self.tiles + t, self.place.device(self.b, j))
            return 0

        lax.fori_loop(1, 2**self.b, step, 0)


COPIES = (4, 6, 7, 15)


def forward_kernel(
    q_ref, kv_ref, w_out_ref, fin_out, att_ref, w_out_other, s1, s2, s3, s4, s5, s6, s7, s8,
    fin_ref, q1, q2, q3, q4, kv1, kv2, kv3, kv4, acc, tops, o1, o2, o3, o4, r1, r2, r3, r4, places, *sems
):
    place = Place()
    trades = [None] + [Trade(place, b) for b in (1, 2, 3, 4)]
    qs, kvs = (None, q1, q2, q3, q4), (None, kv1, kv2, kv3, kv4)
    os, rs = (None, o1, o2, o3, o4), (None, r1, r2, r3, r4)
    *sems, w_send, w_recv, fin_sem, saved_sem = sems
    q_send, q_recv, kv_send, kv_recv, back_send, back_recv = (
        (None,) + tuple(sems[4 * k : 4 * k + 4]) for k in range(6)
    )

    def go(b, action):
        trade = trades[b]

        def body(j, t, k, device):
            for copy in (
                remote(
                    q_ref.at[trade.head(j, t), trade.folded_rows(j, t), :],
                    qs[b].at[t, trade.folded_slot(trade.i), :],
                    q_send[b].at[k],
                    q_recv[b].at[k],
                    device,
                ),
                remote(
                    kv_ref.at[trade.head(j, t), trade.rows(j, t), :],
                    kvs[b].at[t, trade.slot(trade.i), :],
                    kv_send[b].at[k],
                    kv_recv[b].at[k],
                    device,
                ),
            ):
                action(copy)

        trade.each(body)

    def back(b, action):
        trade = trades[b]

        def body(j, t, k, device):
            action(
                remote(
                    os[b].at[t, trade.folded_slot(j), :],
                    trade.home(rs[b], trade.i, t),
                    back_send[b].at[k],
                    back_recv[b].at[k],
                    device,
                )
            )

        trade.each(body)

    def fin_copy(h):
        return pltpu.make_async_copy(fin_ref.at[h], fin_out.at[h], fin_sem.at[h])

    saved = [
        pltpu.make_async_copy(src, dst, saved_sem.at[k])
        for k, (src, dst) in enumerate(
            zip((q1, q2, q3, q4, kv1, kv2, kv3, kv4), (s1, s2, s3, s4, s5, s6, s7, s8))
        )
    ]
    start, arrived, sent = (lambda c: c.start()), (lambda c: c.wait_recv()), (lambda c: c.wait_send())
    place.greet(16, True)
    for b in (1, 4, 3, 2):
        go(b, start)
    w_copy = remote(w_out_ref, w_out_other, w_send, w_recv, (place.me, 1 - place.y))
    w_copy.start()

    for b in (1, 2, 3, 4):
        trade = trades[b]
        for t in range(trade.tiles):
            head = trade.head(trade.i, t)
            qs[b][t, trade.folded_slot(trade.i), :] = q_ref[head, trade.folded_rows(trade.i, t), :]
            kvs[b][t, trade.slot(trade.i), :] = kv_ref[head, trade.rows(trade.i, t), :]
    places[...] = placing(64, 0, LOCAL * HEAD_DIM).astype(BF)

    def local_heads(k, _):
        for h in (k * 2, k * 2 + 1):
            for half in range(2):
                rows = pl.ds(half * 512, 512)
                out, top = attend(q_ref[h, pl.ds(half * 256, 256), :], kv_ref[h])
                acc[h, rows, :] = out
                tops[h, rows, :] = jnp.broadcast_to(top, out.shape)
        return 0

    def half_tile(b, t, half):
        rows = pl.ds(half * 256, 256)
        os[b][t, rows, :] = packed(*attend(qs[b][t, rows, :], kvs[b][t]))

    def send_back(b):
        trade = trades[b]
        back(b, start)
        saved[b - 1].start()
        saved[b + 3].start()
        for t in range(trade.tiles):
            trade.home(rs[b], trade.i, t)[...] = os[b][t, trade.folded_slot(trade.i), :]

    lax.fori_loop(0, 2, local_heads, 0)
    go(1, arrived)

    def tiles_1(k, _):
        for t in (k * 2, k * 2 + 1):
            for half in range(2):
                half_tile(1, t, half)
        return 0

    lax.fori_loop(0, 2, tiles_1, 0)
    send_back(1)
    go(4, arrived)
    go(3, arrived)
    half_tile(4, 0, 0)
    half_tile(3, 0, 0)
    half_tile(3, 0, 1)
    send_back(4)
    send_back(3)
    go(2, arrived)
    for t in range(2):
        for half in range(2):
            half_tile(2, t, half)
    send_back(2)
    lax.fori_loop(2, 4, local_heads, 0)

    for b in (1, 4, 3, 2):
        back(b, arrived)

    row = lax.broadcasted_iota(jnp.int32, (128, 256), 0)
    column = lax.broadcasted_iota(jnp.int32, (128, 256), 1)
    first = jnp.where(column < 128, 114, 117)
    picks = jnp.where((row >= first) & (row < first + 3), 1.0, 0.0).astype(BF)

    def merge_head(h, _):
        for b in (1, 2, 3, 4):
            n = SEGMENT // 2**b
            rows = pl.ds(place.start(b, h), n)
            part = unfold(rs[b][h], 64)
            stats = dot(part.astype(BF), picks, NN)
            top = jnp.maximum(tops[h, rows, :], stats[:, 0:128])
            keep = jnp.exp2(tops[h, rows, :] - top)
            gain = jnp.exp2(stats[:, 0:128] - top) * stats[:, 128:256]
            acc[h, rows, :] = acc[h, rows, :] * keep + part * gain
            tops[h, rows, :] = top
        out = acc[h]
        lane = lanes(out.shape)
        inverse = 1.0 / out[:, 112:113]
        out = jnp.where((lane >= 64) & (lane < 112), out * inverse, jnp.where(lane == 112, inverse, 0.0))
        for k, piece in enumerate(split3(-tops[h])):
            out = jnp.where(lane == 116 + k, piece, out)
        fin_ref[h] = out
        fin_copy(h).start()
        return 0

    lax.fori_loop(0, LOCAL, merge_head, 0)

    def compact(n, _):
        rows = ds(n * 256, 256)
        wide = jnp.concatenate([fin_ref[h, rows, :].astype(BF) for h in range(LOCAL)], axis=1)
        att_ref[rows, :] = dot(wide, places[...], NN).astype(BF)
        return 0

    lax.fori_loop(0, 4, compact, 0)

    for b in (4, 3, 2, 1):
        go(b, sent)
        back(b, sent)
    w_copy.wait()
    for copy in saved:
        copy.wait()
    for h in range(LOCAL):
        fin_copy(h).wait()


ROWS = 768
HALVES = (384, 192, 96, 48)
LANDING = (0, 384, 576, 672, 720)


def far_bits(seq):
    return list(range(4, seq.bit_length() - 1))


X_FIRST = (0, 1, 2, 3)
Z_FIRST = (0, 2, 3, 1)
ORDERS = (X_FIRST, X_FIRST, X_FIRST, Z_FIRST)


class Halving:
    def __init__(self, place, seq, order, grads, share, scratch):
        self.place, self.seq, self.order, self.grads, self.share = place, seq, order, grads, share
        self.landing, self.send, self.recv, self.far_send, self.far_recv = scratch

    @staticmethod
    def scratch(seq, width=ROWS):
        far = len(far_bits(seq))
        return [pltpu.VMEM((720 + 48 * far, width), BF)] + [pltpu.SemaphoreType.DMA((max(4, far),)) for _ in range(4)]

    def copy(self, k):
        size = HALVES[k]
        bit = self.order[k]
        start = self.place.low(self.order, k) + (1 - self.place.bit(bit)) * size
        return remote(
            self.grads.at[pl.ds(pl.multiple_of(start, 48), size), :],
            self.landing.at[pl.ds(LANDING[k], size), :],
            self.send.at[k],
            self.recv.at[k],
            self.place.partner(bit),
        )

    def add(self, k):
        start = self.place.low(self.order, k + 1)

        def step(i, _):
            rows = pl.ds(pl.multiple_of(start + i * 48, 48), 48)
            arrived = self.landing[pl.ds(pl.multiple_of(LANDING[k] + i * 48, 48), 48), :]
            value = (self.grads[rows, :].astype(F32) + arrived.astype(F32)).astype(BF)
            if k < 3:
                self.grads[rows, :] = value
            else:
                self.share[...] = value
            return 0

        lax.fori_loop(0, HALVES[k] // 48, step, 0)

    def step(self, k):
        if k > 0:
            self.copy(k - 1).wait_recv()
            self.add(k - 1)
        if k < 4:
            self.copy(k).start()
            return
        for n, bit in enumerate(far_bits(self.seq)):
            landing = self.landing.at[pl.ds(720 + 48 * n, 48), :]
            copy = remote(self.share, landing, self.far_send.at[n], self.far_recv.at[n], self.place.partner(bit))
            copy.start()
            copy.wait()
            self.share[...] = (self.share[...].astype(F32) + landing[...].astype(F32)).astype(BF)

    def finish(self):
        for k in range(4):
            self.copy(k).wait_send()


class Doubling:
    def __init__(self, place, order, share, result, sems):
        self.place, self.order, self.share, self.result = place, order, share, result
        self.send, self.recv = sems

    @staticmethod
    def scratch():
        return [pltpu.SemaphoreType.DMA((4,)) for _ in range(2)]

    def copy(self, k):
        rows = pl.ds(pl.multiple_of(self.place.low(self.order, k + 1), 48), HALVES[k])
        view = self.result.at[rows, :]
        return remote(view, view, self.send.at[k], self.recv.at[k], self.place.partner(self.order[k]))

    def step(self, k):
        if k == 0:
            self.result[pl.ds(pl.multiple_of(self.place.low(self.order, 4), 48), 48), :] = self.share[...]
        else:
            self.copy(4 - k).wait_recv()
        if k < 4:
            self.copy(3 - k).start()

    def finish(self):
        for k in range(4):
            self.copy(k).wait_send()


def run_at(slot, work, times):
    for k, time in enumerate(times):

        @pl.when(slot == time)
        def _():
            work.step(k)


def sem_shapes(times):
    return [pltpu.SemaphoreType.DMA((c,)) for _ in range(times) for c in COPIES]


VMEM = pl.BlockSpec(memory_space=pltpu.VMEM)
ANY = pl.BlockSpec(memory_space=pl.ANY)
ORDER = tuple(int(f"{c:04b}"[::-1], 2) for c in range(16))


FOLDED = [((4, 512, 128), BF), ((2, 512, 128), BF), ((1, 512, 128), BF), ((1, 256, 128), BF)]
WHOLE = [((n, SEGMENT, 128), BF) for n in (4, 2, 1, 1)]
FOLDED_HOME = [((LOCAL, n, 128), BF) for n in (256, 128, 64, 32)]


def attention_forward(queries, key_values, w_output):
    shapes = [
        ((LOCAL, SEGMENT, 128), F32),
        ((SEGMENT, LOCAL * HEAD_DIM), BF),
        (w_output.shape, BF),
    ] + FOLDED + WHOLE
    scratch = (
        [((LOCAL, SEGMENT, 128), F32)] + FOLDED + WHOLE
        + [((LOCAL, SEGMENT, 128), F32)] * 2 + FOLDED + FOLDED_HOME + [((LOCAL * 128, LOCAL * HEAD_DIM), BF)]
    )
    return pl.pallas_call(
        forward_kernel,
        out_shape=[jax.ShapeDtypeStruct(*s) for s in shapes],
        in_specs=[VMEM, VMEM, ANY],
        out_specs=[ANY, VMEM, ANY] + [ANY] * 8,
        scratch_shapes=[pltpu.VMEM(*s) for s in scratch] + sem_shapes(6)
        + [pltpu.SemaphoreType.DMA] * 2 + [pltpu.SemaphoreType.DMA((8,))] * 2,
        compiler_params=pltpu.CompilerParams(
            collective_id=0, has_side_effects=True, vmem_limit_bytes=56 * 2**20
        ),
        name="attention_forward",
    )(queries, key_values, w_output)


def pair_grads(q, d, kv_at, put):
    d = unfold(d, 64)
    lane = lanes(d.shape)
    top = jnp.where((lane >= 52) & (lane < 55), pltpu.roll(d, 64, 1), 0.0)
    queries = (unfold(q, 0) + top).astype(BF)
    grads = d.astype(BF)
    total = None
    for half in range(2):
        kv = kv_at(half)
        probs = jnp.exp2(dot(kv, queries, NT))
        grad_scores = (probs * dot(kv, grads, NT)).astype(BF)
        put(half, dot(grad_scores, queries, NN) + dot(probs.astype(BF), grads, NN))
        part = dot(kv, grad_scores, TN)
        total = part if total is None else total + part
    return total.T


def backward_kernel(
    q_ref, kv_ref, shares_in, fin_in, do_in, ffn_ref, s1, s2, s3, s4, s5, s6, s7, s8,
    g_ref, sum_ref, grads, ffn_other,
    q1, q2, q3, q4, kv1, kv2, kv3, kv4, fin_ref, do_ref, d0, d1, d2, d3, d4, total_q, total_kv, gq1, gq2, gq3, gq4, gkv1, gkv2, gkv3, gkv4,
    rq1, rq2, rq3, rq4, rkv1, rkv2, rkv3, rkv4, places_q, places_kv, *sems
):
    place = Place()
    trades = [None] + [Trade(place, b) for b in (1, 2, 3, 4)]
    qs, kvs, dd = (None, q1, q2, q3, q4), (None, kv1, kv2, kv3, kv4), (None, d1, d2, d3, d4)
    gqs, gkvs = (None, gq1, gq2, gq3, gq4), (None, gkv1, gkv2, gkv3, gkv4)
    rqs, rkvs = (None, rq1, rq2, rq3, rq4), (None, rkv1, rkv2, rkv3, rkv4)
    *sems, ffn_send, ffn_recv, fin_sem, do_sem, saved_sem = sems
    go_send, go_recv, q_send, q_recv, kv_send, kv_recv = ((None,) + tuple(sems[4 * k : 4 * k + 4]) for k in range(6))
    doubling = [
        Doubling(place, ORDERS[c], shares_in.at[c], grads.at[c], sems[24 + 2 * c : 26 + 2 * c]) for c in range(4)
    ]

    def reduce_at(slot):
        run_at(slot, doubling[0], (0, 2, 4, 7, 9))
        run_at(slot, doubling[1], (1, 3, 7, 10, 12))
        run_at(slot, doubling[2], (2, 4, 10, 13, 14))
        run_at(slot, doubling[3], (3, 5, 8, 11, 13))

    ffn_copy = remote(ffn_ref, ffn_other, ffn_send, ffn_recv, (place.me, 1 - place.y))

    def go(b, action):
        trade = trades[b]

        def body(j, t, k, device):
            action(
                remote(
                    d0.at[trade.head(j, t), trade.folded_rows(j, t), :],
                    dd[b].at[t, trade.folded_slot(trade.i), :],
                    go_send[b].at[k],
                    go_recv[b].at[k],
                    device,
                )
            )

        trade.each(body)

    def back(b, action):
        trade = trades[b]

        def body(j, t, k, device):
            for copy in (
                remote(
                    gqs[b].at[t, trade.folded_slot(j), :],
                    trade.home(rqs[b], trade.i, t),
                    q_send[b].at[k],
                    q_recv[b].at[k],
                    device,
                ),
                remote(
                    gkvs[b].at[t, trade.slot(j), :],
                    trade.whole_home(rkvs[b], trade.i, t),
                    kv_send[b].at[k],
                    kv_recv[b].at[k],
                    device,
                ),
            ):
                action(copy)

        trade.each(body)

    start, arrived, sent = (lambda c: c.start()), (lambda c: c.wait_recv()), (lambda c: c.wait_send())

    do_copy = pltpu.make_async_copy(do_in, do_ref, do_sem)
    do_copy.start()

    def fin_copy(h):
        return pltpu.make_async_copy(fin_in.at[h], fin_ref.at[h], fin_sem.at[h])

    for h in range(LOCAL):
        fin_copy(h).start()
    saved = [
        pltpu.make_async_copy(src, dst, saved_sem.at[k])
        for k, (src, dst) in enumerate(
            zip((s1, s2, s3, s4, s5, s6, s7, s8), (q1, q2, q3, q4, kv1, kv2, kv3, kv4))
        )
    ]
    for copy in saved:
        copy.start()
    do_copy.wait()

    def prepare(h, _):
        fin_copy(h).wait()
        fin = fin_ref[h]
        lane = lanes(fin.shape)
        grad = (do_ref[:, ds(h * 128, 128)].astype(F32) * fin[:, 112:113]).astype(BF).astype(F32)
        delta = -jnp.sum(grad * fin, axis=1, keepdims=True)
        high = delta.astype(BF).astype(F32)
        tile = jnp.where(lane < 112, grad, jnp.where(lane < 116, 0.0, jnp.where(lane < 119, fin, 0.0)))
        tile = jnp.where(lane == 112, high, jnp.where(lane == 113, delta - high, tile))
        d0[h] = fold(tile, 64).astype(BF)
        return 0

    lax.fori_loop(0, LOCAL, prepare, 0)
    place.greet(16, True)
    for b in (1, 4, 3, 2):
        go(b, start)
    ffn_copy.start()
    for b in (1, 2, 3, 4):
        trade = trades[b]
        for t in range(trade.tiles):
            head = trade.head(trade.i, t)
            dd[b][t, trade.folded_slot(trade.i), :] = d0[head, trade.folded_rows(trade.i, t), :]
    places_q[...] = placing(0, 0, LOCAL * HEAD_DIM).astype(BF)
    places_kv[...] = (
        placing(0, 0, 2 * LOCAL * HEAD_DIM) + placing(64, LOCAL * HEAD_DIM, 2 * LOCAL * HEAD_DIM)
    ).astype(BF)

    def local_head(h, _):
        def put(half, grad):
            total_kv[h, pl.ds(half * 512, 512), :] = grad

        total_q[h] = pair_grads(q_ref[h], d0[h], lambda half: kv_ref[h, pl.ds(half * 512, 512), :], put)
        reduce_at(jnp.where(h < 4, h, h + 8))
        return 0

    def tile_grads(b, t):
        def put(half, grad):
            gkvs[b][t, pl.ds(half * 512, 512), :] = grad.astype(BF)

        grad = pair_grads(qs[b][t], dd[b][t], lambda half: kvs[b][t, pl.ds(half * 512, 512), :], put)
        gqs[b][t] = fold(jnp.where(lanes(grad.shape) < 64, grad, 0.0), 0).astype(BF)

    def branch(b, slot):
        trade = trades[b]
        saved[b - 1].wait()
        saved[b + 3].wait()
        go(b, arrived)

        def tile(t, _):
            tile_grads(b, t)
            reduce_at(slot + t)
            return 0

        lax.fori_loop(0, trade.tiles, tile, 0)
        back(b, start)
        for t in range(trade.tiles):
            trade.home(rqs[b], trade.i, t)[...] = gqs[b][t, trade.folded_slot(trade.i), :]
            trade.whole_home(rkvs[b], trade.i, t)[...] = gkvs[b][t, trade.slot(trade.i), :]

    lax.fori_loop(0, 4, local_head, 0)
    branch(1, 4)
    branch(4, 8)
    branch(3, 9)
    branch(2, 10)
    lax.fori_loop(4, 8, local_head, 0)

    for b in (1, 4, 3, 2):
        back(b, arrived)

    def finish(h, _):
        for b in (1, 2, 3, 4):
            rows = pl.ds(place.start(b, h), SEGMENT // 2**b)
            total_q[h, rows, :] += unfold(rqs[b][h], 0)
            if b < 4:
                total_kv[h, rows, :] += rkvs[b][h].astype(F32)
            else:
                total_kv[h, rows, :] += rkv4[0, h].astype(F32) + rkv4[1, h].astype(F32)
        return 0

    lax.fori_loop(0, LOCAL, finish, 0)
    sum_ref[...] = jnp.zeros_like(sum_ref)

    def compact(i, _):
        rows = ds(i * 256, 256)
        key_lane = lanes((256, 128)) < 64
        wide_q, wide_kv = [], []
        for h in range(LOCAL):
            factor = jnp.where(kv_ref[h, rows, 48:49].astype(F32) >= 0.0, 1.0 / LOG2E, 0.0)
            wide_q.append((total_q[h, rows, :] * SCALE).astype(BF))
            wide_kv.append((total_kv[h, rows, :] * jnp.where(key_lane, factor, 1.0)).astype(BF))
        grad_q = dot(jnp.concatenate(wide_q, axis=1), places_q[...], NN)
        grad_kv = dot(jnp.concatenate(wide_kv, axis=1), places_kv[...], NN)
        for k, grad in enumerate((grad_q, grad_kv[:, :384], grad_kv[:, 384:])):
            g_ref[k, rows, :] = grad.astype(BF)
            sum_ref[k] += row_sums(grad)
        return 0

    lax.fori_loop(0, 4, compact, 0)

    for b in (4, 3, 2, 1):
        go(b, sent)
        back(b, sent)
    for work in doubling:
        work.finish()
    ffn_copy.wait()


def attention_backward(queries, key_values, saved, fin, grad_out, shares, ffn_part):
    width = LOCAL * HEAD_DIM
    shapes = [
        ((3, SEGMENT, width), BF),
        ((3, 8, width), F32),
        ((4, ROWS, ROWS), BF),
        (ffn_part.shape, BF),
    ]
    scratch = (
        FOLDED
        + WHOLE
        + [((LOCAL, SEGMENT, 128), F32), ((SEGMENT, LOCAL * 128), BF)]
        + [((LOCAL, 512, 128), BF)]
        + FOLDED
        + [((LOCAL, SEGMENT, 128), F32)] * 2
        + FOLDED
        + WHOLE
        + FOLDED_HOME
        + [((LOCAL, n, 128), BF) for n in (512, 256, 128)]
        + [((2, LOCAL, 64, 128), BF), ((LOCAL * 128, width), BF), ((LOCAL * 128, 2 * width), BF)]
    )
    return pl.pallas_call(
        backward_kernel,
        out_shape=[jax.ShapeDtypeStruct(*s) for s in shapes],
        in_specs=[VMEM] * 3 + [ANY] * 11,
        out_specs=[VMEM, VMEM, VMEM, ANY],
        scratch_shapes=[pltpu.VMEM(*s) for s in scratch]
        + sem_shapes(6)
        + [shape for _ in range(4) for shape in Doubling.scratch()]
        + [pltpu.SemaphoreType.DMA] * 2
        + [pltpu.SemaphoreType.DMA((LOCAL,)), pltpu.SemaphoreType.DMA, pltpu.SemaphoreType.DMA((8,))],
        compiler_params=pltpu.CompilerParams(
            collective_id=1, has_side_effects=True, vmem_limit_bytes=60 * 2**20
        ),
        name="attention_backward",
    )(queries, key_values, shares, fin, grad_out, ffn_part, *saved)


CHUNK = 128


def put_spread(planes, block, value):
    for t in range(value.shape[1] // 128):
        planes[t, pl.ds(ORDER[block], 64, stride=16), :] = value[:, t * 128 : (t + 1) * 128]


def to_planes(value_ref, planes):
    def step(i, _):
        rows = ds(i * 128, 128)
        for t in range(planes.shape[0]):
            planes[t, rows, :] = value_ref[rows, pl.ds(t * 128, 128)].astype(F32)
        return 0

    lax.fori_loop(0, SEGMENT // 128, step, 0)


def take_spread(planes, block):
    return jnp.concatenate(
        [planes[t, pl.ds(ORDER[block], 64, stride=16), :] for t in range(planes.shape[0])], axis=1
    )


def first_kernel(
    tokens_ref, valid_ref, vec_ref, w_ref, bias_ref, q_ref, kv_ref, normed_ref, tokens_out, stats_ref, planes
):
    to_planes(tokens_ref, planes)
    for b in range(16):
        tokens_out[pl.ds(b * 64, 64), :] = take_spread(planes, b).astype(BF)
    count = jnp.sum(valid_ref[...])

    def chunk(n, _):
        rows = ds(n * 256, 256)
        x = tokens_out[rows, :].astype(F32)
        mean, rs = norm_stats(x)
        stats_ref[0, rows, :], stats_ref[1, rows, :] = mean, rs
        normed = ((x - widen(mean, x)) * widen(rs, x) * vector(vec_ref, 0) + vector(vec_ref, 1)).astype(BF)
        normed_ref[rows, :] = normed
        queries = (dot(normed, w_ref[0], NN) + bias_ref[0:1, :]) * (SCALE * LOG2E)
        keys = dot(normed, w_ref[1], NN)
        values = dot(normed, w_ref[2], NN) + bias_ref[1:2, :]
        at = n * 256 + lax.broadcasted_iota(jnp.int32, (256, 128), 0)
        live = (at % 64 * 16 + reversed_bits(at // 64, 4)) < count
        lane = lanes((256, 128))
        padding = jnp.where(live, 0.0, masked_score)
        ones = ((lane >= 52) & (lane < 55)) | (lane == 112) | (lane == 113)
        for h in range(LOCAL):
            query = jnp.where(lane == 48, 1.0, take_48(queries, h, 0))
            q_ref[h, ds(n * 128, 128), :] = fold(query, 0).astype(BF)
            key = jnp.where(live, take_48(keys, h, 0), 0.0) + take_48(values, h, 64)
            kv_ref[h, rows, :] = jnp.where(ones, 1.0, jnp.where(lane == 48, padding, key)).astype(BF)
        return 0

    lax.fori_loop(0, 4, chunk, 0)


def first_part(tokens, valid, vectors, w_project, bias):
    width = tokens.shape[1]
    shapes = [
        ((LOCAL, SEGMENT // 2, 128), BF),
        ((LOCAL, SEGMENT, 128), BF),
        (tokens.shape, BF),
        (tokens.shape, BF),
        ((2, SEGMENT, 128), F32),
    ]
    return pl.pallas_call(
        first_kernel,
        out_shape=[jax.ShapeDtypeStruct(*s) for s in shapes],
        in_specs=[VMEM] * 5,
        out_specs=[VMEM] * len(shapes),
        scratch_shapes=[pltpu.VMEM((width // 128, SEGMENT, 128), F32)],
        compiler_params=pltpu.CompilerParams(vmem_limit_bytes=56 * 2**20),
        name="first_part",
    )(tokens, valid, vectors, w_project, bias)


GELU_C = math.sqrt(2 / math.pi)


def middle_kernel(
    seq, att_ref, w_out_ref, vec_ref, w_out_other, tokens_in, cot_ref, w_expand_in, w_reduce_in,
    middle_out, gm_out, do_out, ffn_hbm, shares_ref, grads_o, small_ref,
    middle_ref, gm_ref, do_ref, ffn, tokens_ref, w_expand, w_reduce, att, w_out, stats, normed, active, grad_expand, cot_low, part, other, gm_low, grads, sums, sums_e, planes, cot,
    att_send, att_recv, part_send, part_recv, fill_sem, out_sem, *sems
):
    place = Place()
    y = place.y
    peer = (place.me, 1 - y)
    b_output, gain, shift = (vector(vec_ref, k) for k in (2, 3, 4))
    n = len(sems) // 4
    halving = [
        Halving(place, seq, ORDERS[c], grads.at[c], shares_ref.at[c], sems[c * n : c * n + n]) for c in range(4)
    ]
    chunk, chunks, width = 256, SEGMENT // 256, tokens_ref.shape[1]

    def att_copy(n):
        rows = ds(n * chunk, chunk)
        return remote(att_ref.at[rows, :], att.at[y, rows, :], att_send.at[n], att_recv.at[n], peer)

    def part_copy(n):
        rows = ds(n * chunk, chunk)
        return remote(part.at[rows, :], other.at[rows, :], part_send.at[n], part_recv.at[n], peer)

    fills = [
        pltpu.make_async_copy(cot_ref.at[:, pl.ds(t * 128, 128)], planes.at[t], fill_sem.at[t])
        for t in range(width // 128)
    ]
    loads = [
        pltpu.make_async_copy(src, dst, fill_sem.at[6 + k])
        for k, (src, dst) in enumerate(
            (
                (w_out_other, w_out.at[1 - y]),
                (tokens_in, tokens_ref),
                (w_expand_in, w_expand),
                (w_reduce_in, w_reduce),
            )
        )
    ]
    for fill in fills + loads:
        fill.start()
    ffn_out = pltpu.make_async_copy(ffn, ffn_hbm, out_sem.at[12])

    def out(k, n):
        rows = ds(n * chunk, chunk)
        src, dst = ((middle_ref, middle_out), (gm_ref, gm_out), (do_ref, do_out))[k]
        return pltpu.make_async_copy(src.at[rows, :], dst.at[rows, :], out_sem.at[k * 4 + n])

    place.greet(seq, True)
    for n in range(chunks):
        att_copy(n).start()
    att[y] = att_ref[...]
    w_out[y] = w_out_ref[...]
    sums[...] = jnp.zeros_like(sums)
    sums_e[...] = jnp.zeros_like(sums_e)
    for fill in fills + loads:
        fill.wait()
    for b in range(16):
        cot[pl.ds(b * 64, 64), :] = take_spread(planes, b)

    def ahead(n, _):
        rows = ds(n * chunk, chunk)
        grad_out = cot[rows, :]
        sums[0:8] += row_sums(grad_out)
        low = grad_out.astype(BF)
        cot_low[rows, :] = low
        att_copy(n).wait_recv()
        branch = dot(att[0, rows, :], w_out[0], NN) + dot(att[1, rows, :], w_out[1], NN)
        middle = tokens_ref[rows, :].astype(F32) + (branch + b_output)
        middle_ref[rows, :] = middle
        out(0, n).start()
        mean, rs = norm_stats(middle)
        stats[0, rows, :], stats[1, rows, :] = mean, rs
        norm = ((middle - widen(mean, middle)) * widen(rs, middle) * gain + shift).astype(BF)
        normed[rows, :] = norm
        value = None
        for k in range(w_expand.shape[1] // width):
            at = pl.ds(k * width, width)
            expand = dot(norm, w_expand[:, at], NN) + vector(vec_ref, 5 + k)
            square = expand * expand
            bent = jnp.tanh(GELU_C * expand * (1.0 + 0.044715 * square))
            gate = 0.5 * (1.0 + bent)
            active[rows, at] = (expand * gate).astype(BF)
            slope = gate + (0.5 * GELU_C) * expand * (1.0 - bent * bent) * (1.0 + (3 * 0.044715) * square)
            grad = dot(low, w_reduce[at, :], NT) * slope
            sums_e[:, at] += row_sums(grad)
            grad = grad.astype(BF)
            grad_expand[rows, at] = grad
            piece = dot(grad, w_expand[:, at], NT)
            value = piece if value is None else value + piece
        part[rows, :] = value.astype(BF)
        part_copy(n).start()
        return 0

    lax.fori_loop(0, chunks, ahead, 0)

    def behind(n, _):
        rows = ds(n * chunk, chunk)
        part_copy(n).wait_recv()
        grad = part[rows, :].astype(F32) + other[rows, :].astype(F32)
        rs = widen(stats[1, rows, :], grad)
        xhat = (middle_ref[rows, :] - widen(stats[0, rows, :], grad)) * rs
        sums[8:16] += row_sums(grad * xhat)
        sums[16:24] += row_sums(grad)
        gm = cot[rows, :] + norm_back(grad, xhat, rs, gain)
        gm_ref[rows, :] = gm
        sums[24:32] += row_sums(gm)
        low = gm.astype(BF)
        gm_low[rows, :] = low
        grad_att = dot(low, w_out_ref[...], NT)
        for h in range(LOCAL):
            do_ref[rows, pl.ds(h * 128, 128)] = take_48(grad_att, h, 64).astype(BF)
        out(1, n).start()
        out(2, n).start()
        return 0

    for k in range(2):
        grads[k] = dot(active[:, pl.ds(k * width, width)], cot_low[...], TN).astype(BF)
        halving[k].step(0)
    for k in range(2):
        grads[2 + k] = dot(normed[...], grad_expand[:, pl.ds(k * width, width)], TN).astype(BF)
        halving[2 + k].step(0)
        halving[k].step(1)
    halving[3].step(1)
    ffn[...] = dot(active[...], w_reduce[...], NN).astype(BF)
    ffn_out.start()
    halving[2].step(1)
    behind(0, 0)
    behind(1, 0)
    halving[0].step(2)
    halving[1].step(2)
    halving[3].step(2)
    behind(2, 0)
    halving[2].step(2)
    halving[0].step(3)
    halving[1].step(3)
    halving[3].step(3)
    behind(3, 0)
    halving[0].step(4)
    halving[1].step(4)
    halving[2].step(3)
    halving[3].step(4)
    for k in range(2):
        at = pl.ds(k * (width // 2), width // 2)
        grads_o[pl.ds(k * 384, 384), :] = dot(att_ref[...], gm_low[:, at], TN).astype(BF)
    halving[2].step(4)
    put_vector(small_ref, 0, sums[24:32])
    put_vector(small_ref, 6, sums[8:16])
    put_vector(small_ref, 12, sums[16:24])
    put_vector(small_ref, 18, sums_e[...])
    put_vector(small_ref, 30, sums[0:8])
    small_ref[36:48, :] = jnp.zeros((12, 128), F32)
    for n in range(chunks):
        att_copy(n).wait_send()
        part_copy(n).wait_send()
        for k in range(3):
            out(k, n).wait()
    ffn_out.wait()
    for work in halving:
        work.finish()


def middle_part(attended, w_output, w_out_other, tokens, cot, w_expand, w_reduce, vectors):
    seq = lax.axis_size("seq")
    rows, width = tokens.shape
    hidden = w_expand.shape[1]
    shapes = [
        ((rows, width), F32),
        ((rows, width), F32),
        ((rows, LOCAL * 128), BF),
        ((rows, width), BF),
        ((4, 48, ROWS), BF),
        ((ROWS, ROWS // 2), BF),
        ((48, 128), F32),
    ]
    scratch = shapes[:4] + [
        (tokens.shape, BF),
        (w_expand.shape, BF),
        (w_reduce.shape, BF),
        ((2,) + attended.shape, BF),
        ((2,) + w_output.shape, BF),
        ((2, rows, 128), F32),
        ((rows, width), BF),
        ((rows, hidden), BF),
        ((rows, hidden), BF),
        ((rows, width), BF),
        ((rows, width), BF),
        ((rows, width), BF),
        ((rows, width), BF),
        ((4, ROWS, ROWS), BF),
        ((32, width), F32),
        ((8, hidden), F32),
        ((width // 128, rows, 128), F32),
        ((rows, width), F32),
    ]
    return pl.pallas_call(
        functools.partial(middle_kernel, seq),
        out_shape=[jax.ShapeDtypeStruct(*s) for s in shapes],
        in_specs=[VMEM] * 3 + [ANY] * 5,
        out_specs=[ANY] * 4 + [VMEM] * 3,
        scratch_shapes=[pltpu.VMEM(*s) for s in scratch]
        + [pltpu.SemaphoreType.DMA((4,)) for _ in range(4)]
        + [pltpu.SemaphoreType.DMA((10,)), pltpu.SemaphoreType.DMA((13,))]
        + [shape for _ in range(4) for shape in Halving.scratch(seq)],
        compiler_params=pltpu.CompilerParams(
            collective_id=3, has_side_effects=True, vmem_limit_bytes=60 * 2**20
        ),
        name="middle_part",
    )(attended, w_output, vectors, w_out_other, tokens, cot, w_expand, w_reduce)


def last_kernel(
    seq, g_ref, w_ref, normed_ref, w_out_ref, small_in, sum_ref, vec_ref,
    tokens_in, gm_in, stats_in, middle_in, ffn_in, ffn_other_in,
    planes, layer_out, grads_ref, early_ref, late_ref,
    layer_planes, tokens_ref, gm_ref, stats, middle_ref, ffn_ref, ffn_other,
    grads, shares, part, other, small_ref, early_in, late, late_in, sums, layer_sem, fill_sem,
    part_send, part_recv, early_send, early_recv, late_send, late_recv, far_send, far_recv, *sems
):
    place = Place()
    orders = (X_FIRST, X_FIRST, Z_FIRST, X_FIRST)
    halving = [Halving(place, seq, orders[c], grads.at[c], shares.at[c], sems[5 * c : 5 * c + 5]) for c in range(4)]
    gathers = [
        Doubling(place, orders[c], shares.at[c], grads_ref.at[c], sems[20 + 2 * c : 22 + 2 * c]) for c in range(4)
    ]
    i = place.member(4)
    chunks = SEGMENT // CHUNK
    fills = [
        pltpu.make_async_copy(src, dst, fill_sem.at[k])
        for k, (src, dst) in enumerate(
            zip(
                (tokens_in, gm_in, stats_in, middle_in, ffn_in, ffn_other_in),
                (tokens_ref, gm_ref, stats, middle_ref, ffn_ref, ffn_other),
            )
        )
    ]
    for fill in fills:
        fill.start()
    put_vector(small_ref, 0, sum_ref[0])
    put_vector(small_ref, 3, sum_ref[2])
    small_ref[6:48, :] = small_in[0:42, :]

    def to_all(src, landing, send, recv):
        def each(action):
            def step(d, _):
                action(remote(src, landing.at[i], send.at[d - 1], recv.at[d - 1], place.device(4, (i + d) % 16)))
                return 0

            lax.fori_loop(1, 16, step, 0)

        return each

    def total_of(src, landing):
        def step(j, value):
            return value + landing[j]

        landing[i] = src[...]
        return lax.fori_loop(1, 16, step, landing[0])

    def far_total(result, n):
        for k, bit in enumerate(far_bits(seq)):
            landing = (early_in, late_in)[n].at[16 + k]
            copy = remote(result, landing, far_send.at[n * 8 + k], far_recv.at[n * 8 + k], place.partner(bit))
            copy.start()
            copy.wait()
            result[...] = result[...] + landing[...]

    def exchange(n):
        rows = ds(n * CHUNK, CHUNK)
        return remote(
            part.at[rows, :], other.at[rows, :], part_send.at[n], part_recv.at[n], (place.me, 1 - place.y)
        )

    def partial(n, _):
        rows = ds(n * CHUNK, CHUNK)
        value = dot(g_ref[0, rows, :], w_ref[0], NT)
        value += dot(g_ref[1, rows, :], w_ref[1], NT)
        value += dot(g_ref[2, rows, :], w_ref[2], NT)
        part[rows, :] = value.astype(BF)
        exchange(n).start()
        return 0

    def grad_w(k):
        grads[k] = dot(normed_ref[...], g_ref[k], TN).astype(BF)

    def layer(b):
        rows = pl.ds(b * 64, 64)
        total = ffn_ref[rows, :].astype(F32) + ffn_other[rows, :].astype(F32)
        put_spread(layer_planes, b, middle_ref[rows, :] + total + vector(vec_ref, 7))

    place.greet(seq, True)
    grads[3] = w_out_ref[...]
    halving[3].step(0)
    lax.fori_loop(0, 2, partial, 0)
    halving[3].step(1)
    for k in range(3):
        grad_w(k)
        halving[k].step(0)
    halving[0].step(1)
    halving[2].step(1)
    lax.fori_loop(2, chunks, partial, 0)
    early_all = to_all(small_ref, early_in, early_send, early_recv)
    halving[3].step(2)
    halving[1].step(1)
    sums[...] = jnp.zeros_like(sums)
    early_all(lambda copy: copy.start())
    h0, h1, h2, h3, g0, g1, g2, g3 = halving + gathers
    after = (
        ((h0, 2), (h3, 3)),
        ((h1, 2), (h3, 4), (g3, 0), (h2, 2)),
        ((h0, 3), (g3, 1)),
        ((h0, 4), (g0, 0), (h1, 3), (g3, 2), (h2, 3)),
        ((h1, 4), (g1, 0), (h2, 4), (g2, 0), (g0, 1)),
        ((g3, 3), (g0, 2), (g1, 1), (g2, 1)),
        ((g3, 4), (g1, 2), (g2, 2)),
        ((g0, 3),),
    )
    for fill in fills:
        fill.wait()
    for n in range(chunks):
        for b in range(n * 2, n * 2 + 2):
            layer(b)
        exchange(n).wait_recv()
        rows = pl.ds(n * CHUNK, CHUNK)
        grad = part[rows, :].astype(F32) + other[rows, :].astype(F32)
        rs = widen(stats[1, rows, :], grad)
        xhat = (tokens_ref[rows, :].astype(F32) - widen(stats[0, rows, :], grad)) * rs
        sums[0:8] += row_sums(grad * xhat)
        sums[8:16] += row_sums(grad)
        grad = gm_ref[rows, :] + norm_back(grad, xhat, rs, vector(vec_ref, 0))
        for k in range(CHUNK // 64):
            put_spread(planes, n * (CHUNK // 64) + k, grad[k * 64 : (k + 1) * 64])
        for work, k in after[n]:
            work.step(k)
    for k in range(2):
        put_vector(late, k * 8, sums[k * 8 : k * 8 + 8])
        late[pl.ds(k * 8 + 6, 2), :] = jnp.zeros((2, 128), F32)
    layer_copy = pltpu.make_async_copy(layer_planes, layer_out, layer_sem)
    layer_copy.start()
    late_all = to_all(late, late_in, late_send, late_recv)
    late_all(lambda copy: copy.start())
    g1.step(3)
    g2.step(3)
    early_all(lambda copy: copy.wait_recv())
    early_ref[...] = total_of(small_ref, early_in)
    far_total(early_ref, 0)
    late_all(lambda copy: copy.wait_recv())
    late_ref[...] = total_of(late, late_in)
    far_total(late_ref, 1)
    for work in (g0, g1, g2):
        work.step(4)

    def sent(n, _):
        exchange(n).wait_send()
        return 0

    lax.fori_loop(0, chunks, sent, 0)
    early_all(lambda copy: copy.wait_send())
    late_all(lambda copy: copy.wait_send())
    for work in halving + gathers:
        work.finish()
    layer_copy.wait()


def last_part(g, w_project, normed, grad_w_out, small, g_sums, vectors, *late_inputs):
    seq = lax.axis_size("seq")
    far = len(far_bits(seq))
    width = normed.shape[1]
    shapes = [
        ((width // 128, SEGMENT, 128), F32),
        ((width // 128, SEGMENT, 128), F32),
        ((4, ROWS, ROWS // 2), BF),
        (small.shape, F32),
        ((16, 128), F32),
    ]
    scratch = shapes[:1] + [(a.shape, a.dtype) for a in late_inputs] + [
        ((4, ROWS, ROWS // 2), BF),
        ((4, 48, ROWS // 2), BF),
        (normed.shape, BF),
        (normed.shape, BF),
        (small.shape, F32),
        ((16 + far,) + small.shape, F32),
        ((16, 128), F32),
        ((16 + far, 16, 128), F32),
        ((16, width), F32),
    ]
    chunks = SEGMENT // CHUNK
    counts = (len(late_inputs), chunks, chunks, 15, 15, 15, 15, 16, 16)
    return pl.pallas_call(
        functools.partial(last_kernel, seq),
        out_shape=[jax.ShapeDtypeStruct(*s) for s in shapes],
        in_specs=[VMEM] * 7 + [ANY] * len(late_inputs),
        out_specs=[VMEM, ANY, VMEM, VMEM, VMEM],
        scratch_shapes=[pltpu.VMEM(*s) for s in scratch]
        + [pltpu.SemaphoreType.DMA]
        + [pltpu.SemaphoreType.DMA((c,)) for c in counts]
        + [shape for _ in range(4) for shape in Halving.scratch(seq, ROWS // 2)]
        + [shape for _ in range(4) for shape in Doubling.scratch()],
        compiler_params=pltpu.CompilerParams(
            collective_id=2, has_side_effects=True, vmem_limit_bytes=58 * 2**20
        ),
        name="last_part",
    )(g, w_project, normed, grad_w_out, small, g_sums, vectors, *late_inputs)


def out_kernel(r_ref, e_ref, p_ref, o_ref, o2_ref, t_ref, l_ref, r_out, e_out, p_out, o_out, t_out, l_out):
    half = ROWS // 2
    r_out[...] = r_ref[...].astype(F32)
    for k in range(2):
        e_out[:, k * ROWS : (k + 1) * ROWS] = e_ref[k].astype(F32)
    p_out[...] = p_ref[...].astype(F32)
    o_out[:, :half] = o_ref[0].astype(F32)
    o_out[:, half:] = o2_ref[0].astype(F32)
    for k in range(t_ref.shape[0]):
        at = slice(k * 128, (k + 1) * 128)
        t_out[:, at] = t_ref[k]
        l_out[:, at] = l_ref[k]


def results(grads, grads_p, planes, layer_planes):
    half = ROWS // 2
    n = 8
    rows, width = planes.shape[1], planes.shape[0] * 128
    plane_spec = pl.BlockSpec((planes.shape[0], rows // n, 128), lambda i: (0, i, 0))
    row_spec = pl.BlockSpec((rows // n, width), lambda i: (i, 0))
    return pl.pallas_call(
        out_kernel,
        grid=(n,),
        out_shape=[
            jax.ShapeDtypeStruct((2 * ROWS, ROWS), F32),
            jax.ShapeDtypeStruct((ROWS, 2 * ROWS), F32),
            jax.ShapeDtypeStruct((3, ROWS, half), F32),
            jax.ShapeDtypeStruct((half, ROWS), F32),
            jax.ShapeDtypeStruct((rows, width), F32),
            jax.ShapeDtypeStruct((rows, width), F32),
        ],
        in_specs=[
            pl.BlockSpec((2 * ROWS // n, ROWS), lambda i: (i, 0)),
            pl.BlockSpec((2, ROWS // n, ROWS), lambda i: (1, i, 0)),
            pl.BlockSpec((3, ROWS // n, half), lambda i: (0, i, 0)),
            pl.BlockSpec((1, half // n, half), lambda i: (3, i, 0)),
            pl.BlockSpec((1, half // n, half), lambda i: (3, n + i, 0)),
            plane_spec,
            plane_spec,
        ],
        out_specs=[
            pl.BlockSpec((2 * ROWS // n, ROWS), lambda i: (i, 0)),
            pl.BlockSpec((ROWS // n, 2 * ROWS), lambda i: (i, 0)),
            pl.BlockSpec((3, ROWS // n, half), lambda i: (0, i, 0)),
            pl.BlockSpec((half // n, ROWS), lambda i: (i, 0)),
            row_spec,
            row_spec,
        ],
        name="results",
    )(grads.reshape(-1, ROWS), grads, grads_p, grads_p, grads_p, planes, layer_planes)


def body(
    tokens,
    cotangent,
    valid_tiles,
    gain_first,
    shift_first,
    w_project,
    bias_project,
    w_output,
    bias_output,
    gain_second,
    shift_second,
    w_expand,
    bias_expand,
    w_reduce,
    bias_reduce,
):
    width = tokens.shape[1]
    half = width // 2
    w_project = w_project.transpose(1, 0, 2)
    vectors = jnp.concatenate(
        [gain_first, shift_first, bias_output, gain_second, shift_second, bias_expand, bias_reduce]
    ).reshape(-1, 128)
    queries, key_values, normed, tokens, stats = first_part(
        tokens, valid_tiles.reshape(8, -1), vectors, w_project, bias_project
    )
    fin, attended, w_out_other, *saved = attention_forward(queries, key_values, w_output)
    middle, grad_middle, grad_attended, ffn_part, shares, grads_o, small = middle_part(
        attended, w_output, w_out_other, tokens, cotangent, w_expand, w_reduce, vectors
    )
    g, g_sums, grads, ffn_other = attention_backward(
        queries, key_values, saved, fin, grad_attended, shares, ffn_part
    )
    planes, layer_planes, grads_p, small, late = last_part(
        g, w_project, normed, grads_o, small, g_sums, vectors,
        tokens, grad_middle, stats, middle, ffn_part, ffn_other,
    )
    small = small.reshape(-1)
    late = late.reshape(2, 8 * 128)[:, :width]
    parts = [small[k * width : (k + 1) * width] for k in range(7)]
    grad_w_reduce, grad_w_expand, grad_w_project, grad_w_output, grad_tokens, layer_out = results(
        grads, grads_p, planes, layer_planes
    )
    return (
        layer_out,
        grad_tokens,
        late[0],
        late[1],
        grad_w_project.transpose(1, 0, 2),
        parts[0].reshape(2, half),
        grad_w_output,
        parts[1],
        parts[2],
        parts[3],
        grad_w_expand,
        small[4 * width : 6 * width],
        grad_w_reduce,
        parts[6],
    )


def solution(mesh):
    in_specs = (
        P("seq", None),
        P("seq", None),
        P("seq"),
        P(),
        P(),
        P(None, None, "heads"),
        P(None, "heads"),
        P("heads", None),
        P(),
        P(),
        P(),
        P(None, "heads"),
        P("heads"),
        P("heads", None),
        P(),
    )
    out_specs = (
        P("seq", None),
        P("seq", None),
        P(),
        P(),
        P(None, None, "heads"),
        P(None, "heads"),
        P("heads", None),
        P(),
        P(),
        P(),
        P(None, "heads"),
        P("heads"),
        P("heads", None),
        P(),
    )
    return jax.shard_map(body, mesh=mesh, in_specs=in_specs, out_specs=out_specs, check_vma=False)
```

```python
import functools
import math

import jax
import jax.numpy as jnp
from jax import lax
from jax.experimental import pallas as pl
from jax.experimental.pallas import tpu as pltpu
from jax.sharding import PartitionSpec as P

HEADS = 16
HEAD_DIM = 48
SEGMENT = 1024
BRANCHES = 5
LOCAL = 8

MESH = pl.DeviceIdType.MESH
BF = jnp.bfloat16
F32 = jnp.float32
NT = (((1,), (1,)), ((), ()))
TN = (((0,), (0,)), ((), ()))
NN = (((1,), (0,)), ((), ()))

masked_score = -1000000000.0
layer_eps = 1e-05
SCALE = HEAD_DIM ** (-0.5)
LOG2E = math.log2(math.e)


def dot(a, b, dims):
    return lax.dot_general(a, b, dims, preferred_element_type=F32)


def lanes(shape):
    return lax.broadcasted_iota(jnp.int32, shape, len(shape) - 1)


def reversed_bits(value, bits):
    out = value * 0
    for k in range(bits):
        out = out * 2 + (value // 2**k) % 2
    return out


def split3(value):
    high = value.astype(BF).astype(F32)
    rest = value - high
    middle = rest.astype(BF).astype(F32)
    return high, middle, rest - middle


def take_48(value, head, at):
    tile, off = head * 48 // 128, head * 48 % 128
    shift = (at - off) % 128
    turn = lambda k: pltpu.roll(value[:, k * 128 : (k + 1) * 128], shift, 1) if shift else value[:, k * 128 : (k + 1) * 128]
    out = turn(tile)
    lane = lanes(out.shape)
    if off + 48 > 128:
        out = jnp.where(lane < at + 128 - off, out, turn(tile + 1))
    return jnp.where((lane >= at) & (lane < at + 48), out, 0.0)


def fold(value, at):
    pairs = value.reshape(value.shape[0] // 32, 2, 16, 128)
    even, odd = pairs[:, 0].reshape(-1, 128), pairs[:, 1].reshape(-1, 128)
    return pltpu.roll(even, 64, 1) + odd if at else even + pltpu.roll(odd, 64, 1)


def unfold(value, at):
    value = value.astype(F32)
    keep = lanes(value.shape) >= 64 if at else lanes(value.shape) < 64
    turned = jnp.where(keep, pltpu.roll(value, 64, 1), 0.0)
    straight = jnp.where(keep, value, 0.0)
    even, odd = (turned, straight) if at else (straight, turned)
    pairs = [part.reshape(-1, 1, 16, 128) for part in (even, odd)]
    return jnp.concatenate(pairs, axis=1).reshape(-1, 128)


def placing(source, target, columns):
    row = lax.broadcasted_iota(jnp.int32, (LOCAL * 128, columns), 0)
    column = lax.broadcasted_iota(jnp.int32, (LOCAL * 128, columns), 1)
    lane = row % 128 - source
    hit = (lane >= 0) & (lane < HEAD_DIM) & (column == target + row // 128 * HEAD_DIM + lane)
    return jnp.where(hit, 1.0, 0.0)


def row_mean(value):
    ones = jnp.ones((value.shape[1], 128), BF)
    high = value.astype(BF)
    low = (value - high.astype(F32)).astype(BF)
    return (dot(high, ones, NN) + dot(low, ones, NN)) * (1.0 / value.shape[1])


def vector(ref, k=0, width=768):
    n = width // 128
    return jnp.concatenate([ref[k * n + t : k * n + t + 1, :] for t in range(n)], axis=1)


def widen(tile, like):
    return jnp.concatenate([tile] * (like.shape[1] // 128), axis=1)


def row_sums(value):
    return jnp.sum(value.reshape(value.shape[0] // 8, 8, value.shape[1]), axis=0)


def put_vector(rows, first, partial):
    value = jnp.sum(partial, axis=0, keepdims=True)
    for t in range(value.shape[1] // 128):
        rows[pl.ds(first + t, 1), :] = value[:, t * 128 : (t + 1) * 128]


def norm_stats(value):
    mean = row_mean(value)
    centered = value - widen(mean, value)
    rs = lax.rsqrt(row_mean(centered * centered) + layer_eps)
    return mean, rs


def norm_back(grad, xhat, rs, gain):
    grad = grad * gain
    return rs * (grad - widen(row_mean(grad), grad) - xhat * widen(row_mean(grad * xhat), grad))


class Place:
    def __init__(self):
        self.me = lax.axis_index("seq")
        self.y = lax.axis_index("heads")

    def member(self, b):
        return self.me % 2**b

    def device(self, b, j):
        return (self.me // 2**b * 2**b + j, self.y)

    def start(self, b, head):
        stride = 2**b
        place = (self.y * LOCAL + head) % stride
        return pl.multiple_of(reversed_bits(place, b) * (SEGMENT // stride), SEGMENT // stride)

    def bit(self, k):
        return self.me // 2**k % 2

    def partner(self, k):
        return (self.me + 2**k * (1 - 2 * self.bit(k)), self.y)

    def low(self, order, k):
        return sum((self.bit(order[i]) * HALVES[i] for i in range(k)), self.me * 0)

    def greet(self, seq=16, other=False):
        barrier = pltpu.get_barrier_semaphore()
        i = self.member(4)
        count = 15
        if other:
            pl.semaphore_signal(barrier, inc=1, device_id=(self.me, 1 - self.y), device_id_type=MESH)
            count += 1
        for k in far_bits(seq):
            pl.semaphore_signal(barrier, inc=1, device_id=self.partner(k), device_id_type=MESH)
            count += 1

        def signal(d, _):
            pl.semaphore_signal(barrier, inc=1, device_id=self.device(4, (i + d) % 16), device_id_type=MESH)
            return 0

        lax.fori_loop(1, 16, signal, 0)
        pl.semaphore_wait(barrier, count)


def remote(src, dst, send, recv, device):
    return pltpu.make_async_remote_copy(
        src_ref=src, dst_ref=dst, send_sem=send, recv_sem=recv, device_id=device, device_id_type=MESH
    )


def ds(start, size):
    return pl.ds(pl.multiple_of(start, size), size)


def attend(queries, kv):
    scores = dot(unfold(queries, 0).astype(BF), kv, NT)
    top = jnp.max(scores, axis=1, keepdims=True)
    raised = jnp.exp2(scores - top).astype(BF)
    return dot(raised, kv, NN), top


def packed(out, top):
    lane = lanes(out.shape)
    total = out[:, 112:113]
    tile = jnp.where(lane == 112, 1.0, jnp.where(lane >= 64, out * (1.0 / total), 0.0))
    for k, piece in enumerate(split3(top) + split3(total)):
        tile = jnp.where(lane == 114 + k, piece, tile)
    return fold(tile, 64).astype(BF)


class Trade:
    def __init__(self, place, b):
        self.place, self.b = place, b
        self.n = SEGMENT // 2**b
        self.tiles = max(LOCAL // 2**b, 1)
        self.folded = self.n // 2 if b < 4 else 16
        self.i = place.member(b)

    def head(self, j, t):
        return j * self.tiles + t if self.b < 4 else j // 2

    def rows(self, j, t):
        return pl.ds(self.place.start(self.b, self.head(j, t)), self.n)

    def folded_rows(self, j, t):
        start = self.place.start(self.b, self.head(j, t)) // 2
        if self.b == 4:
            start = start + j % 2 * 16
        return pl.ds(pl.multiple_of(start, 16), self.folded)

    def slot(self, j):
        return ds(j * self.n, self.n)

    def folded_slot(self, j):
        return ds(j * self.folded, self.folded)

    def home(self, ref, j, t):
        ref = ref.at[self.head(j, t)]
        return ref if self.b < 4 else ref.at[ds(j % 2 * 16, 16), :]

    def whole_home(self, ref, j, t):
        return ref.at[self.head(j, t)] if self.b < 4 else ref.at[j % 2, j // 2]

    def each(self, body):
        def step(d, _):
            j = (self.i + d) % 2**self.b
            for t in range(self.tiles):
                body(j, t, (d - 1) * self.tiles + t, self.place.device(self.b, j))
            return 0

        lax.fori_loop(1, 2**self.b, step, 0)


COPIES = (4, 6, 7, 15)


def forward_kernel(
    q_ref, kv_ref, w_out_ref, fin_out, att_ref, w_out_other, s1, s2, s3, s4, s5, s6, s7, s8,
    fin_ref, q1, q2, q3, q4, kv1, kv2, kv3, kv4, acc, tops, o1, o2, o3, o4, r1, r2, r3, r4, places, *sems
):
    place = Place()
    trades = [None] + [Trade(place, b) for b in (1, 2, 3, 4)]
    qs, kvs = (None, q1, q2, q3, q4), (None, kv1, kv2, kv3, kv4)
    os, rs = (None, o1, o2, o3, o4), (None, r1, r2, r3, r4)
    *sems, w_send, w_recv, fin_sem, saved_sem = sems
    q_send, q_recv, kv_send, kv_recv, back_send, back_recv = (
        (None,) + tuple(sems[4 * k : 4 * k + 4]) for k in range(6)
    )

    def go(b, action):
        trade = trades[b]

        def body(j, t, k, device):
            for copy in (
                remote(
                    q_ref.at[trade.head(j, t), trade.folded_rows(j, t), :],
                    qs[b].at[t, trade.folded_slot(trade.i), :],
                    q_send[b].at[k],
                    q_recv[b].at[k],
                    device,
                ),
                remote(
                    kv_ref.at[trade.head(j, t), trade.rows(j, t), :],
                    kvs[b].at[t, trade.slot(trade.i), :],
                    kv_send[b].at[k],
                    kv_recv[b].at[k],
                    device,
                ),
            ):
                action(copy)

        trade.each(body)

    def back(b, action):
        trade = trades[b]

        def body(j, t, k, device):
            action(
                remote(
                    os[b].at[t, trade.folded_slot(j), :],
                    trade.home(rs[b], trade.i, t),
                    back_send[b].at[k],
                    back_recv[b].at[k],
                    device,
                )
            )

        trade.each(body)

    def fin_copy(h):
        return pltpu.make_async_copy(fin_ref.at[h], fin_out.at[h], fin_sem.at[h])

    saved = [
        pltpu.make_async_copy(src, dst, saved_sem.at[k])
        for k, (src, dst) in enumerate(
            zip((q1, q2, q3, q4, kv1, kv2, kv3, kv4), (s1, s2, s3, s4, s5, s6, s7, s8))
        )
    ]
    start, arrived, sent = (lambda c: c.start()), (lambda c: c.wait_recv()), (lambda c: c.wait_send())
    place.greet(16, True)
    for b in (1, 4, 3, 2):
        go(b, start)
    w_copy = remote(w_out_ref, w_out_other, w_send, w_recv, (place.me, 1 - place.y))
    w_copy.start()

    for b in (1, 2, 3, 4):
        trade = trades[b]
        for t in range(trade.tiles):
            head = trade.head(trade.i, t)
            qs[b][t, trade.folded_slot(trade.i), :] = q_ref[head, trade.folded_rows(trade.i, t), :]
            kvs[b][t, trade.slot(trade.i), :] = kv_ref[head, trade.rows(trade.i, t), :]
    places[...] = placing(64, 0, LOCAL * HEAD_DIM).astype(BF)

    def local_heads(k, _):
        for h in (k * 2, k * 2 + 1):
            for half in range(2):
                rows = pl.ds(half * 512, 512)
                out, top = attend(q_ref[h, pl.ds(half * 256, 256), :], kv_ref[h])
                acc[h, rows, :] = out
                tops[h, rows, :] = jnp.broadcast_to(top, out.shape)
        return 0

    def half_tile(b, t, half):
        rows = pl.ds(half * 256, 256)
        os[b][t, rows, :] = packed(*attend(qs[b][t, rows, :], kvs[b][t]))

    def send_back(b):
        trade = trades[b]
        back(b, start)
        saved[b - 1].start()
        saved[b + 3].start()
        for t in range(trade.tiles):
            trade.home(rs[b], trade.i, t)[...] = os[b][t, trade.folded_slot(trade.i), :]

    lax.fori_loop(0, 2, local_heads, 0)
    go(1, arrived)

    def tiles_1(k, _):
        for t in (k * 2, k * 2 + 1):
            for half in range(2):
                half_tile(1, t, half)
        return 0

    lax.fori_loop(0, 2, tiles_1, 0)
    send_back(1)
    go(4, arrived)
    go(3, arrived)
    half_tile(4, 0, 0)
    half_tile(3, 0, 0)
    half_tile(3, 0, 1)
    send_back(4)
    send_back(3)
    go(2, arrived)
    for t in range(2):
        for half in range(2):
            half_tile(2, t, half)
    send_back(2)
    lax.fori_loop(2, 4, local_heads, 0)

    for b in (1, 4, 3, 2):
        back(b, arrived)

    row = lax.broadcasted_iota(jnp.int32, (128, 256), 0)
    column = lax.broadcasted_iota(jnp.int32, (128, 256), 1)
    first = jnp.where(column < 128, 114, 117)
    picks = jnp.where((row >= first) & (row < first + 3), 1.0, 0.0).astype(BF)

    def merge_head(h, _):
        for b in (1, 2, 3, 4):
            n = SEGMENT // 2**b
            rows = pl.ds(place.start(b, h), n)
            part = unfold(rs[b][h], 64)
            stats = dot(part.astype(BF), picks, NN)
            top = jnp.maximum(tops[h, rows, :], stats[:, 0:128])
            keep = jnp.exp2(tops[h, rows, :] - top)
            gain = jnp.exp2(stats[:, 0:128] - top) * stats[:, 128:256]
            acc[h, rows, :] = acc[h, rows, :] * keep + part * gain
            tops[h, rows, :] = top
        out = acc[h]
        lane = lanes(out.shape)
        inverse = 1.0 / out[:, 112:113]
        out = jnp.where((lane >= 64) & (lane < 112), out * inverse, jnp.where(lane == 112, inverse, 0.0))
        for k, piece in enumerate(split3(-tops[h])):
            out = jnp.where(lane == 116 + k, piece, out)
        fin_ref[h] = out
        fin_copy(h).start()
        return 0

    lax.fori_loop(0, LOCAL, merge_head, 0)

    def compact(n, _):
        rows = ds(n * 256, 256)
        wide = jnp.concatenate([fin_ref[h, rows, :].astype(BF) for h in range(LOCAL)], axis=1)
        att_ref[rows, :] = dot(wide, places[...], NN).astype(BF)
        return 0

    lax.fori_loop(0, 4, compact, 0)

    for b in (4, 3, 2, 1):
        go(b, sent)
        back(b, sent)
    w_copy.wait()
    for copy in saved:
        copy.wait()
    for h in range(LOCAL):
        fin_copy(h).wait()


ROWS = 768
HALVES = (384, 192, 96, 48)
LANDING = (0, 384, 576, 672, 720)


def far_bits(seq):
    return list(range(4, seq.bit_length() - 1))


X_FIRST = (0, 1, 2, 3)
Z_FIRST = (0, 2, 3, 1)
ORDERS = (X_FIRST, X_FIRST, X_FIRST, Z_FIRST)


class Halving:
    def __init__(self, place, seq, order, grads, share, scratch):
        self.place, self.seq, self.order, self.grads, self.share = place, seq, order, grads, share
        self.landing, self.send, self.recv, self.far_send, self.far_recv = scratch

    @staticmethod
    def scratch(seq, width=ROWS):
        far = len(far_bits(seq))
        return [pltpu.VMEM((720 + 48 * far, width), BF)] + [pltpu.SemaphoreType.DMA((max(4, far),)) for _ in range(4)]

    def copy(self, k):
        size = HALVES[k]
        bit = self.order[k]
        start = self.place.low(self.order, k) + (1 - self.place.bit(bit)) * size
        return remote(
            self.grads.at[pl.ds(pl.multiple_of(start, 48), size), :],
            self.landing.at[pl.ds(LANDING[k], size), :],
            self.send.at[k],
            self.recv.at[k],
            self.place.partner(bit),
        )

    def add(self, k):
        start = self.place.low(self.order, k + 1)

        def step(i, _):
            rows = pl.ds(pl.multiple_of(start + i * 48, 48), 48)
            arrived = self.landing[pl.ds(pl.multiple_of(LANDING[k] + i * 48, 48), 48), :]
            value = (self.grads[rows, :].astype(F32) + arrived.astype(F32)).astype(BF)
            if k < 3:
                self.grads[rows, :] = value
            else:
                self.share[...] = value
            return 0

        lax.fori_loop(0, HALVES[k] // 48, step, 0)

    def step(self, k):
        if k > 0:
            self.copy(k - 1).wait_recv()
            self.add(k - 1)
        if k < 4:
            self.copy(k).start()
            return
        for n, bit in enumerate(far_bits(self.seq)):
            landing = self.landing.at[pl.ds(720 + 48 * n, 48), :]
            copy = remote(self.share, landing, self.far_send.at[n], self.far_recv.at[n], self.place.partner(bit))
            copy.start()
            copy.wait()
            self.share[...] = (self.share[...].astype(F32) + landing[...].astype(F32)).astype(BF)

    def finish(self):
        for k in range(4):
            self.copy(k).wait_send()


class Doubling:
    def __init__(self, place, order, share, result, sems):
        self.place, self.order, self.share, self.result = place, order, share, result
        self.send, self.recv = sems

    @staticmethod
    def scratch():
        return [pltpu.SemaphoreType.DMA((4,)) for _ in range(2)]

    def copy(self, k):
        rows = pl.ds(pl.multiple_of(self.place.low(self.order, k + 1), 48), HALVES[k])
        view = self.result.at[rows, :]
        return remote(view, view, self.send.at[k], self.recv.at[k], self.place.partner(self.order[k]))

    def step(self, k):
        if k == 0:
            self.result[pl.ds(pl.multiple_of(self.place.low(self.order, 4), 48), 48), :] = self.share[...]
        else:
            self.copy(4 - k).wait_recv()
        if k < 4:
            self.copy(3 - k).start()

    def finish(self):
        for k in range(4):
            self.copy(k).wait_send()


def run_at(slot, work, times):
    for k, time in enumerate(times):

        @pl.when(slot == time)
        def _():
            work.step(k)


def sem_shapes(times):
    return [pltpu.SemaphoreType.DMA((c,)) for _ in range(times) for c in COPIES]


VMEM = pl.BlockSpec(memory_space=pltpu.VMEM)
ANY = pl.BlockSpec(memory_space=pl.ANY)
ORDER = tuple(int(f"{c:04b}"[::-1], 2) for c in range(16))


FOLDED = [((4, 512, 128), BF), ((2, 512, 128), BF), ((1, 512, 128), BF), ((1, 256, 128), BF)]
WHOLE = [((n, SEGMENT, 128), BF) for n in (4, 2, 1, 1)]
FOLDED_HOME = [((LOCAL, n, 128), BF) for n in (256, 128, 64, 32)]


def attention_forward(queries, key_values, w_output):
    shapes = [
        ((LOCAL, SEGMENT, 128), F32),
        ((SEGMENT, LOCAL * HEAD_DIM), BF),
        (w_output.shape, BF),
    ] + FOLDED + WHOLE
    scratch = (
        [((LOCAL, SEGMENT, 128), F32)] + FOLDED + WHOLE
        + [((LOCAL, SEGMENT, 128), F32)] * 2 + FOLDED + FOLDED_HOME + [((LOCAL * 128, LOCAL * HEAD_DIM), BF)]
    )
    return pl.pallas_call(
        forward_kernel,
        out_shape=[jax.ShapeDtypeStruct(*s) for s in shapes],
        in_specs=[VMEM, VMEM, ANY],
        out_specs=[ANY, VMEM, ANY] + [ANY] * 8,
        scratch_shapes=[pltpu.VMEM(*s) for s in scratch] + sem_shapes(6)
        + [pltpu.SemaphoreType.DMA] * 2 + [pltpu.SemaphoreType.DMA((8,))] * 2,
        compiler_params=pltpu.CompilerParams(
            collective_id=0, has_side_effects=True, vmem_limit_bytes=56 * 2**20
        ),
        name="attention_forward",
    )(queries, key_values, w_output)


def pair_grads(q, d, kv_at, put):
    d = unfold(d, 64)
    lane = lanes(d.shape)
    top = jnp.where((lane >= 52) & (lane < 55), pltpu.roll(d, 64, 1), 0.0)
    queries = (unfold(q, 0) + top).astype(BF)
    grads = d.astype(BF)
    total = None
    for half in range(2):
        kv = kv_at(half)
        probs = jnp.exp2(dot(kv, queries, NT))
        grad_scores = (probs * dot(kv, grads, NT)).astype(BF)
        put(half, dot(grad_scores, queries, NN) + dot(probs.astype(BF), grads, NN))
        part = dot(kv, grad_scores, TN)
        total = part if total is None else total + part
    return total.T


def backward_kernel(
    q_ref, kv_ref, shares_in, fin_in, do_in, ffn_ref, s1, s2, s3, s4, s5, s6, s7, s8,
    g_ref, sum_ref, grads, ffn_other,
    q1, q2, q3, q4, kv1, kv2, kv3, kv4, fin_ref, do_ref, d0, d1, d2, d3, d4, total_q, total_kv, gq1, gq2, gq3, gq4, gkv1, gkv2, gkv3, gkv4,
    rq1, rq2, rq3, rq4, rkv1, rkv2, rkv3, rkv4, places_q, places_kv, *sems
):
    place = Place()
    trades = [None] + [Trade(place, b) for b in (1, 2, 3, 4)]
    qs, kvs, dd = (None, q1, q2, q3, q4), (None, kv1, kv2, kv3, kv4), (None, d1, d2, d3, d4)
    gqs, gkvs = (None, gq1, gq2, gq3, gq4), (None, gkv1, gkv2, gkv3, gkv4)
    rqs, rkvs = (None, rq1, rq2, rq3, rq4), (None, rkv1, rkv2, rkv3, rkv4)
    *sems, ffn_send, ffn_recv, fin_sem, do_sem, saved_sem = sems
    go_send, go_recv, q_send, q_recv, kv_send, kv_recv = ((None,) + tuple(sems[4 * k : 4 * k + 4]) for k in range(6))
    doubling = [
        Doubling(place, ORDERS[c], shares_in.at[c], grads.at[c], sems[24 + 2 * c : 26 + 2 * c]) for c in range(4)
    ]

    def reduce_at(slot):
        run_at(slot, doubling[0], (0, 2, 4, 7, 9))
        run_at(slot, doubling[1], (1, 3, 7, 10, 12))
        run_at(slot, doubling[2], (2, 4, 10, 13, 14))
        run_at(slot, doubling[3], (3, 5, 8, 11, 13))

    ffn_copy = remote(ffn_ref, ffn_other, ffn_send, ffn_recv, (place.me, 1 - place.y))

    def go(b, action):
        trade = trades[b]

        def body(j, t, k, device):
            action(
                remote(
                    d0.at[trade.head(j, t), trade.folded_rows(j, t), :],
                    dd[b].at[t, trade.folded_slot(trade.i), :],
                    go_send[b].at[k],
                    go_recv[b].at[k],
                    device,
                )
            )

        trade.each(body)

    def back(b, action):
        trade = trades[b]

        def body(j, t, k, device):
            for copy in (
                remote(
                    gqs[b].at[t, trade.folded_slot(j), :],
                    trade.home(rqs[b], trade.i, t),
                    q_send[b].at[k],
                    q_recv[b].at[k],
                    device,
                ),
                remote(
                    gkvs[b].at[t, trade.slot(j), :],
                    trade.whole_home(rkvs[b], trade.i, t),
                    kv_send[b].at[k],
                    kv_recv[b].at[k],
                    device,
                ),
            ):
                action(copy)

        trade.each(body)

    start, arrived, sent = (lambda c: c.start()), (lambda c: c.wait_recv()), (lambda c: c.wait_send())

    do_copy = pltpu.make_async_copy(do_in, do_ref, do_sem)
    do_copy.start()

    def fin_copy(h):
        return pltpu.make_async_copy(fin_in.at[h], fin_ref.at[h], fin_sem.at[h])

    for h in range(LOCAL):
        fin_copy(h).start()
    saved = [
        pltpu.make_async_copy(src, dst, saved_sem.at[k])
        for k, (src, dst) in enumerate(
            zip((s1, s2, s3, s4, s5, s6, s7, s8), (q1, q2, q3, q4, kv1, kv2, kv3, kv4))
        )
    ]
    for copy in saved:
        copy.start()
    do_copy.wait()

    def prepare(h, _):
        fin_copy(h).wait()
        fin = fin_ref[h]
        lane = lanes(fin.shape)
        grad = (do_ref[:, ds(h * 128, 128)].astype(F32) * fin[:, 112:113]).astype(BF).astype(F32)
        delta = -jnp.sum(grad * fin, axis=1, keepdims=True)
        high = delta.astype(BF).astype(F32)
        tile = jnp.where(lane < 112, grad, jnp.where(lane < 116, 0.0, jnp.where(lane < 119, fin, 0.0)))
        tile = jnp.where(lane == 112, high, jnp.where(lane == 113, delta - high, tile))
        d0[h] = fold(tile, 64).astype(BF)
        return 0

    lax.fori_loop(0, LOCAL, prepare, 0)
    place.greet(16, True)
    for b in (1, 4, 3, 2):
        go(b, start)
    ffn_copy.start()
    for b in (1, 2, 3, 4):
        trade = trades[b]
        for t in range(trade.tiles):
            head = trade.head(trade.i, t)
            dd[b][t, trade.folded_slot(trade.i), :] = d0[head, trade.folded_rows(trade.i, t), :]
    places_q[...] = placing(0, 0, LOCAL * HEAD_DIM).astype(BF)
    places_kv[...] = (
        placing(0, 0, 2 * LOCAL * HEAD_DIM) + placing(64, LOCAL * HEAD_DIM, 2 * LOCAL * HEAD_DIM)
    ).astype(BF)

    def local_head(h, _):
        def put(half, grad):
            total_kv[h, pl.ds(half * 512, 512), :] = grad

        total_q[h] = pair_grads(q_ref[h], d0[h], lambda half: kv_ref[h, pl.ds(half * 512, 512), :], put)
        reduce_at(jnp.where(h < 4, h, h + 8))
        return 0

    def tile_grads(b, t):
        def put(half, grad):
            gkvs[b][t, pl.ds(half * 512, 512), :] = grad.astype(BF)

        grad = pair_grads(qs[b][t], dd[b][t], lambda half: kvs[b][t, pl.ds(half * 512, 512), :], put)
        gqs[b][t] = fold(jnp.where(lanes(grad.shape) < 64, grad, 0.0), 0).astype(BF)

    def branch(b, slot):
        trade = trades[b]
        saved[b - 1].wait()
        saved[b + 3].wait()
        go(b, arrived)

        def tile(t, _):
            tile_grads(b, t)
            reduce_at(slot + t)
            return 0

        lax.fori_loop(0, trade.tiles, tile, 0)
        back(b, start)
        for t in range(trade.tiles):
            trade.home(rqs[b], trade.i, t)[...] = gqs[b][t, trade.folded_slot(trade.i), :]
            trade.whole_home(rkvs[b], trade.i, t)[...] = gkvs[b][t, trade.slot(trade.i), :]

    lax.fori_loop(0, 4, local_head, 0)
    branch(1, 4)
    branch(4, 8)
    branch(3, 9)
    branch(2, 10)
    lax.fori_loop(4, 8, local_head, 0)

    for b in (1, 4, 3, 2):
        back(b, arrived)

    def finish(h, _):
        for b in (1, 2, 3, 4):
            rows = pl.ds(place.start(b, h), SEGMENT // 2**b)
            total_q[h, rows, :] += unfold(rqs[b][h], 0)
            if b < 4:
                total_kv[h, rows, :] += rkvs[b][h].astype(F32)
            else:
                total_kv[h, rows, :] += rkv4[0, h].astype(F32) + rkv4[1, h].astype(F32)
        return 0

    lax.fori_loop(0, LOCAL, finish, 0)
    sum_ref[...] = jnp.zeros_like(sum_ref)

    def compact(i, _):
        rows = ds(i * 256, 256)
        key_lane = lanes((256, 128)) < 64
        wide_q, wide_kv = [], []
        for h in range(LOCAL):
            factor = jnp.where(kv_ref[h, rows, 48:49].astype(F32) >= 0.0, 1.0 / LOG2E, 0.0)
            wide_q.append((total_q[h, rows, :] * SCALE).astype(BF))
            wide_kv.append((total_kv[h, rows, :] * jnp.where(key_lane, factor, 1.0)).astype(BF))
        grad_q = dot(jnp.concatenate(wide_q, axis=1), places_q[...], NN)
        grad_kv = dot(jnp.concatenate(wide_kv, axis=1), places_kv[...], NN)
        for k, grad in enumerate((grad_q, grad_kv[:, :384], grad_kv[:, 384:])):
            g_ref[k, rows, :] = grad.astype(BF)
            sum_ref[k] += row_sums(grad)
        return 0

    lax.fori_loop(0, 4, compact, 0)

    for b in (4, 3, 2, 1):
        go(b, sent)
        back(b, sent)
    for work in doubling:
        work.finish()
    ffn_copy.wait()


def attention_backward(queries, key_values, saved, fin, grad_out, shares, ffn_part):
    width = LOCAL * HEAD_DIM
    shapes = [
        ((3, SEGMENT, width), BF),
        ((3, 8, width), F32),
        ((4, ROWS, ROWS), BF),
        (ffn_part.shape, BF),
    ]
    scratch = (
        FOLDED
        + WHOLE
        + [((LOCAL, SEGMENT, 128), F32), ((SEGMENT, LOCAL * 128), BF)]
        + [((LOCAL, 512, 128), BF)]
        + FOLDED
        + [((LOCAL, SEGMENT, 128), F32)] * 2
        + FOLDED
        + WHOLE
        + FOLDED_HOME
        + [((LOCAL, n, 128), BF) for n in (512, 256, 128)]
        + [((2, LOCAL, 64, 128), BF), ((LOCAL * 128, width), BF), ((LOCAL * 128, 2 * width), BF)]
    )
    return pl.pallas_call(
        backward_kernel,
        out_shape=[jax.ShapeDtypeStruct(*s) for s in shapes],
        in_specs=[VMEM] * 3 + [ANY] * 11,
        out_specs=[VMEM, VMEM, VMEM, ANY],
        scratch_shapes=[pltpu.VMEM(*s) for s in scratch]
        + sem_shapes(6)
        + [shape for _ in range(4) for shape in Doubling.scratch()]
        + [pltpu.SemaphoreType.DMA] * 2
        + [pltpu.SemaphoreType.DMA((LOCAL,)), pltpu.SemaphoreType.DMA, pltpu.SemaphoreType.DMA((8,))],
        compiler_params=pltpu.CompilerParams(
            collective_id=1, has_side_effects=True, vmem_limit_bytes=60 * 2**20
        ),
        name="attention_backward",
    )(queries, key_values, shares, fin, grad_out, ffn_part, *saved)


CHUNK = 128


def put_spread(planes, block, value):
    for t in range(value.shape[1] // 128):
        planes[t, pl.ds(ORDER[block], 64, stride=16), :] = value[:, t * 128 : (t + 1) * 128]


def to_planes(value_ref, planes):
    def step(i, _):
        rows = ds(i * 128, 128)
        for t in range(planes.shape[0]):
            planes[t, rows, :] = value_ref[rows, pl.ds(t * 128, 128)].astype(F32)
        return 0

    lax.fori_loop(0, SEGMENT // 128, step, 0)


def take_spread(planes, block):
    return jnp.concatenate(
        [planes[t, pl.ds(ORDER[block], 64, stride=16), :] for t in range(planes.shape[0])], axis=1
    )


def first_kernel(
    tokens_ref, valid_ref, gain_ref, shift_ref, w_ref, bias_ref, q_ref, kv_ref, normed_ref, tokens_out, stats_ref, planes
):
    to_planes(tokens_ref, planes)
    for b in range(16):
        tokens_out[pl.ds(b * 64, 64), :] = take_spread(planes, b).astype(BF)
    count = jnp.sum(valid_ref[...])

    def chunk(n, _):
        rows = ds(n * 256, 256)
        x = tokens_out[rows, :].astype(F32)
        mean, rs = norm_stats(x)
        stats_ref[0, rows, :], stats_ref[1, rows, :] = mean, rs
        normed = ((x - widen(mean, x)) * widen(rs, x) * vector(gain_ref) + vector(shift_ref)).astype(BF)
        normed_ref[rows, :] = normed
        queries = (dot(normed, w_ref[0], NN) + bias_ref[0:1, :]) * (SCALE * LOG2E)
        keys = dot(normed, w_ref[1], NN)
        values = dot(normed, w_ref[2], NN) + bias_ref[1:2, :]
        at = n * 256 + lax.broadcasted_iota(jnp.int32, (256, 128), 0)
        live = (at % 64 * 16 + reversed_bits(at // 64, 4)) < count
        lane = lanes((256, 128))
        padding = jnp.where(live, 0.0, masked_score)
        ones = ((lane >= 52) & (lane < 55)) | (lane == 112) | (lane == 113)
        for h in range(LOCAL):
            query = jnp.where(lane == 48, 1.0, take_48(queries, h, 0))
            q_ref[h, ds(n * 128, 128), :] = fold(query, 0).astype(BF)
            key = jnp.where(live, take_48(keys, h, 0), 0.0) + take_48(values, h, 64)
            kv_ref[h, rows, :] = jnp.where(ones, 1.0, jnp.where(lane == 48, padding, key)).astype(BF)
        return 0

    lax.fori_loop(0, 4, chunk, 0)


def first_part(tokens, valid, gain, shift, w_project, bias):
    width = tokens.shape[1]
    shapes = [
        ((LOCAL, SEGMENT // 2, 128), BF),
        ((LOCAL, SEGMENT, 128), BF),
        (tokens.shape, BF),
        (tokens.shape, BF),
        ((2, SEGMENT, 128), F32),
    ]
    return pl.pallas_call(
        first_kernel,
        out_shape=[jax.ShapeDtypeStruct(*s) for s in shapes],
        in_specs=[VMEM] * 6,
        out_specs=[VMEM] * len(shapes),
        scratch_shapes=[pltpu.VMEM((width // 128, SEGMENT, 128), F32)],
        compiler_params=pltpu.CompilerParams(vmem_limit_bytes=56 * 2**20),
        name="first_part",
    )(tokens, valid, gain, shift, w_project, bias)


GELU_C = math.sqrt(2 / math.pi)


def middle_kernel(
    seq, att_ref, w_out_ref, b_out_ref, gain_ref, shift_ref, b_expand_ref, w_out_other, tokens_in, cot_ref, w_expand_in, w_reduce_in,
    middle_out, gm_out, do_out, ffn_hbm, shares_ref, grads_o, small_ref,
    middle_ref, gm_ref, do_ref, ffn, tokens_ref, w_expand, w_reduce, att, w_out, stats, normed, active, grad_expand, cot_low, part, other, gm_low, grads, sums, sums_e, planes, cot,
    att_send, att_recv, part_send, part_recv, fill_sem, out_sem, *sems
):
    place = Place()
    y = place.y
    peer = (place.me, 1 - y)
    b_output, gain, shift = vector(b_out_ref), vector(gain_ref), vector(shift_ref)
    n = len(sems) // 4
    halving = [
        Halving(place, seq, ORDERS[c], grads.at[c], shares_ref.at[c], sems[c * n : c * n + n]) for c in range(4)
    ]
    chunk, chunks, width = 256, SEGMENT // 256, tokens_ref.shape[1]

    def att_copy(n):
        rows = ds(n * chunk, chunk)
        return remote(att_ref.at[rows, :], att.at[y, rows, :], att_send.at[n], att_recv.at[n], peer)

    def part_copy(n):
        rows = ds(n * chunk, chunk)
        return remote(part.at[rows, :], other.at[rows, :], part_send.at[n], part_recv.at[n], peer)

    fills = [
        pltpu.make_async_copy(cot_ref.at[:, pl.ds(t * 128, 128)], planes.at[t], fill_sem.at[t])
        for t in range(width // 128)
    ]
    loads = [
        pltpu.make_async_copy(src, dst, fill_sem.at[6 + k])
        for k, (src, dst) in enumerate(
            (
                (w_out_other, w_out.at[1 - y]),
                (tokens_in, tokens_ref),
                (w_expand_in, w_expand),
                (w_reduce_in, w_reduce),
            )
        )
    ]
    for fill in fills + loads:
        fill.start()
    ffn_out = pltpu.make_async_copy(ffn, ffn_hbm, out_sem.at[12])

    def out(k, n):
        rows = ds(n * chunk, chunk)
        src, dst = ((middle_ref, middle_out), (gm_ref, gm_out), (do_ref, do_out))[k]
        return pltpu.make_async_copy(src.at[rows, :], dst.at[rows, :], out_sem.at[k * 4 + n])

    place.greet(seq, True)
    for n in range(chunks):
        att_copy(n).start()
    att[y] = att_ref[...]
    w_out[y] = w_out_ref[...]
    sums[...] = jnp.zeros_like(sums)
    sums_e[...] = jnp.zeros_like(sums_e)
    for fill in fills + loads:
        fill.wait()
    for b in range(16):
        cot[pl.ds(b * 64, 64), :] = take_spread(planes, b)

    def ahead(n, _):
        rows = ds(n * chunk, chunk)
        grad_out = cot[rows, :]
        sums[0:8] += row_sums(grad_out)
        low = grad_out.astype(BF)
        cot_low[rows, :] = low
        att_copy(n).wait_recv()
        branch = dot(att[0, rows, :], w_out[0], NN) + dot(att[1, rows, :], w_out[1], NN)
        middle = tokens_ref[rows, :].astype(F32) + (branch + b_output)
        middle_ref[rows, :] = middle
        out(0, n).start()
        mean, rs = norm_stats(middle)
        stats[0, rows, :], stats[1, rows, :] = mean, rs
        norm = ((middle - widen(mean, middle)) * widen(rs, middle) * gain + shift).astype(BF)
        normed[rows, :] = norm
        value = None
        for k in range(w_expand.shape[1] // width):
            at = pl.ds(k * width, width)
            expand = dot(norm, w_expand[:, at], NN) + vector(b_expand_ref, k)
            square = expand * expand
            bent = jnp.tanh(GELU_C * expand * (1.0 + 0.044715 * square))
            gate = 0.5 * (1.0 + bent)
            active[rows, at] = (expand * gate).astype(BF)
            slope = gate + (0.5 * GELU_C) * expand * (1.0 - bent * bent) * (1.0 + (3 * 0.044715) * square)
            grad = dot(low, w_reduce[at, :], NT) * slope
            sums_e[:, at] += row_sums(grad)
            grad = grad.astype(BF)
            grad_expand[rows, at] = grad
            piece = dot(grad, w_expand[:, at], NT)
            value = piece if value is None else value + piece
        part[rows, :] = value.astype(BF)
        part_copy(n).start()
        return 0

    lax.fori_loop(0, chunks, ahead, 0)

    def behind(n, _):
        rows = ds(n * chunk, chunk)
        part_copy(n).wait_recv()
        grad = part[rows, :].astype(F32) + other[rows, :].astype(F32)
        rs = widen(stats[1, rows, :], grad)
        xhat = (middle_ref[rows, :] - widen(stats[0, rows, :], grad)) * rs
        sums[8:16] += row_sums(grad * xhat)
        sums[16:24] += row_sums(grad)
        gm = cot[rows, :] + norm_back(grad, xhat, rs, gain)
        gm_ref[rows, :] = gm
        sums[24:32] += row_sums(gm)
        low = gm.astype(BF)
        gm_low[rows, :] = low
        grad_att = dot(low, w_out_ref[...], NT)
        for h in range(LOCAL):
            do_ref[rows, pl.ds(h * 128, 128)] = take_48(grad_att, h, 64).astype(BF)
        out(1, n).start()
        out(2, n).start()
        return 0

    for k in range(2):
        grads[k] = dot(active[:, pl.ds(k * width, width)], cot_low[...], TN).astype(BF)
        halving[k].step(0)
    for k in range(2):
        grads[2 + k] = dot(normed[...], grad_expand[:, pl.ds(k * width, width)], TN).astype(BF)
        halving[2 + k].step(0)
        halving[k].step(1)
    halving[3].step(1)
    ffn[...] = dot(active[...], w_reduce[...], NN).astype(BF)
    ffn_out.start()
    halving[2].step(1)
    behind(0, 0)
    behind(1, 0)
    halving[0].step(2)
    halving[1].step(2)
    halving[3].step(2)
    behind(2, 0)
    halving[2].step(2)
    halving[0].step(3)
    halving[1].step(3)
    halving[3].step(3)
    behind(3, 0)
    halving[0].step(4)
    halving[1].step(4)
    halving[2].step(3)
    halving[3].step(4)
    for k in range(2):
        at = pl.ds(k * (width // 2), width // 2)
        grads_o[pl.ds(k * 384, 384), :] = dot(att_ref[...], gm_low[:, at], TN).astype(BF)
    halving[2].step(4)
    put_vector(small_ref, 0, sums[24:32])
    put_vector(small_ref, 6, sums[8:16])
    put_vector(small_ref, 12, sums[16:24])
    put_vector(small_ref, 18, sums_e[...])
    put_vector(small_ref, 30, sums[0:8])
    small_ref[36:48, :] = jnp.zeros((12, 128), F32)
    for n in range(chunks):
        att_copy(n).wait_send()
        part_copy(n).wait_send()
        for k in range(3):
            out(k, n).wait()
    ffn_out.wait()
    for work in halving:
        work.finish()


def middle_part(attended, w_output, w_out_other, tokens, cot, w_expand, w_reduce, *vectors):
    seq = lax.axis_size("seq")
    rows, width = tokens.shape
    hidden = w_expand.shape[1]
    shapes = [
        ((rows, width), F32),
        ((rows, width), F32),
        ((rows, LOCAL * 128), BF),
        ((rows, width), BF),
        ((4, 48, ROWS), BF),
        ((ROWS, ROWS // 2), BF),
        ((48, 128), F32),
    ]
    scratch = shapes[:4] + [
        (tokens.shape, BF),
        (w_expand.shape, BF),
        (w_reduce.shape, BF),
        ((2,) + attended.shape, BF),
        ((2,) + w_output.shape, BF),
        ((2, rows, 128), F32),
        ((rows, width), BF),
        ((rows, hidden), BF),
        ((rows, hidden), BF),
        ((rows, width), BF),
        ((rows, width), BF),
        ((rows, width), BF),
        ((rows, width), BF),
        ((4, ROWS, ROWS), BF),
        ((32, width), F32),
        ((8, hidden), F32),
        ((width // 128, rows, 128), F32),
        ((rows, width), F32),
    ]
    return pl.pallas_call(
        functools.partial(middle_kernel, seq),
        out_shape=[jax.ShapeDtypeStruct(*s) for s in shapes],
        in_specs=[VMEM] * 6 + [ANY] * 5,
        out_specs=[ANY] * 4 + [VMEM] * 3,
        scratch_shapes=[pltpu.VMEM(*s) for s in scratch]
        + [pltpu.SemaphoreType.DMA((4,)) for _ in range(4)]
        + [pltpu.SemaphoreType.DMA((10,)), pltpu.SemaphoreType.DMA((13,))]
        + [shape for _ in range(4) for shape in Halving.scratch(seq)],
        compiler_params=pltpu.CompilerParams(
            collective_id=3, has_side_effects=True, vmem_limit_bytes=60 * 2**20
        ),
        name="middle_part",
    )(attended, w_output, *vectors, w_out_other, tokens, cot, w_expand, w_reduce)


def last_kernel(
    seq, g_ref, w_ref, normed_ref, w_out_ref, small_in, sum_ref, gain_ref, bias_ref,
    tokens_in, gm_in, stats_in, middle_in, ffn_in, ffn_other_in,
    planes, layer_out, grads_ref, early_ref, late_ref,
    layer_planes, tokens_ref, gm_ref, stats, middle_ref, ffn_ref, ffn_other,
    grads, shares, part, other, small_ref, early_in, late, late_in, sums, layer_sem, fill_sem,
    part_send, part_recv, early_send, early_recv, late_send, late_recv, far_send, far_recv, *sems
):
    place = Place()
    orders = (X_FIRST, X_FIRST, Z_FIRST, X_FIRST)
    halving = [Halving(place, seq, orders[c], grads.at[c], shares.at[c], sems[5 * c : 5 * c + 5]) for c in range(4)]
    gathers = [
        Doubling(place, orders[c], shares.at[c], grads_ref.at[c], sems[20 + 2 * c : 22 + 2 * c]) for c in range(4)
    ]
    i = place.member(4)
    chunks = SEGMENT // CHUNK
    fills = [
        pltpu.make_async_copy(src, dst, fill_sem.at[k])
        for k, (src, dst) in enumerate(
            zip(
                (tokens_in, gm_in, stats_in, middle_in, ffn_in, ffn_other_in),
                (tokens_ref, gm_ref, stats, middle_ref, ffn_ref, ffn_other),
            )
        )
    ]
    for fill in fills:
        fill.start()
    put_vector(small_ref, 0, sum_ref[0])
    put_vector(small_ref, 3, sum_ref[2])
    small_ref[6:48, :] = small_in[0:42, :]

    def to_all(src, landing, send, recv):
        def each(action):
            def step(d, _):
                action(remote(src, landing.at[i], send.at[d - 1], recv.at[d - 1], place.device(4, (i + d) % 16)))
                return 0

            lax.fori_loop(1, 16, step, 0)

        return each

    def total_of(src, landing):
        def step(j, value):
            return value + landing[j]

        landing[i] = src[...]
        return lax.fori_loop(1, 16, step, landing[0])

    def far_total(result, n):
        for k, bit in enumerate(far_bits(seq)):
            landing = (early_in, late_in)[n].at[16 + k]
            copy = remote(result, landing, far_send.at[n * 8 + k], far_recv.at[n * 8 + k], place.partner(bit))
            copy.start()
            copy.wait()
            result[...] = result[...] + landing[...]

    def exchange(n):
        rows = ds(n * CHUNK, CHUNK)
        return remote(
            part.at[rows, :], other.at[rows, :], part_send.at[n], part_recv.at[n], (place.me, 1 - place.y)
        )

    def partial(n, _):
        rows = ds(n * CHUNK, CHUNK)
        value = dot(g_ref[0, rows, :], w_ref[0], NT)
        value += dot(g_ref[1, rows, :], w_ref[1], NT)
        value += dot(g_ref[2, rows, :], w_ref[2], NT)
        part[rows, :] = value.astype(BF)
        exchange(n).start()
        return 0

    def grad_w(k):
        grads[k] = dot(normed_ref[...], g_ref[k], TN).astype(BF)

    def layer(b):
        rows = pl.ds(b * 64, 64)
        total = ffn_ref[rows, :].astype(F32) + ffn_other[rows, :].astype(F32)
        put_spread(layer_planes, b, middle_ref[rows, :] + total + vector(bias_ref))

    place.greet(seq, True)
    grads[3] = w_out_ref[...]
    halving[3].step(0)
    grad_w(0)
    halving[0].step(0)
    grad_w(1)
    halving[1].step(0)
    halving[3].step(1)
    grad_w(2)
    halving[2].step(0)
    lax.fori_loop(0, 2, partial, 0)
    halving[0].step(1)
    halving[2].step(1)
    lax.fori_loop(2, chunks, partial, 0)
    halving[1].step(1)
    early_all = to_all(small_ref, early_in, early_send, early_recv)
    halving[3].step(2)
    sums[...] = jnp.zeros_like(sums)
    h0, h1, h2, h3, g0, g1, g2, g3 = halving + gathers
    h0.step(2)
    early_all(lambda copy: copy.start())
    after = (
        ((h2, 2), (h1, 2), (h3, 3)),
        ((h0, 3), (h3, 4), (g3, 0), (h2, 3)),
        ((h1, 3), (h0, 4), (g0, 0), (g3, 1)),
        ((h2, 4), (g2, 0), (h1, 4), (g1, 0), (g0, 1), (g3, 2)),
        ((g2, 1), (g1, 1), (g0, 2)),
        ((g3, 3), (g1, 2), (g2, 2)),
        ((g0, 3), (g3, 4)),
        (),
    )
    for fill in fills:
        fill.wait()
    for n in range(chunks):
        for b in range(n * 2, n * 2 + 2):
            layer(b)
        exchange(n).wait_recv()
        rows = pl.ds(n * CHUNK, CHUNK)
        grad = part[rows, :].astype(F32) + other[rows, :].astype(F32)
        rs = widen(stats[1, rows, :], grad)
        xhat = (tokens_ref[rows, :].astype(F32) - widen(stats[0, rows, :], grad)) * rs
        sums[0:8] += row_sums(grad * xhat)
        sums[8:16] += row_sums(grad)
        grad = gm_ref[rows, :] + norm_back(grad, xhat, rs, vector(gain_ref))
        for k in range(CHUNK // 64):
            put_spread(planes, n * (CHUNK // 64) + k, grad[k * 64 : (k + 1) * 64])
        for work, k in after[n]:
            work.step(k)
    for k in range(2):
        put_vector(late, k * 8, sums[k * 8 : k * 8 + 8])
        late[pl.ds(k * 8 + 6, 2), :] = jnp.zeros((2, 128), F32)
    layer_copy = pltpu.make_async_copy(layer_planes, layer_out, layer_sem)
    layer_copy.start()
    late_all = to_all(late, late_in, late_send, late_recv)
    late_all(lambda copy: copy.start())
    g1.step(3)
    g2.step(3)
    early_all(lambda copy: copy.wait_recv())
    early_ref[...] = total_of(small_ref, early_in)
    far_total(early_ref, 0)
    late_all(lambda copy: copy.wait_recv())
    late_ref[...] = total_of(late, late_in)
    far_total(late_ref, 1)
    for work in (g0, g1, g2):
        work.step(4)

    def sent(n, _):
        exchange(n).wait_send()
        return 0

    lax.fori_loop(0, chunks, sent, 0)
    early_all(lambda copy: copy.wait_send())
    late_all(lambda copy: copy.wait_send())
    for work in halving + gathers:
        work.finish()
    layer_copy.wait()


def last_part(g, w_project, normed, grad_w_out, small, g_sums, gain, bias, *late_inputs):
    seq = lax.axis_size("seq")
    far = len(far_bits(seq))
    width = normed.shape[1]
    shapes = [
        ((width // 128, SEGMENT, 128), F32),
        ((width // 128, SEGMENT, 128), F32),
        ((4, ROWS, ROWS // 2), BF),
        (small.shape, F32),
        ((16, 128), F32),
    ]
    scratch = shapes[:1] + [(a.shape, a.dtype) for a in late_inputs] + [
        ((4, ROWS, ROWS // 2), BF),
        ((4, 48, ROWS // 2), BF),
        (normed.shape, BF),
        (normed.shape, BF),
        (small.shape, F32),
        ((16 + far,) + small.shape, F32),
        ((16, 128), F32),
        ((16 + far, 16, 128), F32),
        ((16, width), F32),
    ]
    chunks = SEGMENT // CHUNK
    counts = (len(late_inputs), chunks, chunks, 15, 15, 15, 15, 16, 16)
    return pl.pallas_call(
        functools.partial(last_kernel, seq),
        out_shape=[jax.ShapeDtypeStruct(*s) for s in shapes],
        in_specs=[VMEM] * 8 + [ANY] * len(late_inputs),
        out_specs=[VMEM, ANY, VMEM, VMEM, VMEM],
        scratch_shapes=[pltpu.VMEM(*s) for s in scratch]
        + [pltpu.SemaphoreType.DMA]
        + [pltpu.SemaphoreType.DMA((c,)) for c in counts]
        + [shape for _ in range(4) for shape in Halving.scratch(seq, ROWS // 2)]
        + [shape for _ in range(4) for shape in Doubling.scratch()],
        compiler_params=pltpu.CompilerParams(
            collective_id=2, has_side_effects=True, vmem_limit_bytes=58 * 2**20
        ),
        name="last_part",
    )(g, w_project, normed, grad_w_out, small, g_sums, gain, bias, *late_inputs)


def out_kernel(
    r_ref, e_ref, p_ref, o_ref, o2_ref, t_ref, l_ref, early_ref, late_ref, r_out, e_out, p_out, o_out, t_out, l_out, *small
):
    half = ROWS // 2
    r_out[...] = r_ref[...].astype(F32)
    for k in range(2):
        e_out[:, k * ROWS : (k + 1) * ROWS] = e_ref[k].astype(F32)
    p_out[...] = p_ref[...].astype(F32)
    o_out[:, :half] = o_ref[0].astype(F32)
    o_out[:, half:] = o2_ref[0].astype(F32)
    for k in range(t_ref.shape[0]):
        at = slice(k * 128, (k + 1) * 128)
        t_out[:, at] = t_ref[k]
        l_out[:, at] = l_ref[k]

    @pl.when(pl.program_id(0) == 0)
    def _():
        for k in range(2):
            small[0][k : k + 1, :] = vector(early_ref, k, half)
            small[6 + k][...] = late_ref[k * 8 : k * 8 + 6, :]
        for k, (first, rows) in enumerate(((6, 6), (12, 6), (18, 6), (24, 12), (36, 6))):
            small[1 + k][...] = early_ref[first : first + rows, :]


def results(grads, grads_p, planes, layer_planes, early, late):
    half = ROWS // 2
    n = 8
    rows, width = planes.shape[1], planes.shape[0] * 128
    plane_spec = pl.BlockSpec((planes.shape[0], rows // n, 128), lambda i: (0, i, 0))
    small = [(2, half)] + [(n, 128) for n in (6, 6, 6, 12, 6, 6, 6)]
    whole_spec = lambda shape: pl.BlockSpec(shape, lambda i: (0, 0))
    row_spec = pl.BlockSpec((rows // n, width), lambda i: (i, 0))
    return pl.pallas_call(
        out_kernel,
        grid=(n,),
        out_shape=[
            jax.ShapeDtypeStruct((2 * ROWS, ROWS), F32),
            jax.ShapeDtypeStruct((ROWS, 2 * ROWS), F32),
            jax.ShapeDtypeStruct((3, ROWS, half), F32),
            jax.ShapeDtypeStruct((half, ROWS), F32),
            jax.ShapeDtypeStruct((rows, width), F32),
            jax.ShapeDtypeStruct((rows, width), F32),
        ]
        + [jax.ShapeDtypeStruct(shape, F32) for shape in small],
        in_specs=[
            pl.BlockSpec((2 * ROWS // n, ROWS), lambda i: (i, 0)),
            pl.BlockSpec((2, ROWS // n, ROWS), lambda i: (1, i, 0)),
            pl.BlockSpec((3, ROWS // n, half), lambda i: (0, i, 0)),
            pl.BlockSpec((1, half // n, half), lambda i: (3, i, 0)),
            pl.BlockSpec((1, half // n, half), lambda i: (3, n + i, 0)),
            plane_spec,
            plane_spec,
            whole_spec(early.shape),
            whole_spec(late.shape),
        ],
        out_specs=[
            pl.BlockSpec((2 * ROWS // n, ROWS), lambda i: (i, 0)),
            pl.BlockSpec((ROWS // n, 2 * ROWS), lambda i: (i, 0)),
            pl.BlockSpec((3, ROWS // n, half), lambda i: (0, i, 0)),
            pl.BlockSpec((half // n, ROWS), lambda i: (i, 0)),
            row_spec,
            row_spec,
        ]
        + [whole_spec(shape) for shape in small],
        name="results",
    )(grads.reshape(-1, ROWS), grads, grads_p, grads_p, grads_p, planes, layer_planes, early, late)


def body(
    tokens,
    cotangent,
    valid_tiles,
    gain_first,
    shift_first,
    w_project,
    bias_project,
    w_output,
    bias_output,
    gain_second,
    shift_second,
    w_expand,
    bias_expand,
    w_reduce,
    bias_reduce,
):
    w_project = w_project.transpose(1, 0, 2)
    by_rows = lambda value: value.reshape(-1, 128)
    queries, key_values, normed, tokens, stats = first_part(
        tokens, by_rows(valid_tiles), by_rows(gain_first), by_rows(shift_first), w_project, bias_project
    )
    fin, attended, w_out_other, *saved = attention_forward(queries, key_values, w_output)
    middle, grad_middle, grad_attended, ffn_part, shares, grads_o, small = middle_part(
        attended, w_output, w_out_other, tokens, cotangent, w_expand, w_reduce,
        by_rows(bias_output), by_rows(gain_second), by_rows(shift_second), by_rows(bias_expand),
    )
    g, g_sums, grads, ffn_other = attention_backward(
        queries, key_values, saved, fin, grad_attended, shares, ffn_part
    )
    planes, layer_planes, grads_p, early, late = last_part(
        g, w_project, normed, grads_o, small, g_sums, by_rows(gain_first), by_rows(bias_reduce),
        tokens, grad_middle, stats, middle, ffn_part, ffn_other,
    )
    (
        grad_w_reduce, grad_w_expand, grad_w_project, grad_w_output, grad_tokens, layer_out,
        grad_bias_project, grad_bias_output, grad_gain_second, grad_shift_second, grad_bias_expand, grad_bias_reduce,
        grad_gain_first, grad_shift_first,
    ) = results(grads, grads_p, planes, layer_planes, early, late)
    return (
        layer_out,
        grad_tokens,
        grad_gain_first.reshape(-1),
        grad_shift_first.reshape(-1),
        grad_w_project.transpose(1, 0, 2),
        grad_bias_project,
        grad_w_output,
        grad_bias_output.reshape(-1),
        grad_gain_second.reshape(-1),
        grad_shift_second.reshape(-1),
        grad_w_expand,
        grad_bias_expand.reshape(-1),
        grad_w_reduce,
        grad_bias_reduce.reshape(-1),
    )


def solution(mesh):
    in_specs = (
        P("seq", None),
        P("seq", None),
        P("seq"),
        P(),
        P(),
        P(None, None, "heads"),
        P(None, "heads"),
        P("heads", None),
        P(),
        P(),
        P(),
        P(None, "heads"),
        P("heads"),
        P("heads", None),
        P(),
    )
    out_specs = (
        P("seq", None),
        P("seq", None),
        P(),
        P(),
        P(None, None, "heads"),
        P(None, "heads"),
        P("heads", None),
        P(),
        P(),
        P(),
        P(None, "heads"),
        P("heads"),
        P("heads", None),
        P(),
    )
    return jax.shard_map(body, mesh=mesh, in_specs=in_specs, out_specs=out_specs, check_vma=False)
```

```python
import functools
import math

import jax
import jax.numpy as jnp
from jax import lax
from jax.experimental import pallas as pl
from jax.experimental.pallas import tpu as pltpu
from jax.sharding import PartitionSpec as P

HEADS = 16
HEAD_DIM = 48
SEGMENT = 1024
BRANCHES = 5
LOCAL = 8

MESH = pl.DeviceIdType.MESH
BF = jnp.bfloat16
F32 = jnp.float32
NT = (((1,), (1,)), ((), ()))
TN = (((0,), (0,)), ((), ()))
NN = (((1,), (0,)), ((), ()))

masked_score = -1000000000.0
layer_eps = 1e-05
SCALE = HEAD_DIM ** (-0.5)
LOG2E = math.log2(math.e)


def dot(a, b, dims):
    return lax.dot_general(a, b, dims, preferred_element_type=F32)


def lanes(shape):
    return lax.broadcasted_iota(jnp.int32, shape, len(shape) - 1)


def reversed_bits(value, bits):
    out = value * 0
    for k in range(bits):
        out = out * 2 + (value // 2**k) % 2
    return out


def split3(value):
    high = value.astype(BF).astype(F32)
    rest = value - high
    middle = rest.astype(BF).astype(F32)
    return high, middle, rest - middle


def take_48(value, head, at):
    tile, off = head * 48 // 128, head * 48 % 128
    shift = (at - off) % 128
    turn = lambda k: pltpu.roll(value[:, k * 128 : (k + 1) * 128], shift, 1) if shift else value[:, k * 128 : (k + 1) * 128]
    out = turn(tile)
    lane = lanes(out.shape)
    if off + 48 > 128:
        out = jnp.where(lane < at + 128 - off, out, turn(tile + 1))
    return jnp.where((lane >= at) & (lane < at + 48), out, 0.0)


def fold(value, at):
    pairs = value.reshape(value.shape[0] // 32, 2, 16, 128)
    even, odd = pairs[:, 0].reshape(-1, 128), pairs[:, 1].reshape(-1, 128)
    return pltpu.roll(even, 64, 1) + odd if at else even + pltpu.roll(odd, 64, 1)


def unfold(value, at):
    value = value.astype(F32)
    keep = lanes(value.shape) >= 64 if at else lanes(value.shape) < 64
    turned = jnp.where(keep, pltpu.roll(value, 64, 1), 0.0)
    straight = jnp.where(keep, value, 0.0)
    even, odd = (turned, straight) if at else (straight, turned)
    pairs = [part.reshape(-1, 1, 16, 128) for part in (even, odd)]
    return jnp.concatenate(pairs, axis=1).reshape(-1, 128)


def placing(source, target, columns):
    row = lax.broadcasted_iota(jnp.int32, (LOCAL * 128, columns), 0)
    column = lax.broadcasted_iota(jnp.int32, (LOCAL * 128, columns), 1)
    lane = row % 128 - source
    hit = (lane >= 0) & (lane < HEAD_DIM) & (column == target + row // 128 * HEAD_DIM + lane)
    return jnp.where(hit, 1.0, 0.0)


def row_mean(value):
    ones = jnp.ones((value.shape[1], 128), BF)
    high = value.astype(BF)
    low = (value - high.astype(F32)).astype(BF)
    return (dot(high, ones, NN) + dot(low, ones, NN)) * (1.0 / value.shape[1])


def vector(ref, k=0, width=768):
    n = width // 128
    return jnp.concatenate([ref[k * n + t : k * n + t + 1, :] for t in range(n)], axis=1)


def widen(tile, like):
    return jnp.concatenate([tile] * (like.shape[1] // 128), axis=1)


def row_sums(value):
    return jnp.sum(value.reshape(value.shape[0] // 8, 8, value.shape[1]), axis=0)


def put_vector(rows, first, partial):
    value = jnp.sum(partial, axis=0, keepdims=True)
    for t in range(value.shape[1] // 128):
        rows[pl.ds(first + t, 1), :] = value[:, t * 128 : (t + 1) * 128]


def norm_stats(value):
    mean = row_mean(value)
    centered = value - widen(mean, value)
    rs = lax.rsqrt(row_mean(centered * centered) + layer_eps)
    return mean, rs


def norm_back(grad, xhat, rs, gain):
    grad = grad * gain
    return rs * (grad - widen(row_mean(grad), grad) - xhat * widen(row_mean(grad * xhat), grad))


class Place:
    def __init__(self):
        self.me = lax.axis_index("seq")
        self.y = lax.axis_index("heads")

    def member(self, b):
        return self.me % 2**b

    def device(self, b, j):
        return (self.me // 2**b * 2**b + j, self.y)

    def start(self, b, head):
        stride = 2**b
        place = (self.y * LOCAL + head) % stride
        return pl.multiple_of(reversed_bits(place, b) * (SEGMENT // stride), SEGMENT // stride)

    def bit(self, k):
        return self.me // 2**k % 2

    def partner(self, k):
        return (self.me + 2**k * (1 - 2 * self.bit(k)), self.y)

    def low(self, order, k):
        return sum((self.bit(order[i]) * HALVES[i] for i in range(k)), self.me * 0)

    def greet(self, seq=16, other=False):
        barrier = pltpu.get_barrier_semaphore()
        i = self.member(4)
        count = 15
        if other:
            pl.semaphore_signal(barrier, inc=1, device_id=(self.me, 1 - self.y), device_id_type=MESH)
            count += 1
        for k in far_bits(seq):
            pl.semaphore_signal(barrier, inc=1, device_id=self.partner(k), device_id_type=MESH)
            count += 1

        def signal(d, _):
            pl.semaphore_signal(barrier, inc=1, device_id=self.device(4, (i + d) % 16), device_id_type=MESH)
            return 0

        lax.fori_loop(1, 16, signal, 0)
        pl.semaphore_wait(barrier, count)


def remote(src, dst, send, recv, device):
    return pltpu.make_async_remote_copy(
        src_ref=src, dst_ref=dst, send_sem=send, recv_sem=recv, device_id=device, device_id_type=MESH
    )


def ds(start, size):
    return pl.ds(pl.multiple_of(start, size), size)


def attend(queries, kv):
    scores = dot(unfold(queries, 0).astype(BF), kv, NT)
    top = jnp.max(scores, axis=1, keepdims=True)
    raised = jnp.exp2(scores - top).astype(BF)
    return dot(raised, kv, NN), top


def packed(out, top):
    lane = lanes(out.shape)
    total = out[:, 112:113]
    tile = jnp.where(lane == 112, 1.0, jnp.where(lane >= 64, out * (1.0 / total), 0.0))
    for k, piece in enumerate(split3(top) + split3(total)):
        tile = jnp.where(lane == 114 + k, piece, tile)
    return fold(tile, 64).astype(BF)


class Trade:
    def __init__(self, place, b):
        self.place, self.b = place, b
        self.n = SEGMENT // 2**b
        self.tiles = max(LOCAL // 2**b, 1)
        self.folded = self.n // 2 if b < 4 else 16
        self.i = place.member(b)

    def head(self, j, t):
        return j * self.tiles + t if self.b < 4 else j // 2

    def rows(self, j, t):
        return pl.ds(self.place.start(self.b, self.head(j, t)), self.n)

    def folded_rows(self, j, t):
        start = self.place.start(self.b, self.head(j, t)) // 2
        if self.b == 4:
            start = start + j % 2 * 16
        return pl.ds(pl.multiple_of(start, 16), self.folded)

    def slot(self, j):
        return ds(j * self.n, self.n)

    def folded_slot(self, j):
        return ds(j * self.folded, self.folded)

    def home(self, ref, j, t):
        ref = ref.at[self.head(j, t)]
        return ref if self.b < 4 else ref.at[ds(j % 2 * 16, 16), :]

    def whole_home(self, ref, j, t):
        return ref.at[self.head(j, t)] if self.b < 4 else ref.at[j % 2, j // 2]

    def each(self, body):
        def step(d, _):
            j = (self.i + d) % 2**self.b
            for t in range(self.tiles):
                body(j, t, (d - 1) * self.tiles + t, self.place.device(self.b, j))
            return 0

        lax.fori_loop(1, 2**self.b, step, 0)


COPIES = (4, 6, 7, 15)


def forward_kernel(
    q_ref, kv_ref, w_out_ref, fin_out, att_ref, w_out_other, s1, s2, s3, s4, s5, s6, s7, s8,
    fin_ref, q1, q2, q3, q4, kv1, kv2, kv3, kv4, acc, tops, o1, o2, o3, o4, r1, r2, r3, r4, places, *sems
):
    place = Place()
    trades = [None] + [Trade(place, b) for b in (1, 2, 3, 4)]
    qs, kvs = (None, q1, q2, q3, q4), (None, kv1, kv2, kv3, kv4)
    os, rs = (None, o1, o2, o3, o4), (None, r1, r2, r3, r4)
    *sems, w_send, w_recv, fin_sem, saved_sem = sems
    q_send, q_recv, kv_send, kv_recv, back_send, back_recv = (
        (None,) + tuple(sems[4 * k : 4 * k + 4]) for k in range(6)
    )

    def go(b, action):
        trade = trades[b]

        def body(j, t, k, device):
            for copy in (
                remote(
                    q_ref.at[trade.head(j, t), trade.folded_rows(j, t), :],
                    qs[b].at[t, trade.folded_slot(trade.i), :],
                    q_send[b].at[k],
                    q_recv[b].at[k],
                    device,
                ),
                remote(
                    kv_ref.at[trade.head(j, t), trade.rows(j, t), :],
                    kvs[b].at[t, trade.slot(trade.i), :],
                    kv_send[b].at[k],
                    kv_recv[b].at[k],
                    device,
                ),
            ):
                action(copy)

        trade.each(body)

    def back(b, action):
        trade = trades[b]

        def body(j, t, k, device):
            action(
                remote(
                    os[b].at[t, trade.folded_slot(j), :],
                    trade.home(rs[b], trade.i, t),
                    back_send[b].at[k],
                    back_recv[b].at[k],
                    device,
                )
            )

        trade.each(body)

    def fin_copy(h):
        return pltpu.make_async_copy(fin_ref.at[h], fin_out.at[h], fin_sem.at[h])

    saved = [
        pltpu.make_async_copy(src, dst, saved_sem.at[k])
        for k, (src, dst) in enumerate(
            zip((q1, q2, q3, q4, kv1, kv2, kv3, kv4), (s1, s2, s3, s4, s5, s6, s7, s8))
        )
    ]
    start, arrived, sent = (lambda c: c.start()), (lambda c: c.wait_recv()), (lambda c: c.wait_send())
    place.greet(16, True)
    for b in (1, 4, 3, 2):
        go(b, start)
    w_copy = remote(w_out_ref, w_out_other, w_send, w_recv, (place.me, 1 - place.y))
    w_copy.start()

    for b in (1, 2, 3, 4):
        trade = trades[b]
        for t in range(trade.tiles):
            head = trade.head(trade.i, t)
            qs[b][t, trade.folded_slot(trade.i), :] = q_ref[head, trade.folded_rows(trade.i, t), :]
            kvs[b][t, trade.slot(trade.i), :] = kv_ref[head, trade.rows(trade.i, t), :]
    places[...] = placing(64, 0, LOCAL * HEAD_DIM).astype(BF)

    def local_heads(k, _):
        for h in (k * 2, k * 2 + 1):
            for half in range(2):
                rows = pl.ds(half * 512, 512)
                out, top = attend(q_ref[h, pl.ds(half * 256, 256), :], kv_ref[h])
                acc[h, rows, :] = out
                tops[h, rows, :] = jnp.broadcast_to(top, out.shape)
        return 0

    def half_tile(b, t, half):
        rows = pl.ds(half * 256, 256)
        os[b][t, rows, :] = packed(*attend(qs[b][t, rows, :], kvs[b][t]))

    def send_back(b):
        trade = trades[b]
        back(b, start)
        saved[b - 1].start()
        saved[b + 3].start()
        for t in range(trade.tiles):
            trade.home(rs[b], trade.i, t)[...] = os[b][t, trade.folded_slot(trade.i), :]

    lax.fori_loop(0, 2, local_heads, 0)
    go(1, arrived)

    def tiles_1(k, _):
        for t in (k * 2, k * 2 + 1):
            for half in range(2):
                half_tile(1, t, half)
        return 0

    lax.fori_loop(0, 2, tiles_1, 0)
    send_back(1)
    go(4, arrived)
    go(3, arrived)
    half_tile(4, 0, 0)
    half_tile(3, 0, 0)
    half_tile(3, 0, 1)
    send_back(4)
    send_back(3)
    go(2, arrived)
    for t in range(2):
        for half in range(2):
            half_tile(2, t, half)
    send_back(2)
    lax.fori_loop(2, 4, local_heads, 0)

    for b in (1, 4, 3, 2):
        back(b, arrived)

    row = lax.broadcasted_iota(jnp.int32, (128, 256), 0)
    column = lax.broadcasted_iota(jnp.int32, (128, 256), 1)
    first = jnp.where(column < 128, 114, 117)
    picks = jnp.where((row >= first) & (row < first + 3), 1.0, 0.0).astype(BF)

    def merge_head(h, _):
        for b in (1, 2, 3, 4):
            n = SEGMENT // 2**b
            rows = pl.ds(place.start(b, h), n)
            part = unfold(rs[b][h], 64)
            stats = dot(part.astype(BF), picks, NN)
            top = jnp.maximum(tops[h, rows, :], stats[:, 0:128])
            keep = jnp.exp2(tops[h, rows, :] - top)
            gain = jnp.exp2(stats[:, 0:128] - top) * stats[:, 128:256]
            acc[h, rows, :] = acc[h, rows, :] * keep + part * gain
            tops[h, rows, :] = top
        out = acc[h]
        lane = lanes(out.shape)
        inverse = 1.0 / out[:, 112:113]
        out = jnp.where((lane >= 64) & (lane < 112), out * inverse, jnp.where(lane == 112, inverse, 0.0))
        for k, piece in enumerate(split3(-tops[h])):
            out = jnp.where(lane == 116 + k, piece, out)
        fin_ref[h] = out
        fin_copy(h).start()
        return 0

    lax.fori_loop(0, LOCAL, merge_head, 0)

    def compact(n, _):
        rows = ds(n * 256, 256)
        wide = jnp.concatenate([fin_ref[h, rows, :].astype(BF) for h in range(LOCAL)], axis=1)
        att_ref[rows, :] = dot(wide, places[...], NN).astype(BF)
        return 0

    lax.fori_loop(0, 4, compact, 0)

    for b in (4, 3, 2, 1):
        go(b, sent)
        back(b, sent)
    w_copy.wait()
    for copy in saved:
        copy.wait()
    for h in range(LOCAL):
        fin_copy(h).wait()


ROWS = 768
HALVES = (384, 192, 96, 48)
LANDING = (0, 384, 576, 672, 720)


def far_bits(seq):
    return list(range(4, seq.bit_length() - 1))


X_FIRST = (0, 1, 2, 3)
Z_FIRST = (0, 2, 3, 1)
ORDERS = (X_FIRST, X_FIRST, X_FIRST, Z_FIRST)


class Halving:
    def __init__(self, place, seq, order, grads, share, scratch):
        self.place, self.seq, self.order, self.grads, self.share = place, seq, order, grads, share
        self.landing, self.send, self.recv, self.far_send, self.far_recv = scratch

    @staticmethod
    def scratch(seq, width=ROWS):
        far = len(far_bits(seq))
        return [pltpu.VMEM((720 + 48 * far, width), BF)] + [pltpu.SemaphoreType.DMA((max(4, far),)) for _ in range(4)]

    def copy(self, k):
        size = HALVES[k]
        bit = self.order[k]
        start = self.place.low(self.order, k) + (1 - self.place.bit(bit)) * size
        return remote(
            self.grads.at[pl.ds(pl.multiple_of(start, 48), size), :],
            self.landing.at[pl.ds(LANDING[k], size), :],
            self.send.at[k],
            self.recv.at[k],
            self.place.partner(bit),
        )

    def add(self, k):
        start = self.place.low(self.order, k + 1)

        def step(i, _):
            rows = pl.ds(pl.multiple_of(start + i * 48, 48), 48)
            arrived = self.landing[pl.ds(pl.multiple_of(LANDING[k] + i * 48, 48), 48), :]
            value = (self.grads[rows, :].astype(F32) + arrived.astype(F32)).astype(BF)
            if k < 3:
                self.grads[rows, :] = value
            else:
                self.share[...] = value
            return 0

        lax.fori_loop(0, HALVES[k] // 48, step, 0)

    def step(self, k):
        if k > 0:
            self.copy(k - 1).wait_recv()
            self.add(k - 1)
        if k < 4:
            self.copy(k).start()
            return
        for n, bit in enumerate(far_bits(self.seq)):
            landing = self.landing.at[pl.ds(720 + 48 * n, 48), :]
            copy = remote(self.share, landing, self.far_send.at[n], self.far_recv.at[n], self.place.partner(bit))
            copy.start()
            copy.wait()
            self.share[...] = (self.share[...].astype(F32) + landing[...].astype(F32)).astype(BF)

    def finish(self):
        for k in range(4):
            self.copy(k).wait_send()


class Doubling:
    def __init__(self, place, order, share, result, sems):
        self.place, self.order, self.share, self.result = place, order, share, result
        self.send, self.recv = sems

    @staticmethod
    def scratch():
        return [pltpu.SemaphoreType.DMA((4,)) for _ in range(2)]

    def copy(self, k):
        rows = pl.ds(pl.multiple_of(self.place.low(self.order, k + 1), 48), HALVES[k])
        view = self.result.at[rows, :]
        return remote(view, view, self.send.at[k], self.recv.at[k], self.place.partner(self.order[k]))

    def step(self, k):
        if k == 0:
            self.result[pl.ds(pl.multiple_of(self.place.low(self.order, 4), 48), 48), :] = self.share[...]
        else:
            self.copy(4 - k).wait_recv()
        if k < 4:
            self.copy(3 - k).start()

    def finish(self):
        for k in range(4):
            self.copy(k).wait_send()


def run_at(slot, work, times):
    for k, time in enumerate(times):

        @pl.when(slot == time)
        def _():
            work.step(k)


def sem_shapes(times):
    return [pltpu.SemaphoreType.DMA((c,)) for _ in range(times) for c in COPIES]


VMEM = pl.BlockSpec(memory_space=pltpu.VMEM)
ANY = pl.BlockSpec(memory_space=pl.ANY)
ORDER = tuple(int(f"{c:04b}"[::-1], 2) for c in range(16))


FOLDED = [((4, 512, 128), BF), ((2, 512, 128), BF), ((1, 512, 128), BF), ((1, 256, 128), BF)]
WHOLE = [((n, SEGMENT, 128), BF) for n in (4, 2, 1, 1)]
FOLDED_HOME = [((LOCAL, n, 128), BF) for n in (256, 128, 64, 32)]


def attention_forward(queries, key_values, w_output):
    shapes = [
        ((LOCAL, SEGMENT, 128), F32),
        ((SEGMENT, LOCAL * HEAD_DIM), BF),
        (w_output.shape, BF),
    ] + FOLDED + WHOLE
    scratch = (
        [((LOCAL, SEGMENT, 128), F32)] + FOLDED + WHOLE
        + [((LOCAL, SEGMENT, 128), F32)] * 2 + FOLDED + FOLDED_HOME + [((LOCAL * 128, LOCAL * HEAD_DIM), BF)]
    )
    return pl.pallas_call(
        forward_kernel,
        out_shape=[jax.ShapeDtypeStruct(*s) for s in shapes],
        in_specs=[VMEM, VMEM, ANY],
        out_specs=[ANY, VMEM, ANY] + [ANY] * 8,
        scratch_shapes=[pltpu.VMEM(*s) for s in scratch] + sem_shapes(6)
        + [pltpu.SemaphoreType.DMA] * 2 + [pltpu.SemaphoreType.DMA((8,))] * 2,
        compiler_params=pltpu.CompilerParams(
            collective_id=0, has_side_effects=True, vmem_limit_bytes=56 * 2**20
        ),
        name="attention_forward",
    )(queries, key_values, w_output)


def pair_grads(q, d, kv_at, put):
    d = unfold(d, 64)
    lane = lanes(d.shape)
    top = jnp.where((lane >= 52) & (lane < 55), pltpu.roll(d, 64, 1), 0.0)
    queries = (unfold(q, 0) + top).astype(BF)
    grads = d.astype(BF)
    total = None
    for half in range(2):
        kv = kv_at(half)
        probs = jnp.exp2(dot(kv, queries, NT))
        grad_scores = (probs * dot(kv, grads, NT)).astype(BF)
        put(half, dot(grad_scores, queries, NN) + dot(probs.astype(BF), grads, NN))
        part = dot(kv, grad_scores, TN)
        total = part if total is None else total + part
    return total.T


def backward_kernel(
    q_ref, kv_ref, shares_in, fin_in, do_in, ffn_ref, s1, s2, s3, s4, s5, s6, s7, s8,
    g_ref, sum_ref, grads, ffn_other,
    q1, q2, q3, q4, kv1, kv2, kv3, kv4, fin_ref, do_ref, d0, d1, d2, d3, d4, total_q, total_kv, gq1, gq2, gq3, gq4, gkv1, gkv2, gkv3, gkv4,
    rq1, rq2, rq3, rq4, rkv1, rkv2, rkv3, rkv4, places_q, places_kv, *sems
):
    place = Place()
    trades = [None] + [Trade(place, b) for b in (1, 2, 3, 4)]
    qs, kvs, dd = (None, q1, q2, q3, q4), (None, kv1, kv2, kv3, kv4), (None, d1, d2, d3, d4)
    gqs, gkvs = (None, gq1, gq2, gq3, gq4), (None, gkv1, gkv2, gkv3, gkv4)
    rqs, rkvs = (None, rq1, rq2, rq3, rq4), (None, rkv1, rkv2, rkv3, rkv4)
    *sems, ffn_send, ffn_recv, fin_sem, do_sem, saved_sem = sems
    go_send, go_recv, q_send, q_recv, kv_send, kv_recv = ((None,) + tuple(sems[4 * k : 4 * k + 4]) for k in range(6))
    doubling = [
        Doubling(place, ORDERS[c], shares_in.at[c], grads.at[c], sems[24 + 2 * c : 26 + 2 * c]) for c in range(4)
    ]

    def reduce_at(slot):
        run_at(slot, doubling[0], (0, 2, 4, 7, 9))
        run_at(slot, doubling[1], (1, 3, 7, 10, 12))
        run_at(slot, doubling[2], (2, 4, 10, 13, 14))
        run_at(slot, doubling[3], (3, 5, 8, 11, 13))

    ffn_copy = remote(ffn_ref, ffn_other, ffn_send, ffn_recv, (place.me, 1 - place.y))

    def go(b, action):
        trade = trades[b]

        def body(j, t, k, device):
            action(
                remote(
                    d0.at[trade.head(j, t), trade.folded_rows(j, t), :],
                    dd[b].at[t, trade.folded_slot(trade.i), :],
                    go_send[b].at[k],
                    go_recv[b].at[k],
                    device,
                )
            )

        trade.each(body)

    def back(b, action):
        trade = trades[b]

        def body(j, t, k, device):
            for copy in (
                remote(
                    gqs[b].at[t, trade.folded_slot(j), :],
                    trade.home(rqs[b], trade.i, t),
                    q_send[b].at[k],
                    q_recv[b].at[k],
                    device,
                ),
                remote(
                    gkvs[b].at[t, trade.slot(j), :],
                    trade.whole_home(rkvs[b], trade.i, t),
                    kv_send[b].at[k],
                    kv_recv[b].at[k],
                    device,
                ),
            ):
                action(copy)

        trade.each(body)

    start, arrived, sent = (lambda c: c.start()), (lambda c: c.wait_recv()), (lambda c: c.wait_send())

    do_copy = pltpu.make_async_copy(do_in, do_ref, do_sem)
    do_copy.start()

    def fin_copy(h):
        return pltpu.make_async_copy(fin_in.at[h], fin_ref.at[h], fin_sem.at[h])

    for h in range(LOCAL):
        fin_copy(h).start()
    saved = [
        pltpu.make_async_copy(src, dst, saved_sem.at[k])
        for k, (src, dst) in enumerate(
            zip((s1, s2, s3, s4, s5, s6, s7, s8), (q1, q2, q3, q4, kv1, kv2, kv3, kv4))
        )
    ]
    for copy in saved:
        copy.start()
    do_copy.wait()

    def prepare(h, _):
        fin_copy(h).wait()
        fin = fin_ref[h]
        lane = lanes(fin.shape)
        grad = (do_ref[:, ds(h * 128, 128)].astype(F32) * fin[:, 112:113]).astype(BF).astype(F32)
        delta = -jnp.sum(grad * fin, axis=1, keepdims=True)
        high = delta.astype(BF).astype(F32)
        tile = jnp.where(lane < 112, grad, jnp.where(lane < 116, 0.0, jnp.where(lane < 119, fin, 0.0)))
        tile = jnp.where(lane == 112, high, jnp.where(lane == 113, delta - high, tile))
        d0[h] = fold(tile, 64).astype(BF)
        return 0

    lax.fori_loop(0, LOCAL, prepare, 0)
    place.greet(16, True)
    for b in (1, 4, 3, 2):
        go(b, start)
    ffn_copy.start()
    for b in (1, 2, 3, 4):
        trade = trades[b]
        for t in range(trade.tiles):
            head = trade.head(trade.i, t)
            dd[b][t, trade.folded_slot(trade.i), :] = d0[head, trade.folded_rows(trade.i, t), :]
    places_q[...] = placing(0, 0, LOCAL * HEAD_DIM).astype(BF)
    places_kv[...] = (
        placing(0, 0, 2 * LOCAL * HEAD_DIM) + placing(64, LOCAL * HEAD_DIM, 2 * LOCAL * HEAD_DIM)
    ).astype(BF)

    def local_head(h, _):
        def put(half, grad):
            total_kv[h, pl.ds(half * 512, 512), :] = grad

        total_q[h] = pair_grads(q_ref[h], d0[h], lambda half: kv_ref[h, pl.ds(half * 512, 512), :], put)
        reduce_at(jnp.where(h < 4, h, h + 8))
        return 0

    def tile_grads(b, t):
        def put(half, grad):
            gkvs[b][t, pl.ds(half * 512, 512), :] = grad.astype(BF)

        grad = pair_grads(qs[b][t], dd[b][t], lambda half: kvs[b][t, pl.ds(half * 512, 512), :], put)
        gqs[b][t] = fold(jnp.where(lanes(grad.shape) < 64, grad, 0.0), 0).astype(BF)

    def branch(b, slot):
        trade = trades[b]
        saved[b - 1].wait()
        saved[b + 3].wait()
        go(b, arrived)

        def tile(t, _):
            tile_grads(b, t)
            reduce_at(slot + t)
            return 0

        lax.fori_loop(0, trade.tiles, tile, 0)
        back(b, start)
        for t in range(trade.tiles):
            trade.home(rqs[b], trade.i, t)[...] = gqs[b][t, trade.folded_slot(trade.i), :]
            trade.whole_home(rkvs[b], trade.i, t)[...] = gkvs[b][t, trade.slot(trade.i), :]

    lax.fori_loop(0, 4, local_head, 0)
    branch(1, 4)
    branch(4, 8)
    branch(3, 9)
    branch(2, 10)
    lax.fori_loop(4, 8, local_head, 0)

    for b in (1, 4, 3, 2):
        back(b, arrived)

    def finish(h, _):
        for b in (1, 2, 3, 4):
            rows = pl.ds(place.start(b, h), SEGMENT // 2**b)
            total_q[h, rows, :] += unfold(rqs[b][h], 0)
            if b < 4:
                total_kv[h, rows, :] += rkvs[b][h].astype(F32)
            else:
                total_kv[h, rows, :] += rkv4[0, h].astype(F32) + rkv4[1, h].astype(F32)
        return 0

    lax.fori_loop(0, LOCAL, finish, 0)
    sum_ref[...] = jnp.zeros_like(sum_ref)

    def compact(i, _):
        rows = ds(i * 256, 256)
        key_lane = lanes((256, 128)) < 64
        wide_q, wide_kv = [], []
        for h in range(LOCAL):
            factor = jnp.where(kv_ref[h, rows, 48:49].astype(F32) >= 0.0, 1.0 / LOG2E, 0.0)
            wide_q.append((total_q[h, rows, :] * SCALE).astype(BF))
            wide_kv.append((total_kv[h, rows, :] * jnp.where(key_lane, factor, 1.0)).astype(BF))
        grad_q = dot(jnp.concatenate(wide_q, axis=1), places_q[...], NN)
        grad_kv = dot(jnp.concatenate(wide_kv, axis=1), places_kv[...], NN)
        for k, grad in enumerate((grad_q, grad_kv[:, :384], grad_kv[:, 384:])):
            g_ref[k, rows, :] = grad.astype(BF)
            sum_ref[k] += row_sums(grad)
        return 0

    lax.fori_loop(0, 4, compact, 0)

    for b in (4, 3, 2, 1):
        go(b, sent)
        back(b, sent)
    for work in doubling:
        work.finish()
    ffn_copy.wait()


def attention_backward(queries, key_values, saved, fin, grad_out, shares, ffn_part):
    width = LOCAL * HEAD_DIM
    shapes = [
        ((3, SEGMENT, width), BF),
        ((3, 8, width), F32),
        ((4, ROWS, ROWS), BF),
        (ffn_part.shape, BF),
    ]
    scratch = (
        FOLDED
        + WHOLE
        + [((LOCAL, SEGMENT, 128), F32), ((SEGMENT, LOCAL * 128), BF)]
        + [((LOCAL, 512, 128), BF)]
        + FOLDED
        + [((LOCAL, SEGMENT, 128), F32)] * 2
        + FOLDED
        + WHOLE
        + FOLDED_HOME
        + [((LOCAL, n, 128), BF) for n in (512, 256, 128)]
        + [((2, LOCAL, 64, 128), BF), ((LOCAL * 128, width), BF), ((LOCAL * 128, 2 * width), BF)]
    )
    return pl.pallas_call(
        backward_kernel,
        out_shape=[jax.ShapeDtypeStruct(*s) for s in shapes],
        in_specs=[VMEM] * 3 + [ANY] * 11,
        out_specs=[VMEM, VMEM, VMEM, ANY],
        scratch_shapes=[pltpu.VMEM(*s) for s in scratch]
        + sem_shapes(6)
        + [shape for _ in range(4) for shape in Doubling.scratch()]
        + [pltpu.SemaphoreType.DMA] * 2
        + [pltpu.SemaphoreType.DMA((LOCAL,)), pltpu.SemaphoreType.DMA, pltpu.SemaphoreType.DMA((8,))],
        compiler_params=pltpu.CompilerParams(
            collective_id=1, has_side_effects=True, vmem_limit_bytes=60 * 2**20
        ),
        name="attention_backward",
    )(queries, key_values, shares, fin, grad_out, ffn_part, *saved)


CHUNK = 128


def put_spread(planes, block, value):
    for t in range(value.shape[1] // 128):
        planes[t, pl.ds(ORDER[block], 64, stride=16), :] = value[:, t * 128 : (t + 1) * 128]


def to_planes(value_ref, planes):
    def step(i, _):
        rows = ds(i * 128, 128)
        for t in range(planes.shape[0]):
            planes[t, rows, :] = value_ref[rows, pl.ds(t * 128, 128)].astype(F32)
        return 0

    lax.fori_loop(0, SEGMENT // 128, step, 0)


def take_spread(planes, block):
    return jnp.concatenate(
        [planes[t, pl.ds(ORDER[block], 64, stride=16), :] for t in range(planes.shape[0])], axis=1
    )


def first_kernel(
    tokens_ref, valid_ref, gain_ref, shift_ref, bias_ref, w_in, q_hbm, kv_hbm, normed_hbm, tokens_hbm, stats_hbm,
    q_ref, kv_ref, normed_ref, tokens_out, stats_ref, w_ref, planes, out_sem, tokens_sem, w_sem
):
    w_copy = pltpu.make_async_copy(w_in, w_ref, w_sem)
    w_copy.start()
    to_planes(tokens_ref, planes)
    for b in range(16):
        tokens_out[pl.ds(b * 64, 64), :] = take_spread(planes, b).astype(BF)
    tokens_copy = pltpu.make_async_copy(tokens_out, tokens_hbm, tokens_sem)
    tokens_copy.start()
    count = jnp.sum(valid_ref[...])
    w_copy.wait()

    def outs(n):
        rows = ds(n * 256, 256)
        pairs = (
            (q_ref.at[:, ds(n * 128, 128), :], q_hbm.at[:, ds(n * 128, 128), :]),
            (kv_ref.at[:, rows, :], kv_hbm.at[:, rows, :]),
            (normed_ref.at[rows, :], normed_hbm.at[rows, :]),
            (stats_ref.at[:, rows, :], stats_hbm.at[:, rows, :]),
        )
        return [pltpu.make_async_copy(src, dst, out_sem.at[n * 4 + k]) for k, (src, dst) in enumerate(pairs)]

    def chunk(n, _):
        rows = ds(n * 256, 256)
        x = tokens_out[rows, :].astype(F32)
        mean, rs = norm_stats(x)
        stats_ref[0, rows, :], stats_ref[1, rows, :] = mean, rs
        normed = ((x - widen(mean, x)) * widen(rs, x) * vector(gain_ref) + vector(shift_ref)).astype(BF)
        normed_ref[rows, :] = normed
        queries = (dot(normed, w_ref[0], NN) + bias_ref[0:1, :]) * (SCALE * LOG2E)
        keys = dot(normed, w_ref[1], NN)
        values = dot(normed, w_ref[2], NN) + bias_ref[1:2, :]
        at = n * 256 + lax.broadcasted_iota(jnp.int32, (256, 128), 0)
        live = (at % 64 * 16 + reversed_bits(at // 64, 4)) < count
        lane = lanes((256, 128))
        padding = jnp.where(live, 0.0, masked_score)
        ones = ((lane >= 52) & (lane < 55)) | (lane == 112) | (lane == 113)
        for h in range(LOCAL):
            query = jnp.where(lane == 48, 1.0, take_48(queries, h, 0))
            q_ref[h, ds(n * 128, 128), :] = fold(query, 0).astype(BF)
            key = jnp.where(live, take_48(keys, h, 0), 0.0) + take_48(values, h, 64)
            kv_ref[h, rows, :] = jnp.where(ones, 1.0, jnp.where(lane == 48, padding, key)).astype(BF)
        for copy in outs(n):
            copy.start()
        return 0

    lax.fori_loop(0, 4, chunk, 0)
    tokens_copy.wait()
    for n in range(4):
        for copy in outs(n):
            copy.wait()


def first_part(tokens, valid, gain, shift, w_project, bias):
    width = tokens.shape[1]
    shapes = [
        ((LOCAL, SEGMENT // 2, 128), BF),
        ((LOCAL, SEGMENT, 128), BF),
        (tokens.shape, BF),
        (tokens.shape, BF),
        ((2, SEGMENT, 128), F32),
    ]
    return pl.pallas_call(
        first_kernel,
        out_shape=[jax.ShapeDtypeStruct(*s) for s in shapes],
        in_specs=[VMEM] * 5 + [ANY],
        out_specs=[ANY] * len(shapes),
        scratch_shapes=[pltpu.VMEM(*s) for s in shapes]
        + [pltpu.VMEM(w_project.shape, BF), pltpu.VMEM((width // 128, SEGMENT, 128), F32)]
        + [pltpu.SemaphoreType.DMA((16,)), pltpu.SemaphoreType.DMA, pltpu.SemaphoreType.DMA],
        compiler_params=pltpu.CompilerParams(vmem_limit_bytes=56 * 2**20),
        name="first_part",
    )(tokens, valid, gain, shift, bias, w_project)


GELU_C = math.sqrt(2 / math.pi)


def middle_kernel(
    seq, att_ref, w_out_ref, b_out_ref, gain_ref, shift_ref, b_expand_ref, w_out_other, tokens_in, cot_ref, w_expand_in, w_reduce_in,
    middle_out, gm_out, do_out, ffn_hbm, shares_ref, grads_o, small_ref,
    middle_ref, gm_ref, do_ref, ffn, tokens_ref, w_expand, w_reduce, att, w_out, stats, normed, active, grad_expand, cot_low, part, other, gm_low, grads, sums, sums_e, planes, cot,
    att_send, att_recv, part_send, part_recv, fill_sem, out_sem, *sems
):
    place = Place()
    y = place.y
    peer = (place.me, 1 - y)
    b_output, gain, shift = vector(b_out_ref), vector(gain_ref), vector(shift_ref)
    n = len(sems) // 4
    halving = [
        Halving(place, seq, ORDERS[c], grads.at[c], shares_ref.at[c], sems[c * n : c * n + n]) for c in range(4)
    ]
    chunk, chunks, width = 256, SEGMENT // 256, tokens_ref.shape[1]

    def att_copy(n):
        rows = ds(n * chunk, chunk)
        return remote(att_ref.at[rows, :], att.at[y, rows, :], att_send.at[n], att_recv.at[n], peer)

    def part_copy(n):
        rows = ds(n * chunk, chunk)
        return remote(part.at[rows, :], other.at[rows, :], part_send.at[n], part_recv.at[n], peer)

    fills = [
        pltpu.make_async_copy(cot_ref.at[:, pl.ds(t * 128, 128)], planes.at[t], fill_sem.at[t])
        for t in range(width // 128)
    ]
    loads = [
        pltpu.make_async_copy(src, dst, fill_sem.at[6 + k])
        for k, (src, dst) in enumerate(
            (
                (w_out_other, w_out.at[1 - y]),
                (tokens_in, tokens_ref),
                (w_expand_in, w_expand),
                (w_reduce_in, w_reduce),
            )
        )
    ]
    for fill in fills + loads:
        fill.start()
    ffn_out = pltpu.make_async_copy(ffn, ffn_hbm, out_sem.at[12])

    def out(k, n):
        rows = ds(n * chunk, chunk)
        src, dst = ((middle_ref, middle_out), (gm_ref, gm_out), (do_ref, do_out))[k]
        return pltpu.make_async_copy(src.at[rows, :], dst.at[rows, :], out_sem.at[k * 4 + n])

    place.greet(seq, True)
    for n in range(chunks):
        att_copy(n).start()
    att[y] = att_ref[...]
    w_out[y] = w_out_ref[...]
    sums[...] = jnp.zeros_like(sums)
    sums_e[...] = jnp.zeros_like(sums_e)
    for fill in fills + loads:
        fill.wait()
    for b in range(16):
        cot[pl.ds(b * 64, 64), :] = take_spread(planes, b)

    def ahead(n, _):
        rows = ds(n * chunk, chunk)
        grad_out = cot[rows, :]
        sums[0:8] += row_sums(grad_out)
        low = grad_out.astype(BF)
        cot_low[rows, :] = low
        att_copy(n).wait_recv()
        branch = dot(att[0, rows, :], w_out[0], NN) + dot(att[1, rows, :], w_out[1], NN)
        middle = tokens_ref[rows, :].astype(F32) + (branch + b_output)
        middle_ref[rows, :] = middle
        out(0, n).start()
        mean, rs = norm_stats(middle)
        stats[0, rows, :], stats[1, rows, :] = mean, rs
        norm = ((middle - widen(mean, middle)) * widen(rs, middle) * gain + shift).astype(BF)
        normed[rows, :] = norm
        value = None
        for k in range(w_expand.shape[1] // width):
            at = pl.ds(k * width, width)
            expand = dot(norm, w_expand[:, at], NN) + vector(b_expand_ref, k)
            square = expand * expand
            bent = jnp.tanh(GELU_C * expand * (1.0 + 0.044715 * square))
            gate = 0.5 * (1.0 + bent)
            active[rows, at] = (expand * gate).astype(BF)
            slope = gate + (0.5 * GELU_C) * expand * (1.0 - bent * bent) * (1.0 + (3 * 0.044715) * square)
            grad = dot(low, w_reduce[at, :], NT) * slope
            sums_e[:, at] += row_sums(grad)
            grad = grad.astype(BF)
            grad_expand[rows, at] = grad
            piece = dot(grad, w_expand[:, at], NT)
            value = piece if value is None else value + piece
        part[rows, :] = value.astype(BF)
        part_copy(n).start()
        return 0

    lax.fori_loop(0, chunks, ahead, 0)

    def behind(n, _):
        rows = ds(n * chunk, chunk)
        part_copy(n).wait_recv()
        grad = part[rows, :].astype(F32) + other[rows, :].astype(F32)
        rs = widen(stats[1, rows, :], grad)
        xhat = (middle_ref[rows, :] - widen(stats[0, rows, :], grad)) * rs
        sums[8:16] += row_sums(grad * xhat)
        sums[16:24] += row_sums(grad)
        gm = cot[rows, :] + norm_back(grad, xhat, rs, gain)
        gm_ref[rows, :] = gm
        sums[24:32] += row_sums(gm)
        low = gm.astype(BF)
        gm_low[rows, :] = low
        grad_att = dot(low, w_out_ref[...], NT)
        for h in range(LOCAL):
            do_ref[rows, pl.ds(h * 128, 128)] = take_48(grad_att, h, 64).astype(BF)
        out(1, n).start()
        out(2, n).start()
        return 0

    for k in range(2):
        grads[k] = dot(active[:, pl.ds(k * width, width)], cot_low[...], TN).astype(BF)
        halving[k].step(0)
    for k in range(2):
        grads[2 + k] = dot(normed[...], grad_expand[:, pl.ds(k * width, width)], TN).astype(BF)
        halving[2 + k].step(0)
        halving[k].step(1)
    halving[3].step(1)
    ffn[...] = dot(active[...], w_reduce[...], NN).astype(BF)
    ffn_out.start()
    halving[2].step(1)
    behind(0, 0)
    behind(1, 0)
    halving[0].step(2)
    halving[1].step(2)
    halving[3].step(2)
    behind(2, 0)
    halving[2].step(2)
    halving[0].step(3)
    halving[1].step(3)
    halving[3].step(3)
    behind(3, 0)
    halving[0].step(4)
    halving[1].step(4)
    halving[2].step(3)
    halving[3].step(4)
    for k in range(2):
        at = pl.ds(k * (width // 2), width // 2)
        grads_o[pl.ds(k * 384, 384), :] = dot(att_ref[...], gm_low[:, at], TN).astype(BF)
    halving[2].step(4)
    put_vector(small_ref, 0, sums[24:32])
    put_vector(small_ref, 6, sums[8:16])
    put_vector(small_ref, 12, sums[16:24])
    put_vector(small_ref, 18, sums_e[...])
    put_vector(small_ref, 30, sums[0:8])
    small_ref[36:48, :] = jnp.zeros((12, 128), F32)
    for n in range(chunks):
        att_copy(n).wait_send()
        part_copy(n).wait_send()
        for k in range(3):
            out(k, n).wait()
    ffn_out.wait()
    for work in halving:
        work.finish()


def middle_part(attended, w_output, w_out_other, tokens, cot, w_expand, w_reduce, *vectors):
    seq = lax.axis_size("seq")
    rows, width = tokens.shape
    hidden = w_expand.shape[1]
    shapes = [
        ((rows, width), F32),
        ((rows, width), F32),
        ((rows, LOCAL * 128), BF),
        ((rows, width), BF),
        ((4, 48, ROWS), BF),
        ((ROWS, ROWS // 2), BF),
        ((48, 128), F32),
    ]
    scratch = shapes[:4] + [
        (tokens.shape, BF),
        (w_expand.shape, BF),
        (w_reduce.shape, BF),
        ((2,) + attended.shape, BF),
        ((2,) + w_output.shape, BF),
        ((2, rows, 128), F32),
        ((rows, width), BF),
        ((rows, hidden), BF),
        ((rows, hidden), BF),
        ((rows, width), BF),
        ((rows, width), BF),
        ((rows, width), BF),
        ((rows, width), BF),
        ((4, ROWS, ROWS), BF),
        ((32, width), F32),
        ((8, hidden), F32),
        ((width // 128, rows, 128), F32),
        ((rows, width), F32),
    ]
    return pl.pallas_call(
        functools.partial(middle_kernel, seq),
        out_shape=[jax.ShapeDtypeStruct(*s) for s in shapes],
        in_specs=[VMEM] * 6 + [ANY] * 5,
        out_specs=[ANY] * 4 + [VMEM] * 3,
        scratch_shapes=[pltpu.VMEM(*s) for s in scratch]
        + [pltpu.SemaphoreType.DMA((4,)) for _ in range(4)]
        + [pltpu.SemaphoreType.DMA((10,)), pltpu.SemaphoreType.DMA((13,))]
        + [shape for _ in range(4) for shape in Halving.scratch(seq)],
        compiler_params=pltpu.CompilerParams(
            collective_id=3, has_side_effects=True, vmem_limit_bytes=60 * 2**20
        ),
        name="middle_part",
    )(attended, w_output, *vectors, w_out_other, tokens, cot, w_expand, w_reduce)


def last_kernel(
    seq, g_ref, w_ref, normed_ref, w_out_ref, small_in, sum_ref, gain_ref, bias_ref,
    tokens_in, gm_in, stats_in, middle_in, ffn_in, ffn_other_in,
    planes, layer_out, grads_ref, early_ref, late_ref,
    layer_planes, tokens_ref, gm_ref, stats, middle_ref, ffn_ref, ffn_other,
    grads, shares, part, other, small_ref, early_in, late, late_in, sums, layer_sem, fill_sem,
    part_send, part_recv, early_send, early_recv, late_send, late_recv, far_send, far_recv, *sems
):
    place = Place()
    orders = (X_FIRST, X_FIRST, Z_FIRST, X_FIRST)
    halving = [Halving(place, seq, orders[c], grads.at[c], shares.at[c], sems[5 * c : 5 * c + 5]) for c in range(4)]
    gathers = [
        Doubling(place, orders[c], shares.at[c], grads_ref.at[c], sems[20 + 2 * c : 22 + 2 * c]) for c in range(4)
    ]
    i = place.member(4)
    chunks = SEGMENT // CHUNK
    fills = [
        pltpu.make_async_copy(src, dst, fill_sem.at[k])
        for k, (src, dst) in enumerate(
            zip(
                (tokens_in, gm_in, stats_in, middle_in, ffn_in, ffn_other_in),
                (tokens_ref, gm_ref, stats, middle_ref, ffn_ref, ffn_other),
            )
        )
    ]
    for fill in fills:
        fill.start()
    put_vector(small_ref, 0, sum_ref[0])
    put_vector(small_ref, 3, sum_ref[2])
    small_ref[6:48, :] = small_in[0:42, :]

    def to_all(src, landing, send, recv):
        def each(action):
            def step(d, _):
                action(remote(src, landing.at[i], send.at[d - 1], recv.at[d - 1], place.device(4, (i + d) % 16)))
                return 0

            lax.fori_loop(1, 16, step, 0)

        return each

    def total_of(src, landing):
        def step(j, value):
            return value + landing[j]

        landing[i] = src[...]
        return lax.fori_loop(1, 16, step, landing[0])

    def far_total(result, n):
        for k, bit in enumerate(far_bits(seq)):
            landing = (early_in, late_in)[n].at[16 + k]
            copy = remote(result, landing, far_send.at[n * 8 + k], far_recv.at[n * 8 + k], place.partner(bit))
            copy.start()
            copy.wait()
            result[...] = result[...] + landing[...]

    def exchange(n):
        rows = ds(n * CHUNK, CHUNK)
        return remote(
            part.at[rows, :], other.at[rows, :], part_send.at[n], part_recv.at[n], (place.me, 1 - place.y)
        )

    def partial(n, _):
        rows = ds(n * CHUNK, CHUNK)
        value = dot(g_ref[0, rows, :], w_ref[0], NT)
        value += dot(g_ref[1, rows, :], w_ref[1], NT)
        value += dot(g_ref[2, rows, :], w_ref[2], NT)
        part[rows, :] = value.astype(BF)
        exchange(n).start()
        return 0

    def grad_w(k):
        grads[k] = dot(normed_ref[...], g_ref[k], TN).astype(BF)

    def layer(b):
        rows = pl.ds(b * 64, 64)
        total = ffn_ref[rows, :].astype(F32) + ffn_other[rows, :].astype(F32)
        put_spread(layer_planes, b, middle_ref[rows, :] + total + vector(bias_ref))

    place.greet(seq, True)
    grads[3] = w_out_ref[...]
    halving[3].step(0)
    grad_w(0)
    halving[0].step(0)
    grad_w(1)
    halving[1].step(0)
    halving[3].step(1)
    grad_w(2)
    halving[2].step(0)
    lax.fori_loop(0, 2, partial, 0)
    halving[0].step(1)
    halving[2].step(1)
    lax.fori_loop(2, chunks, partial, 0)
    halving[1].step(1)
    early_all = to_all(small_ref, early_in, early_send, early_recv)
    halving[3].step(2)
    sums[...] = jnp.zeros_like(sums)
    h0, h1, h2, h3, g0, g1, g2, g3 = halving + gathers
    h0.step(2)
    early_all(lambda copy: copy.start())
    after = (
        ((h2, 2), (h1, 2), (h3, 3)),
        ((h0, 3), (h3, 4), (g3, 0), (h2, 3)),
        ((h1, 3), (h0, 4), (g0, 0), (g3, 1)),
        ((h2, 4), (g2, 0), (h1, 4), (g1, 0), (g0, 1), (g3, 2)),
        ((g2, 1), (g1, 1), (g0, 2)),
        ((g3, 3), (g1, 2), (g2, 2)),
        ((g0, 3), (g3, 4)),
        (),
    )
    for fill in fills:
        fill.wait()
    for n in range(chunks):
        for b in range(n * 2, n * 2 + 2):
            layer(b)
        exchange(n).wait_recv()
        rows = pl.ds(n * CHUNK, CHUNK)
        grad = part[rows, :].astype(F32) + other[rows, :].astype(F32)
        rs = widen(stats[1, rows, :], grad)
        xhat = (tokens_ref[rows, :].astype(F32) - widen(stats[0, rows, :], grad)) * rs
        sums[0:8] += row_sums(grad * xhat)
        sums[8:16] += row_sums(grad)
        grad = gm_ref[rows, :] + norm_back(grad, xhat, rs, vector(gain_ref))
        for k in range(CHUNK // 64):
            put_spread(planes, n * (CHUNK // 64) + k, grad[k * 64 : (k + 1) * 64])
        for work, k in after[n]:
            work.step(k)
    for k in range(2):
        put_vector(late, k * 8, sums[k * 8 : k * 8 + 8])
        late[pl.ds(k * 8 + 6, 2), :] = jnp.zeros((2, 128), F32)
    layer_copy = pltpu.make_async_copy(layer_planes, layer_out, layer_sem)
    layer_copy.start()
    late_all = to_all(late, late_in, late_send, late_recv)
    late_all(lambda copy: copy.start())
    g1.step(3)
    g2.step(3)
    early_all(lambda copy: copy.wait_recv())
    early_ref[...] = total_of(small_ref, early_in)
    far_total(early_ref, 0)
    late_all(lambda copy: copy.wait_recv())
    late_ref[...] = total_of(late, late_in)
    far_total(late_ref, 1)
    for work in (g0, g1, g2):
        work.step(4)

    def sent(n, _):
        exchange(n).wait_send()
        return 0

    lax.fori_loop(0, chunks, sent, 0)
    early_all(lambda copy: copy.wait_send())
    late_all(lambda copy: copy.wait_send())
    for work in halving + gathers:
        work.finish()
    layer_copy.wait()


def last_part(g, w_project, normed, grad_w_out, small, g_sums, gain, bias, *late_inputs):
    seq = lax.axis_size("seq")
    far = len(far_bits(seq))
    width = normed.shape[1]
    shapes = [
        ((width // 128, SEGMENT, 128), F32),
        ((width // 128, SEGMENT, 128), F32),
        ((4, ROWS, ROWS // 2), BF),
        (small.shape, F32),
        ((16, 128), F32),
    ]
    scratch = shapes[:1] + [(a.shape, a.dtype) for a in late_inputs] + [
        ((4, ROWS, ROWS // 2), BF),
        ((4, 48, ROWS // 2), BF),
        (normed.shape, BF),
        (normed.shape, BF),
        (small.shape, F32),
        ((16 + far,) + small.shape, F32),
        ((16, 128), F32),
        ((16 + far, 16, 128), F32),
        ((16, width), F32),
    ]
    chunks = SEGMENT // CHUNK
    counts = (len(late_inputs), chunks, chunks, 15, 15, 15, 15, 16, 16)
    return pl.pallas_call(
        functools.partial(last_kernel, seq),
        out_shape=[jax.ShapeDtypeStruct(*s) for s in shapes],
        in_specs=[VMEM] * 8 + [ANY] * len(late_inputs),
        out_specs=[VMEM, ANY, VMEM, VMEM, VMEM],
        scratch_shapes=[pltpu.VMEM(*s) for s in scratch]
        + [pltpu.SemaphoreType.DMA]
        + [pltpu.SemaphoreType.DMA((c,)) for c in counts]
        + [shape for _ in range(4) for shape in Halving.scratch(seq, ROWS // 2)]
        + [shape for _ in range(4) for shape in Doubling.scratch()],
        compiler_params=pltpu.CompilerParams(
            collective_id=2, has_side_effects=True, vmem_limit_bytes=58 * 2**20
        ),
        name="last_part",
    )(g, w_project, normed, grad_w_out, small, g_sums, gain, bias, *late_inputs)


def out_kernel(
    r_ref, e_ref, p_ref, o_ref, o2_ref, t_ref, l_ref, early_ref, late_ref, r_out, e_out, p_out, o_out, t_out, l_out, *small
):
    half = ROWS // 2
    r_out[...] = r_ref[...].astype(F32)
    for k in range(2):
        e_out[:, k * ROWS : (k + 1) * ROWS] = e_ref[k].astype(F32)
    p_out[...] = p_ref[...].astype(F32)
    o_out[:, :half] = o_ref[0].astype(F32)
    o_out[:, half:] = o2_ref[0].astype(F32)
    for k in range(t_ref.shape[0]):
        at = slice(k * 128, (k + 1) * 128)
        t_out[:, at] = t_ref[k]
        l_out[:, at] = l_ref[k]

    @pl.when(pl.program_id(0) == 0)
    def _():
        for k in range(2):
            small[0][k : k + 1, :] = vector(early_ref, k, half)
            small[6 + k][...] = late_ref[k * 8 : k * 8 + 6, :]
        for k, (first, rows) in enumerate(((6, 6), (12, 6), (18, 6), (24, 12), (36, 6))):
            small[1 + k][...] = early_ref[first : first + rows, :]


def results(grads, grads_p, planes, layer_planes, early, late):
    half = ROWS // 2
    n = 8
    rows, width = planes.shape[1], planes.shape[0] * 128
    plane_spec = pl.BlockSpec((planes.shape[0], rows // n, 128), lambda i: (0, i, 0))
    small = [(2, half)] + [(n, 128) for n in (6, 6, 6, 12, 6, 6, 6)]
    whole_spec = lambda shape: pl.BlockSpec(shape, lambda i: (0, 0))
    row_spec = pl.BlockSpec((rows // n, width), lambda i: (i, 0))
    return pl.pallas_call(
        out_kernel,
        grid=(n,),
        out_shape=[
            jax.ShapeDtypeStruct((2 * ROWS, ROWS), F32),
            jax.ShapeDtypeStruct((ROWS, 2 * ROWS), F32),
            jax.ShapeDtypeStruct((3, ROWS, half), F32),
            jax.ShapeDtypeStruct((half, ROWS), F32),
            jax.ShapeDtypeStruct((rows, width), F32),
            jax.ShapeDtypeStruct((rows, width), F32),
        ]
        + [jax.ShapeDtypeStruct(shape, F32) for shape in small],
        in_specs=[
            pl.BlockSpec((2 * ROWS // n, ROWS), lambda i: (i, 0)),
            pl.BlockSpec((2, ROWS // n, ROWS), lambda i: (1, i, 0)),
            pl.BlockSpec((3, ROWS // n, half), lambda i: (0, i, 0)),
            pl.BlockSpec((1, half // n, half), lambda i: (3, i, 0)),
            pl.BlockSpec((1, half // n, half), lambda i: (3, n + i, 0)),
            plane_spec,
            plane_spec,
            whole_spec(early.shape),
            whole_spec(late.shape),
        ],
        out_specs=[
            pl.BlockSpec((2 * ROWS // n, ROWS), lambda i: (i, 0)),
            pl.BlockSpec((ROWS // n, 2 * ROWS), lambda i: (i, 0)),
            pl.BlockSpec((3, ROWS // n, half), lambda i: (0, i, 0)),
            pl.BlockSpec((half // n, ROWS), lambda i: (i, 0)),
            row_spec,
            row_spec,
        ]
        + [whole_spec(shape) for shape in small],
        name="results",
    )(grads.reshape(-1, ROWS), grads, grads_p, grads_p, grads_p, planes, layer_planes, early, late)


def body(
    tokens,
    cotangent,
    valid_tiles,
    gain_first,
    shift_first,
    w_project,
    bias_project,
    w_output,
    bias_output,
    gain_second,
    shift_second,
    w_expand,
    bias_expand,
    w_reduce,
    bias_reduce,
):
    w_project = w_project.transpose(1, 0, 2)
    by_rows = lambda value: value.reshape(-1, 128)
    queries, key_values, normed, tokens, stats = first_part(
        tokens, by_rows(valid_tiles), by_rows(gain_first), by_rows(shift_first), w_project, bias_project
    )
    fin, attended, w_out_other, *saved = attention_forward(queries, key_values, w_output)
    middle, grad_middle, grad_attended, ffn_part, shares, grads_o, small = middle_part(
        attended, w_output, w_out_other, tokens, cotangent, w_expand, w_reduce,
        by_rows(bias_output), by_rows(gain_second), by_rows(shift_second), by_rows(bias_expand),
    )
    g, g_sums, grads, ffn_other = attention_backward(
        queries, key_values, saved, fin, grad_attended, shares, ffn_part
    )
    planes, layer_planes, grads_p, early, late = last_part(
        g, w_project, normed, grads_o, small, g_sums, by_rows(gain_first), by_rows(bias_reduce),
        tokens, grad_middle, stats, middle, ffn_part, ffn_other,
    )
    (
        grad_w_reduce, grad_w_expand, grad_w_project, grad_w_output, grad_tokens, layer_out,
        grad_bias_project, grad_bias_output, grad_gain_second, grad_shift_second, grad_bias_expand, grad_bias_reduce,
        grad_gain_first, grad_shift_first,
    ) = results(grads, grads_p, planes, layer_planes, early, late)
    return (
        layer_out,
        grad_tokens,
        grad_gain_first.reshape(-1),
        grad_shift_first.reshape(-1),
        grad_w_project.transpose(1, 0, 2),
        grad_bias_project,
        grad_w_output,
        grad_bias_output.reshape(-1),
        grad_gain_second.reshape(-1),
        grad_shift_second.reshape(-1),
        grad_w_expand,
        grad_bias_expand.reshape(-1),
        grad_w_reduce,
        grad_bias_reduce.reshape(-1),
    )


def solution(mesh):
    in_specs = (
        P("seq", None),
        P("seq", None),
        P("seq"),
        P(),
        P(),
        P(None, None, "heads"),
        P(None, "heads"),
        P("heads", None),
        P(),
        P(),
        P(),
        P(None, "heads"),
        P("heads"),
        P("heads", None),
        P(),
    )
    out_specs = (
        P("seq", None),
        P("seq", None),
        P(),
        P(),
        P(None, None, "heads"),
        P(None, "heads"),
        P("heads", None),
        P(),
        P(),
        P(),
        P(None, "heads"),
        P("heads"),
        P("heads", None),
        P(),
    )
    return jax.shard_map(body, mesh=mesh, in_specs=in_specs, out_specs=out_specs, check_vma=False)
```
